128 devices in a mesh: slab: 16 (over z, x), level: 2 (over core), bottom: 4 (over y).
Axes of the slice: x: 4, y: 4, z: 4, core: 2. Of those that a mesh axis runs over, the one named last changes fastest.
Arguments:
- u_init: float32 [128, 32, 32, 128], P(('slab', 'level', 'bottom')), may hold values from -6 to 6
- source: float32 [128, 32, 32, 128], P(('slab', 'level', 'bottom')), may hold values from -10 to 13
- coeffs: float32 [128, 32, 32, 128], P(('slab', 'level', 'bottom')), may hold values from 0.01 to 1
- brick_map: int32 [16, 8], replicated, may hold values from 0 to 7, each once within a row
Outputs:
- solution: float32 [128, 32, 32, 128], P(('slab', 'level', 'bottom'))
The draws below stay inside these ranges and needn't reach their ends.
Inputs may be any that keep to these rules, and one draw needn't show every extreme that they name: `brick_map`: each row is a permutation of 0 to 7.
All inputs are finite; a program needn't handle non-finite values.
Results may differ from the reference program's by a relative error of at most 0.0003.
Values sent between devices are 32-bit elements; how exact they have to be, the bound alone decides.
No kernel may reach another device: no remote copies, remote signals or barrier semaphores. Data moves between devices by JAX's collectives and lax.ppermute only.
A program may use at most 128 MiB of HBM per device.

```python
import jax
import jax.numpy as jnp
from jax import lax

CZ = 32
CY = 32
CX = 128
SWEEPS_FINE = 2
SWEEPS_COARSE = 2
SWEEPS_BOTTOM = 8
SLABS = 16
DEVICES = 128


def draw_source(key, part):
    key = jax.random.fold_in(key, 11)
    rough_key, offset_key = jax.random.split(key)
    shape = (DEVICES, CZ, CY, CX)
    rough = jnp.clip(2.0 * jax.random.normal(rough_key, shape, jnp.float32), -10.0, 10.0)
    offset = jax.random.uniform(offset_key, (DEVICES, 1, 1, 1), jnp.float32, 0.5, 2.0)
    return jnp.clip(rough + offset, -10.0, 13.0).astype(jnp.float32)


def draw_coeffs(key, part):
    key = jax.random.fold_in(key, 23)
    cell_key, group_key = jax.random.split(key)
    shape = (DEVICES, CZ, CY, CX)
    group_scale = jnp.exp(jax.random.uniform(group_key, (DEVICES, 1, 1, 1), jnp.float32, jnp.log(0.02), jnp.log(0.5)))
    cell_scale = jnp.exp(jax.random.uniform(cell_key, shape, jnp.float32, jnp.log(0.5), jnp.log(2.0)))
    return jnp.clip(group_scale * cell_scale, 0.01, 1.0).astype(jnp.float32)


def steps_of(own_key, dims, shards, low, largest):
    level, own = 1.0, jax.random.fold_in(own_key, 6)
    for dim, shards_of in shards:
        steps = jnp.exp(jax.random.uniform(jax.random.fold_in(own, dim), (shards_of,), jnp.float32, low / len(shards), largest / len(shards)))
        level = level * jnp.repeat(steps, dims[dim] // shards_of).reshape([-1 if axis == dim else 1 for axis in range(len(dims))])
    return level


def centred(stream_key, extent, deviation, bound, pieces=(), kind=jnp.bfloat16):
    result = deviation * jax.random.normal(stream_key, extent, jnp.float32)
    if pieces:
        result = result * steps_of(stream_key, extent, pieces, -0.22, 0.18)
    return jnp.clip(result, -bound, bound).astype(kind)


def setup_inputs(seed: int = 0) -> dict:
    key_list = jax.random.split(jax.random.key(seed), 5)
    u_init = centred(key_list[0], (DEVICES, CZ, CY, CX), 1.0, 6.0, ((0, 128),), jnp.float32)
    source = draw_source(jax.random.fold_in(key_list[4], 71), 0)
    coeffs = draw_coeffs(jax.random.fold_in(key_list[4], 71), 0)
    brick_map = jax.vmap(lambda own: jax.random.permutation(own, 8))(jax.random.split(key_list[3], SLABS)).reshape((SLABS, 8)).astype(jnp.int32)
    return dict(u_init=u_init, source=source, coeffs=coeffs, brick_map=brick_map)


def neighbours(padded):
    total = padded[2:, 1:-1, 1:-1] + padded[:-2, 1:-1, 1:-1]
    total = total + padded[1:-1, 2:, 1:-1] + padded[1:-1, :-2, 1:-1]
    return total + padded[1:-1, 1:-1, 2:] + padded[1:-1, 1:-1, :-2]


def parity_mask(shape):
    total = lax.broadcasted_iota(jnp.int32, shape, 0) + lax.broadcasted_iota(jnp.int32, shape, 1)
    total = total + lax.broadcasted_iota(jnp.int32, shape, 2)
    return total % 2


def relax_colour(values, padded, forcing, diag_coef, inv_h2, colour):
    update = (forcing + inv_h2 * neighbours(padded)) / (diag_coef + 6.0 * inv_h2)
    return jnp.where(parity_mask(values.shape) == colour, update, values)


def apply_operator(values, padded, diag_coef, inv_h2):
    return diag_coef * values + inv_h2 * (6.0 * values - neighbours(padded))


def restrict(values):
    shaped = values.reshape(values.shape[0] // 2, 2, values.shape[1] // 2, 2, values.shape[2] // 2, 2)
    return shaped.mean(axis=(1, 3, 5))


def prolong(values):
    return jnp.repeat(jnp.repeat(jnp.repeat(values, 2, 0), 2, 1), 2, 2)


def smooth(values, forcing, diag_coef, inv_h2, sweeps):
    for repeat in range(sweeps):
        for colour in (0, 1):
            values = relax_colour(values, jnp.pad(values, 1), forcing, diag_coef, inv_h2, colour)
    return values


def assemble(blocks_in, brick_map):
    slabs = brick_map.shape[0]
    inner = blocks_in.shape[1:]
    blocks = blocks_in.reshape((slabs, 8) + inner)
    ordered = jax.vmap(lambda members, mapping: members[mapping])(blocks, brick_map)
    ordered = ordered.reshape((slabs, 2, 2, 2) + inner)
    ordered = ordered.transpose(0, 1, 4, 2, 5, 3, 6)
    return ordered.reshape(slabs * 2 * inner[0], 2 * inner[1], 2 * inner[2])


def disassemble(grid_cells, brick_map, inner):
    slabs = brick_map.shape[0]
    ordered = grid_cells.reshape(slabs, 2, inner[0], 2, inner[1], 2, inner[2])
    ordered = ordered.transpose(0, 1, 3, 5, 2, 4, 6).reshape((slabs, 8) + inner)
    inverse = jax.vmap(lambda mapping: jnp.zeros(8, jnp.int32).at[mapping].set(jnp.arange(8, dtype=jnp.int32)))(brick_map.astype(jnp.int32))
    blocks = jax.vmap(lambda members, mapping: members[mapping])(ordered, inverse)
    return blocks.reshape((slabs * 8,) + inner)


def reference(u_init, source, coeffs, brick_map):
    inner = u_init.shape[1:]
    values = assemble(u_init, brick_map)
    forcing = assemble(source, brick_map)
    diag_coef = assemble(coeffs, brick_map)
    coarse_coef = restrict(diag_coef)
    bottom_coef = restrict(coarse_coef)
    values = smooth(values, forcing, diag_coef, 1.0, SWEEPS_FINE)
    fine_resid = forcing - apply_operator(values, jnp.pad(values, 1), diag_coef, 1.0)
    coarse_rhs = restrict(fine_resid)
    coarse_err = smooth(jnp.zeros_like(coarse_rhs), coarse_rhs, coarse_coef, 0.25, SWEEPS_COARSE)
    coarse_resid = coarse_rhs - apply_operator(coarse_err, jnp.pad(coarse_err, 1), coarse_coef, 0.25)
    bottom_rhs = restrict(coarse_resid)
    bottom_err = smooth(jnp.zeros_like(bottom_rhs), bottom_rhs, bottom_coef, 0.0625, SWEEPS_BOTTOM)
    bottom_err = bottom_err - jnp.mean(bottom_err)
    coarse_err = coarse_err + prolong(bottom_err)
    coarse_err = smooth(coarse_err, coarse_rhs, coarse_coef, 0.25, SWEEPS_COARSE)
    values = values + prolong(coarse_err)
    values = smooth(values, forcing, diag_coef, 1.0, SWEEPS_FINE)
    return disassemble(values, brick_map, inner)
```

```python
import functools
import math

import jax
import jax.numpy as jnp
from jax import lax
from jax.experimental import pallas as pl
from jax.experimental.pallas import tpu as pltpu
from jax.sharding import PartitionSpec as P

LB = ("level", "bottom")
ALL = ("slab", "level", "bottom")
SLABS = 16
F32 = jnp.float32
VMEM_SPEC = pl.BlockSpec(memory_space=pltpu.VMEM)
SMEM_SPEC = pl.BlockSpec(memory_space=pltpu.SMEM)
EXACT = lax.Precision.HIGHEST


def run(kernel, outs, smem, vmem, scratch=()):
    shapes = [jax.ShapeDtypeStruct(s, F32) for s in outs]
    single = len(shapes) == 1
    return pl.pallas_call(
        kernel,
        out_shape=shapes[0] if single else shapes,
        in_specs=[SMEM_SPEC] * len(smem) + [VMEM_SPEC] * len(vmem),
        out_specs=VMEM_SPEC if single else [VMEM_SPEC] * len(shapes),
        scratch_shapes=[pltpu.VMEM(s, F32) for s in scratch],
        compiler_params=pltpu.CompilerParams(vmem_limit_bytes=50 << 20),
    )(*smem, *vmem)


def iota(shape, dim):
    return lax.broadcasted_iota(jnp.int32, shape, dim)


def odd(rows, cols):
    return ((iota((rows, cols), 0) + iota((rows, cols), 1)) & 1) == 1


def place_of(meta, bricks):
    slab, me = meta[0], meta[1]
    place = jnp.int32(0)
    for i in range(8):
        place = place + jnp.where(bricks[slab, i] == me, i, 0)
    return slab, me, place & 1, (place >> 1) & 1, place >> 2


def is_zero(scalar, shape=(8, 128)):
    return jnp.full(shape, scalar, jnp.int32) == 0


class Shell:
    def __init__(self, low, high, comps, arrays):
        self.low, self.high, self.comps, self.arrays = low, high, comps, arrays
        self.planes = math.ceil(len(low) / 4)
        self.nz = 4 * self.planes
        self.ny = 2 * len(comps)
        self.strips = 8 * arrays
        self.nx = math.ceil(self.strips / 16)
        self.sent = self.nz + self.ny + self.nx
        self.nz2 = 5 * self.planes
        self.y2 = self.nz2 + 1
        self.x2 = self.y2 + self.ny
        self.got = self.x2 + self.nx
        assert 5 * self.planes <= 16 and self.strips % 16 + self.ny <= 16


DOWN = Shell(
    [(0, 0), (0, 1), (0, 2)] + [(c, t) for c in (1, 2, 3, 4) for t in (0, 1)],
    [(0, 13), (0, 14), (0, 15)] + [(c, t) for c in (1, 2, 3, 4) for t in (14, 15)],
    [(0,), (1, 2), (3, 4)],
    5,
)
UP = Shell([(0, 0), (0, 1)], [(0, 14), (0, 15)], [(0,)], 1)


def merge_strips(strips, first=0, base=None):
    group = iota((8, 128), 1) // 8
    total = jnp.zeros((8, 128), F32) if base is None else base
    for i, strip in enumerate(strips):
        pos = first + i
        moved = pltpu.roll(strip, 8 * pos, 1) if pos else strip
        total = jnp.where(group == pos, moved, total)
    return total


def pack_shell(shell, get, out, bit_x, bit_y):
    row = iota((8, 128), 0)
    x0, y0 = is_zero(bit_x), is_zero(bit_y)
    for first, faces in ((0, shell.low), (4, shell.high)):
        for i, (c, t) in enumerate(faces):
            j = 4 * (i % shell.planes)
            out[first + i // shell.planes, j : j + 4] = get(c, t).reshape(4, 8, 128)
    for k in range(8):
        strips = []
        for tl in range(2):
            cells = [get(c, 2 * k + tl) for c in range(shell.arrays)]
            rows = [jnp.where(y0, v[24:32], v[0:8]) for v in cells]
            for ci, comp in enumerate(shell.comps):
                tile = rows[comp[0]]
                if len(comp) == 2:
                    red, black = rows[comp[0]], rows[comp[1]]
                    red = jnp.where(y0, pltpu.roll(red, 4, 0), red)
                    black = jnp.where(y0, black, pltpu.roll(black, 4, 0))
                    tile = jnp.where(row < 4, red, black)
                out[k, shell.nz + tl * len(shell.comps) + ci] = tile
            for v in cells:
                for g in range(4):
                    tile = v[8 * g : 8 * g + 8]
                    strips.append(jnp.where(x0, pltpu.roll(tile, 8, 1), tile))
        for i in range(shell.nx):
            out[k, shell.nz + shell.ny + i] = merge_strips(strips[16 * i : 16 * i + 16])


def cross_kernel(shell, meta, bricks, recv, out):
    slab, me = meta[0], meta[1]
    for i in range(4):
        src = jnp.where(me >= 4, bricks[slab, 4 + i], bricks[slab, i])
        out[i] = recv[src, 0 : shell.nz]


def mid_kernel(shell, meta, bricks, recv, cross, out, faces):
    slab, me = meta[0], meta[1]
    faces[0:8] = recv[:, 0 : shell.nz]
    faces[8:12] = cross[...]
    for p in range(8):
        bx, by, bz = p & 1, (p >> 1) & 1, p >> 2
        dest = bricks[slab, p]
        same = me >= 4 if bz else me < 4

        def src(q):
            return jnp.where(same, bricks[slab, (q & 3) + 4 * (1 - bz)], 8 + (q & 3))

        def strip_of(tile):
            return pltpu.roll(tile, 8, 1) if bx else tile

        at_own, at_y, at_x, at_xy = src(p), src(p ^ 2), src(p ^ 1), src(p ^ 3)
        gy = 3 if by else 0
        strips = []
        for j in range(shell.planes):
            out[dest, 5 * j : 5 * j + 4] = faces[at_own, 4 * j : 4 * j + 4]
            out[dest, 5 * j + 4] = faces[at_y, 4 * j + gy]
            strips += [strip_of(faces[at_x, 4 * j + g]) for g in range(4)]
            strips.append(strip_of(faces[at_xy, 4 * j + gy]))
        out[dest, shell.nz2] = merge_strips(strips)
        from_y, from_x, from_xy = bricks[slab, p ^ 2], bricks[slab, p ^ 1], bricks[slab, p ^ 3]
        y1 = shell.nz
        out[dest, shell.y2 : shell.x2] = recv[from_y, y1 : y1 + shell.ny]
        x1 = shell.nz + shell.ny
        if shell.nx > 1:
            out[dest, shell.x2 : shell.x2 + shell.nx - 1] = recv[from_x, x1 : x1 + shell.nx - 1]
        edge = [strip_of(recv[from_xy, y1 + i]) for i in range(shell.ny)]
        out[dest, shell.x2 + shell.nx - 1] = merge_strips(
            edge, shell.strips % 16, recv[from_x, x1 + shell.nx - 1]
        )


def unpack_shell(shell, recv, grids, bit_x, bit_y):
    row, lane = iota((8, 128), 0), iota((8, 128), 1)
    x0, y0 = is_zero(bit_x), is_zero(bit_y)
    in_x = (x0 & (lane < 8)) | (jnp.logical_not(x0) & (lane >= 120))
    in_y = (y0 & (row != 7)) | (jnp.logical_not(y0) & (row != 0))

    def strip(tile, pos):
        shift = (jnp.where(bit_x == 0, 0, 120) + 128 - 8 * pos) % 128
        return jnp.where(in_x, pltpu.roll(tile, shift, 1), 0.0)

    def split(comp, tile):
        if len(comp) == 1:
            return [tile]
        moved = pltpu.roll(tile, 4, 0)
        return [jnp.where(y0, tile, moved), jnp.where(y0, moved, tile)]

    for first, faces, shift in ((0, shell.low, 19), (4, shell.high, -13)):
        for i, (c, t) in enumerate(faces):
            k, j = first + i // shell.planes, i % shell.planes
            for g in range(5):
                tile, side = recv[k, 5 * j + g], strip(recv[k, shell.nz2], 5 * j + g)
                if g == 4:
                    tile, side = jnp.where(in_y, tile, 0.0), jnp.where(in_y, side, 0.0)
                grids[c][shift + t, 8 * g : 8 * g + 8, 0:128] = tile
                grids[c][shift + t, 8 * g : 8 * g + 8, 128:256] = side
    for t in range(16):
        k, tl = t // 2, t % 2
        for ci, comp in enumerate(shell.comps):
            i = tl * len(shell.comps) + ci
            tile = recv[k, shell.y2 + i]
            side = strip(recv[k, shell.x2 + shell.nx - 1], shell.strips % 16 + i)
            for c, one, two in zip(comp, split(comp, tile), split(comp, side)):
                grids[c][3 + t, 32:40, 0:128] = jnp.where(in_y, one, 0.0)
                grids[c][3 + t, 32:40, 128:256] = jnp.where(in_y, two, 0.0)
        for c in range(shell.arrays):
            for g in range(4):
                i = 4 * (tl * shell.arrays + c) + g
                grids[c][3 + t, 8 * g : 8 * g + 8, 128:256] = strip(recv[k, shell.x2 + i // 16], i % 16)


def pair_of(cells, t, red, mask):
    low, high = cells[0, 2 * t], cells[0, 2 * t + 1]
    return jnp.where(mask, high, low) if red else jnp.where(mask, low, high)


def first_kernel(meta, bricks, u, f, a, out):
    _, _, bit_x, bit_y, _ = place_of(meta, bricks)
    mask = odd(32, 128)
    sources = ((u, False), (f, True), (f, False), (a, True), (a, False))

    def get(c, t):
        return pair_of(sources[c][0], t, sources[c][1], mask)

    pack_shell(DOWN, get, out, bit_x, bit_y)


def around(src, k, red, mask, edges):
    here = src[k]
    rows, cols = here.shape
    above, below = src[k + 1], src[k - 1]
    other = jnp.where(mask, above, below) if red else jnp.where(mask, below, above)
    up, down = pltpu.roll(here, 1, 0), pltpu.roll(here, rows - 1, 0)
    left, right = pltpu.roll(here, 1, 1), pltpu.roll(here, cols - 1, 1)
    if edges:
        row, lane = iota((rows, cols), 0), iota((rows, cols), 1)
        up, down = jnp.where(row == 0, 0.0, up), jnp.where(row == rows - 1, 0.0, down)
        if edges == 2:
            left, right = jnp.where(lane == 0, 0.0, left), jnp.where(lane == cols - 1, 0.0, right)
    return ((here + other) + (up + down)) + (left + right)


def half_sweep(dst, src, force, inverse, lo, hi, red, mask, scale, edges, unroll=2):
    def step(k, carry):
        total = around(src, k, red, mask, edges)
        if scale != 1.0:
            total = scale * total
        dst[k] = (force[k] + total) * inverse[k]
        return carry

    lax.fori_loop(lo, hi, step, 0, unroll=unroll)


def pick(rows, cols, keep):
    return jnp.where(keep(iota((rows, cols), 0), iota((rows, cols), 1)), 1.0, 0.0).astype(F32)


def fine_down_kernel(meta, bricks, u, f, a, recv, rc, u_b, f_r, f_b, i_r, i_b, u_r, resid, small):
    slab, _, bit_x, bit_y, bit_z = place_of(meta, bricks)
    own = odd(32, 128)
    grids = (u_b, f_r, f_b, i_r, i_b)
    sources = ((u, False), (f, True), (f, False), (a, True), (a, False))
    for t in range(16):
        for grid, (cells, red) in zip(grids, sources):
            grid[3 + t, 0:32, 0:128] = pair_of(cells, t, red, own)
    unpack_shell(DOWN, recv, grids, bit_x, bit_y)
    u_r[0] = jnp.zeros((40, 256), F32)
    u_r[21] = jnp.zeros((40, 256), F32)
    row, lane = iota((40, 256), 0), iota((40, 256), 1)
    x0, y0 = is_zero(bit_x, (40, 256)), is_zero(bit_y, (40, 256))
    x1, y1 = jnp.logical_not(x0), jnp.logical_not(y0)
    inside = (row < 32) | (y0 & (row < 36)) | (y1 & (row >= 36))
    inside = inside & ((lane < 128) | (x0 & (lane < 136)) | (x1 & (lane >= 248)))
    no_low = (slab == 0) & (bit_z == 0)
    no_high = (slab == SLABS - 1) & (bit_z == 1)

    def invert(k, carry):
        gone = jnp.where((no_low & (k < 3)) | (no_high & (k >= 19)), 1, 0)
        keep = inside & is_zero(gone, (40, 256))
        i_r[k] = jnp.where(keep, 1.0 / (i_r[k] + 6.0), 0.0)
        i_b[k] = jnp.where(keep, 1.0 / (i_b[k] + 6.0), 0.0)
        return carry

    lax.fori_loop(1, 21, invert, 0)
    mask = odd(40, 256)
    for _ in range(2):
        half_sweep(u_r, u_b, f_r, i_r, 1, 21, True, mask, 1.0, 0)
        half_sweep(u_b, u_r, f_b, i_b, 1, 21, False, mask, 1.0, 0)
    for t in range(16):
        total = around(u_b, 3 + t, True, mask, 0)[0:32, 0:128]
        diag = pair_of(a, t, True, own) + 6.0
        resid[0, t] = pair_of(f, t, True, own) + total - diag * u_r[3 + t, 0:32, 0:128]
        resid[1, t] = a[0, 2 * t] + a[0, 2 * t + 1]
    twice = pick(128, 128, lambda r, c: (r >> 1) == (c & 63)) * 0.125
    row, lane = iota((16, 128), 0), iota((16, 128), 1)
    even = ((row + lane + (lane >> 6)) & 1) == 0
    for i in range(2):
        for t in range(16):
            small[16 * t : 16 * t + 16] = (
                resid[i, t, pl.ds(0, 16, stride=2), :] + resid[i, t, pl.ds(1, 16, stride=2), :]
            )
        summed = jnp.dot(small[...], twice, precision=EXACT, preferred_element_type=F32)
        summed = summed.reshape(16, 16, 128)
        for j in range(8):
            rc[i, j] = jnp.where(even, summed[2 * j], summed[2 * j + 1])


def up_pack_kernel(meta, bricks, u_b, out):
    _, _, bit_x, bit_y, _ = place_of(meta, bricks)
    pack_shell(UP, lambda c, t: u_b[3 + t, 0:32, 0:128], out, bit_x, bit_y)


def slot_of(member, me):
    return jnp.where((member >> 2) == (me >> 2), 0, 4) + ((me - member) & 3)


def faces_kernel(meta, bricks, *refs):
    boxes, (out, held) = refs[:8], refs[8:]
    slab, me = meta[0], meta[1]
    for i, box in enumerate(boxes):
        held[i] = box[...]
    start = jnp.where(me < 4, 3, 0)
    for i in range(4):
        member = jnp.where(me < 4, bricks[slab, 4 + i], bricks[slab, i])
        out[i] = held[slot_of(member, me), :, pl.ds(start, 5)]


def coarse_down_kernel(meta, bricks, *refs):
    boxes, (one, two) = refs[:8], refs[8:10]
    rb, rb_send, e_b, r_r, r_b, i_r, i_b = refs[10:17]
    held, low, high, e_r, a_r, a_b, resid, small = refs[17:]
    slab, me = meta[0], meta[1]
    for i, box in enumerate(boxes):
        held[i] = box[...]

    @pl.when(me < 4)
    def _():
        low[...] = one[...]
        high[...] = two[...]

    @pl.when(me >= 4)
    def _():
        low[...] = two[...]
        high[...] = one[...]

    left = iota((16, 128), 1) < 64
    for q, (red, black) in enumerate(((r_r, r_b), (a_r, a_b))):

        def put(k, by, west, east):
            rows = slice(16 * by, 16 * by + 16)
            red[k, rows] = jnp.where(left, west, pltpu.roll(east, 64, 1))
            black[k, rows] = jnp.where(left, pltpu.roll(west, 64, 1), east)

        for by in range(2):
            for bz in range(2):
                west = slot_of(bricks[slab, 2 * by + 4 * bz], me)
                east = slot_of(bricks[slab, 2 * by + 4 * bz + 1], me)
                for j in range(8):
                    put(6 + 8 * bz + j, by, held[west, q, j], held[east, q, j])
            for j in range(5):
                put(1 + j, by, low[2 * by, q, j], low[2 * by + 1, q, j])
                put(22 + j, by, high[2 * by, q, j], high[2 * by + 1, q, j])
    for k in (0, 27):
        e_r[k] = jnp.zeros((32, 128), F32)
        e_b[k] = jnp.zeros((32, 128), F32)

    def start(k, carry):
        gone = jnp.where(((slab == 0) & (k < 6)) | ((slab == SLABS - 1) & (k >= 22)), 1, 0)
        keep = is_zero(gone, (32, 128))
        inverse = jnp.where(keep, 1.0 / (a_r[k] + 1.5), 0.0)
        i_r[k] = inverse
        i_b[k] = jnp.where(keep, 1.0 / (a_b[k] + 1.5), 0.0)
        e_r[k] = r_r[k] * inverse
        return carry

    lax.fori_loop(1, 27, start, 0)
    mask = odd(32, 128)
    half_sweep(e_b, e_r, r_b, i_b, 1, 27, False, mask, 0.25, 2)
    half_sweep(e_r, e_b, r_r, i_r, 1, 27, True, mask, 0.25, 2)
    half_sweep(e_b, e_r, r_b, i_b, 1, 27, False, mask, 0.25, 2)

    def residual(n, carry):
        k = n + 3
        total = 0.25 * around(e_b, k, True, mask, 2)
        resid[0, n] = r_r[k] + total - (a_r[k] + 1.5) * e_r[k]
        resid[1, n] = a_r[k] + a_b[k]
        return carry

    lax.fori_loop(0, 22, residual, 0, unroll=2)
    total = jnp.zeros((352, 128), F32)
    for i in range(2):
        for n in range(22):
            small[16 * n : 16 * n + 16] = (
                resid[i, n, pl.ds(0, 16, stride=2), :] + resid[i, n, pl.ds(1, 16, stride=2), :]
            )
        half = pick(128, 128, lambda r, c: (r >> 1) == c - 64 * i) * 0.125
        total = total + jnp.dot(small[...], half, precision=EXACT, preferred_element_type=F32)
    rb[...] = total.reshape(22, 16, 128)
    rb_send[...] = rb[pl.ds(jnp.where(me < 4, 1, 3), 18)]


def bottom_kernel(meta, rb, one, two, es, part, e_r, e_b, g_r, g_b, i_r, i_b, low, high):
    slab, me = meta[0], meta[1]

    @pl.when(me < 4)
    def _():
        low[...] = one[...]
        high[...] = two[...]

    @pl.when(me >= 4)
    def _():
        low[...] = two[...]
        high[...] = one[...]

    mask = odd(16, 128)
    left = iota((16, 128), 1) < 64
    zero = jnp.zeros((16, 128), F32)
    for k in (0, 27):
        e_r[k] = zero
        e_b[k] = zero
    for j in range(26):
        planes = []
        for n in (2 * j, 2 * j + 1):
            planes.append(low[n] if n < 18 else rb[n - 15] if n < 34 else high[n - 34])
        keep = left
        if j < 9:
            keep = left & jnp.logical_not(is_zero(slab, (16, 128)))
        if j >= 17:
            keep = left & jnp.logical_not(is_zero(slab - (SLABS - 1), (16, 128)))
        for red in (True, False):
            cells = jnp.where(mask, planes[1], planes[0]) if red else jnp.where(mask, planes[0], planes[1])
            force = jnp.where(left, cells, 0.0)
            inverse = jnp.where(keep, 1.0 / (pltpu.roll(cells, 64, 1) + 0.375), 0.0)
            if red:
                g_r[1 + j], i_r[1 + j], e_r[1 + j] = force, inverse, force * inverse
            else:
                g_b[1 + j], i_b[1 + j] = force, inverse
    half_sweep(e_b, e_r, g_b, i_b, 1, 27, False, mask, 0.0625, 1, unroll=True)

    def sweep(n, carry):
        half_sweep(e_r, e_b, g_r, i_r, 1, 27, True, mask, 0.0625, 1, unroll=True)
        half_sweep(e_b, e_r, g_b, i_b, 1, 27, False, mask, 0.0625, 1, unroll=True)
        return carry

    lax.fori_loop(0, 7, sweep, 0)
    for i in range(22):
        k, upper = (15 + i) // 2 + 1, (15 + i) % 2
        es[i] = jnp.where(mask, e_r[k], e_b[k]) if upper else jnp.where(mask, e_b[k], e_r[k])
    total = zero
    for k in range(10, 18):
        total = total + (e_r[k] + e_b[k])
    total = total[0:8] + total[8:16]
    for i in range(SLABS):
        part[i] = total


def up_kernel(
    meta, bricks, sums, es, ec_b, r_r, r_b, ci_r, ci_b, u1_b, f_r, f_b, i_r, i_b, recv, out,
    e_r, e_b, small, wide, planes, tall, u_r, u_b,
):
    slab, _, bit_x, bit_y, bit_z = place_of(meta, bricks)
    total = sums[0]
    for i in range(1, SLABS):
        total = total + sums[i]
    mean = jnp.sum(total) * (1.0 / (SLABS * 16 * 16 * 64))
    for i in range(22):
        shifted = es[i] - mean
        if i < 3:
            shifted = jnp.where(is_zero(slab, (16, 128)), 0.0, shifted)
        if i >= 19:
            shifted = jnp.where(is_zero(slab - (SLABS - 1), (16, 128)), 0.0, shifted)
        small[16 * i : 16 * i + 16] = shifted
    spread = pick(128, 128, lambda r, c: r == (c >> 1))
    small[...] = jnp.dot(small[...], spread, precision=EXACT, preferred_element_type=F32)
    for i in range(22):
        rows = small[16 * i : 16 * i + 16]
        wide[i, pl.ds(0, 16, stride=2), :] = rows
        wide[i, pl.ds(1, 16, stride=2), :] = rows
    for k in (0, 1, 2, 25, 26, 27):
        e_r[k] = jnp.zeros((32, 128), F32)
        e_b[k] = jnp.zeros((32, 128), F32)
    for i in range(22):
        e_b[3 + i] = ec_b[3 + i] + wide[i]
    coarse = odd(32, 128)
    for _ in range(2):
        half_sweep(e_r, e_b, r_r, ci_r, 3, 25, True, coarse, 0.25, 2)
        half_sweep(e_b, e_r, r_b, ci_b, 3, 25, False, coarse, 0.25, 2)
    for n in range(20):
        z = n - 2
        k = 8 * bit_z + (z // 2 + 6)
        red, black = e_r[k], e_b[k]
        planes[32 * n : 32 * n + 32] = jnp.where(coarse, red, black) if z % 2 else jnp.where(coarse, black, red)

    lane = iota((128, 256), 1)
    x0 = is_zero(bit_x, (128, 256))
    start = jnp.where(lane < 128, 64 * bit_x + (lane >> 1), (lane >> 1) + jnp.where(x0, 0, -64))
    usable = (lane < 128) | (x0 & (lane < 136)) | (jnp.logical_not(x0) & (lane >= 248))
    spread = jnp.where(usable & (iota((128, 256), 0) == start), 1.0, 0.0).astype(F32)
    tall_rows = jnp.dot(planes[...], spread, precision=EXACT, preferred_element_type=F32)
    for n in range(20):
        rows = tall_rows[32 * n : 32 * n + 32]
        for h in range(2):
            tall[n, h, pl.ds(0, 32, stride=2), :] = rows[:, 128 * h : 128 * h + 128]
            tall[n, h, pl.ds(1, 32, stride=2), :] = rows[:, 128 * h : 128 * h + 128]
    u_b[...] = u1_b[...]
    unpack_shell(UP, recv, (u_b,), bit_x, bit_y)
    for k in (0, 21):
        u_r[k] = jnp.zeros((40, 256), F32)
        u_b[k] = jnp.zeros((40, 256), F32)
    row = iota((8, 128), 0)
    y0 = is_zero(bit_y)
    in_y = (y0 & (row != 7)) | (jnp.logical_not(y0) & (row != 0))
    own_start = pl.multiple_of(32 * bit_y, 32)
    side_start = pl.multiple_of(32 - 8 * bit_y, 8)
    for n in range(20):
        for h in range(2):
            lanes = slice(128 * h, 128 * h + 128)
            side = jnp.where(in_y, tall[n, h, pl.ds(side_start, 8), :], 0.0)
            u_b[1 + n, 0:32, lanes] = u_b[1 + n, 0:32, lanes] + tall[n, h, pl.ds(own_start, 32), :]
            u_b[1 + n, 32:40, lanes] = u_b[1 + n, 32:40, lanes] + side
    mask = odd(40, 256)
    for _ in range(2):
        half_sweep(u_r, u_b, f_r, i_r, 1, 21, True, mask, 1.0, 0)
        half_sweep(u_b, u_r, f_b, i_b, 1, 21, False, mask, 1.0, 0)
    own = odd(32, 128)
    for t in range(16):
        red, black = u_r[3 + t, 0:32, 0:128], u_b[3 + t, 0:32, 0:128]
        out[0, 2 * t] = jnp.where(own, black, red)
        out[0, 2 * t + 1] = jnp.where(own, red, black)


def swap_cores(x):
    return lax.ppermute(x, "level", [(0, 1), (1, 0)])


def to_slabs(x, up_first):
    pairs = []
    for s in range(SLABS - 1):
        for m in range(8):
            low, high = s * 8 + m, (s + 1) * 8 + m
            pairs.append((low, high) if (m < 4) == up_first else (high, low))
    return lax.ppermute(x, ALL, pairs)


def exchange(shell, packed, smem):
    got = lax.all_to_all(packed, LB, split_axis=0, concat_axis=0, tiled=True)
    leaving = run(functools.partial(cross_kernel, shell), [(4, shell.nz, 8, 128)], smem, [got])
    cross = to_slabs(leaving, False)
    sent = run(
        functools.partial(mid_kernel, shell), [(8, shell.got, 8, 128)], smem, [got, cross],
        [(12, shell.nz, 8, 128)],
    )
    return lax.all_to_all(sent, LB, split_axis=0, concat_axis=0, tiled=True)


def body(u_init, source, coeffs, brick_map):
    meta = jnp.stack([lax.axis_index("slab"), lax.axis_index(LB)]).astype(jnp.int32)
    smem = [meta, brick_map]
    fine = (22, 40, 256)
    packed = run(first_kernel, [(8, DOWN.sent, 8, 128)], smem, [u_init, source, coeffs])
    halo = exchange(DOWN, packed, smem)
    rc, u_b, f_r, f_b, i_r, i_b = run(
        fine_down_kernel, [(2, 8, 16, 128)] + [fine] * 5, smem, [u_init, source, coeffs, halo],
        [fine, (2, 16, 32, 128), (256, 128)],
    )
    boxes = [rc] + [
        lax.ppermute(rc, "bottom", [(i, (i + d) % 4) for i in range(4)]) for d in range(1, 4)
    ]
    boxes = boxes + [swap_cores(box) for box in boxes]
    leaving = run(faces_kernel, [(4, 2, 5, 16, 128)], smem, boxes, [(8, 2, 8, 16, 128)])
    cross = to_slabs(leaving, True)
    other = swap_cores(cross)
    coarse = (28, 32, 128)
    faces = (4, 2, 5, 16, 128)
    rb, rb_send, ec_b, r_r, r_b, ci_r, ci_b = run(
        coarse_down_kernel, [(22, 16, 128), (18, 16, 128)] + [coarse] * 5, smem, boxes + [cross, other],
        [(8, 2, 8, 16, 128), faces, faces, coarse, coarse, coarse, (2, 22, 32, 128), (352, 128)],
    )
    packed = run(up_pack_kernel, [(8, UP.sent, 8, 128)], smem, [u_b])
    up_halo = exchange(UP, packed, smem)
    cross = to_slabs(rb_send, True)
    other = swap_cores(cross)
    bottom = (28, 16, 128)
    es, part = run(
        bottom_kernel, [(22, 16, 128), (SLABS, 8, 128)], [meta], [rb, cross, other],
        [bottom] * 6 + [(18, 16, 128)] * 2,
    )
    sums = lax.all_to_all(part, "slab", split_axis=0, concat_axis=0, tiled=True)
    return run(
        up_kernel, [(1, 32, 32, 128)], smem,
        [sums, es, ec_b, r_r, r_b, ci_r, ci_b, u_b, f_r, f_b, i_r, i_b, up_halo],
        [coarse, coarse, (352, 128), (22, 32, 128), (640, 128), (20, 2, 64, 128), fine, fine],
    )


def solution(mesh):
    placed = P(ALL, None, None, None)
    return jax.shard_map(
        body, mesh=mesh, in_specs=(placed, placed, placed, P()), out_specs=placed, check_vma=False
    )
```

```python
import functools
import math

import jax
import jax.numpy as jnp
from jax import lax
from jax.experimental import pallas as pl
from jax.experimental.pallas import tpu as pltpu
from jax.sharding import PartitionSpec as P

LB = ("level", "bottom")
ALL = ("slab", "level", "bottom")
SLABS = 16
OWN = 5
F32 = jnp.float32
VMEM_SPEC = pl.BlockSpec(memory_space=pltpu.VMEM)
SMEM_SPEC = pl.BlockSpec(memory_space=pltpu.SMEM)
EXACT = lax.Precision.HIGHEST


def run(kernel, outs, smem, vmem, scratch=()):
    shapes = [jax.ShapeDtypeStruct(s, F32) for s in outs]
    single = len(shapes) == 1
    return pl.pallas_call(
        kernel,
        out_shape=shapes[0] if single else shapes,
        in_specs=[SMEM_SPEC] * len(smem) + [VMEM_SPEC] * len(vmem),
        out_specs=VMEM_SPEC if single else [VMEM_SPEC] * len(shapes),
        scratch_shapes=[pltpu.VMEM(s, F32) for s in scratch],
        compiler_params=pltpu.CompilerParams(vmem_limit_bytes=50 << 20),
    )(*smem, *vmem)


def iota(shape, dim):
    return lax.broadcasted_iota(jnp.int32, shape, dim)


def odd(rows, cols):
    return ((iota((rows, cols), 0) + iota((rows, cols), 1)) & 1) == 1


def place_of(meta, bricks):
    slab, me = meta[0], meta[1]
    place = jnp.int32(0)
    for i in range(8):
        place = place + jnp.where(bricks[slab, i] == me, i, 0)
    return slab, me, place & 1, (place >> 1) & 1, place >> 2


def is_zero(scalar, shape=(8, 128)):
    return jnp.full(shape, scalar, jnp.int32) == 0


class Shell:
    def __init__(self, low, high, arrays):
        self.low, self.high, self.arrays = low, high, arrays
        self.planes = math.ceil(len(low) / 4)
        self.nz = 4 * self.planes
        self.ny = 2 * arrays
        self.strips = 8 * arrays
        self.nx = math.ceil(self.strips / 16)
        self.sent = self.nz + self.ny + self.nx
        self.nz2 = 5 * self.planes
        self.side = math.ceil(self.nz2 / 16)
        self.y2 = self.nz2 + self.side
        self.x2 = self.y2 + self.ny
        self.got = self.x2 + self.nx
        self.first = min(16 * self.side - self.nz2, self.ny)
        assert self.strips + self.ny - self.first <= 16 * self.nx

    def edge(self, i):
        if i < self.first:
            pos = self.nz2 + i
            return self.nz2 + pos // 16, pos % 16
        pos = self.strips + i - self.first
        return self.x2 + pos // 16, pos % 16


DOWN = Shell(
    [(c, t) for c in (0, 1, 3) for t in range(4)] + [(c, t) for c in (2, 4) for t in range(3)],
    [(c, 15 - t) for c in (0, 1, 3) for t in range(4)] + [(c, 15 - t) for c in (2, 4) for t in range(3)],
    5,
)


def merge_strips(placed, base=None):
    group = iota((8, 128), 1) // 8
    total = jnp.zeros((8, 128), F32) if base is None else base
    for pos, strip in placed:
        moved = pltpu.roll(strip, 8 * pos, 1) if pos else strip
        total = jnp.where(group == pos, moved, total)
    return total


def pack_shell(shell, get, out, bit_x, bit_y):
    x0, y0 = is_zero(bit_x), is_zero(bit_y)
    for first, faces in ((0, shell.low), (4, shell.high)):
        for i, (c, t) in enumerate(faces):
            j = 4 * (i % shell.planes)
            out[first + i // shell.planes, j : j + 4] = get(c, t).reshape(4, 8, 128)
    for k in range(8):
        strips = []
        for tl in range(2):
            for c in range(shell.arrays):
                v = get(c, 2 * k + tl)
                out[k, shell.nz + tl * shell.arrays + c] = jnp.where(y0, v[24:32], v[0:8])
                for g in range(4):
                    tile = v[8 * g : 8 * g + 8]
                    strips.append(jnp.where(x0, pltpu.roll(tile, 8, 1), tile))
        for i in range(shell.nx):
            out[k, shell.nz + shell.ny + i] = merge_strips(list(enumerate(strips[16 * i : 16 * i + 16])))


def cross_kernel(shell, meta, bricks, recv, out):
    slab, me = meta[0], meta[1]
    for i in range(4):
        src = jnp.where(me >= 4, bricks[slab, 4 + i], bricks[slab, i])
        out[i] = recv[src, 0 : shell.nz]


def mid_kernel(shell, meta, bricks, recv, cross, out, faces):
    slab, me = meta[0], meta[1]
    faces[0:8] = recv[:, 0 : shell.nz]
    faces[8:12] = cross[...]
    for p in range(8):
        bx, by, bz = p & 1, (p >> 1) & 1, p >> 2
        dest = bricks[slab, p]
        same = me >= 4 if bz else me < 4

        def src(q):
            return jnp.where(same, bricks[slab, (q & 3) + 4 * (1 - bz)], 8 + (q & 3))

        def strip_of(tile):
            return pltpu.roll(tile, 8, 1) if bx else tile

        at_own, at_y, at_x, at_xy = src(p), src(p ^ 2), src(p ^ 1), src(p ^ 3)
        gy = 3 if by else 0
        strips = []
        for j in range(shell.planes):
            out[dest, 5 * j : 5 * j + 4] = faces[at_own, 4 * j : 4 * j + 4]
            out[dest, 5 * j + 4] = faces[at_y, 4 * j + gy]
            strips += [strip_of(faces[at_x, 4 * j + g]) for g in range(4)]
            strips.append(strip_of(faces[at_xy, 4 * j + gy]))
        from_y, from_x, from_xy = bricks[slab, p ^ 2], bricks[slab, p ^ 1], bricks[slab, p ^ 3]
        y1, x1 = shell.nz, shell.nz + shell.ny
        out[dest, shell.y2 : shell.x2] = recv[from_y, y1:x1]
        placed = {}
        for i, strip in enumerate(strips):
            placed.setdefault(shell.nz2 + i // 16, []).append((i % 16, strip))
        for i in range(shell.ny):
            tile, pos = shell.edge(i)
            placed.setdefault(tile, []).append((pos, strip_of(recv[from_xy, y1 + i])))
        for i in range(shell.nx):
            tile = recv[from_x, x1 + i]
            out[dest, shell.x2 + i] = merge_strips(placed.get(shell.x2 + i, []), tile)
        for i in range(shell.side):
            out[dest, shell.nz2 + i] = merge_strips(placed[shell.nz2 + i])


def unpack_shell(shell, recv, grids, bit_x):
    lane = iota((8, 128), 1)
    x0 = is_zero(bit_x)
    in_x = (x0 & (lane < 8)) | (jnp.logical_not(x0) & (lane >= 120))

    def strip(tile, pos):
        shift = (jnp.where(bit_x == 0, 0, 120) + 128 - 8 * pos) % 128
        return jnp.where(in_x, pltpu.roll(tile, shift, 1), 0.0)

    for first, faces, shift in ((0, shell.low, OWN + 16), (4, shell.high, OWN - 16)):
        for i, (c, t) in enumerate(faces):
            k, j = first + i // shell.planes, i % shell.planes
            for g in range(5):
                n = 5 * j + g
                rows = slice(8 * g, 8 * g + 8)
                grids[c][shift + t, rows, 0:128] = recv[k, n]
                grids[c][shift + t, rows, 128:256] = strip(recv[k, shell.nz2 + n // 16], n % 16)
    for t in range(16):
        k, tl = t // 2, t % 2
        for c in range(shell.arrays):
            i = tl * shell.arrays + c
            tile, pos = shell.edge(i)
            grids[c][OWN + t, 32:40, 0:128] = recv[k, shell.y2 + i]
            grids[c][OWN + t, 32:40, 128:256] = strip(recv[k, tile], pos)
            for g in range(4):
                n = 4 * i + g
                grids[c][OWN + t, 8 * g : 8 * g + 8, 128:256] = strip(recv[k, shell.x2 + n // 16], n % 16)


def pair_of(cells, t, red, mask):
    low, high = cells[0, 2 * t], cells[0, 2 * t + 1]
    return jnp.where(mask, high, low) if red else jnp.where(mask, low, high)


def first_kernel(meta, bricks, u, f, a, out):
    _, _, bit_x, bit_y, _ = place_of(meta, bricks)
    mask = odd(32, 128)
    sources = ((u, False), (f, True), (f, False), (a, True), (a, False))

    def get(c, t):
        return pair_of(sources[c][0], t, sources[c][1], mask)

    pack_shell(DOWN, get, out, bit_x, bit_y)


def around(src, k, red, mask, edges, cut=None):
    here = src[k]
    rows, cols = here.shape
    above, below = src[k + 1], src[k - 1]
    other = jnp.where(mask, above, below) if red else jnp.where(mask, below, above)
    up, down = pltpu.roll(here, 1, 0), pltpu.roll(here, rows - 1, 0)
    left, right = pltpu.roll(here, 1, 1), pltpu.roll(here, cols - 1, 1)
    if edges:
        row, lane = iota((rows, cols), 0), iota((rows, cols), 1)
        up, down = jnp.where(row == 0, 0.0, up), jnp.where(row == rows - 1, 0.0, down)
        if edges == 2:
            left, right = jnp.where(lane == 0, 0.0, left), jnp.where(lane == cols - 1, 0.0, right)
    if cut is not None:
        up, down = jnp.where(cut[0], 0.0, up), jnp.where(cut[1], 0.0, down)
    return ((here + other) + (up + down)) + (left + right)


def half_sweep(dst, src, force, inverse, lo, hi, red, mask, scale, edges, cut=None):
    def step(k, carry):
        total = around(src, k, red, mask, edges, cut)
        if scale != 1.0:
            total = scale * total
        dst[k] = (force[k] + total) * inverse[k]
        return carry

    lax.fori_loop(lo, hi, step, 0, unroll=True)


def pick(rows, cols, keep):
    return jnp.where(keep(iota((rows, cols), 0), iota((rows, cols), 1)), 1.0, 0.0).astype(F32)


def fine_down_kernel(meta, bricks, u, f, a, recv, rc, u_b, f_r, f_b, i_r, i_b, u_r, resid, small):
    slab, _, bit_x, bit_y, bit_z = place_of(meta, bricks)
    own = odd(32, 128)
    grids = (u_b, f_r, f_b, i_r, i_b)
    sources = ((u, False), (f, True), (f, False), (a, True), (a, False))
    for t in range(16):
        for grid, (cells, red) in zip(grids, sources):
            grid[OWN + t, 0:32, 0:128] = pair_of(cells, t, red, own)
    unpack_shell(DOWN, recv, grids, bit_x)
    zero = jnp.zeros((40, 256), F32)
    for k in (0, 25):
        u_r[k] = zero
        u_b[k] = zero
    for k in (1, 24):
        f_b[k] = zero
        i_b[k] = zero
    row, lane = iota((40, 256), 0), iota((40, 256), 1)
    x0, y0 = is_zero(bit_x, (40, 256)), is_zero(bit_y, (40, 256))
    x1, y1 = jnp.logical_not(x0), jnp.logical_not(y0)
    inside = (row < 32) | (y0 & (row < 39)) | (y1 & (row >= 33))
    inside = inside & ((lane < 128) | (x0 & (lane < 136)) | (x1 & (lane >= 248)))
    no_low = (slab == 0) & (bit_z == 0)
    no_high = (slab == SLABS - 1) & (bit_z == 1)

    def invert(k, carry):
        gone = jnp.where((no_low & (k < OWN)) | (no_high & (k >= OWN + 16)), 1, 0)
        keep = inside & is_zero(gone, (40, 256))
        i_r[k] = jnp.where(keep, 1.0 / (i_r[k] + 6.0), 0.0)
        ends = jnp.where((k == 1) | (k == 24), 1, 0)
        i_b[k] = jnp.where(keep & is_zero(ends, (40, 256)), 1.0 / (i_b[k] + 6.0), 0.0)
        return carry

    lax.fori_loop(1, 25, invert, 0, unroll=4)
    mask = odd(40, 256)
    cut = (y0 & (row == 0), y1 & (row == 31))
    half_sweep(u_r, u_b, f_r, i_r, 1, 25, True, mask, 1.0, 0, cut)
    half_sweep(u_b, u_r, f_b, i_b, 1, 25, False, mask, 1.0, 0)
    half_sweep(u_r, u_b, f_r, i_r, 2, 24, True, mask, 1.0, 0)
    half_sweep(u_b, u_r, f_b, i_b, 3, 23, False, mask, 1.0, 0)
    for t in range(16):
        total = around(u_b, OWN + t, True, mask, 0)[0:32, 0:128]
        diag = pair_of(a, t, True, own) + 6.0
        resid[0, t] = pair_of(f, t, True, own) + total - diag * u_r[OWN + t, 0:32, 0:128]
        resid[1, t] = a[0, 2 * t] + a[0, 2 * t + 1]
    twice = pick(128, 128, lambda r, c: (r >> 1) == (c & 63)) * 0.125
    row, lane = iota((16, 128), 0), iota((16, 128), 1)
    even = ((row + lane + (lane >> 6)) & 1) == 0
    for i in range(2):
        for t in range(16):
            small[16 * t : 16 * t + 16] = (
                resid[i, t, pl.ds(0, 16, stride=2), :] + resid[i, t, pl.ds(1, 16, stride=2), :]
            )
        summed = jnp.dot(small[...], twice, precision=EXACT, preferred_element_type=F32)
        summed = summed.reshape(16, 16, 128)
        for j in range(8):
            rc[i, j] = jnp.where(even, summed[2 * j], summed[2 * j + 1])


def slot_of(member, me):
    return jnp.where((member >> 2) == (me >> 2), 0, 4) + ((me - member) & 3)


def faces_kernel(meta, bricks, *refs):
    boxes, (out, held) = refs[:8], refs[8:]
    slab, me = meta[0], meta[1]
    for i, box in enumerate(boxes):
        held[i] = box[...]
    start = jnp.where(me < 4, 3, 0)
    for i in range(4):
        member = jnp.where(me < 4, bricks[slab, 4 + i], bricks[slab, i])
        out[i] = held[slot_of(member, me), :, pl.ds(start, 5)]


def coarse_down_kernel(meta, bricks, *refs):
    boxes, (one, two) = refs[:8], refs[8:10]
    rb, rb_send, e_b, r_r, r_b, i_r, i_b = refs[10:17]
    held, low, high, e_r, a_r, a_b, resid, small = refs[17:]
    slab, me = meta[0], meta[1]
    for i, box in enumerate(boxes):
        held[i] = box[...]

    @pl.when(me < 4)
    def _():
        low[...] = one[...]
        high[...] = two[...]

    @pl.when(me >= 4)
    def _():
        low[...] = two[...]
        high[...] = one[...]

    left = iota((16, 128), 1) < 64
    for q, (red, black) in enumerate(((r_r, r_b), (a_r, a_b))):

        def put(k, by, west, east):
            rows = slice(16 * by, 16 * by + 16)
            red[k, rows] = jnp.where(left, west, pltpu.roll(east, 64, 1))
            black[k, rows] = jnp.where(left, pltpu.roll(west, 64, 1), east)

        for by in range(2):
            for bz in range(2):
                west = slot_of(bricks[slab, 2 * by + 4 * bz], me)
                east = slot_of(bricks[slab, 2 * by + 4 * bz + 1], me)
                for j in range(8):
                    put(6 + 8 * bz + j, by, held[west, q, j], held[east, q, j])
            for j in range(5):
                put(1 + j, by, low[2 * by, q, j], low[2 * by + 1, q, j])
                put(22 + j, by, high[2 * by, q, j], high[2 * by + 1, q, j])
    for k in (0, 27):
        e_r[k] = jnp.zeros((32, 128), F32)
        e_b[k] = jnp.zeros((32, 128), F32)

    def start(k, carry):
        gone = jnp.where(((slab == 0) & (k < 6)) | ((slab == SLABS - 1) & (k >= 22)), 1, 0)
        keep = is_zero(gone, (32, 128))
        inverse = jnp.where(keep, 1.0 / (a_r[k] + 1.5), 0.0)
        i_r[k] = inverse
        i_b[k] = jnp.where(keep, 1.0 / (a_b[k] + 1.5), 0.0)
        e_r[k] = r_r[k] * inverse
        return carry

    lax.fori_loop(1, 27, start, 0, unroll=13)
    mask = odd(32, 128)
    half_sweep(e_b, e_r, r_b, i_b, 1, 27, False, mask, 0.25, 2)
    half_sweep(e_r, e_b, r_r, i_r, 1, 27, True, mask, 0.25, 2)
    half_sweep(e_b, e_r, r_b, i_b, 1, 27, False, mask, 0.25, 2)

    def residual(n, carry):
        k = n + 3
        total = 0.25 * around(e_b, k, True, mask, 2)
        resid[0, n] = r_r[k] + total - (a_r[k] + 1.5) * e_r[k]
        resid[1, n] = a_r[k] + a_b[k]
        return carry

    lax.fori_loop(0, 22, residual, 0, unroll=True)
    total = jnp.zeros((352, 128), F32)
    for i in range(2):
        for n in range(22):
            small[16 * n : 16 * n + 16] = (
                resid[i, n, pl.ds(0, 16, stride=2), :] + resid[i, n, pl.ds(1, 16, stride=2), :]
            )
        half = pick(128, 128, lambda r, c: (r >> 1) == c - 64 * i) * 0.125
        total = total + jnp.dot(small[...], half, precision=EXACT, preferred_element_type=F32)
    rb[...] = total.reshape(22, 16, 128)
    rb_send[...] = rb[pl.ds(jnp.where(me < 4, 1, 3), 18)]


def bottom_kernel(meta, rb, one, two, es, part, e_r, e_b, g_r, g_b, i_r, i_b, low, high):
    slab, me = meta[0], meta[1]

    @pl.when(me < 4)
    def _():
        low[...] = one[...]
        high[...] = two[...]

    @pl.when(me >= 4)
    def _():
        low[...] = two[...]
        high[...] = one[...]

    mask = odd(16, 128)
    left = iota((16, 128), 1) < 64
    zero = jnp.zeros((16, 128), F32)
    for k in (0, 27):
        e_r[k] = zero
        e_b[k] = zero
    for j in range(26):
        planes = []
        for n in (2 * j, 2 * j + 1):
            planes.append(low[n] if n < 18 else rb[n - 15] if n < 34 else high[n - 34])
        keep = left
        if j < 9:
            keep = left & jnp.logical_not(is_zero(slab, (16, 128)))
        if j >= 17:
            keep = left & jnp.logical_not(is_zero(slab - (SLABS - 1), (16, 128)))
        for red in (True, False):
            cells = jnp.where(mask, planes[1], planes[0]) if red else jnp.where(mask, planes[0], planes[1])
            force = jnp.where(left, cells, 0.0)
            inverse = jnp.where(keep, 1.0 / (pltpu.roll(cells, 64, 1) + 0.375), 0.0)
            if red:
                g_r[1 + j], i_r[1 + j], e_r[1 + j] = force, inverse, force * inverse
            else:
                g_b[1 + j], i_b[1 + j] = force, inverse
    half_sweep(e_b, e_r, g_b, i_b, 1, 27, False, mask, 0.0625, 1)

    def sweep(n, carry):
        half_sweep(e_r, e_b, g_r, i_r, 1, 27, True, mask, 0.0625, 1)
        half_sweep(e_b, e_r, g_b, i_b, 1, 27, False, mask, 0.0625, 1)
        return carry

    lax.fori_loop(0, 7, sweep, 0)
    for i in range(22):
        k, upper = (15 + i) // 2 + 1, (15 + i) % 2
        es[i] = jnp.where(mask, e_r[k], e_b[k]) if upper else jnp.where(mask, e_b[k], e_r[k])
    total = zero
    for k in range(10, 18):
        total = total + (e_r[k] + e_b[k])
    total = total[0:8] + total[8:16]
    for i in range(SLABS):
        part[i] = total


def up_kernel(
    meta, bricks, sums, es, ec_b, r_r, r_b, ci_r, ci_b, u1_b, f_r, f_b, i_r, i_b, out,
    e_r, e_b, small, wide, planes, tall, u_r, u_b,
):
    slab, _, bit_x, bit_y, bit_z = place_of(meta, bricks)
    total = sums[0]
    for i in range(1, SLABS):
        total = total + sums[i]
    mean = jnp.sum(total) * (1.0 / (SLABS * 16 * 16 * 64))
    for i in range(22):
        shifted = es[i] - mean
        if i < 3:
            shifted = jnp.where(is_zero(slab, (16, 128)), 0.0, shifted)
        if i >= 19:
            shifted = jnp.where(is_zero(slab - (SLABS - 1), (16, 128)), 0.0, shifted)
        small[16 * i : 16 * i + 16] = shifted
    spread = pick(128, 128, lambda r, c: r == (c >> 1))
    small[...] = jnp.dot(small[...], spread, precision=EXACT, preferred_element_type=F32)
    for i in range(22):
        rows = small[16 * i : 16 * i + 16]
        wide[i, pl.ds(0, 16, stride=2), :] = rows
        wide[i, pl.ds(1, 16, stride=2), :] = rows
    for k in (0, 1, 2, 25, 26, 27):
        e_r[k] = jnp.zeros((32, 128), F32)
        e_b[k] = jnp.zeros((32, 128), F32)
    for i in range(22):
        e_b[3 + i] = ec_b[3 + i] + wide[i]
    coarse = odd(32, 128)
    for _ in range(2):
        half_sweep(e_r, e_b, r_r, ci_r, 3, 25, True, coarse, 0.25, 2)
        half_sweep(e_b, e_r, r_b, ci_b, 3, 25, False, coarse, 0.25, 2)
    for n in range(20):
        z = n - 2
        k = 8 * bit_z + (z // 2 + 6)
        red, black = e_r[k], e_b[k]
        planes[32 * n : 32 * n + 32] = jnp.where(coarse, red, black) if z % 2 else jnp.where(coarse, black, red)

    lane = iota((128, 256), 1)
    x0 = is_zero(bit_x, (128, 256))
    start = jnp.where(lane < 128, 64 * bit_x + (lane >> 1), (lane >> 1) + jnp.where(x0, 0, -64))
    usable = (lane < 128) | (x0 & (lane < 136)) | (jnp.logical_not(x0) & (lane >= 248))
    spread = jnp.where(usable & (iota((128, 256), 0) == start), 1.0, 0.0).astype(F32)
    tall_rows = jnp.dot(planes[...], spread, precision=EXACT, preferred_element_type=F32)
    for n in range(20):
        rows = tall_rows[32 * n : 32 * n + 32]
        for h in range(2):
            tall[n, h, pl.ds(0, 32, stride=2), :] = rows[:, 128 * h : 128 * h + 128]
            tall[n, h, pl.ds(1, 32, stride=2), :] = rows[:, 128 * h : 128 * h + 128]
    for k in (0, 21):
        u_r[k] = jnp.zeros((40, 256), F32)
        u_b[k] = jnp.zeros((40, 256), F32)
    row = iota((8, 128), 0)
    y0 = is_zero(bit_y)
    in_y = (y0 & (row != 7)) | (jnp.logical_not(y0) & (row != 0))
    own_start = pl.multiple_of(32 * bit_y, 32)
    side_start = pl.multiple_of(32 - 8 * bit_y, 8)
    for n in range(20):
        for h in range(2):
            lanes = slice(128 * h, 128 * h + 128)
            side = jnp.where(in_y, tall[n, h, pl.ds(side_start, 8), :], 0.0)
            u_b[1 + n, 0:32, lanes] = u1_b[3 + n, 0:32, lanes] + tall[n, h, pl.ds(own_start, 32), :]
            u_b[1 + n, 32:40, lanes] = u1_b[3 + n, 32:40, lanes] + side
    mask = odd(40, 256)
    f_r, f_b, i_r, i_b = (grid.at[2:24] for grid in (f_r, f_b, i_r, i_b))
    half_sweep(u_r, u_b, f_r, i_r, 1, 21, True, mask, 1.0, 0)
    half_sweep(u_b, u_r, f_b, i_b, 2, 20, False, mask, 1.0, 0)
    half_sweep(u_r, u_b, f_r, i_r, 2, 20, True, mask, 1.0, 0)
    half_sweep(u_b, u_r, f_b, i_b, 3, 19, False, mask, 1.0, 0)
    own = odd(32, 128)
    for t in range(16):
        red, black = u_r[3 + t, 0:32, 0:128], u_b[3 + t, 0:32, 0:128]
        out[0, 2 * t] = jnp.where(own, black, red)
        out[0, 2 * t + 1] = jnp.where(own, red, black)


def swap_cores(x):
    return lax.ppermute(x, "level", [(0, 1), (1, 0)])


def to_slabs(x, up_first):
    pairs = []
    for s in range(SLABS - 1):
        for m in range(8):
            low, high = s * 8 + m, (s + 1) * 8 + m
            pairs.append((low, high) if (m < 4) == up_first else (high, low))
    return lax.ppermute(x, ALL, pairs)


def among(x):
    return lax.all_to_all(x, LB, split_axis=0, concat_axis=0, tiled=True)


def deliver(shell, got, smem):
    leaving = run(functools.partial(cross_kernel, shell), [(4, shell.nz, 8, 128)], smem, [got])
    cross = to_slabs(leaving, False)
    sent = run(
        functools.partial(mid_kernel, shell), [(8, shell.got, 8, 128)], smem, [got, cross],
        [(12, shell.nz, 8, 128)],
    )
    return among(sent)


def body(u_init, source, coeffs, brick_map):
    meta = jnp.stack([lax.axis_index("slab"), lax.axis_index(LB)]).astype(jnp.int32)
    smem = [meta, brick_map]
    fine = (26, 40, 256)
    packed = run(first_kernel, [(8, DOWN.sent, 8, 128)], smem, [u_init, source, coeffs])
    halo = deliver(DOWN, among(packed), smem)
    rc, u_b, f_r, f_b, i_r, i_b = run(
        fine_down_kernel, [(2, 8, 16, 128)] + [fine] * 5, smem, [u_init, source, coeffs, halo],
        [fine, (2, 16, 32, 128), (256, 128)],
    )
    boxes = [rc] + [
        lax.ppermute(rc, "bottom", [(i, (i + d) % 4) for i in range(4)]) for d in range(1, 4)
    ]
    boxes = boxes + [swap_cores(box) for box in boxes]
    leaving = run(faces_kernel, [(4, 2, 5, 16, 128)], smem, boxes, [(8, 2, 8, 16, 128)])
    cross = to_slabs(leaving, True)
    other = swap_cores(cross)
    coarse = (28, 32, 128)
    faces = (4, 2, 5, 16, 128)
    rb, rb_send, ec_b, r_r, r_b, ci_r, ci_b = run(
        coarse_down_kernel, [(22, 16, 128), (18, 16, 128)] + [coarse] * 5, smem, boxes + [cross, other],
        [(8, 2, 8, 16, 128), faces, faces, coarse, coarse, coarse, (2, 22, 32, 128), (352, 128)],
    )
    cross = to_slabs(rb_send, True)
    other = swap_cores(cross)
    bottom = (28, 16, 128)
    es, part = run(
        bottom_kernel, [(22, 16, 128), (SLABS, 8, 128)], [meta], [rb, cross, other],
        [bottom] * 6 + [(18, 16, 128)] * 2,
    )
    sums = lax.all_to_all(part, "slab", split_axis=0, concat_axis=0, tiled=True)
    return run(
        up_kernel, [(1, 32, 32, 128)], smem,
        [sums, es, ec_b, r_r, r_b, ci_r, ci_b, u_b, f_r, f_b, i_r, i_b],
        [coarse, coarse, (352, 128), (22, 32, 128), (640, 128), (20, 2, 64, 128), (22, 40, 256), (22, 40, 256)],
    )


def solution(mesh):
    placed = P(ALL, None, None, None)
    return jax.shard_map(
        body, mesh=mesh, in_specs=(placed, placed, placed, P()), out_specs=placed, check_vma=False
    )
```

```python
import functools
import math

import jax
import jax.numpy as jnp
from jax import lax
from jax.experimental import pallas as pl
from jax.experimental.pallas import tpu as pltpu
from jax.sharding import PartitionSpec as P

LB = ("level", "bottom")
ALL = ("slab", "level", "bottom")
SLABS = 16
OWN = 5
F32 = jnp.float32
VMEM_SPEC = pl.BlockSpec(memory_space=pltpu.VMEM)
SMEM_SPEC = pl.BlockSpec(memory_space=pltpu.SMEM)
EXACT = lax.Precision.HIGHEST


def run(kernel, outs, smem, vmem, scratch=()):
    shapes = [jax.ShapeDtypeStruct(s, F32) for s in outs]
    single = len(shapes) == 1
    return pl.pallas_call(
        kernel,
        out_shape=shapes[0] if single else shapes,
        in_specs=[SMEM_SPEC] * len(smem) + [VMEM_SPEC] * len(vmem),
        out_specs=VMEM_SPEC if single else [VMEM_SPEC] * len(shapes),
        scratch_shapes=[pltpu.VMEM(s, F32) for s in scratch],
        compiler_params=pltpu.CompilerParams(vmem_limit_bytes=20 << 20),
    )(*smem, *vmem)


def iota(shape, dim):
    return lax.broadcasted_iota(jnp.int32, shape, dim)


def odd(rows, cols):
    return ((iota((rows, cols), 0) + iota((rows, cols), 1)) & 1) == 1


def place_of(meta, bricks):
    slab, me = meta[0], meta[1]
    place = jnp.int32(0)
    for i in range(8):
        place = place + jnp.where(bricks[slab, i] == me, i, 0)
    return slab, me, place & 1, (place >> 1) & 1, place >> 2


def is_zero(scalar, shape=(8, 128)):
    return jnp.full(shape, scalar, jnp.int32) == 0


class Shell:
    def __init__(self, low, high, arrays):
        self.low, self.high, self.arrays = low, high, arrays
        self.planes = math.ceil(len(low) / 4)
        self.nz = 4 * self.planes
        self.ny = 2 * arrays
        self.strips = 8 * arrays
        self.nx = math.ceil(self.strips / 16)
        self.coef = self.nz + self.ny + self.nx
        self.sent = self.coef + 2
        self.nz2 = 5 * self.planes
        self.side = math.ceil(self.nz2 / 16)
        self.y2 = self.nz2 + self.side
        self.x2 = self.y2 + self.ny
        self.got = self.x2 + self.nx
        self.first = min(16 * self.side - self.nz2, self.ny)
        assert self.strips + self.ny - self.first <= 16 * self.nx

    def edge(self, i):
        if i < self.first:
            pos = self.nz2 + i
            return self.nz2 + pos // 16, pos % 16
        pos = self.strips + i - self.first
        return self.x2 + pos // 16, pos % 16


DOWN = Shell(
    [(c, t) for c in (0, 1, 3) for t in range(4)] + [(c, t) for c in (2, 4) for t in range(3)],
    [(c, 15 - t) for c in (0, 1, 3) for t in range(4)] + [(c, 15 - t) for c in (2, 4) for t in range(3)],
    5,
)


def merge_strips(placed, base=None):
    group = iota((8, 128), 1) // 8
    total = jnp.zeros((8, 128), F32) if base is None else base
    for pos, strip in placed:
        moved = pltpu.roll(strip, 8 * pos, 1) if pos else strip
        total = jnp.where(group == pos, moved, total)
    return total


def pack_shell(shell, get, out, bit_x, bit_y):
    x0, y0 = is_zero(bit_x), is_zero(bit_y)
    for first, faces in ((0, shell.low), (4, shell.high)):
        for i, (c, t) in enumerate(faces):
            j = 4 * (i % shell.planes)
            out[first + i // shell.planes, j : j + 4] = get(c, t).reshape(4, 8, 128)
    for k in range(8):
        strips = []
        for tl in range(2):
            for c in range(shell.arrays):
                v = get(c, 2 * k + tl)
                out[k, shell.nz + tl * shell.arrays + c] = jnp.where(y0, v[24:32], v[0:8])
                for g in range(4):
                    tile = v[8 * g : 8 * g + 8]
                    strips.append(jnp.where(x0, pltpu.roll(tile, 8, 1), tile))
        for i in range(shell.nx):
            out[k, shell.nz + shell.ny + i] = merge_strips(list(enumerate(strips[16 * i : 16 * i + 16])))


def cross_kernel(shell, meta, bricks, recv, out):
    slab, me = meta[0], meta[1]
    for i in range(4):
        src = jnp.where(me >= 4, bricks[slab, 4 + i], bricks[slab, i])
        out[i, 0 : shell.nz] = recv[src, 0 : shell.nz]
        for j in range(2):
            coef = recv[bricks[slab, 2 * i + j], shell.coef : shell.coef + 2]
            out[i, shell.nz + 2 * j : shell.nz + 2 * j + 2] = coef


def mid_kernel(shell, meta, bricks, recv, cross, out, coef, faces):
    slab, me = meta[0], meta[1]
    faces[0:8] = recv[:, 0 : shell.nz]
    faces[8:12] = cross[:, 0 : shell.nz]
    for p in range(8):
        coef[0, p] = recv[bricks[slab, p], shell.coef : shell.coef + 2]
        j = shell.nz + 2 * (p & 1)
        coef[1, p] = cross[p >> 1, j : j + 2]
    for p in range(8):
        bx, by, bz = p & 1, (p >> 1) & 1, p >> 2
        dest = bricks[slab, p]
        same = me >= 4 if bz else me < 4

        def src(q):
            return jnp.where(same, bricks[slab, (q & 3) + 4 * (1 - bz)], 8 + (q & 3))

        def strip_of(tile):
            return pltpu.roll(tile, 8, 1) if bx else tile

        at_own, at_y, at_x, at_xy = src(p), src(p ^ 2), src(p ^ 1), src(p ^ 3)
        gy = 3 if by else 0
        strips = []
        for j in range(shell.planes):
            out[dest, 5 * j : 5 * j + 4] = faces[at_own, 4 * j : 4 * j + 4]
            out[dest, 5 * j + 4] = faces[at_y, 4 * j + gy]
            strips += [strip_of(faces[at_x, 4 * j + g]) for g in range(4)]
            strips.append(strip_of(faces[at_xy, 4 * j + gy]))
        from_y, from_x, from_xy = bricks[slab, p ^ 2], bricks[slab, p ^ 1], bricks[slab, p ^ 3]
        y1, x1 = shell.nz, shell.nz + shell.ny
        out[dest, shell.y2 : shell.x2] = recv[from_y, y1:x1]
        placed = {}
        for i, strip in enumerate(strips):
            placed.setdefault(shell.nz2 + i // 16, []).append((i % 16, strip))
        for i in range(shell.ny):
            tile, pos = shell.edge(i)
            placed.setdefault(tile, []).append((pos, strip_of(recv[from_xy, y1 + i])))
        for i in range(shell.nx):
            tile = recv[from_x, x1 + i]
            out[dest, shell.x2 + i] = merge_strips(placed.get(shell.x2 + i, []), tile)
        for i in range(shell.side):
            out[dest, shell.nz2 + i] = merge_strips(placed[shell.nz2 + i])


def unpack_shell(shell, recv, grids, bit_x):
    lane = iota((8, 128), 1)
    x0 = is_zero(bit_x)
    in_x = (x0 & (lane < 8)) | (jnp.logical_not(x0) & (lane >= 120))

    def strip(tile, pos):
        shift = (jnp.where(bit_x == 0, 0, 120) + 128 - 8 * pos) % 128
        return jnp.where(in_x, pltpu.roll(tile, shift, 1), 0.0)

    for first, faces, shift in ((0, shell.low, OWN + 16), (4, shell.high, OWN - 16)):
        for i, (c, t) in enumerate(faces):
            k, j = first + i // shell.planes, i % shell.planes
            for g in range(5):
                n = 5 * j + g
                rows = slice(8 * g, 8 * g + 8)
                grids[c][shift + t, rows, 0:128] = recv[k, n]
                grids[c][shift + t, rows, 128:256] = strip(recv[k, shell.nz2 + n // 16], n % 16)
    for t in range(16):
        k, tl = t // 2, t % 2
        for c in range(shell.arrays):
            i = tl * shell.arrays + c
            tile, pos = shell.edge(i)
            grids[c][OWN + t, 32:40, 0:128] = recv[k, shell.y2 + i]
            grids[c][OWN + t, 32:40, 128:256] = strip(recv[k, tile], pos)
            for g in range(4):
                n = 4 * i + g
                grids[c][OWN + t, 8 * g : 8 * g + 8, 128:256] = strip(recv[k, shell.x2 + n // 16], n % 16)


def pair_of(cells, t, red, mask):
    low, high = cells[0, 2 * t], cells[0, 2 * t + 1]
    return jnp.where(mask, high, low) if red else jnp.where(mask, low, high)


def pack_bottom_coef(a, out, small):
    for i in range(8):
        planes = (a[0, 4 * i] + a[0, 4 * i + 1]) + (a[0, 4 * i + 2] + a[0, 4 * i + 3])
        small[i] = planes
    rows = []
    for i in range(8):
        first = small[i, pl.ds(0, 8, stride=4), :] + small[i, pl.ds(1, 8, stride=4), :]
        rows.append(first + (small[i, pl.ds(2, 8, stride=4), :] + small[i, pl.ds(3, 8, stride=4), :]))
    fold = pick(128, 128, lambda r, c: (r >> 2) == (c & 31)) * (1.0 / 64)
    cells = jnp.dot(jnp.concatenate(rows, 0), fold, precision=EXACT, preferred_element_type=F32)
    group = iota((8, 128), 1) >> 5
    for h in range(2):
        tile = cells[32 * h : 32 * h + 8]
        for j in range(1, 4):
            tile = jnp.where(group == j, cells[32 * h + 8 * j : 32 * h + 8 * j + 8], tile)
        for k in range(8):
            out[k, DOWN.coef + h] = tile


def first_kernel(meta, bricks, u, f, a, out, small):
    _, _, bit_x, bit_y, _ = place_of(meta, bricks)
    mask = odd(32, 128)
    sources = ((u, False), (f, True), (f, False), (a, True), (a, False))

    def get(c, t):
        return pair_of(sources[c][0], t, sources[c][1], mask)

    pack_shell(DOWN, get, out, bit_x, bit_y)
    pack_bottom_coef(a, out, small)


def around(src, k, red, mask, edges, cut=None):
    here = src[k]
    rows, cols = here.shape
    above, below = src[k + 1], src[k - 1]
    other = jnp.where(mask, above, below) if red else jnp.where(mask, below, above)
    up, down = pltpu.roll(here, 1, 0), pltpu.roll(here, rows - 1, 0)
    left, right = pltpu.roll(here, 1, 1), pltpu.roll(here, cols - 1, 1)
    if edges:
        row, lane = iota((rows, cols), 0), iota((rows, cols), 1)
        up, down = jnp.where(row == 0, 0.0, up), jnp.where(row == rows - 1, 0.0, down)
        if edges == 2:
            left, right = jnp.where(lane == 0, 0.0, left), jnp.where(lane == cols - 1, 0.0, right)
    if cut is not None:
        up, down = jnp.where(cut[0], 0.0, up), jnp.where(cut[1], 0.0, down)
    return ((here + other) + (up + down)) + (left + right)


def half_sweep(dst, src, force, inverse, lo, hi, red, mask, scale, edges, cut=None):
    def step(k, carry):
        total = around(src, k, red, mask, edges, cut)
        if scale != 1.0:
            total = scale * total
        dst[k] = (force[k] + total) * inverse[k]
        return carry

    lax.fori_loop(lo, hi, step, 0, unroll=True)


def pick(rows, cols, keep):
    return jnp.where(keep(iota((rows, cols), 0), iota((rows, cols), 1)), 1.0, 0.0).astype(F32)


def fine_down_kernel(meta, bricks, u, f, a, recv, rc, u_b, f_r, f_b, i_r, i_b, u_r, resid, small):
    slab, _, bit_x, bit_y, bit_z = place_of(meta, bricks)
    own = odd(32, 128)
    grids = (u_b, f_r, f_b, i_r, i_b)
    sources = ((u, False), (f, True), (f, False), (a, True), (a, False))
    for t in range(16):
        for grid, (cells, red) in zip(grids, sources):
            grid[OWN + t, 0:32, 0:128] = pair_of(cells, t, red, own)
    unpack_shell(DOWN, recv, grids, bit_x)
    zero = jnp.zeros((40, 256), F32)
    for k in (0, 25):
        u_r[k] = zero
        u_b[k] = zero
    for k in (1, 24):
        f_b[k] = zero
        i_b[k] = zero
    row, lane = iota((40, 256), 0), iota((40, 256), 1)
    x0, y0 = is_zero(bit_x, (40, 256)), is_zero(bit_y, (40, 256))
    x1, y1 = jnp.logical_not(x0), jnp.logical_not(y0)
    inside = (row < 32) | (y0 & (row < 39)) | (y1 & (row >= 33))
    inside = inside & ((lane < 128) | (x0 & (lane < 136)) | (x1 & (lane >= 248)))
    no_low = (slab == 0) & (bit_z == 0)
    no_high = (slab == SLABS - 1) & (bit_z == 1)

    def invert(k, carry):
        gone = jnp.where((no_low & (k < OWN)) | (no_high & (k >= OWN + 16)), 1, 0)
        keep = inside & is_zero(gone, (40, 256))
        i_r[k] = jnp.where(keep, 1.0 / (i_r[k] + 6.0), 0.0)
        ends = jnp.where((k == 1) | (k == 24), 1, 0)
        i_b[k] = jnp.where(keep & is_zero(ends, (40, 256)), 1.0 / (i_b[k] + 6.0), 0.0)
        return carry

    lax.fori_loop(1, 25, invert, 0, unroll=4)
    mask = odd(40, 256)
    cut = (y0 & (row == 0), y1 & (row == 31))
    half_sweep(u_r, u_b, f_r, i_r, 1, 25, True, mask, 1.0, 0, cut)
    half_sweep(u_b, u_r, f_b, i_b, 1, 25, False, mask, 1.0, 0)
    half_sweep(u_r, u_b, f_r, i_r, 2, 24, True, mask, 1.0, 0)
    half_sweep(u_b, u_r, f_b, i_b, 3, 23, False, mask, 1.0, 0)
    for t in range(16):
        total = around(u_b, OWN + t, True, mask, 0)[0:32, 0:128]
        diag = pair_of(a, t, True, own) + 6.0
        resid[0, t] = pair_of(f, t, True, own) + total - diag * u_r[OWN + t, 0:32, 0:128]
        resid[1, t] = a[0, 2 * t] + a[0, 2 * t + 1]
    twice = pick(128, 128, lambda r, c: (r >> 1) == (c & 63)) * 0.125
    row, lane = iota((16, 128), 0), iota((16, 128), 1)
    even = ((row + lane + (lane >> 6)) & 1) == 0
    for i in range(2):
        for t in range(16):
            small[16 * t : 16 * t + 16] = (
                resid[i, t, pl.ds(0, 16, stride=2), :] + resid[i, t, pl.ds(1, 16, stride=2), :]
            )
        summed = jnp.dot(small[...], twice, precision=EXACT, preferred_element_type=F32)
        summed = summed.reshape(16, 16, 128)
        for j in range(8):
            rc[i, j] = jnp.where(even, summed[2 * j], summed[2 * j + 1])


def slot_of(member, me):
    return jnp.where((member >> 2) == (me >> 2), 0, 4) + ((me - member) & 3)


def faces_kernel(meta, bricks, *refs):
    boxes, (out, held) = refs[:8], refs[8:]
    slab, me = meta[0], meta[1]
    for i, box in enumerate(boxes):
        held[i] = box[...]
    start = jnp.where(me < 4, 3, 0)
    for i in range(4):
        member = jnp.where(me < 4, bricks[slab, 4 + i], bricks[slab, i])
        out[i] = held[slot_of(member, me), :, pl.ds(start, 5)]


def coarse_down_kernel(meta, bricks, *refs):
    boxes, (one, two, weights) = refs[:8], refs[8:11]
    rb, rb_send, part, e_b, r_r, r_b, i_r, i_b = refs[11:19]
    held, low, high, e_r, a_r, a_b, resid, small = refs[19:]
    slab, me = meta[0], meta[1]
    for i, box in enumerate(boxes):
        held[i] = box[...]

    @pl.when(me < 4)
    def _():
        low[...] = one[...]
        high[...] = two[...]

    @pl.when(me >= 4)
    def _():
        low[...] = two[...]
        high[...] = one[...]

    left = iota((16, 128), 1) < 64
    for q, (red, black) in enumerate(((r_r, r_b), (a_r, a_b))):

        def put(k, by, west, east):
            rows = slice(16 * by, 16 * by + 16)
            red[k, rows] = jnp.where(left, west, pltpu.roll(east, 64, 1))
            black[k, rows] = jnp.where(left, pltpu.roll(west, 64, 1), east)

        for by in range(2):
            for bz in range(2):
                west = slot_of(bricks[slab, 2 * by + 4 * bz], me)
                east = slot_of(bricks[slab, 2 * by + 4 * bz + 1], me)
                for j in range(8):
                    put(6 + 8 * bz + j, by, held[west, q, j], held[east, q, j])
            for j in range(5):
                put(1 + j, by, low[2 * by, q, j], low[2 * by + 1, q, j])
                put(22 + j, by, high[2 * by, q, j], high[2 * by + 1, q, j])
    for k in (0, 27):
        e_r[k] = jnp.zeros((32, 128), F32)
        e_b[k] = jnp.zeros((32, 128), F32)

    def start(k, carry):
        gone = jnp.where(((slab == 0) & (k < 6)) | ((slab == SLABS - 1) & (k >= 22)), 1, 0)
        keep = is_zero(gone, (32, 128))
        inverse = jnp.where(keep, 1.0 / (a_r[k] + 1.5), 0.0)
        i_r[k] = inverse
        i_b[k] = jnp.where(keep, 1.0 / (a_b[k] + 1.5), 0.0)
        e_r[k] = r_r[k] * inverse
        return carry

    lax.fori_loop(1, 27, start, 0, unroll=13)
    mask = odd(32, 128)
    half_sweep(e_b, e_r, r_b, i_b, 1, 27, False, mask, 0.25, 2)
    half_sweep(e_r, e_b, r_r, i_r, 1, 27, True, mask, 0.25, 2)
    half_sweep(e_b, e_r, r_b, i_b, 1, 27, False, mask, 0.25, 2)

    def residual(n, carry):
        k = n + 3
        total = 0.25 * around(e_b, k, True, mask, 2)
        resid[0, n] = r_r[k] + total - (a_r[k] + 1.5) * e_r[k]
        resid[1, n] = a_r[k] + a_b[k]
        return carry

    lax.fori_loop(0, 22, residual, 0, unroll=True)
    total = jnp.zeros((352, 128), F32)
    for i in range(2):
        for n in range(22):
            small[16 * n : 16 * n + 16] = (
                resid[i, n, pl.ds(0, 16, stride=2), :] + resid[i, n, pl.ds(1, 16, stride=2), :]
            )
        half = pick(128, 128, lambda r, c: (r >> 1) == c - 64 * i) * 0.125
        total = total + jnp.dot(small[...], half, precision=EXACT, preferred_element_type=F32)
    rb[...] = total.reshape(22, 16, 128)
    rb_send[...] = rb[pl.ds(jnp.where(me < 4, 1, 3), 18)]
    total = jnp.zeros((16, 128), F32)
    for i in range(16):
        total = total + rb[3 + i] * weights[i]
    total = total[0:8] + total[8:16]
    for i in range(SLABS):
        part[i] = total


def bottom_kernel(meta, rb, one, two, es, e_r, e_b, g_r, g_b, i_r, i_b, low, high):
    slab, me = meta[0], meta[1]

    @pl.when(me < 4)
    def _():
        low[...] = one[...]
        high[...] = two[...]

    @pl.when(me >= 4)
    def _():
        low[...] = two[...]
        high[...] = one[...]

    mask = odd(16, 128)
    left = iota((16, 128), 1) < 64
    zero = jnp.zeros((16, 128), F32)
    for k in (0, 27):
        e_r[k] = zero
        e_b[k] = zero
    for j in range(26):
        planes = []
        for n in (2 * j, 2 * j + 1):
            planes.append(low[n] if n < 18 else rb[n - 15] if n < 34 else high[n - 34])
        keep = left
        if j < 9:
            keep = left & jnp.logical_not(is_zero(slab, (16, 128)))
        if j >= 17:
            keep = left & jnp.logical_not(is_zero(slab - (SLABS - 1), (16, 128)))
        for red in (True, False):
            cells = jnp.where(mask, planes[1], planes[0]) if red else jnp.where(mask, planes[0], planes[1])
            force = jnp.where(left, cells, 0.0)
            inverse = jnp.where(keep, 1.0 / (pltpu.roll(cells, 64, 1) + 0.375), 0.0)
            if red:
                g_r[1 + j], i_r[1 + j], e_r[1 + j] = force, inverse, force * inverse
            else:
                g_b[1 + j], i_b[1 + j] = force, inverse
    half_sweep(e_b, e_r, g_b, i_b, 1, 27, False, mask, 0.0625, 1)

    def sweep(n, carry):
        half_sweep(e_r, e_b, g_r, i_r, 1, 27, True, mask, 0.0625, 1)
        half_sweep(e_b, e_r, g_b, i_b, 1, 27, False, mask, 0.0625, 1)
        return carry

    lax.fori_loop(0, 7, sweep, 0)
    for i in range(22):
        k, upper = (15 + i) // 2 + 1, (15 + i) % 2
        es[i] = jnp.where(mask, e_r[k], e_b[k]) if upper else jnp.where(mask, e_b[k], e_r[k])


def weights_kernel(meta, here, there, out, t_r, t_b, w_r, w_b, i_r, i_b, low, high):
    slab, me = meta[0], meta[1]

    @pl.when(me < 4)
    def _():
        low[...] = there[1]
        high[...] = here[1]

    @pl.when(me >= 4)
    def _():
        low[...] = here[1]
        high[...] = there[1]

    lane = iota((8, 128), 1)

    def plane(boxes, z):
        rows = []
        for by in range(2):
            place, shift = 4 * (z >> 3) + 2 * by, 32 * (z & 3)
            west = pltpu.roll(boxes(place, (z & 7) >> 2), (128 - shift) % 128, 1)
            east = pltpu.roll(boxes(place + 1, (z & 7) >> 2), (160 - shift) % 128, 1)
            rows.append(jnp.where(lane < 32, west, east))
        return jnp.concatenate(rows, 0)

    parts = (lambda p, h: low[p, h], lambda p, h: here[0, p, h], lambda p, h: high[p, h])
    mask = odd(16, 128)
    left = iota((16, 128), 1) < 64
    zero = jnp.zeros((16, 128), F32)
    for k in (0, 25):
        t_r[k] = zero
        t_b[k] = zero
    for j in range(24):
        lower, upper = (plane(parts[(2 * j + i) // 16], (2 * j + i) % 16) for i in range(2))
        keep = left
        if j < 8:
            keep = left & jnp.logical_not(is_zero(slab, (16, 128)))
        if j >= 16:
            keep = left & jnp.logical_not(is_zero(slab - (SLABS - 1), (16, 128)))
        i_r[1 + j] = jnp.where(keep, 1.0 / (jnp.where(mask, upper, lower) + 0.375), 0.0)
        i_b[1 + j] = jnp.where(keep, 1.0 / (jnp.where(mask, lower, upper) + 0.375), 0.0)
    for k in range(1, 25):
        t_b[k] = i_b[k]
        w_b[k] = i_b[k]
    for k in range(1, 25):
        t = i_r[k] * (1.0 + 0.0625 * around(t_b, k, True, mask, 1))
        t_r[k] = t
        w_r[k] = t

    def sweep(n, carry):
        for k in range(1, 25):
            t = i_b[k] * (0.0625 * around(t_r, k, False, mask, 1))
            t_b[k] = t
            w_b[k] = w_b[k] + t
        for k in range(1, 25):
            t = i_r[k] * (0.0625 * around(t_b, k, True, mask, 1))
            t_r[k] = t
            w_r[k] = w_r[k] + t
        return carry

    lax.fori_loop(0, 7, sweep, 0)
    for j in range(8):
        red, black = w_r[9 + j], w_b[9 + j]
        out[2 * j] = jnp.where(mask, black, red)
        out[2 * j + 1] = jnp.where(mask, red, black)


def up_kernel(
    meta, bricks, sums, es, ec_b, r_r, r_b, ci_r, ci_b, u1_b, f_r, f_b, i_r, i_b, out,
    e_r, e_b, small, wide, planes, tall, u_r, u_b,
):
    slab, _, bit_x, bit_y, bit_z = place_of(meta, bricks)
    total = sums[0]
    for i in range(1, SLABS):
        total = total + sums[i]
    mean = jnp.sum(total) * (1.0 / (SLABS * 16 * 16 * 64))
    for i in range(22):
        shifted = es[i] - mean
        if i < 3:
            shifted = jnp.where(is_zero(slab, (16, 128)), 0.0, shifted)
        if i >= 19:
            shifted = jnp.where(is_zero(slab - (SLABS - 1), (16, 128)), 0.0, shifted)
        small[16 * i : 16 * i + 16] = shifted
    spread = pick(128, 128, lambda r, c: r == (c >> 1))
    small[...] = jnp.dot(small[...], spread, precision=EXACT, preferred_element_type=F32)
    for i in range(22):
        rows = small[16 * i : 16 * i + 16]
        wide[i, pl.ds(0, 16, stride=2), :] = rows
        wide[i, pl.ds(1, 16, stride=2), :] = rows
    for k in (0, 1, 2, 25, 26, 27):
        e_r[k] = jnp.zeros((32, 128), F32)
        e_b[k] = jnp.zeros((32, 128), F32)
    for i in range(22):
        e_b[3 + i] = ec_b[3 + i] + wide[i]
    coarse = odd(32, 128)
    for _ in range(2):
        half_sweep(e_r, e_b, r_r, ci_r, 3, 25, True, coarse, 0.25, 2)
        half_sweep(e_b, e_r, r_b, ci_b, 3, 25, False, coarse, 0.25, 2)
    for n in range(20):
        z = n - 2
        k = 8 * bit_z + (z // 2 + 6)
        red, black = e_r[k], e_b[k]
        planes[32 * n : 32 * n + 32] = jnp.where(coarse, red, black) if z % 2 else jnp.where(coarse, black, red)

    lane = iota((128, 256), 1)
    x0 = is_zero(bit_x, (128, 256))
    start = jnp.where(lane < 128, 64 * bit_x + (lane >> 1), (lane >> 1) + jnp.where(x0, 0, -64))
    usable = (lane < 128) | (x0 & (lane < 136)) | (jnp.logical_not(x0) & (lane >= 248))
    spread = jnp.where(usable & (iota((128, 256), 0) == start), 1.0, 0.0).astype(F32)
    tall_rows = jnp.dot(planes[...], spread, precision=EXACT, preferred_element_type=F32)
    for n in range(20):
        rows = tall_rows[32 * n : 32 * n + 32]
        for h in range(2):
            tall[n, h, pl.ds(0, 32, stride=2), :] = rows[:, 128 * h : 128 * h + 128]
            tall[n, h, pl.ds(1, 32, stride=2), :] = rows[:, 128 * h : 128 * h + 128]
    for k in (0, 21):
        u_r[k] = jnp.zeros((40, 256), F32)
        u_b[k] = jnp.zeros((40, 256), F32)
    row = iota((8, 128), 0)
    y0 = is_zero(bit_y)
    in_y = (y0 & (row != 7)) | (jnp.logical_not(y0) & (row != 0))
    own_start = pl.multiple_of(32 * bit_y, 32)
    side_start = pl.multiple_of(32 - 8 * bit_y, 8)
    for n in range(20):
        for h in range(2):
            lanes = slice(128 * h, 128 * h + 128)
            side = jnp.where(in_y, tall[n, h, pl.ds(side_start, 8), :], 0.0)
            u_b[1 + n, 0:32, lanes] = u1_b[3 + n, 0:32, lanes] + tall[n, h, pl.ds(own_start, 32), :]
            u_b[1 + n, 32:40, lanes] = u1_b[3 + n, 32:40, lanes] + side
    mask = odd(40, 256)
    f_r, f_b, i_r, i_b = (grid.at[2:24] for grid in (f_r, f_b, i_r, i_b))
    half_sweep(u_r, u_b, f_r, i_r, 1, 21, True, mask, 1.0, 0)
    half_sweep(u_b, u_r, f_b, i_b, 2, 20, False, mask, 1.0, 0)
    half_sweep(u_r, u_b, f_r, i_r, 2, 20, True, mask, 1.0, 0)
    half_sweep(u_b, u_r, f_b, i_b, 3, 19, False, mask, 1.0, 0)
    own = odd(32, 128)
    for t in range(16):
        red, black = u_r[3 + t, 0:32, 0:128], u_b[3 + t, 0:32, 0:128]
        out[0, 2 * t] = jnp.where(own, black, red)
        out[0, 2 * t + 1] = jnp.where(own, red, black)


def swap_cores(x):
    return lax.ppermute(x, "level", [(0, 1), (1, 0)])


def to_slabs(x, up_first):
    pairs = []
    for s in range(SLABS - 1):
        for m in range(8):
            low, high = s * 8 + m, (s + 1) * 8 + m
            pairs.append((low, high) if (m < 4) == up_first else (high, low))
    return lax.ppermute(x, ALL, pairs)


def among(x):
    return lax.all_to_all(x, LB, split_axis=0, concat_axis=0, tiled=True)


def body(u_init, source, coeffs, brick_map):
    meta = jnp.stack([lax.axis_index("slab"), lax.axis_index(LB)]).astype(jnp.int32)
    smem = [meta, brick_map]
    fine = (26, 40, 256)
    packed = run(first_kernel, [(8, DOWN.sent, 8, 128)], smem, [u_init, source, coeffs], [(8, 32, 128)])
    got = among(packed)
    leaving = run(functools.partial(cross_kernel, DOWN), [(4, DOWN.nz + 4, 8, 128)], smem, [got])
    cross = to_slabs(leaving, False)
    sent, coef = run(
        functools.partial(mid_kernel, DOWN), [(8, DOWN.got, 8, 128), (2, 8, 2, 8, 128)], smem, [got, cross],
        [(12, DOWN.nz, 8, 128)],
    )
    coef_other = swap_cores(coef)
    halo = among(sent)
    weights = run(
        weights_kernel, [(16, 16, 128)], [meta], [coef, coef_other],
        [(26, 16, 128)] * 6 + [(8, 2, 8, 128)] * 2,
    )
    halo, weights = lax.optimization_barrier((halo, weights))
    rc, u_b, f_r, f_b, i_r, i_b = run(
        fine_down_kernel, [(2, 8, 16, 128)] + [fine] * 5, smem, [u_init, source, coeffs, halo],
        [fine, (2, 16, 32, 128), (256, 128)],
    )
    boxes = [rc] + [
        lax.ppermute(rc, "bottom", [(i, (i + d) % 4) for i in range(4)]) for d in range(1, 4)
    ]
    boxes = boxes + [swap_cores(box) for box in boxes]
    leaving = run(faces_kernel, [(4, 2, 5, 16, 128)], smem, boxes, [(8, 2, 8, 16, 128)])
    cross = to_slabs(leaving, True)
    other = swap_cores(cross)
    coarse = (28, 32, 128)
    faces = (4, 2, 5, 16, 128)
    rb, rb_send, part, ec_b, r_r, r_b, ci_r, ci_b = run(
        coarse_down_kernel, [(22, 16, 128), (18, 16, 128), (SLABS, 8, 128)] + [coarse] * 5, smem,
        boxes + [cross, other, weights],
        [(8, 2, 8, 16, 128), faces, faces, coarse, coarse, coarse, (2, 22, 32, 128), (352, 128)],
    )
    cross = to_slabs(rb_send, True)
    sums = lax.all_to_all(part, "slab", split_axis=0, concat_axis=0, tiled=True)
    cross, sums = lax.optimization_barrier((cross, sums))
    other = swap_cores(cross)
    bottom = (28, 16, 128)
    es = run(
        bottom_kernel, [(22, 16, 128)], [meta], [rb, cross, other],
        [bottom] * 6 + [(18, 16, 128)] * 2,
    )
    return run(
        up_kernel, [(1, 32, 32, 128)], smem,
        [sums, es, ec_b, r_r, r_b, ci_r, ci_b, u_b, f_r, f_b, i_r, i_b],
        [coarse, coarse, (352, 128), (22, 32, 128), (640, 128), (20, 2, 64, 128), (22, 40, 256), (22, 40, 256)],
    )


def solution(mesh):
    placed = P(ALL, None, None, None)
    return jax.shard_map(
        body, mesh=mesh, in_specs=(placed, placed, placed, P()), out_specs=placed, check_vma=False
    )
```

```python
import jax
import jax.numpy as jnp
from jax import lax
from jax.experimental import pallas as pl
from jax.experimental.pallas import tpu as pltpu
from jax.sharding import PartitionSpec as P

LB = ("level", "bottom")
ALL = ("slab", "level", "bottom")
SLABS = 16
OWN = 5
F32 = jnp.float32
VMEM_SPEC = pl.BlockSpec(memory_space=pltpu.VMEM)
SMEM_SPEC = pl.BlockSpec(memory_space=pltpu.SMEM)
EXACT = lax.Precision.HIGHEST


def run(kernel, outs, smem, vmem, scratch=()):
    shapes = [jax.ShapeDtypeStruct(s, F32) for s in outs]
    single = len(shapes) == 1
    return pl.pallas_call(
        kernel,
        out_shape=shapes[0] if single else shapes,
        in_specs=[SMEM_SPEC] * len(smem) + [VMEM_SPEC] * len(vmem),
        out_specs=VMEM_SPEC if single else [VMEM_SPEC] * len(shapes),
        scratch_shapes=[pltpu.VMEM(s, F32) for s in scratch],
        compiler_params=pltpu.CompilerParams(vmem_limit_bytes=20 << 20),
    )(*smem, *vmem)


def iota(shape, dim):
    return lax.broadcasted_iota(jnp.int32, shape, dim)


def odd(rows, cols):
    return ((iota((rows, cols), 0) + iota((rows, cols), 1)) & 1) == 1


def place_of(meta, bricks):
    slab, me = meta[0], meta[1]
    place = jnp.int32(0)
    for i in range(8):
        place = place + jnp.where(bricks[slab, i] == me, i, 0)
    return slab, me, place & 1, (place >> 1) & 1, place >> 2


def is_zero(scalar, shape=(8, 128)):
    return jnp.full(shape, scalar, jnp.int32) == 0


ARRAYS = 5
FACE = 17
SENT_Y, SENT_X, SENT_COEF, SENT = 17, 27, 30, 32
GOT_ROWS, GOT_STRIPS, GOT_Y, GOT_X, GOT = 17, 20, 22, 32, 35


def face_planes(j):
    return [(1 + j, 0), (1 + j, 1), (1 + j, 2), (0, j)]


def merge_strips(placed, base=None):
    group = iota((8, 128), 1) // 8
    total = jnp.zeros((8, 128), F32) if base is None else base
    for pos, strip in placed:
        moved = pltpu.roll(strip, 8 * pos, 1) if pos else strip
        total = jnp.where(group == pos, moved, total)
    return total


def swap_lanes(cells):
    lane = iota(cells.shape, 1)
    return jnp.where((lane & 1) == 0, pltpu.roll(cells, cells.shape[1] - 1, 1), pltpu.roll(cells, 1, 1))


def pack_shell(get, out, bit_x, bit_y):
    x0, y0 = is_zero(bit_x), is_zero(bit_y)
    mask = odd(32, 128)
    for k in range(8):
        high, j = k >= 4, k % 4
        for i, (c, far) in enumerate(face_planes(j)):
            out[k, 4 * i : 4 * i + 4] = get(c, 15 - far if high else far).reshape(4, 8, 128)
        t = 12 if high else 3
        one, two = get(1, t), swap_lanes(get(3, t))
        both = jnp.where(mask, one, two) if high else jnp.where(mask, two, one)
        out[k, 16] = both[8 * j : 8 * j + 8]
        strips = []
        for tl in range(2):
            for c in range(ARRAYS):
                v = get(c, 2 * k + tl)
                out[k, SENT_Y + tl * ARRAYS + c] = jnp.where(y0, v[24:32], v[0:8])
                for g in range(4):
                    tile = v[8 * g : 8 * g + 8]
                    strips.append(jnp.where(x0, pltpu.roll(tile, 8, 1), tile))
        for i in range(3):
            out[k, SENT_X + i] = merge_strips(list(enumerate(strips[16 * i : 16 * i + 16])))


def cross_kernel(meta, bricks, recv, out):
    slab, me = meta[0], meta[1]
    for i in range(4):
        src = jnp.where(me >= 4, bricks[slab, 4 + i], bricks[slab, i])
        out[i, 0:FACE] = recv[src, 0:FACE]
        for j in range(2):
            coef = recv[bricks[slab, 2 * i + j], SENT_COEF:SENT]
            out[i, FACE + 2 * j : FACE + 2 * j + 2] = coef


def mid_kernel(meta, bricks, recv, cross, out, coef, faces):
    slab, me = meta[0], meta[1]
    faces[0:8] = recv[:, 0:FACE]
    faces[8:12] = cross[:, 0:FACE]
    for p in range(8):
        coef[0, p] = recv[bricks[slab, p], SENT_COEF:SENT]
        j = FACE + 2 * (p & 1)
        coef[1, p] = cross[p >> 1, j : j + 2]
    row = iota((8, 128), 0)
    for p in range(8):
        bx, by, bz = p & 1, (p >> 1) & 1, p >> 2
        dest = bricks[slab, p]
        same = me >= 4 if bz else me < 4

        def src(q):
            return jnp.where(same, bricks[slab, (q & 3) + 4 * (1 - bz)], 8 + (q & 3))

        def strip_of(tile):
            return pltpu.roll(tile, 8, 1) if bx else tile

        def rows_of(at):
            one, two, three, last = (faces[at, 4 * i + (3 if by else 0)] for i in range(4))
            if by:
                shared = jnp.where(row >= 3, two, pltpu.roll(three, 3, 0))
            else:
                shared = jnp.where(row < 5, two, pltpu.roll(three, 5, 0))
            return [one, shared, last]

        at_own, at_y, at_x, at_xy = src(p), src(p ^ 2), src(p ^ 1), src(p ^ 3)
        out[dest, 0:FACE] = faces[at_own]
        for i, tile in enumerate(rows_of(at_y)):
            out[dest, GOT_ROWS + i] = tile
        strips = [strip_of(faces[at_x, i]) for i in range(16)] + [strip_of(tile) for tile in rows_of(at_xy)]
        from_y, from_x, from_xy = bricks[slab, p ^ 2], bricks[slab, p ^ 1], bricks[slab, p ^ 3]
        strips += [strip_of(recv[from_xy, SENT_Y + i]) for i in range(2 * ARRAYS)]
        for i in range(2):
            out[dest, GOT_STRIPS + i] = merge_strips(list(enumerate(strips[16 * i : 16 * i + 16])))
        out[dest, GOT_Y:GOT_X] = recv[from_y, SENT_Y:SENT_X]
        out[dest, GOT_X:GOT] = recv[from_x, SENT_X:SENT_COEF]


def unpack_shell(recv, grids, bit_x, bit_y):
    row, lane = iota((8, 128), 0), iota((8, 128), 1)
    x0, y0 = is_zero(bit_x), is_zero(bit_y)
    in_x = (x0 & (lane < 8)) | (jnp.logical_not(x0) & (lane >= 120))
    five = (y0 & (row < 5)) | (jnp.logical_not(y0) & (row >= 3))
    three = (y0 & (row < 3)) | (jnp.logical_not(y0) & (row >= 5))

    def strip(tile, pos):
        shift = (jnp.where(bit_x == 0, 0, 120) + 128 - 8 * pos) % 128
        return jnp.where(in_x, pltpu.roll(tile, shift, 1), 0.0)

    def rows_of(tiles):
        one, shared, last = tiles
        moved = jnp.where(y0, pltpu.roll(shared, 3, 0), pltpu.roll(shared, 5, 0))
        return [one, jnp.where(five, shared, 0.0), jnp.where(three, moved, 0.0), last]

    for k in range(8):
        high, j = k >= 4, k % 4
        rows = rows_of([recv[k, GOT_ROWS + i] for i in range(3)])
        sides = rows_of([strip(recv[k, GOT_STRIPS + 1], i) for i in range(3)])
        for i, (c, far) in enumerate(face_planes(j)):
            at = OWN - 1 - far if high else OWN + 16 + far
            for g in range(4):
                grids[c][at, 8 * g : 8 * g + 8, 0:128] = recv[k, 4 * i + g]
                grids[c][at, 8 * g : 8 * g + 8, 128:256] = strip(recv[k, GOT_STRIPS], 4 * i + g)
            grids[c][at, 32:40, 0:128] = rows[i]
            grids[c][at, 32:40, 128:256] = sides[i]
        at = 1 if high else 24
        both = recv[k, 16]
        for c, cells in ((1, both), (3, swap_lanes(both))):
            grids[c][at, 8 * j : 8 * j + 8, 0:128] = cells
            grids[c][at, 8 * j : 8 * j + 8, 128:256] = jnp.zeros((8, 128), F32)
            grids[c][at, 32:40] = jnp.zeros((8, 256), F32)
        for tl in range(2):
            for c in range(ARRAYS):
                i = tl * ARRAYS + c
                at = OWN + 2 * k + tl
                grids[c][at, 32:40, 0:128] = recv[k, GOT_Y + i]
                grids[c][at, 32:40, 128:256] = strip(recv[k, GOT_STRIPS + 1], 3 + i)
                for g in range(4):
                    n = 4 * i + g
                    side = strip(recv[k, GOT_X + n // 16], n % 16)
                    grids[c][at, 8 * g : 8 * g + 8, 128:256] = side


def pair_of(cells, t, red, mask):
    low, high = cells[0, 2 * t], cells[0, 2 * t + 1]
    return jnp.where(mask, high, low) if red else jnp.where(mask, low, high)


def pack_bottom_coef(a, out, small):
    for i in range(8):
        planes = (a[0, 4 * i] + a[0, 4 * i + 1]) + (a[0, 4 * i + 2] + a[0, 4 * i + 3])
        small[i] = planes
    rows = []
    for i in range(8):
        first = small[i, pl.ds(0, 8, stride=4), :] + small[i, pl.ds(1, 8, stride=4), :]
        rows.append(first + (small[i, pl.ds(2, 8, stride=4), :] + small[i, pl.ds(3, 8, stride=4), :]))
    fold = pick(128, 128, lambda r, c: (r >> 2) == (c & 31)) * (1.0 / 64)
    cells = jnp.dot(jnp.concatenate(rows, 0), fold, precision=EXACT, preferred_element_type=F32)
    group = iota((8, 128), 1) >> 5
    for h in range(2):
        tile = cells[32 * h : 32 * h + 8]
        for j in range(1, 4):
            tile = jnp.where(group == j, cells[32 * h + 8 * j : 32 * h + 8 * j + 8], tile)
        for k in range(8):
            out[k, SENT_COEF + h] = tile


def first_kernel(meta, bricks, u, f, a, out, small):
    _, _, bit_x, bit_y, _ = place_of(meta, bricks)
    mask = odd(32, 128)
    sources = ((u, False), (f, True), (f, False), (a, True), (a, False))

    def get(c, t):
        return pair_of(sources[c][0], t, sources[c][1], mask)

    pack_shell(get, out, bit_x, bit_y)
    pack_bottom_coef(a, out, small)


def around(src, k, red, mask, edges, cut=None):
    here = src[k]
    rows, cols = here.shape
    above, below = src[k + 1], src[k - 1]
    other = jnp.where(mask, above, below) if red else jnp.where(mask, below, above)
    up, down = pltpu.roll(here, 1, 0), pltpu.roll(here, rows - 1, 0)
    left, right = pltpu.roll(here, 1, 1), pltpu.roll(here, cols - 1, 1)
    if edges:
        row, lane = iota((rows, cols), 0), iota((rows, cols), 1)
        up, down = jnp.where(row == 0, 0.0, up), jnp.where(row == rows - 1, 0.0, down)
        if edges == 2:
            left, right = jnp.where(lane == 0, 0.0, left), jnp.where(lane == cols - 1, 0.0, right)
    if cut is not None:
        up, down = jnp.where(cut[0], 0.0, up), jnp.where(cut[1], 0.0, down)
    return ((here + other) + (up + down)) + (left + right)


def half_sweep(dst, src, force, inverse, lo, hi, red, mask, scale, edges, cut=None):
    def step(k, carry):
        total = around(src, k, red, mask, edges, cut)
        if scale != 1.0:
            total = scale * total
        dst[k] = (force[k] + total) * inverse[k]
        return carry

    lax.fori_loop(lo, hi, step, 0, unroll=True)


def pick(rows, cols, keep):
    return jnp.where(keep(iota((rows, cols), 0), iota((rows, cols), 1)), 1.0, 0.0).astype(F32)


def fine_down_kernel(meta, bricks, u, f, a, recv, rc, u_b, f_r, f_b, i_r, i_b, u_r, resid, small):
    slab, _, bit_x, bit_y, bit_z = place_of(meta, bricks)
    own = odd(32, 128)
    grids = (u_b, f_r, f_b, i_r, i_b)
    sources = ((u, False), (f, True), (f, False), (a, True), (a, False))
    for t in range(16):
        for grid, (cells, red) in zip(grids, sources):
            grid[OWN + t, 0:32, 0:128] = pair_of(cells, t, red, own)
    unpack_shell(recv, grids, bit_x, bit_y)
    zero = jnp.zeros((40, 256), F32)
    for k in (0, 25):
        u_r[k] = zero
        u_b[k] = zero
    for k in (1, 24):
        f_b[k] = zero
        i_b[k] = zero
    row, lane = iota((40, 256), 0), iota((40, 256), 1)
    x0, y0 = is_zero(bit_x, (40, 256)), is_zero(bit_y, (40, 256))
    x1, y1 = jnp.logical_not(x0), jnp.logical_not(y0)
    inside = (row < 32) | (y0 & (row < 39)) | (y1 & (row >= 33))
    inside = inside & ((lane < 128) | (x0 & (lane < 136)) | (x1 & (lane >= 248)))
    no_low = (slab == 0) & (bit_z == 0)
    no_high = (slab == SLABS - 1) & (bit_z == 1)

    mask_int = (row + lane) & 1

    def invert(k, carry):
        gone = jnp.where((no_low & (k < OWN)) | (no_high & (k >= OWN + 16)), 1, 0)
        keep = inside & is_zero(gone, (40, 256))
        far = jnp.where(k == 1, mask_int, jnp.where(k == 24, 1 - mask_int, 1)) == 1
        i_r[k] = jnp.where(keep & far, 1.0 / (i_r[k] + 6.0), 0.0)
        ends = jnp.where((k == 1) | (k == 24), 1, 0)
        i_b[k] = jnp.where(keep & is_zero(ends, (40, 256)), 1.0 / (i_b[k] + 6.0), 0.0)
        return carry

    lax.fori_loop(1, 25, invert, 0, unroll=4)
    mask = odd(40, 256)
    cut = (y0 & (row == 0), y1 & (row == 31))
    half_sweep(u_r, u_b, f_r, i_r, 1, 25, True, mask, 1.0, 0, cut)
    half_sweep(u_b, u_r, f_b, i_b, 1, 25, False, mask, 1.0, 0)
    half_sweep(u_r, u_b, f_r, i_r, 2, 24, True, mask, 1.0, 0)
    half_sweep(u_b, u_r, f_b, i_b, 3, 23, False, mask, 1.0, 0)
    for t in range(16):
        total = around(u_b, OWN + t, True, mask, 0)[0:32, 0:128]
        diag = pair_of(a, t, True, own) + 6.0
        resid[0, t] = pair_of(f, t, True, own) + total - diag * u_r[OWN + t, 0:32, 0:128]
        resid[1, t] = a[0, 2 * t] + a[0, 2 * t + 1]
    twice = pick(128, 128, lambda r, c: (r >> 1) == (c & 63)) * 0.125
    row, lane = iota((16, 128), 0), iota((16, 128), 1)
    even = ((row + lane + (lane >> 6)) & 1) == 0
    for i in range(2):
        for t in range(16):
            small[16 * t : 16 * t + 16] = (
                resid[i, t, pl.ds(0, 16, stride=2), :] + resid[i, t, pl.ds(1, 16, stride=2), :]
            )
        summed = jnp.dot(small[...], twice, precision=EXACT, preferred_element_type=F32)
        summed = summed.reshape(16, 16, 128)
        for j in range(8):
            rc[i, j] = jnp.where(even, summed[2 * j], summed[2 * j + 1])


def slot_of(member, me):
    return jnp.where((member >> 2) == (me >> 2), 0, 4) + ((me - member) & 3)


def faces_kernel(meta, bricks, *refs):
    boxes, (out, held) = refs[:8], refs[8:]
    slab, me = meta[0], meta[1]
    for i, box in enumerate(boxes):
        held[i] = box[...]
    start = jnp.where(me < 4, 3, 0)
    for i in range(4):
        member = jnp.where(me < 4, bricks[slab, 4 + i], bricks[slab, i])
        out[i] = held[slot_of(member, me), :, pl.ds(start, 5)]


def coarse_down_kernel(meta, bricks, *refs):
    boxes, (one, two, weights) = refs[:8], refs[8:11]
    rb, rb_send, part, e_b, r_r, r_b, i_r, i_b = refs[11:19]
    held, low, high, e_r, a_r, a_b, resid, small = refs[19:]
    slab, me = meta[0], meta[1]
    for i, box in enumerate(boxes):
        held[i] = box[...]

    @pl.when(me < 4)
    def _():
        low[...] = one[...]
        high[...] = two[...]

    @pl.when(me >= 4)
    def _():
        low[...] = two[...]
        high[...] = one[...]

    left = iota((16, 128), 1) < 64
    for q, (red, black) in enumerate(((r_r, r_b), (a_r, a_b))):

        def put(k, by, west, east):
            rows = slice(16 * by, 16 * by + 16)
            red[k, rows] = jnp.where(left, west, pltpu.roll(east, 64, 1))
            black[k, rows] = jnp.where(left, pltpu.roll(west, 64, 1), east)

        for by in range(2):
            for bz in range(2):
                west = slot_of(bricks[slab, 2 * by + 4 * bz], me)
                east = slot_of(bricks[slab, 2 * by + 4 * bz + 1], me)
                for j in range(8):
                    put(6 + 8 * bz + j, by, held[west, q, j], held[east, q, j])
            for j in range(5):
                put(1 + j, by, low[2 * by, q, j], low[2 * by + 1, q, j])
                put(22 + j, by, high[2 * by, q, j], high[2 * by + 1, q, j])
    for k in (0, 27):
        e_r[k] = jnp.zeros((32, 128), F32)
        e_b[k] = jnp.zeros((32, 128), F32)

    def start(k, carry):
        gone = jnp.where(((slab == 0) & (k < 6)) | ((slab == SLABS - 1) & (k >= 22)), 1, 0)
        keep = is_zero(gone, (32, 128))
        inverse = jnp.where(keep, 1.0 / (a_r[k] + 1.5), 0.0)
        i_r[k] = inverse
        i_b[k] = jnp.where(keep, 1.0 / (a_b[k] + 1.5), 0.0)
        e_r[k] = r_r[k] * inverse
        return carry

    lax.fori_loop(1, 27, start, 0, unroll=13)
    mask = odd(32, 128)
    half_sweep(e_b, e_r, r_b, i_b, 1, 27, False, mask, 0.25, 2)
    half_sweep(e_r, e_b, r_r, i_r, 1, 27, True, mask, 0.25, 2)
    half_sweep(e_b, e_r, r_b, i_b, 1, 27, False, mask, 0.25, 2)

    def residual(n, carry):
        k = n + 3
        total = 0.25 * around(e_b, k, True, mask, 2)
        resid[0, n] = r_r[k] + total - (a_r[k] + 1.5) * e_r[k]
        resid[1, n] = a_r[k] + a_b[k]
        return carry

    lax.fori_loop(0, 22, residual, 0, unroll=True)
    total = jnp.zeros((352, 128), F32)
    for i in range(2):
        for n in range(22):
            small[16 * n : 16 * n + 16] = (
                resid[i, n, pl.ds(0, 16, stride=2), :] + resid[i, n, pl.ds(1, 16, stride=2), :]
            )
        half = pick(128, 128, lambda r, c: (r >> 1) == c - 64 * i) * 0.125
        total = total + jnp.dot(small[...], half, precision=EXACT, preferred_element_type=F32)
    rb[...] = total.reshape(22, 16, 128)
    rb_send[...] = rb[pl.ds(jnp.where(me < 4, 1, 3), 18)]
    total = jnp.zeros((16, 128), F32)
    for i in range(16):
        total = total + rb[3 + i] * weights[i]
    part[...] = total[0:8] + total[8:16]


def bottom_kernel(meta, rb, one, two, es, e_r, e_b, g_r, g_b, i_r, i_b, low, high):
    slab, me = meta[0], meta[1]

    @pl.when(me < 4)
    def _():
        low[...] = one[...]
        high[...] = two[...]

    @pl.when(me >= 4)
    def _():
        low[...] = two[...]
        high[...] = one[...]

    mask = odd(16, 128)
    left = iota((16, 128), 1) < 64
    zero = jnp.zeros((16, 128), F32)
    for k in (0, 27):
        e_r[k] = zero
        e_b[k] = zero
    for j in range(26):
        planes = []
        for n in (2 * j, 2 * j + 1):
            planes.append(low[n] if n < 18 else rb[n - 15] if n < 34 else high[n - 34])
        keep = left
        if j < 9:
            keep = left & jnp.logical_not(is_zero(slab, (16, 128)))
        if j >= 17:
            keep = left & jnp.logical_not(is_zero(slab - (SLABS - 1), (16, 128)))
        for red in (True, False):
            cells = jnp.where(mask, planes[1], planes[0]) if red else jnp.where(mask, planes[0], planes[1])
            force = jnp.where(left, cells, 0.0)
            inverse = jnp.where(keep, 1.0 / (pltpu.roll(cells, 64, 1) + 0.375), 0.0)
            if red:
                g_r[1 + j], i_r[1 + j], e_r[1 + j] = force, inverse, force * inverse
            else:
                g_b[1 + j], i_b[1 + j] = force, inverse
    half_sweep(e_b, e_r, g_b, i_b, 1, 27, False, mask, 0.0625, 1)

    def sweep(n, carry):
        half_sweep(e_r, e_b, g_r, i_r, 1, 27, True, mask, 0.0625, 1)
        half_sweep(e_b, e_r, g_b, i_b, 1, 27, False, mask, 0.0625, 1)
        return carry

    lax.fori_loop(0, 7, sweep, 0)
    for i in range(22):
        k, upper = (15 + i) // 2 + 1, (15 + i) % 2
        es[i] = jnp.where(mask, e_r[k], e_b[k]) if upper else jnp.where(mask, e_b[k], e_r[k])


def weights_kernel(meta, here, there, out, t_r, t_b, w_r, w_b, i_r, i_b, low, high):
    slab, me = meta[0], meta[1]

    @pl.when(me < 4)
    def _():
        low[...] = there[1]
        high[...] = here[1]

    @pl.when(me >= 4)
    def _():
        low[...] = here[1]
        high[...] = there[1]

    lane = iota((8, 128), 1)

    def plane(boxes, z):
        rows = []
        for by in range(2):
            place, shift = 4 * (z >> 3) + 2 * by, 32 * (z & 3)
            west = pltpu.roll(boxes(place, (z & 7) >> 2), (128 - shift) % 128, 1)
            east = pltpu.roll(boxes(place + 1, (z & 7) >> 2), (160 - shift) % 128, 1)
            rows.append(jnp.where(lane < 32, west, east))
        return jnp.concatenate(rows, 0)

    parts = (lambda p, h: low[p, h], lambda p, h: here[0, p, h], lambda p, h: high[p, h])
    mask = odd(16, 128)
    left = iota((16, 128), 1) < 64
    zero = jnp.zeros((16, 128), F32)
    for k in (0, 25):
        t_r[k] = zero
        t_b[k] = zero
    for j in range(24):
        lower, upper = (plane(parts[(2 * j + i) // 16], (2 * j + i) % 16) for i in range(2))
        keep = left
        if j < 8:
            keep = left & jnp.logical_not(is_zero(slab, (16, 128)))
        if j >= 16:
            keep = left & jnp.logical_not(is_zero(slab - (SLABS - 1), (16, 128)))
        i_r[1 + j] = jnp.where(keep, 1.0 / (jnp.where(mask, upper, lower) + 0.375), 0.0)
        i_b[1 + j] = jnp.where(keep, 1.0 / (jnp.where(mask, lower, upper) + 0.375), 0.0)
    for k in range(1, 25):
        t_b[k] = i_b[k]
        w_b[k] = i_b[k]
    for k in range(1, 25):
        t = i_r[k] * (1.0 + 0.0625 * around(t_b, k, True, mask, 1))
        t_r[k] = t
        w_r[k] = t

    def sweep(n, carry):
        for k in range(1, 25):
            t = i_b[k] * (0.0625 * around(t_r, k, False, mask, 1))
            t_b[k] = t
            w_b[k] = w_b[k] + t
        for k in range(1, 25):
            t = i_r[k] * (0.0625 * around(t_b, k, True, mask, 1))
            t_r[k] = t
            w_r[k] = w_r[k] + t
        return carry

    lax.fori_loop(0, 7, sweep, 0)
    for j in range(8):
        red, black = w_r[9 + j], w_b[9 + j]
        out[2 * j] = jnp.where(mask, black, red)
        out[2 * j + 1] = jnp.where(mask, red, black)


def up_kernel(
    meta, bricks, sum_0, sum_1, sum_2, sum_3, es, ec_b, r_r, r_b, ci_r, ci_b, u1_b, f_r, f_b, i_r, i_b, out,
    e_r, e_b, small, wide, planes, tall, u_r, u_b,
):
    slab, _, bit_x, bit_y, bit_z = place_of(meta, bricks)
    total = (sum_0[...] + sum_1[...]) + (sum_2[...] + sum_3[...])
    mean = jnp.sum(total) * (1.0 / (SLABS * 16 * 16 * 64))
    for i in range(22):
        shifted = es[i] - mean
        if i < 3:
            shifted = jnp.where(is_zero(slab, (16, 128)), 0.0, shifted)
        if i >= 19:
            shifted = jnp.where(is_zero(slab - (SLABS - 1), (16, 128)), 0.0, shifted)
        small[16 * i : 16 * i + 16] = shifted
    spread = pick(128, 128, lambda r, c: r == (c >> 1))
    small[...] = jnp.dot(small[...], spread, precision=EXACT, preferred_element_type=F32)
    for i in range(22):
        rows = small[16 * i : 16 * i + 16]
        wide[i, pl.ds(0, 16, stride=2), :] = rows
        wide[i, pl.ds(1, 16, stride=2), :] = rows
    for k in (0, 1, 2, 25, 26, 27):
        e_r[k] = jnp.zeros((32, 128), F32)
        e_b[k] = jnp.zeros((32, 128), F32)
    for i in range(22):
        e_b[3 + i] = ec_b[3 + i] + wide[i]
    coarse = odd(32, 128)
    for _ in range(2):
        half_sweep(e_r, e_b, r_r, ci_r, 3, 25, True, coarse, 0.25, 2)
        half_sweep(e_b, e_r, r_b, ci_b, 3, 25, False, coarse, 0.25, 2)
    for n in range(20):
        z = n - 2
        k = 8 * bit_z + (z // 2 + 6)
        red, black = e_r[k], e_b[k]
        planes[32 * n : 32 * n + 32] = jnp.where(coarse, red, black) if z % 2 else jnp.where(coarse, black, red)

    lane = iota((128, 256), 1)
    x0 = is_zero(bit_x, (128, 256))
    start = jnp.where(lane < 128, 64 * bit_x + (lane >> 1), (lane >> 1) + jnp.where(x0, 0, -64))
    usable = (lane < 128) | (x0 & (lane < 136)) | (jnp.logical_not(x0) & (lane >= 248))
    spread = jnp.where(usable & (iota((128, 256), 0) == start), 1.0, 0.0).astype(F32)
    tall_rows = jnp.dot(planes[...], spread, precision=EXACT, preferred_element_type=F32)
    for n in range(20):
        rows = tall_rows[32 * n : 32 * n + 32]
        for h in range(2):
            tall[n, h, pl.ds(0, 32, stride=2), :] = rows[:, 128 * h : 128 * h + 128]
            tall[n, h, pl.ds(1, 32, stride=2), :] = rows[:, 128 * h : 128 * h + 128]
    for k in (0, 21):
        u_r[k] = jnp.zeros((40, 256), F32)
        u_b[k] = jnp.zeros((40, 256), F32)
    row = iota((8, 128), 0)
    y0 = is_zero(bit_y)
    in_y = (y0 & (row != 7)) | (jnp.logical_not(y0) & (row != 0))
    own_start = pl.multiple_of(32 * bit_y, 32)
    side_start = pl.multiple_of(32 - 8 * bit_y, 8)
    for n in range(20):
        for h in range(2):
            lanes = slice(128 * h, 128 * h + 128)
            side = jnp.where(in_y, tall[n, h, pl.ds(side_start, 8), :], 0.0)
            u_b[1 + n, 0:32, lanes] = u1_b[3 + n, 0:32, lanes] + tall[n, h, pl.ds(own_start, 32), :]
            u_b[1 + n, 32:40, lanes] = u1_b[3 + n, 32:40, lanes] + side
    mask = odd(40, 256)
    f_r, f_b, i_r, i_b = (grid.at[2:24] for grid in (f_r, f_b, i_r, i_b))
    half_sweep(u_r, u_b, f_r, i_r, 1, 21, True, mask, 1.0, 0)
    half_sweep(u_b, u_r, f_b, i_b, 2, 20, False, mask, 1.0, 0)
    half_sweep(u_r, u_b, f_r, i_r, 2, 20, True, mask, 1.0, 0)
    half_sweep(u_b, u_r, f_b, i_b, 3, 19, False, mask, 1.0, 0)
    own = odd(32, 128)
    for t in range(16):
        red, black = u_r[3 + t, 0:32, 0:128], u_b[3 + t, 0:32, 0:128]
        out[0, 2 * t] = jnp.where(own, black, red)
        out[0, 2 * t + 1] = jnp.where(own, red, black)


def swap_cores(x):
    return lax.ppermute(x, "level", [(0, 1), (1, 0)])


def to_slabs(x, up_first):
    pairs = []
    for s in range(SLABS - 1):
        for m in range(8):
            low, high = s * 8 + m, (s + 1) * 8 + m
            pairs.append((low, high) if (m < 4) == up_first else (high, low))
    return lax.ppermute(x, ALL, pairs)


def around_ring(x, stride, step):
    pairs = []
    for s in range(SLABS):
        at = s // stride % 4
        pairs.append((s, s + ((at + step) % 4 - at) * stride))
    return lax.ppermute(x, "slab", pairs)


def among(x):
    return lax.all_to_all(x, LB, split_axis=0, concat_axis=0, tiled=True)


def body(u_init, source, coeffs, brick_map):
    meta = jnp.stack([lax.axis_index("slab"), lax.axis_index(LB)]).astype(jnp.int32)
    smem = [meta, brick_map]
    fine = (26, 40, 256)
    packed = run(
        first_kernel, [(8, SENT, 8, 128)], smem, [u_init, source, coeffs], [(8, 32, 128)],
    )
    got = among(packed)
    leaving = run(cross_kernel, [(4, FACE + 4, 8, 128)], smem, [got])
    cross = to_slabs(leaving, False)
    sent, coef = run(
        mid_kernel, [(8, GOT, 8, 128), (2, 8, 2, 8, 128)], smem, [got, cross], [(12, FACE, 8, 128)],
    )
    coef_other = swap_cores(coef)
    halo = among(sent)
    weights = run(
        weights_kernel, [(16, 16, 128)], [meta], [coef, coef_other],
        [(26, 16, 128)] * 6 + [(8, 2, 8, 128)] * 2,
    )
    halo, weights = lax.optimization_barrier((halo, weights))
    rc, u_b, f_r, f_b, i_r, i_b = run(
        fine_down_kernel, [(2, 8, 16, 128)] + [fine] * 5, smem, [u_init, source, coeffs, halo],
        [fine, (2, 16, 32, 128), (256, 128)],
    )
    boxes = [rc] + [
        lax.ppermute(rc, "bottom", [(i, (i + d) % 4) for i in range(4)]) for d in range(1, 4)
    ]
    boxes = boxes + [swap_cores(box) for box in boxes]
    leaving = run(faces_kernel, [(4, 2, 5, 16, 128)], smem, boxes, [(8, 2, 8, 16, 128)])
    cross = to_slabs(leaving, True)
    other = swap_cores(cross)
    coarse = (28, 32, 128)
    faces = (4, 2, 5, 16, 128)
    rb, rb_send, part, ec_b, r_r, r_b, ci_r, ci_b = run(
        coarse_down_kernel, [(22, 16, 128), (18, 16, 128), (8, 128)] + [coarse] * 5, smem,
        boxes + [cross, other, weights],
        [(8, 2, 8, 16, 128), faces, faces, coarse, coarse, coarse, (2, 22, 32, 128), (352, 128)],
    )
    cross = to_slabs(rb_send, True)
    rows = [around_ring(part, 1, d) for d in range(1, 4)]
    cross, *rows = lax.optimization_barrier((cross, *rows))
    other = swap_cores(cross)
    part = (part + rows[0]) + (rows[1] + rows[2])
    sums = [part] + [around_ring(part, 4, d) for d in range(1, 4)]
    bottom = (28, 16, 128)
    es = run(
        bottom_kernel, [(22, 16, 128)], [meta], [rb, cross, other],
        [bottom] * 6 + [(18, 16, 128)] * 2,
    )
    return run(
        up_kernel, [(1, 32, 32, 128)], smem,
        sums + [es, ec_b, r_r, r_b, ci_r, ci_b, u_b, f_r, f_b, i_r, i_b],
        [coarse, coarse, (352, 128), (22, 32, 128), (640, 128), (20, 2, 64, 128), (22, 40, 256), (22, 40, 256)],
    )


def solution(mesh):
    placed = P(ALL, None, None, None)
    return jax.shard_map(
        body, mesh=mesh, in_specs=(placed, placed, placed, P()), out_specs=placed, check_vma=False
    )
```

```python
import jax
import jax.numpy as jnp
from jax import lax
from jax.experimental import pallas as pl
from jax.experimental.pallas import tpu as pltpu
from jax.sharding import PartitionSpec as P

LB = ("level", "bottom")
ALL = ("slab", "level", "bottom")
SLABS = 16
OWN = 5
F32 = jnp.float32
VMEM_SPEC = pl.BlockSpec(memory_space=pltpu.VMEM)
SMEM_SPEC = pl.BlockSpec(memory_space=pltpu.SMEM)
EXACT = lax.Precision.HIGHEST


def run(kernel, outs, smem, vmem, scratch=()):
    shapes = [jax.ShapeDtypeStruct(s, F32) for s in outs]
    single = len(shapes) == 1
    return pl.pallas_call(
        kernel,
        out_shape=shapes[0] if single else shapes,
        in_specs=[SMEM_SPEC] * len(smem) + [VMEM_SPEC] * len(vmem),
        out_specs=VMEM_SPEC if single else [VMEM_SPEC] * len(shapes),
        scratch_shapes=[pltpu.VMEM(s, F32) for s in scratch],
        compiler_params=pltpu.CompilerParams(vmem_limit_bytes=20 << 20),
    )(*smem, *vmem)


def iota(shape, dim):
    return lax.broadcasted_iota(jnp.int32, shape, dim)


def odd(rows, cols):
    return ((iota((rows, cols), 0) + iota((rows, cols), 1)) & 1) == 1


def place_of(meta, bricks):
    slab, me = meta[0], meta[1]
    place = jnp.int32(0)
    for i in range(8):
        place = place + jnp.where(bricks[slab, i] == me, i, 0)
    return slab, me, place & 1, (place >> 1) & 1, place >> 2


def is_zero(scalar, shape=(8, 128)):
    return jnp.full(shape, scalar, jnp.int32) == 0


ARRAYS = 5
FACE = 17
SENT_Y, SENT_X, SENT_COEF, SENT = 17, 27, 30, 32
GOT_ROWS, GOT_STRIPS, GOT_Y, GOT_X, GOT = 17, 20, 22, 32, 35


def face_planes(j):
    return [(1 + j, 0), (1 + j, 1), (1 + j, 2), (0, j)]


def merge_strips(placed, base=None):
    group = iota((8, 128), 1) // 8
    total = jnp.zeros((8, 128), F32) if base is None else base
    for pos, strip in placed:
        moved = pltpu.roll(strip, 8 * pos, 1) if pos else strip
        total = jnp.where(group == pos, moved, total)
    return total


def swap_lanes(cells):
    lane = iota(cells.shape, 1)
    return jnp.where((lane & 1) == 0, pltpu.roll(cells, cells.shape[1] - 1, 1), pltpu.roll(cells, 1, 1))


def pack_shell(get, out, bit_x, bit_y):
    x0, y0 = is_zero(bit_x), is_zero(bit_y)
    mask = odd(32, 128)
    for k in range(8):
        high, j = k >= 4, k % 4
        for i, (c, far) in enumerate(face_planes(j)):
            out[k, 4 * i : 4 * i + 4] = get(c, 15 - far if high else far).reshape(4, 8, 128)
        t = 12 if high else 3
        one, two = get(1, t), swap_lanes(get(3, t))
        both = jnp.where(mask, one, two) if high else jnp.where(mask, two, one)
        out[k, 16] = both[8 * j : 8 * j + 8]
        strips = []
        for tl in range(2):
            for c in range(ARRAYS):
                v = get(c, 2 * k + tl)
                out[k, SENT_Y + tl * ARRAYS + c] = jnp.where(y0, v[24:32], v[0:8])
                for g in range(4):
                    tile = v[8 * g : 8 * g + 8]
                    strips.append(jnp.where(x0, pltpu.roll(tile, 8, 1), tile))
        for i in range(3):
            out[k, SENT_X + i] = merge_strips(list(enumerate(strips[16 * i : 16 * i + 16])))


def cross_kernel(meta, bricks, recv, out):
    slab, me = meta[0], meta[1]
    for i in range(4):
        src = jnp.where(me >= 4, bricks[slab, 4 + i], bricks[slab, i])
        out[i, 0:FACE] = recv[src, 0:FACE]
        for j in range(2):
            coef = recv[bricks[slab, 2 * i + j], SENT_COEF:SENT]
            out[i, FACE + 2 * j : FACE + 2 * j + 2] = coef


def mid_kernel(meta, bricks, recv, cross, out, coef, faces):
    slab, me = meta[0], meta[1]
    faces[0:8] = recv[:, 0:FACE]
    faces[8:12] = cross[:, 0:FACE]
    for p in range(8):
        coef[0, p] = recv[bricks[slab, p], SENT_COEF:SENT]
        j = FACE + 2 * (p & 1)
        coef[1, p] = cross[p >> 1, j : j + 2]
    row = iota((8, 128), 0)
    for p in range(8):
        bx, by, bz = p & 1, (p >> 1) & 1, p >> 2
        dest = bricks[slab, p]
        same = me >= 4 if bz else me < 4

        def src(q):
            return jnp.where(same, bricks[slab, (q & 3) + 4 * (1 - bz)], 8 + (q & 3))

        def strip_of(tile):
            return pltpu.roll(tile, 8, 1) if bx else tile

        def rows_of(at):
            one, two, three, last = (faces[at, 4 * i + (3 if by else 0)] for i in range(4))
            if by:
                shared = jnp.where(row >= 3, two, pltpu.roll(three, 3, 0))
            else:
                shared = jnp.where(row < 5, two, pltpu.roll(three, 5, 0))
            return [one, shared, last]

        at_own, at_y, at_x, at_xy = src(p), src(p ^ 2), src(p ^ 1), src(p ^ 3)
        out[dest, 0:FACE] = faces[at_own]
        for i, tile in enumerate(rows_of(at_y)):
            out[dest, GOT_ROWS + i] = tile
        strips = [strip_of(faces[at_x, i]) for i in range(16)] + [strip_of(tile) for tile in rows_of(at_xy)]
        from_y, from_x, from_xy = bricks[slab, p ^ 2], bricks[slab, p ^ 1], bricks[slab, p ^ 3]
        strips += [strip_of(recv[from_xy, SENT_Y + i]) for i in range(2 * ARRAYS)]
        for i in range(2):
            out[dest, GOT_STRIPS + i] = merge_strips(list(enumerate(strips[16 * i : 16 * i + 16])))
        out[dest, GOT_Y:GOT_X] = recv[from_y, SENT_Y:SENT_X]
        out[dest, GOT_X:GOT] = recv[from_x, SENT_X:SENT_COEF]


def unpack_shell(recv, grids, bit_x, bit_y):
    row, lane = iota((8, 128), 0), iota((8, 128), 1)
    x0, y0 = is_zero(bit_x), is_zero(bit_y)
    in_x = (x0 & (lane < 8)) | (jnp.logical_not(x0) & (lane >= 120))
    five = (y0 & (row < 5)) | (jnp.logical_not(y0) & (row >= 3))
    three = (y0 & (row < 3)) | (jnp.logical_not(y0) & (row >= 5))

    def strip(tile, pos):
        shift = (jnp.where(bit_x == 0, 0, 120) + 128 - 8 * pos) % 128
        return jnp.where(in_x, pltpu.roll(tile, shift, 1), 0.0)

    def rows_of(tiles):
        one, shared, last = tiles
        moved = jnp.where(y0, pltpu.roll(shared, 3, 0), pltpu.roll(shared, 5, 0))
        return [one, jnp.where(five, shared, 0.0), jnp.where(three, moved, 0.0), last]

    for k in range(8):
        high, j = k >= 4, k % 4
        rows = rows_of([recv[k, GOT_ROWS + i] for i in range(3)])
        sides = rows_of([strip(recv[k, GOT_STRIPS + 1], i) for i in range(3)])
        for i, (c, far) in enumerate(face_planes(j)):
            at = OWN - 1 - far if high else OWN + 16 + far
            for g in range(4):
                grids[c][at, 8 * g : 8 * g + 8, 0:128] = recv[k, 4 * i + g]
                grids[c][at, 8 * g : 8 * g + 8, 128:256] = strip(recv[k, GOT_STRIPS], 4 * i + g)
            grids[c][at, 32:40, 0:128] = rows[i]
            grids[c][at, 32:40, 128:256] = sides[i]
        at = 1 if high else 24
        both = recv[k, 16]
        for c, cells in ((1, both), (3, swap_lanes(both))):
            grids[c][at, 8 * j : 8 * j + 8, 0:128] = cells
            grids[c][at, 8 * j : 8 * j + 8, 128:256] = jnp.zeros((8, 128), F32)
            grids[c][at, 32:40] = jnp.zeros((8, 256), F32)
        for tl in range(2):
            for c in range(ARRAYS):
                i = tl * ARRAYS + c
                at = OWN + 2 * k + tl
                grids[c][at, 32:40, 0:128] = recv[k, GOT_Y + i]
                grids[c][at, 32:40, 128:256] = strip(recv[k, GOT_STRIPS + 1], 3 + i)
                for g in range(4):
                    n = 4 * i + g
                    side = strip(recv[k, GOT_X + n // 16], n % 16)
                    grids[c][at, 8 * g : 8 * g + 8, 128:256] = side


def pair_of(cells, t, red, mask):
    low, high = cells[0, 2 * t], cells[0, 2 * t + 1]
    return jnp.where(mask, high, low) if red else jnp.where(mask, low, high)


def pack_bottom_coef(a, out, small):
    for i in range(8):
        planes = (a[0, 4 * i] + a[0, 4 * i + 1]) + (a[0, 4 * i + 2] + a[0, 4 * i + 3])
        small[i] = planes
    rows = []
    for i in range(8):
        first = small[i, pl.ds(0, 8, stride=4), :] + small[i, pl.ds(1, 8, stride=4), :]
        rows.append(first + (small[i, pl.ds(2, 8, stride=4), :] + small[i, pl.ds(3, 8, stride=4), :]))
    fold = pick(128, 128, lambda r, c: (r >> 2) == (c & 31)) * (1.0 / 64)
    cells = jnp.dot(jnp.concatenate(rows, 0), fold, precision=EXACT, preferred_element_type=F32)
    group = iota((8, 128), 1) >> 5
    for h in range(2):
        tile = cells[32 * h : 32 * h + 8]
        for j in range(1, 4):
            tile = jnp.where(group == j, cells[32 * h + 8 * j : 32 * h + 8 * j + 8], tile)
        for k in range(8):
            out[k, SENT_COEF + h] = tile


def pack_coarse(planes, small, out):
    twice = pick(128, 128, lambda r, c: (r >> 1) == (c & 63)) * 0.125
    row, lane = iota((16, 128), 0), iota((16, 128), 1)
    even = ((row + lane + (lane >> 6)) & 1) == 0
    for t in range(16):
        small[16 * t : 16 * t + 16] = planes[t, pl.ds(0, 16, stride=2), :] + planes[t, pl.ds(1, 16, stride=2), :]
    summed = jnp.dot(small[...], twice, precision=EXACT, preferred_element_type=F32)
    summed = summed.reshape(16, 16, 128)
    for j in range(8):
        out[j] = jnp.where(even, summed[2 * j], summed[2 * j + 1])


def first_kernel(meta, bricks, u, f, a, out, ac, small, planes, rows):
    _, _, bit_x, bit_y, _ = place_of(meta, bricks)
    mask = odd(32, 128)
    sources = ((u, False), (f, True), (f, False), (a, True), (a, False))

    def get(c, t):
        return pair_of(sources[c][0], t, sources[c][1], mask)

    pack_shell(get, out, bit_x, bit_y)
    pack_bottom_coef(a, out, small)
    for t in range(16):
        planes[t] = a[0, 2 * t] + a[0, 2 * t + 1]
    pack_coarse(planes, rows, ac)


def around(src, k, red, mask, edges, cut=None):
    here = src[k]
    rows, cols = here.shape
    above, below = src[k + 1], src[k - 1]
    other = jnp.where(mask, above, below) if red else jnp.where(mask, below, above)
    up, down = pltpu.roll(here, 1, 0), pltpu.roll(here, rows - 1, 0)
    left, right = pltpu.roll(here, 1, 1), pltpu.roll(here, cols - 1, 1)
    if edges:
        row, lane = iota((rows, cols), 0), iota((rows, cols), 1)
        up, down = jnp.where(row == 0, 0.0, up), jnp.where(row == rows - 1, 0.0, down)
        if edges == 2:
            left, right = jnp.where(lane == 0, 0.0, left), jnp.where(lane == cols - 1, 0.0, right)
    if cut is not None:
        up, down = jnp.where(cut[0], 0.0, up), jnp.where(cut[1], 0.0, down)
    return ((here + other) + (up + down)) + (left + right)


def half_sweep(dst, src, force, inverse, lo, hi, red, mask, scale, edges, cut=None):
    def step(k, carry):
        total = around(src, k, red, mask, edges, cut)
        if scale != 1.0:
            total = scale * total
        dst[k] = (force[k] + total) * inverse[k]
        return carry

    lax.fori_loop(lo, hi, step, 0, unroll=True)


def pick(rows, cols, keep):
    return jnp.where(keep(iota((rows, cols), 0), iota((rows, cols), 1)), 1.0, 0.0).astype(F32)


def fine_down_kernel(meta, bricks, u, f, a, recv, rc, u_b, f_r, f_b, i_r, i_b, u_r, resid, small):
    slab, _, bit_x, bit_y, bit_z = place_of(meta, bricks)
    own = odd(32, 128)
    grids = (u_b, f_r, f_b, i_r, i_b)
    sources = ((u, False), (f, True), (f, False), (a, True), (a, False))
    for t in range(16):
        for grid, (cells, red) in zip(grids, sources):
            grid[OWN + t, 0:32, 0:128] = pair_of(cells, t, red, own)
    unpack_shell(recv, grids, bit_x, bit_y)
    zero = jnp.zeros((40, 256), F32)
    for k in (0, 25):
        u_r[k] = zero
        u_b[k] = zero
    for k in (1, 24):
        f_b[k] = zero
        i_b[k] = zero
    row, lane = iota((40, 256), 0), iota((40, 256), 1)
    x0, y0 = is_zero(bit_x, (40, 256)), is_zero(bit_y, (40, 256))
    x1, y1 = jnp.logical_not(x0), jnp.logical_not(y0)
    inside = (row < 32) | (y0 & (row < 39)) | (y1 & (row >= 33))
    inside = inside & ((lane < 128) | (x0 & (lane < 136)) | (x1 & (lane >= 248)))
    no_low = (slab == 0) & (bit_z == 0)
    no_high = (slab == SLABS - 1) & (bit_z == 1)

    mask_int = (row + lane) & 1

    def invert(k, carry):
        gone = jnp.where((no_low & (k < OWN)) | (no_high & (k >= OWN + 16)), 1, 0)
        keep = inside & is_zero(gone, (40, 256))
        far = jnp.where(k == 1, mask_int, jnp.where(k == 24, 1 - mask_int, 1)) == 1
        i_r[k] = jnp.where(keep & far, 1.0 / (i_r[k] + 6.0), 0.0)
        ends = jnp.where((k == 1) | (k == 24), 1, 0)
        i_b[k] = jnp.where(keep & is_zero(ends, (40, 256)), 1.0 / (i_b[k] + 6.0), 0.0)
        return carry

    lax.fori_loop(1, 25, invert, 0, unroll=4)
    mask = odd(40, 256)
    cut = (y0 & (row == 0), y1 & (row == 31))
    half_sweep(u_r, u_b, f_r, i_r, 1, 25, True, mask, 1.0, 0, cut)
    half_sweep(u_b, u_r, f_b, i_b, 1, 25, False, mask, 1.0, 0)
    half_sweep(u_r, u_b, f_r, i_r, 2, 24, True, mask, 1.0, 0)
    half_sweep(u_b, u_r, f_b, i_b, 3, 23, False, mask, 1.0, 0)
    for t in range(16):
        total = around(u_b, OWN + t, True, mask, 0)[0:32, 0:128]
        diag = pair_of(a, t, True, own) + 6.0
        resid[t] = pair_of(f, t, True, own) + total - diag * u_r[OWN + t, 0:32, 0:128]
    pack_coarse(resid, small, rc)


def slot_of(member, me):
    return jnp.where((member >> 2) == (me >> 2), 0, 4) + ((me - member) & 3)


def faces_kernel(meta, bricks, *refs):
    boxes, (out, held) = refs[:8], refs[8:]
    slab, me = meta[0], meta[1]
    for i, box in enumerate(boxes):
        held[i] = box[...]
    start = jnp.where(me < 4, 3, 0)
    for i in range(4):
        member = jnp.where(me < 4, bricks[slab, 4 + i], bricks[slab, i])
        out[i] = held[slot_of(member, me), pl.ds(start, 5)]


def sort_sides(me, one, two, low, high):
    @pl.when(me < 4)
    def _():
        low[...] = one[...]
        high[...] = two[...]

    @pl.when(me >= 4)
    def _():
        low[...] = two[...]
        high[...] = one[...]


def assemble(meta, bricks, boxes, one, two, red, black, held, low, high):
    slab, me = meta[0], meta[1]
    for i, box in enumerate(boxes):
        held[i] = box[...]
    sort_sides(me, one, two, low, high)
    left = iota((16, 128), 1) < 64

    def put(k, by, west, east):
        rows = slice(16 * by, 16 * by + 16)
        red[k, rows] = jnp.where(left, west, pltpu.roll(east, 64, 1))
        black[k, rows] = jnp.where(left, pltpu.roll(west, 64, 1), east)

    for by in range(2):
        for bz in range(2):
            west = slot_of(bricks[slab, 2 * by + 4 * bz], me)
            east = slot_of(bricks[slab, 2 * by + 4 * bz + 1], me)
            for j in range(8):
                put(6 + 8 * bz + j, by, held[west, j], held[east, j])
        for j in range(5):
            put(1 + j, by, low[2 * by, j], low[2 * by + 1, j])
            put(22 + j, by, high[2 * by, j], high[2 * by + 1, j])


def to_bottom(planes, small, half):
    for n in range(22):
        small[16 * n : 16 * n + 16] = planes[n, pl.ds(0, 16, stride=2), :] + planes[n, pl.ds(1, 16, stride=2), :]
    fold = pick(128, 128, lambda r, c: (r >> 1) == c - 64 * half) * 0.125
    return jnp.dot(small[...], fold, precision=EXACT, preferred_element_type=F32).reshape(22, 16, 128)


def coarse_coef_kernel(meta, bricks, *refs):
    boxes, (one, two) = refs[:8], refs[8:10]
    a_r, i_r, i_b, ab = refs[10:14]
    held, low, high, a_b, planes, small = refs[14:]
    slab = meta[0]
    assemble(meta, bricks, boxes, one, two, a_r, a_b, held, low, high)
    for k in range(1, 27):
        keep = jnp.full((32, 128), 0, jnp.int32) == 0
        if k < 6:
            keep = jnp.logical_not(is_zero(slab, (32, 128)))
        if k >= 22:
            keep = jnp.logical_not(is_zero(slab - (SLABS - 1), (32, 128)))
        i_r[k] = jnp.where(keep, 1.0 / (a_r[k] + 1.5), 0.0)
        i_b[k] = jnp.where(keep, 1.0 / (a_b[k] + 1.5), 0.0)
    for n in range(22):
        planes[n] = a_r[3 + n] + a_b[3 + n]
    ab[...] = to_bottom(planes, small, 1)


def coarse_down_kernel(meta, bricks, *refs):
    boxes, (one, two, weights, a_r, i_r, i_b, ab) = refs[:8], refs[8:15]
    rb, rb_send, part, e_b, r_r, r_b = refs[15:21]
    held, low, high, e_r, resid, small = refs[21:]
    me = meta[1]
    assemble(meta, bricks, boxes, one, two, r_r, r_b, held, low, high)
    for k in (0, 27):
        e_r[k] = jnp.zeros((32, 128), F32)
        e_b[k] = jnp.zeros((32, 128), F32)
    for k in range(1, 27):
        e_r[k] = r_r[k] * i_r[k]
    mask = odd(32, 128)
    half_sweep(e_b, e_r, r_b, i_b, 1, 27, False, mask, 0.25, 2)
    half_sweep(e_r, e_b, r_r, i_r, 1, 27, True, mask, 0.25, 2)
    half_sweep(e_b, e_r, r_b, i_b, 1, 27, False, mask, 0.25, 2)
    for n in range(22):
        k = n + 3
        total = 0.25 * around(e_b, k, True, mask, 2)
        resid[n] = r_r[k] + total - (a_r[k] + 1.5) * e_r[k]
    rb[...] = to_bottom(resid, small, 0) + ab[...]
    rb_send[...] = rb[pl.ds(jnp.where(me < 4, 1, 3), 18)]
    total = jnp.zeros((16, 128), F32)
    for i in range(16):
        total = total + rb[3 + i] * weights[i]
    part[...] = total[0:8] + total[8:16]


def bottom_kernel(meta, rb, one, two, es, e_r, e_b, g_r, g_b, i_r, i_b, low, high):
    slab, me = meta[0], meta[1]
    sort_sides(me, one, two, low, high)
    mask = odd(16, 128)
    left = iota((16, 128), 1) < 64
    zero = jnp.zeros((16, 128), F32)
    for k in (0, 27):
        e_r[k] = zero
        e_b[k] = zero
    for j in range(26):
        planes = []
        for n in (2 * j, 2 * j + 1):
            planes.append(low[n] if n < 18 else rb[n - 15] if n < 34 else high[n - 34])
        keep = left
        if j < 9:
            keep = left & jnp.logical_not(is_zero(slab, (16, 128)))
        if j >= 17:
            keep = left & jnp.logical_not(is_zero(slab - (SLABS - 1), (16, 128)))
        for red in (True, False):
            cells = jnp.where(mask, planes[1], planes[0]) if red else jnp.where(mask, planes[0], planes[1])
            force = jnp.where(left, cells, 0.0)
            inverse = jnp.where(keep, 1.0 / (pltpu.roll(cells, 64, 1) + 0.375), 0.0)
            if red:
                g_r[1 + j], i_r[1 + j], e_r[1 + j] = force, inverse, force * inverse
            else:
                g_b[1 + j], i_b[1 + j] = force, inverse
    half_sweep(e_b, e_r, g_b, i_b, 1, 27, False, mask, 0.0625, 1)

    def sweep(n, carry):
        half_sweep(e_r, e_b, g_r, i_r, 1, 27, True, mask, 0.0625, 1)
        half_sweep(e_b, e_r, g_b, i_b, 1, 27, False, mask, 0.0625, 1)
        return carry

    lax.fori_loop(0, 7, sweep, 0)
    for i in range(22):
        k, upper = (15 + i) // 2 + 1, (15 + i) % 2
        es[i] = jnp.where(mask, e_r[k], e_b[k]) if upper else jnp.where(mask, e_b[k], e_r[k])


def weights_kernel(meta, here, there, out, t_r, t_b, w_r, w_b, i_r, i_b, low, high):
    slab, me = meta[0], meta[1]

    @pl.when(me < 4)
    def _():
        low[...] = there[1]
        high[...] = here[1]

    @pl.when(me >= 4)
    def _():
        low[...] = here[1]
        high[...] = there[1]

    lane = iota((8, 128), 1)

    def plane(boxes, z):
        rows = []
        for by in range(2):
            place, shift = 4 * (z >> 3) + 2 * by, 32 * (z & 3)
            west = pltpu.roll(boxes(place, (z & 7) >> 2), (128 - shift) % 128, 1)
            east = pltpu.roll(boxes(place + 1, (z & 7) >> 2), (160 - shift) % 128, 1)
            rows.append(jnp.where(lane < 32, west, east))
        return jnp.concatenate(rows, 0)

    parts = (lambda p, h: low[p, h], lambda p, h: here[0, p, h], lambda p, h: high[p, h])
    mask = odd(16, 128)
    left = iota((16, 128), 1) < 64
    zero = jnp.zeros((16, 128), F32)
    for k in (0, 25):
        t_r[k] = zero
        t_b[k] = zero
    for j in range(24):
        lower, upper = (plane(parts[(2 * j + i) // 16], (2 * j + i) % 16) for i in range(2))
        keep = left
        if j < 8:
            keep = left & jnp.logical_not(is_zero(slab, (16, 128)))
        if j >= 16:
            keep = left & jnp.logical_not(is_zero(slab - (SLABS - 1), (16, 128)))
        i_r[1 + j] = jnp.where(keep, 1.0 / (jnp.where(mask, upper, lower) + 0.375), 0.0)
        i_b[1 + j] = jnp.where(keep, 1.0 / (jnp.where(mask, lower, upper) + 0.375), 0.0)
    for k in range(1, 25):
        t_b[k] = i_b[k]
        w_b[k] = i_b[k]
    for k in range(1, 25):
        t = i_r[k] * (1.0 + 0.0625 * around(t_b, k, True, mask, 1))
        t_r[k] = t
        w_r[k] = t

    def sweep(n, carry):
        for k in range(1, 25):
            t = i_b[k] * (0.0625 * around(t_r, k, False, mask, 1))
            t_b[k] = t
            w_b[k] = w_b[k] + t
        for k in range(1, 25):
            t = i_r[k] * (0.0625 * around(t_b, k, True, mask, 1))
            t_r[k] = t
            w_r[k] = w_r[k] + t
        return carry

    lax.fori_loop(0, 7, sweep, 0)
    for j in range(8):
        red, black = w_r[9 + j], w_b[9 + j]
        out[2 * j] = jnp.where(mask, black, red)
        out[2 * j + 1] = jnp.where(mask, red, black)


def up_kernel(
    meta, bricks, sum_0, sum_1, sum_2, sum_3, es, ec_b, r_r, r_b, ci_r, ci_b, u1_b, f_r, f_b, i_r, i_b, out,
    e_r, e_b, small, wide, planes, tall, u_r, u_b,
):
    slab, _, bit_x, bit_y, bit_z = place_of(meta, bricks)
    total = (sum_0[...] + sum_1[...]) + (sum_2[...] + sum_3[...])
    mean = jnp.sum(total) * (1.0 / (SLABS * 16 * 16 * 64))
    for i in range(22):
        shifted = es[i] - mean
        if i < 3:
            shifted = jnp.where(is_zero(slab, (16, 128)), 0.0, shifted)
        if i >= 19:
            shifted = jnp.where(is_zero(slab - (SLABS - 1), (16, 128)), 0.0, shifted)
        small[16 * i : 16 * i + 16] = shifted
    spread = pick(128, 128, lambda r, c: r == (c >> 1))
    small[...] = jnp.dot(small[...], spread, precision=EXACT, preferred_element_type=F32)
    for i in range(22):
        rows = small[16 * i : 16 * i + 16]
        wide[i, pl.ds(0, 16, stride=2), :] = rows
        wide[i, pl.ds(1, 16, stride=2), :] = rows
    for k in (0, 1, 2, 25, 26, 27):
        e_r[k] = jnp.zeros((32, 128), F32)
        e_b[k] = jnp.zeros((32, 128), F32)
    for i in range(22):
        e_b[3 + i] = ec_b[3 + i] + wide[i]
    coarse = odd(32, 128)
    for _ in range(2):
        half_sweep(e_r, e_b, r_r, ci_r, 3, 25, True, coarse, 0.25, 2)
        half_sweep(e_b, e_r, r_b, ci_b, 3, 25, False, coarse, 0.25, 2)
    for n in range(20):
        z = n - 2
        k = 8 * bit_z + (z // 2 + 6)
        red, black = e_r[k], e_b[k]
        planes[32 * n : 32 * n + 32] = jnp.where(coarse, red, black) if z % 2 else jnp.where(coarse, black, red)

    lane = iota((128, 256), 1)
    x0 = is_zero(bit_x, (128, 256))
    start = jnp.where(lane < 128, 64 * bit_x + (lane >> 1), (lane >> 1) + jnp.where(x0, 0, -64))
    usable = (lane < 128) | (x0 & (lane < 136)) | (jnp.logical_not(x0) & (lane >= 248))
    spread = jnp.where(usable & (iota((128, 256), 0) == start), 1.0, 0.0).astype(F32)
    tall_rows = jnp.dot(planes[...], spread, precision=EXACT, preferred_element_type=F32)
    for n in range(20):
        rows = tall_rows[32 * n : 32 * n + 32]
        for h in range(2):
            tall[n, h, pl.ds(0, 32, stride=2), :] = rows[:, 128 * h : 128 * h + 128]
            tall[n, h, pl.ds(1, 32, stride=2), :] = rows[:, 128 * h : 128 * h + 128]
    for k in (0, 21):
        u_r[k] = jnp.zeros((40, 256), F32)
        u_b[k] = jnp.zeros((40, 256), F32)
    row = iota((8, 128), 0)
    y0 = is_zero(bit_y)
    in_y = (y0 & (row != 7)) | (jnp.logical_not(y0) & (row != 0))
    own_start = pl.multiple_of(32 * bit_y, 32)
    side_start = pl.multiple_of(32 - 8 * bit_y, 8)
    for n in range(20):
        for h in range(2):
            lanes = slice(128 * h, 128 * h + 128)
            side = jnp.where(in_y, tall[n, h, pl.ds(side_start, 8), :], 0.0)
            u_b[1 + n, 0:32, lanes] = u1_b[3 + n, 0:32, lanes] + tall[n, h, pl.ds(own_start, 32), :]
            u_b[1 + n, 32:40, lanes] = u1_b[3 + n, 32:40, lanes] + side
    mask = odd(40, 256)
    f_r, f_b, i_r, i_b = (grid.at[2:24] for grid in (f_r, f_b, i_r, i_b))
    half_sweep(u_r, u_b, f_r, i_r, 1, 21, True, mask, 1.0, 0)
    half_sweep(u_b, u_r, f_b, i_b, 2, 20, False, mask, 1.0, 0)
    half_sweep(u_r, u_b, f_r, i_r, 2, 20, True, mask, 1.0, 0)
    half_sweep(u_b, u_r, f_b, i_b, 3, 19, False, mask, 1.0, 0)
    own = odd(32, 128)
    for t in range(16):
        red, black = u_r[3 + t, 0:32, 0:128], u_b[3 + t, 0:32, 0:128]
        out[0, 2 * t] = jnp.where(own, black, red)
        out[0, 2 * t + 1] = jnp.where(own, red, black)


def swap_cores(x):
    return lax.ppermute(x, "level", [(0, 1), (1, 0)])


def to_slabs(x, up_first):
    pairs = []
    for s in range(SLABS - 1):
        for m in range(8):
            low, high = s * 8 + m, (s + 1) * 8 + m
            pairs.append((low, high) if (m < 4) == up_first else (high, low))
    return lax.ppermute(x, ALL, pairs)


def around_chips(x):
    return [x] + [lax.ppermute(x, "bottom", [(i, (i + d) % 4) for i in range(4)]) for d in range(1, 4)]


def both_cores(boxes):
    return boxes + [swap_cores(box) for box in boxes]


def ring_sums(x, stride):
    def moved(s, step):
        at = s // stride % 4
        return s + ((at + step) % 4 - at) * stride

    beside = [(8 * s + m, 8 * moved(s, 1 if m < 4 else 3) + m) for s in range(SLABS) for m in range(8)]
    across = [(s, moved(s, 2)) for s in range(SLABS)]
    return lax.ppermute(x, ALL, beside), lax.ppermute(x, "slab", across)


def among(x):
    return lax.all_to_all(x, LB, split_axis=0, concat_axis=0, tiled=True)


def body(u_init, source, coeffs, brick_map):
    meta = jnp.stack([lax.axis_index("slab"), lax.axis_index(LB)]).astype(jnp.int32)
    smem = [meta, brick_map]
    fine = (26, 40, 256)
    packed, ac = run(
        first_kernel, [(8, SENT, 8, 128), (8, 16, 128)], smem, [u_init, source, coeffs],
        [(8, 32, 128), (16, 32, 128), (256, 128)],
    )
    got = among(packed)
    leaving = run(cross_kernel, [(4, FACE + 4, 8, 128)], smem, [got])
    leaving, ac = lax.optimization_barrier((leaving, ac))
    cross = to_slabs(leaving, False)
    cross, *ac_boxes = lax.optimization_barrier((cross, *around_chips(ac)))
    sent, coef = run(
        mid_kernel, [(8, GOT, 8, 128), (2, 8, 2, 8, 128)], smem, [got, cross], [(12, FACE, 8, 128)],
    )
    coef_other = swap_cores(coef)
    halo = among(sent)
    faces = (4, 5, 16, 128)
    coarse = (28, 32, 128)
    held = [(8, 8, 16, 128), faces, faces]
    ac_boxes = both_cores(ac_boxes)
    ac_cross = to_slabs(run(faces_kernel, [faces], smem, ac_boxes, held[:1]), True)
    ac_other = swap_cores(ac_cross)
    halo, ac_cross, ac_other, coef_other = lax.optimization_barrier((halo, ac_cross, ac_other, coef_other))
    rc, u_b, f_r, f_b, i_r, i_b = run(
        fine_down_kernel, [(8, 16, 128)] + [fine] * 5, smem, [u_init, source, coeffs, halo],
        [fine, (16, 32, 128), (256, 128)],
    )
    boxes = both_cores(around_chips(rc))
    leaving = run(faces_kernel, [faces], smem, boxes, held[:1])
    leaving, ac_cross, ac_other, coef = lax.optimization_barrier((leaving, ac_cross, ac_other, coef))
    cross = to_slabs(leaving, True)
    weights = run(
        weights_kernel, [(16, 16, 128)], [meta], [coef, coef_other],
        [(26, 16, 128)] * 6 + [(8, 2, 8, 128)] * 2,
    )
    ca_r, ci_r, ci_b, ab = run(
        coarse_coef_kernel, [coarse] * 3 + [(22, 16, 128)], smem, ac_boxes + [ac_cross, ac_other],
        held + [coarse, (22, 32, 128), (352, 128)],
    )
    cross, weights, ca_r, ci_r, ci_b, ab = lax.optimization_barrier((cross, weights, ca_r, ci_r, ci_b, ab))
    rb, rb_send, part, ec_b, r_r, r_b = run(
        coarse_down_kernel, [(22, 16, 128), (18, 16, 128), (8, 128)] + [coarse] * 3, smem,
        boxes + [cross, swap_cores(cross), weights, ca_r, ci_r, ci_b, ab],
        held + [coarse, (22, 32, 128), (352, 128)],
    )
    cross = to_slabs(rb_send, True)
    near, far = ring_sums(part, 1)
    cross, near, far = lax.optimization_barrier((cross, near, far))
    other = swap_cores(cross)
    part = (part + swap_cores(near)) + (near + far)
    near, far = ring_sums(part, 4)
    sums = [part, near, far, swap_cores(near)]
    bottom = (28, 16, 128)
    es = run(
        bottom_kernel, [(22, 16, 128)], [meta], [rb, cross, other],
        [bottom] * 6 + [(18, 16, 128)] * 2,
    )
    return run(
        up_kernel, [(1, 32, 32, 128)], smem,
        sums + [es, ec_b, r_r, r_b, ci_r, ci_b, u_b, f_r, f_b, i_r, i_b],
        [coarse, coarse, (352, 128), (22, 32, 128), (640, 128), (20, 2, 64, 128), (22, 40, 256), (22, 40, 256)],
    )


def solution(mesh):
    placed = P(ALL, None, None, None)
    return jax.shard_map(
        body, mesh=mesh, in_specs=(placed, placed, placed, P()), out_specs=placed, check_vma=False
    )
```

```python
import jax
import jax.numpy as jnp
from jax import lax
from jax.experimental import pallas as pl
from jax.experimental.pallas import tpu as pltpu
from jax.sharding import PartitionSpec as P

LB = ("level", "bottom")
ALL = ("slab", "level", "bottom")
SLABS = 16
OWN = 5
F32 = jnp.float32
VMEM_SPEC = pl.BlockSpec(memory_space=pltpu.VMEM)
SMEM_SPEC = pl.BlockSpec(memory_space=pltpu.SMEM)
EXACT = lax.Precision.HIGHEST


def run(kernel, outs, smem, vmem, scratch=()):
    shapes = [jax.ShapeDtypeStruct(s, F32) for s in outs]
    single = len(shapes) == 1
    return pl.pallas_call(
        kernel,
        out_shape=shapes[0] if single else shapes,
        in_specs=[SMEM_SPEC] * len(smem) + [VMEM_SPEC] * len(vmem),
        out_specs=VMEM_SPEC if single else [VMEM_SPEC] * len(shapes),
        scratch_shapes=[pltpu.VMEM(s, F32) for s in scratch],
        compiler_params=pltpu.CompilerParams(vmem_limit_bytes=20 << 20),
    )(*smem, *vmem)


def iota(shape, dim):
    return lax.broadcasted_iota(jnp.int32, shape, dim)


def odd(rows, cols):
    return ((iota((rows, cols), 0) + iota((rows, cols), 1)) & 1) == 1


def place_of(meta, bricks):
    slab, me = meta[0], meta[1]
    place = jnp.int32(0)
    for i in range(8):
        place = place + jnp.where(bricks[slab, i] == me, i, 0)
    return slab, me, place & 1, (place >> 1) & 1, place >> 2


def is_zero(scalar, shape=(8, 128)):
    return jnp.full(shape, scalar, jnp.int32) == 0


ARRAYS = 5
FACE = 17
SENT_Y, SENT_X, SENT_COEF, SENT = 17, 27, 30, 32
GOT_ROWS, GOT_STRIPS, GOT_Y, GOT_X, GOT = 17, 20, 22, 32, 35


def face_planes(j):
    return [(1 + j, 0), (1 + j, 1), (1 + j, 2), (0, j)]


def merge_strips(placed, base=None):
    group = iota((8, 128), 1) // 8
    total = jnp.zeros((8, 128), F32) if base is None else base
    for pos, strip in placed:
        moved = pltpu.roll(strip, 8 * pos, 1) if pos else strip
        total = jnp.where(group == pos, moved, total)
    return total


def swap_lanes(cells):
    lane = iota(cells.shape, 1)
    return jnp.where((lane & 1) == 0, pltpu.roll(cells, cells.shape[1] - 1, 1), pltpu.roll(cells, 1, 1))


def pack_shell(get, out, bit_x, bit_y):
    x0, y0 = is_zero(bit_x), is_zero(bit_y)
    mask = odd(32, 128)
    for k in range(8):
        high, j = k >= 4, k % 4
        for i, (c, far) in enumerate(face_planes(j)):
            out[k, 4 * i : 4 * i + 4] = get(c, 15 - far if high else far).reshape(4, 8, 128)
        t = 12 if high else 3
        one, two = get(1, t), swap_lanes(get(3, t))
        both = jnp.where(mask, one, two) if high else jnp.where(mask, two, one)
        out[k, 16] = both[8 * j : 8 * j + 8]
        strips = []
        for tl in range(2):
            for c in range(ARRAYS):
                v = get(c, 2 * k + tl)
                out[k, SENT_Y + tl * ARRAYS + c] = jnp.where(y0, v[24:32], v[0:8])
                for g in range(4):
                    tile = v[8 * g : 8 * g + 8]
                    strips.append(jnp.where(x0, pltpu.roll(tile, 8, 1), tile))
        for i in range(3):
            out[k, SENT_X + i] = merge_strips(list(enumerate(strips[16 * i : 16 * i + 16])))


def cross_kernel(meta, bricks, recv, out):
    slab, me = meta[0], meta[1]
    for i in range(4):
        src = jnp.where(me >= 4, bricks[slab, 4 + i], bricks[slab, i])
        out[i, 0:FACE] = recv[src, 0:FACE]
        for j in range(2):
            coef = recv[bricks[slab, 2 * i + j], SENT_COEF:SENT]
            out[i, FACE + 2 * j : FACE + 2 * j + 2] = coef


def mid_kernel(meta, bricks, recv, cross, out, coef, faces):
    slab, me = meta[0], meta[1]
    faces[0:8] = recv[:, 0:FACE]
    faces[8:12] = cross[:, 0:FACE]
    for p in range(8):
        coef[0, p] = recv[bricks[slab, p], SENT_COEF:SENT]
        j = FACE + 2 * (p & 1)
        coef[1, p] = cross[p >> 1, j : j + 2]
    row = iota((8, 128), 0)
    for p in range(8):
        bx, by, bz = p & 1, (p >> 1) & 1, p >> 2
        dest = bricks[slab, p]
        same = me >= 4 if bz else me < 4

        def src(q):
            return jnp.where(same, bricks[slab, (q & 3) + 4 * (1 - bz)], 8 + (q & 3))

        def strip_of(tile):
            return pltpu.roll(tile, 8, 1) if bx else tile

        def rows_of(at):
            one, two, three, last = (faces[at, 4 * i + (3 if by else 0)] for i in range(4))
            if by:
                shared = jnp.where(row >= 3, two, pltpu.roll(three, 3, 0))
            else:
                shared = jnp.where(row < 5, two, pltpu.roll(three, 5, 0))
            return [one, shared, last]

        at_own, at_y, at_x, at_xy = src(p), src(p ^ 2), src(p ^ 1), src(p ^ 3)
        out[dest, 0:FACE] = faces[at_own]
        for i, tile in enumerate(rows_of(at_y)):
            out[dest, GOT_ROWS + i] = tile
        strips = [strip_of(faces[at_x, i]) for i in range(16)] + [strip_of(tile) for tile in rows_of(at_xy)]
        from_y, from_x, from_xy = bricks[slab, p ^ 2], bricks[slab, p ^ 1], bricks[slab, p ^ 3]
        strips += [strip_of(recv[from_xy, SENT_Y + i]) for i in range(2 * ARRAYS)]
        for i in range(2):
            out[dest, GOT_STRIPS + i] = merge_strips(list(enumerate(strips[16 * i : 16 * i + 16])))
        out[dest, GOT_Y:GOT_X] = recv[from_y, SENT_Y:SENT_X]
        out[dest, GOT_X:GOT] = recv[from_x, SENT_X:SENT_COEF]


def unpack_shell(recv, grids, bit_x, bit_y):
    row, lane = iota((8, 128), 0), iota((8, 128), 1)
    x0, y0 = is_zero(bit_x), is_zero(bit_y)
    in_x = (x0 & (lane < 8)) | (jnp.logical_not(x0) & (lane >= 120))
    five = (y0 & (row < 5)) | (jnp.logical_not(y0) & (row >= 3))
    three = (y0 & (row < 3)) | (jnp.logical_not(y0) & (row >= 5))
    seven = (y0 & (row != 7)) | (jnp.logical_not(y0) & (row != 0))
    mask = odd(8, 128)

    def cut(c, tile):
        return jnp.where(seven, tile, 0.0) if c >= 3 else tile

    def strip(tile, pos):
        shift = (jnp.where(bit_x == 0, 0, 120) + 128 - 8 * pos) % 128
        return jnp.where(in_x, pltpu.roll(tile, shift, 1), 0.0)

    def rows_of(tiles):
        one, shared, last = tiles
        moved = jnp.where(y0, pltpu.roll(shared, 3, 0), pltpu.roll(shared, 5, 0))
        return [one, jnp.where(five, shared, 0.0), jnp.where(three, moved, 0.0), last]

    for k in range(8):
        high, j = k >= 4, k % 4
        rows = rows_of([recv[k, GOT_ROWS + i] for i in range(3)])
        sides = rows_of([strip(recv[k, GOT_STRIPS + 1], i) for i in range(3)])
        for i, (c, far) in enumerate(face_planes(j)):
            at = OWN - 1 - far if high else OWN + 16 + far
            for g in range(4):
                grids[c][at, 8 * g : 8 * g + 8, 0:128] = recv[k, 4 * i + g]
                grids[c][at, 8 * g : 8 * g + 8, 128:256] = strip(recv[k, GOT_STRIPS], 4 * i + g)
            grids[c][at, 32:40, 0:128] = cut(c, rows[i])
            grids[c][at, 32:40, 128:256] = cut(c, sides[i])
        at = 1 if high else 24
        both = recv[k, 16]
        other = swap_lanes(both)
        other = jnp.where(mask, other, 0.0) if high else jnp.where(mask, 0.0, other)
        for c, cells in ((1, both), (3, other)):
            grids[c][at, 8 * j : 8 * j + 8, 0:128] = cells
            grids[c][at, 8 * j : 8 * j + 8, 128:256] = jnp.zeros((8, 128), F32)
            grids[c][at, 32:40] = jnp.zeros((8, 256), F32)
        for tl in range(2):
            for c in range(ARRAYS):
                i = tl * ARRAYS + c
                at = OWN + 2 * k + tl
                grids[c][at, 32:40, 0:128] = cut(c, recv[k, GOT_Y + i])
                grids[c][at, 32:40, 128:256] = cut(c, strip(recv[k, GOT_STRIPS + 1], 3 + i))
                for g in range(4):
                    n = 4 * i + g
                    side = strip(recv[k, GOT_X + n // 16], n % 16)
                    grids[c][at, 8 * g : 8 * g + 8, 128:256] = side


def pair_of(cells, t, red, mask):
    low, high = cells[0, 2 * t], cells[0, 2 * t + 1]
    return jnp.where(mask, high, low) if red else jnp.where(mask, low, high)


def pack_bottom_coef(a, out, small):
    for i in range(8):
        planes = (a[0, 4 * i] + a[0, 4 * i + 1]) + (a[0, 4 * i + 2] + a[0, 4 * i + 3])
        small[i] = planes
    rows = []
    for i in range(8):
        first = small[i, pl.ds(0, 8, stride=4), :] + small[i, pl.ds(1, 8, stride=4), :]
        rows.append(first + (small[i, pl.ds(2, 8, stride=4), :] + small[i, pl.ds(3, 8, stride=4), :]))
    fold = pick(128, 128, lambda r, c: (r >> 2) == (c & 31)) * (1.0 / 64)
    cells = jnp.dot(jnp.concatenate(rows, 0), fold, precision=EXACT, preferred_element_type=F32)
    group = iota((8, 128), 1) >> 5
    for h in range(2):
        tile = cells[32 * h : 32 * h + 8]
        for j in range(1, 4):
            tile = jnp.where(group == j, cells[32 * h + 8 * j : 32 * h + 8 * j + 8], tile)
        for k in range(8):
            out[k, SENT_COEF + h] = tile


def pack_coarse(planes, small, out):
    twice = pick(128, 128, lambda r, c: (r >> 1) == (c & 63)) * 0.125
    row, lane = iota((16, 128), 0), iota((16, 128), 1)
    even = ((row + lane + (lane >> 6)) & 1) == 0
    for t in range(16):
        small[16 * t : 16 * t + 16] = planes[t, pl.ds(0, 16, stride=2), :] + planes[t, pl.ds(1, 16, stride=2), :]
    summed = jnp.dot(small[...], twice, precision=EXACT, preferred_element_type=F32)
    summed = summed.reshape(16, 16, 128)
    for j in range(8):
        out[j] = jnp.where(even, summed[2 * j], summed[2 * j + 1])


def first_kernel(meta, bricks, u, f, a, out, ac, small, planes, rows, inverse):
    _, _, bit_x, bit_y, _ = place_of(meta, bricks)
    mask = odd(32, 128)
    inverse[...] = 1.0 / (a[...] + 6.0)
    sources = ((u, False), (f, True), (f, False), (inverse, True), (inverse, False))

    def get(c, t):
        return pair_of(sources[c][0], t, sources[c][1], mask)

    pack_shell(get, out, bit_x, bit_y)
    pack_bottom_coef(a, out, small)
    for t in range(16):
        planes[t] = a[0, 2 * t] + a[0, 2 * t + 1]
    pack_coarse(planes, rows, ac)


def around(src, k, red, mask, edges, cut=None):
    here = src[k]
    rows, cols = here.shape
    above, below = src[k + 1], src[k - 1]
    other = jnp.where(mask, above, below) if red else jnp.where(mask, below, above)
    up, down = pltpu.roll(here, 1, 0), pltpu.roll(here, rows - 1, 0)
    left, right = pltpu.roll(here, 1, 1), pltpu.roll(here, cols - 1, 1)
    if edges:
        row, lane = iota((rows, cols), 0), iota((rows, cols), 1)
        up, down = jnp.where(row == 0, 0.0, up), jnp.where(row == rows - 1, 0.0, down)
        if edges == 2:
            left, right = jnp.where(lane == 0, 0.0, left), jnp.where(lane == cols - 1, 0.0, right)
    if cut is not None:
        up, down = jnp.where(cut[0], 0.0, up), jnp.where(cut[1], 0.0, down)
    return ((here + other) + (up + down)) + (left + right)


def half_sweep(dst, src, force, inverse, lo, hi, red, mask, scale, edges, cut=None):
    def step(k, carry):
        total = around(src, k, red, mask, edges, cut)
        if scale != 1.0:
            total = scale * total
        dst[k] = (force[k] + total) * inverse[k]
        return carry

    lax.fori_loop(lo, hi, step, 0, unroll=True)


def select_dot(cells, chosen):
    half, total = chosen.astype(jnp.bfloat16), None
    for _ in range(3):
        part = cells.astype(jnp.bfloat16)
        cells = cells - part.astype(F32)
        moved = jnp.dot(part, half, preferred_element_type=F32)
        total = moved if total is None else total + moved
    return total


def pick(rows, cols, keep):
    return jnp.where(keep(iota((rows, cols), 0), iota((rows, cols), 1)), 1.0, 0.0).astype(F32)


def fine_down_kernel(meta, bricks, u, f, a, recv, rc, u_b, f_r, f_b, i_r, i_b, u_r, resid, small):
    _, _, bit_x, bit_y, _ = place_of(meta, bricks)
    own = odd(32, 128)
    for t in range(16):
        here = (OWN + t, slice(0, 32), slice(0, 128))
        u_b[here] = pair_of(u, t, False, own)
        f_r[here], f_b[here] = pair_of(f, t, True, own), pair_of(f, t, False, own)
        i_r[here], i_b[here] = 1.0 / (pair_of(a, t, True, own) + 6.0), 1.0 / (pair_of(a, t, False, own) + 6.0)
    unpack_shell(recv, (u_b, f_r, f_b, i_r, i_b), bit_x, bit_y)
    zero = jnp.zeros((40, 256), F32)
    for k in (0, 25):
        u_r[k] = zero
        u_b[k] = zero
    for k in (1, 24):
        f_b[k] = zero
        i_b[k] = zero
    row = iota((40, 256), 0)
    y0 = is_zero(bit_y, (40, 256))
    y1 = jnp.logical_not(y0)
    mask = odd(40, 256)
    cut = (y0 & (row == 0), y1 & (row == 31))
    half_sweep(u_r, u_b, f_r, i_r, 1, 25, True, mask, 1.0, 0, cut)
    half_sweep(u_b, u_r, f_b, i_b, 1, 25, False, mask, 1.0, 0)
    half_sweep(u_r, u_b, f_r, i_r, 2, 24, True, mask, 1.0, 0)
    half_sweep(u_b, u_r, f_b, i_b, 3, 23, False, mask, 1.0, 0)
    for t in range(16):
        total = around(u_b, OWN + t, True, mask, 0)[0:32, 0:128]
        diag = pair_of(a, t, True, own) + 6.0
        here = (OWN + t, slice(0, 32), slice(0, 128))
        resid[t] = f_r[here] + total - diag * u_r[here]
    pack_coarse(resid, small, rc)


def slot_of(member, me):
    return jnp.where((member >> 2) == (me >> 2), 0, 4) + ((me - member) & 3)


def faces_kernel(meta, bricks, *refs):
    boxes, (out, held) = refs[:8], refs[8:]
    slab, me = meta[0], meta[1]
    for i, box in enumerate(boxes):
        held[i] = box[...]
    start = jnp.where(me < 4, 3, 0)
    for i in range(4):
        member = jnp.where(me < 4, bricks[slab, 4 + i], bricks[slab, i])
        out[i] = held[slot_of(member, me), pl.ds(start, 5)]


def sort_sides(me, one, two, low, high):
    @pl.when(me < 4)
    def _():
        low[...] = one[...]
        high[...] = two[...]

    @pl.when(me >= 4)
    def _():
        low[...] = two[...]
        high[...] = one[...]


def assemble(meta, bricks, boxes, one, two, red, black, held, low, high):
    slab, me = meta[0], meta[1]
    for i, box in enumerate(boxes):
        held[i] = box[...]
    sort_sides(me, one, two, low, high)
    left = iota((16, 128), 1) < 64

    def put(k, by, west, east):
        rows = slice(16 * by, 16 * by + 16)
        red[k, rows] = jnp.where(left, west, pltpu.roll(east, 64, 1))
        black[k, rows] = jnp.where(left, pltpu.roll(west, 64, 1), east)

    for by in range(2):
        for bz in range(2):
            west = slot_of(bricks[slab, 2 * by + 4 * bz], me)
            east = slot_of(bricks[slab, 2 * by + 4 * bz + 1], me)
            for j in range(8):
                put(6 + 8 * bz + j, by, held[west, j], held[east, j])
        for j in range(5):
            put(1 + j, by, low[2 * by, j], low[2 * by + 1, j])
            put(22 + j, by, high[2 * by, j], high[2 * by + 1, j])


def to_bottom(planes, small, half):
    for n in range(22):
        small[16 * n : 16 * n + 16] = planes[n, pl.ds(0, 16, stride=2), :] + planes[n, pl.ds(1, 16, stride=2), :]
    fold = pick(128, 128, lambda r, c: (r >> 1) == c - 64 * half) * 0.125
    return jnp.dot(small[...], fold, precision=EXACT, preferred_element_type=F32).reshape(22, 16, 128)


def coarse_coef_kernel(meta, bricks, *refs):
    boxes, (one, two) = refs[:8], refs[8:10]
    a_r, i_r, i_b, ab = refs[10:14]
    held, low, high, a_b, planes, small = refs[14:]
    slab = meta[0]
    assemble(meta, bricks, boxes, one, two, a_r, a_b, held, low, high)
    for k in range(1, 27):
        keep = jnp.full((32, 128), 0, jnp.int32) == 0
        if k < 6:
            keep = jnp.logical_not(is_zero(slab, (32, 128)))
        if k >= 22:
            keep = jnp.logical_not(is_zero(slab - (SLABS - 1), (32, 128)))
        i_r[k] = jnp.where(keep, 1.0 / (a_r[k] + 1.5), 0.0)
        i_b[k] = jnp.where(keep, 1.0 / (a_b[k] + 1.5), 0.0)
    for n in range(22):
        planes[n] = a_r[3 + n] + a_b[3 + n]
    ab[...] = to_bottom(planes, small, 1)


def coarse_down_kernel(meta, bricks, *refs):
    boxes, (one, two, weights, a_r, i_r, i_b, ab) = refs[:8], refs[8:15]
    rb, rb_send, part, e_b, r_r, r_b = refs[15:21]
    held, low, high, e_r, resid, small = refs[21:]
    me = meta[1]
    assemble(meta, bricks, boxes, one, two, r_r, r_b, held, low, high)
    for k in (0, 27):
        e_r[k] = jnp.zeros((32, 128), F32)
        e_b[k] = jnp.zeros((32, 128), F32)
    for k in range(1, 27):
        e_r[k] = r_r[k] * i_r[k]
    mask = odd(32, 128)
    half_sweep(e_b, e_r, r_b, i_b, 1, 27, False, mask, 0.25, 2)
    half_sweep(e_r, e_b, r_r, i_r, 1, 27, True, mask, 0.25, 2)
    half_sweep(e_b, e_r, r_b, i_b, 1, 27, False, mask, 0.25, 2)
    for n in range(22):
        k = n + 3
        total = 0.25 * around(e_b, k, True, mask, 2)
        resid[n] = r_r[k] + total - (a_r[k] + 1.5) * e_r[k]
    rb[...] = to_bottom(resid, small, 0) + ab[...]
    rb_send[...] = rb[pl.ds(jnp.where(me < 4, 1, 3), 18)]
    total = jnp.zeros((16, 128), F32)
    for i in range(16):
        total = total + rb[3 + i] * weights[i]
    part[...] = total[0:8] + total[8:16]


def bottom_kernel(meta, rb, one, two, es, e_r, e_b, g_r, g_b, i_r, i_b, low, high):
    slab, me = meta[0], meta[1]
    sort_sides(me, one, two, low, high)
    mask = odd(16, 128)
    left = iota((16, 128), 1) < 64
    zero = jnp.zeros((16, 128), F32)
    for k in (0, 27):
        e_r[k] = zero
        e_b[k] = zero
    for j in range(26):
        planes = []
        for n in (2 * j, 2 * j + 1):
            planes.append(low[n] if n < 18 else rb[n - 15] if n < 34 else high[n - 34])
        keep = left
        if j < 9:
            keep = left & jnp.logical_not(is_zero(slab, (16, 128)))
        if j >= 17:
            keep = left & jnp.logical_not(is_zero(slab - (SLABS - 1), (16, 128)))
        for red in (True, False):
            cells = jnp.where(mask, planes[1], planes[0]) if red else jnp.where(mask, planes[0], planes[1])
            force = jnp.where(left, cells, 0.0)
            inverse = jnp.where(keep, 1.0 / (pltpu.roll(cells, 64, 1) + 0.375), 0.0)
            if red:
                g_r[1 + j], i_r[1 + j], e_r[1 + j] = force, inverse, force * inverse
            else:
                g_b[1 + j], i_b[1 + j] = force, inverse
    half_sweep(e_b, e_r, g_b, i_b, 1, 27, False, mask, 0.0625, 1)

    def sweep(n, carry):
        half_sweep(e_r, e_b, g_r, i_r, 1, 27, True, mask, 0.0625, 1)
        half_sweep(e_b, e_r, g_b, i_b, 1, 27, False, mask, 0.0625, 1)
        return carry

    lax.fori_loop(0, 7, sweep, 0)
    for i in range(22):
        k, upper = (15 + i) // 2 + 1, (15 + i) % 2
        es[i] = jnp.where(mask, e_r[k], e_b[k]) if upper else jnp.where(mask, e_b[k], e_r[k])


def weights_kernel(meta, here, there, out, t_r, t_b, w_r, w_b, i_r, i_b, low, high):
    slab, me = meta[0], meta[1]

    @pl.when(me < 4)
    def _():
        low[...] = there[1]
        high[...] = here[1]

    @pl.when(me >= 4)
    def _():
        low[...] = here[1]
        high[...] = there[1]

    lane = iota((8, 128), 1)

    def plane(boxes, z):
        rows = []
        for by in range(2):
            place, shift = 4 * (z >> 3) + 2 * by, 32 * (z & 3)
            west = pltpu.roll(boxes(place, (z & 7) >> 2), (128 - shift) % 128, 1)
            east = pltpu.roll(boxes(place + 1, (z & 7) >> 2), (160 - shift) % 128, 1)
            rows.append(jnp.where(lane < 32, west, east))
        return jnp.concatenate(rows, 0)

    parts = (lambda p, h: low[p, h], lambda p, h: here[0, p, h], lambda p, h: high[p, h])
    mask = odd(16, 128)
    left = iota((16, 128), 1) < 64
    zero = jnp.zeros((16, 128), F32)
    for k in (0, 25):
        t_r[k] = zero
        t_b[k] = zero
    for j in range(24):
        lower, upper = (plane(parts[(2 * j + i) // 16], (2 * j + i) % 16) for i in range(2))
        keep = left
        if j < 8:
            keep = left & jnp.logical_not(is_zero(slab, (16, 128)))
        if j >= 16:
            keep = left & jnp.logical_not(is_zero(slab - (SLABS - 1), (16, 128)))
        i_r[1 + j] = jnp.where(keep, 1.0 / (jnp.where(mask, upper, lower) + 0.375), 0.0)
        i_b[1 + j] = jnp.where(keep, 1.0 / (jnp.where(mask, lower, upper) + 0.375), 0.0)
    for k in range(1, 25):
        t_b[k] = i_b[k]
        w_b[k] = i_b[k]
    for k in range(1, 25):
        t = i_r[k] * (1.0 + 0.0625 * around(t_b, k, True, mask, 1))
        t_r[k] = t
        w_r[k] = t

    def sweep(n, carry):
        for k in range(1, 25):
            t = i_b[k] * (0.0625 * around(t_r, k, False, mask, 1))
            t_b[k] = t
            w_b[k] = w_b[k] + t
        for k in range(1, 25):
            t = i_r[k] * (0.0625 * around(t_b, k, True, mask, 1))
            t_r[k] = t
            w_r[k] = w_r[k] + t
        return carry

    lax.fori_loop(0, 7, sweep, 0)
    for j in range(8):
        red, black = w_r[9 + j], w_b[9 + j]
        out[2 * j] = jnp.where(mask, black, red)
        out[2 * j + 1] = jnp.where(mask, red, black)


def up_kernel(
    meta, bricks, sum_0, sum_1, sum_2, sum_3, es, ec_b, r_r, r_b, ci_r, ci_b, u1_b, f_r, f_b, i_r, i_b, out,
    e_r, e_b, small, wide, planes, tall, u_r, u_b,
):
    slab, _, bit_x, bit_y, bit_z = place_of(meta, bricks)
    total = (sum_0[...] + sum_1[...]) + (sum_2[...] + sum_3[...])
    mean = jnp.sum(total) * (1.0 / (SLABS * 16 * 16 * 64))
    base = 8 * bit_z
    no_low = jnp.where((slab == 0) & (bit_z == 0), 0, 1)
    no_high = jnp.where((slab == SLABS - 1) & (bit_z == 1), 0, 1)
    for j in range(14):
        shifted = es[base + j] - mean
        if j < 3:
            shifted = jnp.where(is_zero(no_low, (16, 128)), 0.0, shifted)
        if j >= 11:
            shifted = jnp.where(is_zero(no_high, (16, 128)), 0.0, shifted)
        small[16 * j : 16 * j + 16] = shifted
    spread = pick(128, 128, lambda r, c: r == (c >> 1))
    small[...] = select_dot(small[...], spread)
    for j in range(14):
        rows = small[16 * j : 16 * j + 16]
        wide[j, pl.ds(0, 16, stride=2), :] = rows
        wide[j, pl.ds(1, 16, stride=2), :] = rows
    for k in (0, 15):
        e_r[k] = jnp.zeros((32, 128), F32)
        e_b[k] = jnp.zeros((32, 128), F32)
    for j in range(14):
        e_b[1 + j] = ec_b[base + 3 + j] + wide[j]
    coarse = odd(32, 128)
    r_r, r_b, ci_r, ci_b = (grid.at[pl.ds(base + 2, 16)] for grid in (r_r, r_b, ci_r, ci_b))
    half_sweep(e_r, e_b, r_r, ci_r, 1, 15, True, coarse, 0.25, 2)
    half_sweep(e_b, e_r, r_b, ci_b, 2, 14, False, coarse, 0.25, 2)
    half_sweep(e_r, e_b, r_r, ci_r, 2, 14, True, coarse, 0.25, 2)
    half_sweep(e_b, e_r, r_b, ci_b, 3, 13, False, coarse, 0.25, 2)
    for n in range(20):
        k, upper = n // 2 + 3, n % 2
        red, black = e_r[k], e_b[k]
        planes[32 * n : 32 * n + 32] = jnp.where(coarse, red, black) if upper else jnp.where(coarse, black, red)

    lane = iota((128, 256), 1)
    x0 = is_zero(bit_x, (128, 256))
    start = jnp.where(lane < 128, 64 * bit_x + (lane >> 1), (lane >> 1) + jnp.where(x0, 0, -64))
    usable = (lane < 128) | (x0 & (lane < 136)) | (jnp.logical_not(x0) & (lane >= 248))
    spread = jnp.where(usable & (iota((128, 256), 0) == start), 1.0, 0.0).astype(F32)
    tall_rows = select_dot(planes[...], spread)
    for n in range(20):
        rows = tall_rows[32 * n : 32 * n + 32]
        for h in range(2):
            tall[n, h, pl.ds(0, 32, stride=2), :] = rows[:, 128 * h : 128 * h + 128]
            tall[n, h, pl.ds(1, 32, stride=2), :] = rows[:, 128 * h : 128 * h + 128]
    for k in (0, 21):
        u_r[k] = jnp.zeros((40, 256), F32)
        u_b[k] = jnp.zeros((40, 256), F32)
    row = iota((8, 128), 0)
    y0 = is_zero(bit_y)
    in_y = (y0 & (row != 7)) | (jnp.logical_not(y0) & (row != 0))
    own_start = pl.multiple_of(32 * bit_y, 32)
    side_start = pl.multiple_of(32 - 8 * bit_y, 8)
    for n in range(20):
        for h in range(2):
            lanes = slice(128 * h, 128 * h + 128)
            side = jnp.where(in_y, tall[n, h, pl.ds(side_start, 8), :], 0.0)
            u_b[1 + n, 0:32, lanes] = u1_b[3 + n, 0:32, lanes] + tall[n, h, pl.ds(own_start, 32), :]
            u_b[1 + n, 32:40, lanes] = u1_b[3 + n, 32:40, lanes] + side
    mask = odd(40, 256)
    f_r, f_b, i_r, i_b = (grid.at[2:24] for grid in (f_r, f_b, i_r, i_b))
    half_sweep(u_r, u_b, f_r, i_r, 1, 21, True, mask, 1.0, 0)
    half_sweep(u_b, u_r, f_b, i_b, 2, 20, False, mask, 1.0, 0)
    half_sweep(u_r, u_b, f_r, i_r, 2, 20, True, mask, 1.0, 0)
    half_sweep(u_b, u_r, f_b, i_b, 3, 19, False, mask, 1.0, 0)
    own = odd(32, 128)
    for t in range(16):
        red, black = u_r[3 + t, 0:32, 0:128], u_b[3 + t, 0:32, 0:128]
        out[0, 2 * t] = jnp.where(own, black, red)
        out[0, 2 * t + 1] = jnp.where(own, red, black)


def swap_cores(x):
    return lax.ppermute(x, "level", [(0, 1), (1, 0)])


def to_slabs(x, up_first):
    pairs = []
    for s in range(SLABS - 1):
        for m in range(8):
            low, high = s * 8 + m, (s + 1) * 8 + m
            pairs.append((low, high) if (m < 4) == up_first else (high, low))
    return lax.ppermute(x, ALL, pairs)


def around_chips(x):
    return [x] + [lax.ppermute(x, "bottom", [(i, (i + d) % 4) for i in range(4)]) for d in range(1, 4)]


def both_cores(boxes):
    return boxes + [swap_cores(box) for box in boxes]


def ring_sums(x, stride):
    def moved(s, step):
        at = s // stride % 4
        return s + ((at + step) % 4 - at) * stride

    beside = [(8 * s + m, 8 * moved(s, 1 if m < 4 else 3) + m) for s in range(SLABS) for m in range(8)]
    across = [(s, moved(s, 2)) for s in range(SLABS)]
    return lax.ppermute(x, ALL, beside), lax.ppermute(x, "slab", across)


def among(x):
    return lax.all_to_all(x, LB, split_axis=0, concat_axis=0, tiled=True)


def body(u_init, source, coeffs, brick_map):
    meta = jnp.stack([lax.axis_index("slab"), lax.axis_index(LB)]).astype(jnp.int32)
    smem = [meta, brick_map]
    fine = (26, 40, 256)
    packed, ac = run(
        first_kernel, [(8, SENT, 8, 128), (8, 16, 128)], smem, [u_init, source, coeffs],
        [(8, 32, 128), (16, 32, 128), (256, 128), (1, 32, 32, 128)],
    )
    got = among(packed)
    leaving = run(cross_kernel, [(4, FACE + 4, 8, 128)], smem, [got])
    leaving, ac = lax.optimization_barrier((leaving, ac))
    cross = to_slabs(leaving, False)
    cross, *ac_boxes = lax.optimization_barrier((cross, *around_chips(ac)))
    sent, coef = run(
        mid_kernel, [(8, GOT, 8, 128), (2, 8, 2, 8, 128)], smem, [got, cross], [(12, FACE, 8, 128)],
    )
    coef_other = swap_cores(coef)
    halo = among(sent)
    faces = (4, 5, 16, 128)
    coarse = (28, 32, 128)
    held = [(8, 8, 16, 128), faces, faces]
    ac_boxes = both_cores(ac_boxes)
    ac_cross = to_slabs(run(faces_kernel, [faces], smem, ac_boxes, held[:1]), True)
    ac_other = swap_cores(ac_cross)
    halo, ac_cross, ac_other, coef_other = lax.optimization_barrier((halo, ac_cross, ac_other, coef_other))
    rc, u_b, f_r, f_b, i_r, i_b = run(
        fine_down_kernel, [(8, 16, 128)] + [fine] * 5, smem, [u_init, source, coeffs, halo],
        [fine, (16, 32, 128), (256, 128)],
    )
    boxes = both_cores(around_chips(rc))
    leaving = run(faces_kernel, [faces], smem, boxes, held[:1])
    leaving, ac_cross, ac_other, coef = lax.optimization_barrier((leaving, ac_cross, ac_other, coef))
    cross = to_slabs(leaving, True)
    weights = run(
        weights_kernel, [(16, 16, 128)], [meta], [coef, coef_other],
        [(26, 16, 128)] * 6 + [(8, 2, 8, 128)] * 2,
    )
    ca_r, ci_r, ci_b, ab = run(
        coarse_coef_kernel, [coarse] * 3 + [(22, 16, 128)], smem, ac_boxes + [ac_cross, ac_other],
        held + [coarse, (22, 32, 128), (352, 128)],
    )
    cross, weights, ca_r, ci_r, ci_b, ab = lax.optimization_barrier((cross, weights, ca_r, ci_r, ci_b, ab))
    rb, rb_send, part, ec_b, r_r, r_b = run(
        coarse_down_kernel, [(22, 16, 128), (18, 16, 128), (8, 128)] + [coarse] * 3, smem,
        boxes + [cross, swap_cores(cross), weights, ca_r, ci_r, ci_b, ab],
        held + [coarse, (22, 32, 128), (352, 128)],
    )
    cross = to_slabs(rb_send, True)
    near, far = ring_sums(part, 1)
    cross, near, far = lax.optimization_barrier((cross, near, far))
    other = swap_cores(cross)
    part = (part + swap_cores(near)) + (near + far)
    near, far = ring_sums(part, 4)
    sums = [part, near, far, swap_cores(near)]
    bottom = (28, 16, 128)
    es = run(
        bottom_kernel, [(22, 16, 128)], [meta], [rb, cross, other],
        [bottom] * 6 + [(18, 16, 128)] * 2,
    )
    return run(
        up_kernel, [(1, 32, 32, 128)], smem,
        sums + [es, ec_b, r_r, r_b, ci_r, ci_b, u_b, f_r, f_b, i_r, i_b],
        [(16, 32, 128)] * 2 + [(224, 128), (14, 32, 128), (640, 128), (20, 2, 64, 128), (22, 40, 256), (22, 40, 256)],
    )


def solution(mesh):
    placed = P(ALL, None, None, None)
    return jax.shard_map(
        body, mesh=mesh, in_specs=(placed, placed, placed, P()), out_specs=placed, check_vma=False
    )
```

```python
import jax
import jax.numpy as jnp
from jax import lax
from jax.experimental import pallas as pl
from jax.experimental.pallas import tpu as pltpu
from jax.sharding import PartitionSpec as P

LB = ("level", "bottom")
ALL = ("slab", "level", "bottom")
SLABS = 16
OWN = 5
F32 = jnp.float32
VMEM_SPEC = pl.BlockSpec(memory_space=pltpu.VMEM)
SMEM_SPEC = pl.BlockSpec(memory_space=pltpu.SMEM)
EXACT = lax.Precision.HIGHEST


def run(kernel, outs, smem, vmem, scratch=()):
    shapes = [jax.ShapeDtypeStruct(s, F32) for s in outs]
    single = len(shapes) == 1
    return pl.pallas_call(
        kernel,
        out_shape=shapes[0] if single else shapes,
        in_specs=[SMEM_SPEC] * len(smem) + [VMEM_SPEC] * len(vmem),
        out_specs=VMEM_SPEC if single else [VMEM_SPEC] * len(shapes),
        scratch_shapes=[pltpu.VMEM(s, F32) for s in scratch],
        compiler_params=pltpu.CompilerParams(vmem_limit_bytes=20 << 20),
    )(*smem, *vmem)


def iota(shape, dim):
    return lax.broadcasted_iota(jnp.int32, shape, dim)


def odd(rows, cols):
    return ((iota((rows, cols), 0) + iota((rows, cols), 1)) & 1) == 1


def place_of(meta, bricks):
    slab, me = meta[0], meta[1]
    place = jnp.int32(0)
    for i in range(8):
        place = place + jnp.where(bricks[slab, i] == me, i, 0)
    return slab, me, place & 1, (place >> 1) & 1, place >> 2


def is_zero(scalar, shape=(8, 128)):
    return jnp.full(shape, scalar, jnp.int32) == 0


ARRAYS = 5
FACE = 17
SENT_Y, SENT_X, SENT_COEF, SENT = 17, 27, 30, 32
GOT_ROWS, GOT_STRIPS, GOT_Y, GOT_X, GOT = 17, 20, 22, 32, 35


def face_planes(j):
    return [(1 + j, 0), (1 + j, 1), (1 + j, 2), (0, j)]


def merge_strips(placed, base=None):
    group = iota((8, 128), 1) // 8
    total = jnp.zeros((8, 128), F32) if base is None else base
    for pos, strip in placed:
        moved = pltpu.roll(strip, 8 * pos, 1) if pos else strip
        total = jnp.where(group == pos, moved, total)
    return total


def swap_lanes(cells):
    lane = iota(cells.shape, 1)
    return jnp.where((lane & 1) == 0, pltpu.roll(cells, cells.shape[1] - 1, 1), pltpu.roll(cells, 1, 1))


def pack_shell(get, out, bit_x, bit_y):
    x0, y0 = is_zero(bit_x), is_zero(bit_y)
    mask = odd(32, 128)
    for k in range(8):
        high, j = k >= 4, k % 4
        for i, (c, far) in enumerate(face_planes(j)):
            out[k, 4 * i : 4 * i + 4] = get(c, 15 - far if high else far).reshape(4, 8, 128)
        t = 12 if high else 3
        one, two = get(1, t), swap_lanes(get(3, t))
        both = jnp.where(mask, one, two) if high else jnp.where(mask, two, one)
        out[k, 16] = both[8 * j : 8 * j + 8]
        strips = []
        for tl in range(2):
            for c in range(ARRAYS):
                v = get(c, 2 * k + tl)
                out[k, SENT_Y + tl * ARRAYS + c] = jnp.where(y0, v[24:32], v[0:8])
                for g in range(4):
                    tile = v[8 * g : 8 * g + 8]
                    strips.append(jnp.where(x0, pltpu.roll(tile, 8, 1), tile))
        for i in range(3):
            out[k, SENT_X + i] = merge_strips(list(enumerate(strips[16 * i : 16 * i + 16])))


def cross_kernel(meta, bricks, recv, out):
    slab, me = meta[0], meta[1]
    for i in range(4):
        src = jnp.where(me >= 4, bricks[slab, 4 + i], bricks[slab, i])
        out[i, 0:FACE] = recv[src, 0:FACE]
        for j in range(2):
            coef = recv[bricks[slab, 2 * i + j], SENT_COEF:SENT]
            out[i, FACE + 2 * j : FACE + 2 * j + 2] = coef


def mid_kernel(meta, bricks, recv, cross, out, coef, faces):
    slab, me = meta[0], meta[1]
    faces[0:8] = recv[:, 0:FACE]
    faces[8:12] = cross[:, 0:FACE]
    for p in range(8):
        coef[0, p] = recv[bricks[slab, p], SENT_COEF:SENT]
        j = FACE + 2 * (p & 1)
        coef[1, p] = cross[p >> 1, j : j + 2]
    row = iota((8, 128), 0)
    for p in range(8):
        bx, by, bz = p & 1, (p >> 1) & 1, p >> 2
        dest = bricks[slab, p]
        same = me >= 4 if bz else me < 4

        def src(q):
            return jnp.where(same, bricks[slab, (q & 3) + 4 * (1 - bz)], 8 + (q & 3))

        def strip_of(tile):
            return pltpu.roll(tile, 8, 1) if bx else tile

        def rows_of(at):
            one, two, three, last = (faces[at, 4 * i + (3 if by else 0)] for i in range(4))
            if by:
                shared = jnp.where(row >= 3, two, pltpu.roll(three, 3, 0))
            else:
                shared = jnp.where(row < 5, two, pltpu.roll(three, 5, 0))
            return [one, shared, last]

        at_own, at_y, at_x, at_xy = src(p), src(p ^ 2), src(p ^ 1), src(p ^ 3)
        out[dest, 0:FACE] = faces[at_own]
        for i, tile in enumerate(rows_of(at_y)):
            out[dest, GOT_ROWS + i] = tile
        strips = [strip_of(faces[at_x, i]) for i in range(16)] + [strip_of(tile) for tile in rows_of(at_xy)]
        from_y, from_x, from_xy = bricks[slab, p ^ 2], bricks[slab, p ^ 1], bricks[slab, p ^ 3]
        strips += [strip_of(recv[from_xy, SENT_Y + i]) for i in range(2 * ARRAYS)]
        for i in range(2):
            out[dest, GOT_STRIPS + i] = merge_strips(list(enumerate(strips[16 * i : 16 * i + 16])))
        out[dest, GOT_Y:GOT_X] = recv[from_y, SENT_Y:SENT_X]
        out[dest, GOT_X:GOT] = recv[from_x, SENT_X:SENT_COEF]


def unpack_shell(recv, grids, bit_x, bit_y):
    row, lane = iota((8, 128), 0), iota((8, 128), 1)
    x0, y0 = is_zero(bit_x), is_zero(bit_y)
    in_x = (x0 & (lane < 8)) | (jnp.logical_not(x0) & (lane >= 120))
    five = (y0 & (row < 5)) | (jnp.logical_not(y0) & (row >= 3))
    three = (y0 & (row < 3)) | (jnp.logical_not(y0) & (row >= 5))
    seven = (y0 & (row != 7)) | (jnp.logical_not(y0) & (row != 0))
    mask = odd(8, 128)

    def cut(c, tile):
        return jnp.where(seven, tile, 0.0) if c >= 3 else tile

    def strip(tile, pos):
        shift = (jnp.where(bit_x == 0, 0, 120) + 128 - 8 * pos) % 128
        return jnp.where(in_x, pltpu.roll(tile, shift, 1), 0.0)

    def rows_of(tiles):
        one, shared, last = tiles
        moved = jnp.where(y0, pltpu.roll(shared, 3, 0), pltpu.roll(shared, 5, 0))
        return [one, jnp.where(five, shared, 0.0), jnp.where(three, moved, 0.0), last]

    for k in range(8):
        high, j = k >= 4, k % 4
        rows = rows_of([recv[k, GOT_ROWS + i] for i in range(3)])
        sides = rows_of([strip(recv[k, GOT_STRIPS + 1], i) for i in range(3)])
        for i, (c, far) in enumerate(face_planes(j)):
            at = OWN - 1 - far if high else OWN + 16 + far
            for g in range(4):
                grids[c][at, 8 * g : 8 * g + 8, 0:128] = recv[k, 4 * i + g]
                grids[c][at, 8 * g : 8 * g + 8, 128:256] = strip(recv[k, GOT_STRIPS], 4 * i + g)
            grids[c][at, 32:40, 0:128] = cut(c, rows[i])
            grids[c][at, 32:40, 128:256] = cut(c, sides[i])
        at = 1 if high else 24
        both = recv[k, 16]
        other = swap_lanes(both)
        other = jnp.where(mask, other, 0.0) if high else jnp.where(mask, 0.0, other)
        for c, cells in ((1, both), (3, other)):
            grids[c][at, 8 * j : 8 * j + 8, 0:128] = cells
            grids[c][at, 8 * j : 8 * j + 8, 128:256] = jnp.zeros((8, 128), F32)
            grids[c][at, 32:40] = jnp.zeros((8, 256), F32)
        for tl in range(2):
            for c in range(ARRAYS):
                i = tl * ARRAYS + c
                at = OWN + 2 * k + tl
                grids[c][at, 32:40, 0:128] = cut(c, recv[k, GOT_Y + i])
                grids[c][at, 32:40, 128:256] = cut(c, strip(recv[k, GOT_STRIPS + 1], 3 + i))
                for g in range(4):
                    n = 4 * i + g
                    side = strip(recv[k, GOT_X + n // 16], n % 16)
                    grids[c][at, 8 * g : 8 * g + 8, 128:256] = side


def pair_of(cells, t, red, mask):
    low, high = cells[0, 2 * t], cells[0, 2 * t + 1]
    return jnp.where(mask, high, low) if red else jnp.where(mask, low, high)


def pack_bottom_coef(a, out, small):
    for i in range(8):
        planes = (a[0, 4 * i] + a[0, 4 * i + 1]) + (a[0, 4 * i + 2] + a[0, 4 * i + 3])
        small[i] = planes
    rows = []
    for i in range(8):
        first = small[i, pl.ds(0, 8, stride=4), :] + small[i, pl.ds(1, 8, stride=4), :]
        rows.append(first + (small[i, pl.ds(2, 8, stride=4), :] + small[i, pl.ds(3, 8, stride=4), :]))
    fold = pick(128, 128, lambda r, c: (r >> 2) == (c & 31)) * (1.0 / 64)
    cells = jnp.dot(jnp.concatenate(rows, 0), fold, precision=EXACT, preferred_element_type=F32)
    group = iota((8, 128), 1) >> 5
    for h in range(2):
        tile = cells[32 * h : 32 * h + 8]
        for j in range(1, 4):
            tile = jnp.where(group == j, cells[32 * h + 8 * j : 32 * h + 8 * j + 8], tile)
        for k in range(8):
            out[k, SENT_COEF + h] = tile


def pack_coarse(planes, small, out):
    twice = pick(128, 128, lambda r, c: (r >> 1) == (c & 63)) * 0.125
    row, lane = iota((16, 128), 0), iota((16, 128), 1)
    even = ((row + lane + (lane >> 6)) & 1) == 0
    for t in range(16):
        small[16 * t : 16 * t + 16] = planes[t, pl.ds(0, 16, stride=2), :] + planes[t, pl.ds(1, 16, stride=2), :]
    summed = jnp.dot(small[...], twice, precision=EXACT, preferred_element_type=F32)
    summed = summed.reshape(16, 16, 128)
    for j in range(8):
        out[j] = jnp.where(even, summed[2 * j], summed[2 * j + 1])


def first_kernel(meta, bricks, u, f, a, out, ac, small, planes, rows, inverse):
    _, _, bit_x, bit_y, _ = place_of(meta, bricks)
    mask = odd(32, 128)
    inverse[...] = 1.0 / (a[...] + 6.0)
    sources = ((u, False), (f, True), (f, False), (inverse, True), (inverse, False))

    def get(c, t):
        return pair_of(sources[c][0], t, sources[c][1], mask)

    pack_shell(get, out, bit_x, bit_y)
    pack_bottom_coef(a, out, small)
    for t in range(16):
        planes[t] = a[0, 2 * t] + a[0, 2 * t + 1]
    pack_coarse(planes, rows, ac)


def around(src, k, red, mask, edges, cut=None):
    here = src[k]
    rows, cols = here.shape
    above, below = src[k + 1], src[k - 1]
    other = jnp.where(mask, above, below) if red else jnp.where(mask, below, above)
    up, down = pltpu.roll(here, 1, 0), pltpu.roll(here, rows - 1, 0)
    left, right = pltpu.roll(here, 1, 1), pltpu.roll(here, cols - 1, 1)
    if edges:
        row, lane = iota((rows, cols), 0), iota((rows, cols), 1)
        up, down = jnp.where(row == 0, 0.0, up), jnp.where(row == rows - 1, 0.0, down)
        if edges == 2:
            left, right = jnp.where(lane == 0, 0.0, left), jnp.where(lane == cols - 1, 0.0, right)
    if cut is not None:
        up, down = jnp.where(cut[0], 0.0, up), jnp.where(cut[1], 0.0, down)
    return ((here + other) + (up + down)) + (left + right)


def half_sweep(dst, src, force, inverse, lo, hi, red, mask, scale, edges, cut=None):
    def step(k, carry):
        total = around(src, k, red, mask, edges, cut)
        if scale != 1.0:
            total = scale * total
        dst[k] = (force[k] + total) * inverse[k]
        return carry

    lax.fori_loop(lo, hi, step, 0, unroll=True)


def select_dot(cells, chosen):
    half, total = chosen.astype(jnp.bfloat16), None
    for _ in range(3):
        part = cells.astype(jnp.bfloat16)
        cells = cells - part.astype(F32)
        moved = jnp.dot(part, half, preferred_element_type=F32)
        total = moved if total is None else total + moved
    return total


def pick(rows, cols, keep):
    return jnp.where(keep(iota((rows, cols), 0), iota((rows, cols), 1)), 1.0, 0.0).astype(F32)


def fine_down_kernel(meta, bricks, u, f, a, recv, rc, u_b, f_r, f_b, i_r, i_b, u_r, resid, small):
    _, _, bit_x, bit_y, _ = place_of(meta, bricks)
    own = odd(32, 128)
    for t in range(16):
        here = (OWN + t, slice(0, 32), slice(0, 128))
        u_b[here] = pair_of(u, t, False, own)
        f_r[here], f_b[here] = pair_of(f, t, True, own), pair_of(f, t, False, own)
        i_r[here], i_b[here] = 1.0 / (pair_of(a, t, True, own) + 6.0), 1.0 / (pair_of(a, t, False, own) + 6.0)
    unpack_shell(recv, (u_b, f_r, f_b, i_r, i_b), bit_x, bit_y)
    zero = jnp.zeros((40, 256), F32)
    for k in (0, 25):
        u_r[k] = zero
        u_b[k] = zero
    for k in (1, 24):
        f_b[k] = zero
        i_b[k] = zero
    row = iota((40, 256), 0)
    y0 = is_zero(bit_y, (40, 256))
    y1 = jnp.logical_not(y0)
    mask = odd(40, 256)
    cut = (y0 & (row == 0), y1 & (row == 31))
    half_sweep(u_r, u_b, f_r, i_r, 1, 25, True, mask, 1.0, 0, cut)
    half_sweep(u_b, u_r, f_b, i_b, 1, 25, False, mask, 1.0, 0)
    half_sweep(u_r, u_b, f_r, i_r, 2, 24, True, mask, 1.0, 0)
    half_sweep(u_b, u_r, f_b, i_b, 3, 23, False, mask, 1.0, 0)
    for t in range(16):
        total = around(u_b, OWN + t, True, mask, 0)[0:32, 0:128]
        diag = pair_of(a, t, True, own) + 6.0
        here = (OWN + t, slice(0, 32), slice(0, 128))
        resid[t] = f_r[here] + total - diag * u_r[here]
    pack_coarse(resid, small, rc)


def slot_of(member, me):
    return jnp.where((member >> 2) == (me >> 2), 0, 4) + ((me - member) & 3)


def faces_kernel(meta, bricks, *refs):
    boxes, (out, held) = refs[:8], refs[8:]
    slab, me = meta[0], meta[1]
    for i, box in enumerate(boxes):
        held[i] = box[...]
    start = jnp.where(me < 4, 3, 0)
    for i in range(4):
        member = jnp.where(me < 4, bricks[slab, 4 + i], bricks[slab, i])
        out[i] = held[slot_of(member, me), pl.ds(start, 5)]


def sort_sides(me, one, two, low, high):
    @pl.when(me < 4)
    def _():
        low[...] = one[...]
        high[...] = two[...]

    @pl.when(me >= 4)
    def _():
        low[...] = two[...]
        high[...] = one[...]


def assemble(meta, bricks, boxes, one, two, red, black, held, low, high):
    slab, me = meta[0], meta[1]
    for i, box in enumerate(boxes):
        held[i] = box[...]
    sort_sides(me, one, two, low, high)
    left = iota((16, 128), 1) < 64

    def put(k, by, west, east):
        rows = slice(16 * by, 16 * by + 16)
        red[k, rows] = jnp.where(left, west, pltpu.roll(east, 64, 1))
        black[k, rows] = jnp.where(left, pltpu.roll(west, 64, 1), east)

    for by in range(2):
        for bz in range(2):
            west = slot_of(bricks[slab, 2 * by + 4 * bz], me)
            east = slot_of(bricks[slab, 2 * by + 4 * bz + 1], me)
            for j in range(8):
                put(6 + 8 * bz + j, by, held[west, j], held[east, j])
        for j in range(5):
            put(1 + j, by, low[2 * by, j], low[2 * by + 1, j])
            put(22 + j, by, high[2 * by, j], high[2 * by + 1, j])


def to_bottom(planes, small, half):
    for n in range(22):
        small[16 * n : 16 * n + 16] = planes[n, pl.ds(0, 16, stride=2), :] + planes[n, pl.ds(1, 16, stride=2), :]
    fold = pick(128, 128, lambda r, c: (r >> 1) == c - 64 * half) * 0.125
    return jnp.dot(small[...], fold, precision=EXACT, preferred_element_type=F32).reshape(22, 16, 128)


def coarse_coef_kernel(meta, bricks, *refs):
    boxes, (one, two) = refs[:8], refs[8:10]
    a_r, i_r, i_b, ab = refs[10:14]
    held, low, high, a_b, planes, small = refs[14:]
    slab = meta[0]
    assemble(meta, bricks, boxes, one, two, a_r, a_b, held, low, high)
    for k in range(1, 27):
        keep = jnp.full((32, 128), 0, jnp.int32) == 0
        if k < 6:
            keep = jnp.logical_not(is_zero(slab, (32, 128)))
        if k >= 22:
            keep = jnp.logical_not(is_zero(slab - (SLABS - 1), (32, 128)))
        i_r[k] = jnp.where(keep, 1.0 / (a_r[k] + 1.5), 0.0)
        i_b[k] = jnp.where(keep, 1.0 / (a_b[k] + 1.5), 0.0)
    for n in range(22):
        planes[n] = a_r[3 + n] + a_b[3 + n]
    ab[...] = to_bottom(planes, small, 1)


def coarse_down_kernel(meta, bricks, *refs):
    boxes, (one, two, weights, a_r, i_r, i_b, ab) = refs[:8], refs[8:15]
    rb, rb_send, part, e_b, r_r, r_b = refs[15:21]
    held, low, high, e_r, resid, small = refs[21:]
    me = meta[1]
    assemble(meta, bricks, boxes, one, two, r_r, r_b, held, low, high)
    for k in (0, 27):
        e_r[k] = jnp.zeros((32, 128), F32)
        e_b[k] = jnp.zeros((32, 128), F32)
    for k in range(1, 27):
        e_r[k] = r_r[k] * i_r[k]
    mask = odd(32, 128)
    half_sweep(e_b, e_r, r_b, i_b, 1, 27, False, mask, 0.25, 2)
    half_sweep(e_r, e_b, r_r, i_r, 1, 27, True, mask, 0.25, 2)
    half_sweep(e_b, e_r, r_b, i_b, 1, 27, False, mask, 0.25, 2)
    for n in range(22):
        k = n + 3
        total = 0.25 * around(e_b, k, True, mask, 2)
        resid[n] = r_r[k] + total - (a_r[k] + 1.5) * e_r[k]
    rb[...] = to_bottom(resid, small, 0) + ab[...]
    rb_send[...] = rb[pl.ds(jnp.where(me < 4, 1, 3), 18)]
    total = jnp.zeros((16, 128), F32)
    for i in range(16):
        total = total + rb[3 + i] * weights[i]
    part[...] = total[0:8] + total[8:16]


def bottom_kernel(meta, rb, one, two, es, e_r, e_b, g_r, g_b, i_r, i_b, low, high):
    slab, me = meta[0], meta[1]
    sort_sides(me, one, two, low, high)
    mask = odd(16, 128)
    left = iota((16, 128), 1) < 64
    zero = jnp.zeros((16, 128), F32)
    for k in (0, 27):
        e_r[k] = zero
        e_b[k] = zero
    for j in range(26):
        planes = []
        for n in (2 * j, 2 * j + 1):
            planes.append(low[n] if n < 18 else rb[n - 15] if n < 34 else high[n - 34])
        keep = left
        if j < 9:
            keep = left & jnp.logical_not(is_zero(slab, (16, 128)))
        if j >= 17:
            keep = left & jnp.logical_not(is_zero(slab - (SLABS - 1), (16, 128)))
        for red in (True, False):
            cells = jnp.where(mask, planes[1], planes[0]) if red else jnp.where(mask, planes[0], planes[1])
            force = jnp.where(left, cells, 0.0)
            inverse = jnp.where(keep, 1.0 / (pltpu.roll(cells, 64, 1) + 0.375), 0.0)
            if red:
                g_r[1 + j], i_r[1 + j], e_r[1 + j] = force, inverse, force * inverse
            else:
                g_b[1 + j], i_b[1 + j] = force, inverse
    half_sweep(e_b, e_r, g_b, i_b, 1, 27, False, mask, 0.0625, 1)

    def sweep(n, carry):
        half_sweep(e_r, e_b, g_r, i_r, 1, 27, True, mask, 0.0625, 1)
        half_sweep(e_b, e_r, g_b, i_b, 1, 27, False, mask, 0.0625, 1)
        return carry

    lax.fori_loop(0, 7, sweep, 0)
    for i in range(22):
        k, upper = (15 + i) // 2 + 1, (15 + i) % 2
        es[i] = jnp.where(mask, e_r[k], e_b[k]) if upper else jnp.where(mask, e_b[k], e_r[k])


def weights_kernel(meta, here, there, out, t_r, t_b, w_r, w_b, i_r, i_b, low, high):
    slab, me = meta[0], meta[1]

    @pl.when(me < 4)
    def _():
        low[...] = there[1]
        high[...] = here[1]

    @pl.when(me >= 4)
    def _():
        low[...] = here[1]
        high[...] = there[1]

    lane = iota((8, 128), 1)

    def plane(boxes, z):
        rows = []
        for by in range(2):
            place, shift = 4 * (z >> 3) + 2 * by, 32 * (z & 3)
            west = pltpu.roll(boxes(place, (z & 7) >> 2), (128 - shift) % 128, 1)
            east = pltpu.roll(boxes(place + 1, (z & 7) >> 2), (160 - shift) % 128, 1)
            rows.append(jnp.where(lane < 32, west, east))
        return jnp.concatenate(rows, 0)

    parts = (lambda p, h: low[p, h], lambda p, h: here[0, p, h], lambda p, h: high[p, h])
    mask = odd(16, 128)
    left = iota((16, 128), 1) < 64
    zero = jnp.zeros((16, 128), F32)
    for k in (0, 25):
        t_r[k] = zero
        t_b[k] = zero
    for j in range(24):
        lower, upper = (plane(parts[(2 * j + i) // 16], (2 * j + i) % 16) for i in range(2))
        keep = left
        if j < 8:
            keep = left & jnp.logical_not(is_zero(slab, (16, 128)))
        if j >= 16:
            keep = left & jnp.logical_not(is_zero(slab - (SLABS - 1), (16, 128)))
        i_r[1 + j] = jnp.where(keep, 1.0 / (jnp.where(mask, upper, lower) + 0.375), 0.0)
        i_b[1 + j] = jnp.where(keep, 1.0 / (jnp.where(mask, lower, upper) + 0.375), 0.0)
    for k in range(1, 25):
        t_b[k] = i_b[k]
        w_b[k] = i_b[k]
    for k in range(1, 25):
        t = i_r[k] * (1.0 + 0.0625 * around(t_b, k, True, mask, 1))
        t_r[k] = t
        w_r[k] = t

    def sweep(n, carry):
        for k in range(1, 25):
            t = i_b[k] * (0.0625 * around(t_r, k, False, mask, 1))
            t_b[k] = t
            w_b[k] = w_b[k] + t
        for k in range(1, 25):
            t = i_r[k] * (0.0625 * around(t_b, k, True, mask, 1))
            t_r[k] = t
            w_r[k] = w_r[k] + t
        return carry

    lax.fori_loop(0, 7, sweep, 0)
    for j in range(8):
        red, black = w_r[9 + j], w_b[9 + j]
        out[2 * j] = jnp.where(mask, black, red)
        out[2 * j + 1] = jnp.where(mask, red, black)


def up_kernel(
    meta, bricks, sum_0, sum_1, sum_2, sum_3, es, ec_b, r_r, r_b, ci_r, ci_b, u1_b, f_r, f_b, i_r, i_b, out,
    e_r, e_b, small, wide, planes, tall, u_r, u_b,
):
    slab, _, bit_x, bit_y, bit_z = place_of(meta, bricks)
    total = (sum_0[...] + sum_1[...]) + (sum_2[...] + sum_3[...])
    mean = jnp.sum(total) * (1.0 / (SLABS * 16 * 16 * 64))
    base = 8 * bit_z
    no_low = jnp.where((slab == 0) & (bit_z == 0), 0, 1)
    no_high = jnp.where((slab == SLABS - 1) & (bit_z == 1), 0, 1)
    for j in range(14):
        shifted = es[base + j] - mean
        if j < 3:
            shifted = jnp.where(is_zero(no_low, (16, 128)), 0.0, shifted)
        if j >= 11:
            shifted = jnp.where(is_zero(no_high, (16, 128)), 0.0, shifted)
        small[16 * j : 16 * j + 16] = shifted
    spread = pick(128, 128, lambda r, c: r == (c >> 1))
    small[...] = select_dot(small[...], spread)
    for j in range(14):
        rows = small[16 * j : 16 * j + 16]
        wide[j, pl.ds(0, 16, stride=2), :] = rows
        wide[j, pl.ds(1, 16, stride=2), :] = rows
    for k in (0, 15):
        e_r[k] = jnp.zeros((32, 128), F32)
        e_b[k] = jnp.zeros((32, 128), F32)
    for j in range(14):
        e_b[1 + j] = ec_b[base + 3 + j] + wide[j]
    coarse = odd(32, 128)
    r_r, r_b, ci_r, ci_b = (grid.at[pl.ds(base + 2, 16)] for grid in (r_r, r_b, ci_r, ci_b))
    half_sweep(e_r, e_b, r_r, ci_r, 1, 15, True, coarse, 0.25, 2)
    half_sweep(e_b, e_r, r_b, ci_b, 2, 14, False, coarse, 0.25, 2)
    half_sweep(e_r, e_b, r_r, ci_r, 2, 14, True, coarse, 0.25, 2)
    half_sweep(e_b, e_r, r_b, ci_b, 3, 13, False, coarse, 0.25, 2)
    for n in range(20):
        k, upper = n // 2 + 3, n % 2
        red, black = e_r[k], e_b[k]
        planes[32 * n : 32 * n + 32] = jnp.where(coarse, red, black) if upper else jnp.where(coarse, black, red)

    lane = iota((128, 256), 1)
    x0 = is_zero(bit_x, (128, 256))
    start = jnp.where(lane < 128, 64 * bit_x + (lane >> 1), (lane >> 1) + jnp.where(x0, 0, -64))
    usable = (lane < 128) | (x0 & (lane < 136)) | (jnp.logical_not(x0) & (lane >= 248))
    spread = jnp.where(usable & (iota((128, 256), 0) == start), 1.0, 0.0).astype(F32)
    tall_rows = select_dot(planes[...], spread)
    for n in range(20):
        rows = tall_rows[32 * n : 32 * n + 32]
        for h in range(2):
            tall[n, h, pl.ds(0, 32, stride=2), :] = rows[:, 128 * h : 128 * h + 128]
            tall[n, h, pl.ds(1, 32, stride=2), :] = rows[:, 128 * h : 128 * h + 128]
    for k in (0, 21):
        u_r[k] = jnp.zeros((40, 256), F32)
        u_b[k] = jnp.zeros((40, 256), F32)
    row = iota((8, 128), 0)
    y0 = is_zero(bit_y)
    in_y = (y0 & (row != 7)) | (jnp.logical_not(y0) & (row != 0))
    own_start = pl.multiple_of(32 * bit_y, 32)
    side_start = pl.multiple_of(32 - 8 * bit_y, 8)
    for n in range(20):
        for h in range(2):
            lanes = slice(128 * h, 128 * h + 128)
            side = jnp.where(in_y, tall[n, h, pl.ds(side_start, 8), :], 0.0)
            u_b[1 + n, 0:32, lanes] = u1_b[3 + n, 0:32, lanes] + tall[n, h, pl.ds(own_start, 32), :]
            u_b[1 + n, 32:40, lanes] = u1_b[3 + n, 32:40, lanes] + side
    mask = odd(40, 256)
    f_r, f_b, i_r, i_b = (grid.at[2:24] for grid in (f_r, f_b, i_r, i_b))
    half_sweep(u_r, u_b, f_r, i_r, 1, 21, True, mask, 1.0, 0)
    half_sweep(u_b, u_r, f_b, i_b, 2, 20, False, mask, 1.0, 0)
    half_sweep(u_r, u_b, f_r, i_r, 2, 20, True, mask, 1.0, 0)
    half_sweep(u_b, u_r, f_b, i_b, 3, 19, False, mask, 1.0, 0)
    own = odd(32, 128)
    for t in range(16):
        red, black = u_r[3 + t, 0:32, 0:128], u_b[3 + t, 0:32, 0:128]
        out[0, 2 * t] = jnp.where(own, black, red)
        out[0, 2 * t + 1] = jnp.where(own, red, black)


def swap_cores(x):
    return lax.ppermute(x, "level", [(0, 1), (1, 0)])


def to_slabs(x, up_first):
    pairs = []
    for s in range(SLABS - 1):
        for m in range(8):
            low, high = s * 8 + m, (s + 1) * 8 + m
            pairs.append((low, high) if (m < 4) == up_first else (high, low))
    return lax.ppermute(x, ALL, pairs)


def around_chips(x):
    return [x] + [lax.ppermute(x, "bottom", [(i, (i + d) % 4) for i in range(4)]) for d in range(1, 4)]


def both_cores(boxes):
    return boxes + [swap_cores(box) for box in boxes]


def ring_sums(x, stride):
    def moved(s, step):
        at = s // stride % 4
        return s + ((at + step) % 4 - at) * stride

    beside = [(8 * s + m, 8 * moved(s, 1 if m < 4 else 3) + m) for s in range(SLABS) for m in range(8)]
    across = [(s, moved(s, 2)) for s in range(SLABS)]
    return lax.ppermute(x, ALL, beside), lax.ppermute(x, "slab", across)


def among(x):
    return lax.all_to_all(x, LB, split_axis=0, concat_axis=0, tiled=True)


def body(u_init, source, coeffs, brick_map):
    meta = jnp.stack([lax.axis_index("slab"), lax.axis_index(LB)]).astype(jnp.int32)
    smem = [meta, brick_map]
    fine = (26, 40, 256)
    packed, ac = run(
        first_kernel, [(8, SENT, 8, 128), (8, 16, 128)], smem, [u_init, source, coeffs],
        [(8, 32, 128), (16, 32, 128), (256, 128), (1, 32, 32, 128)],
    )
    got = among(packed)
    leaving = run(cross_kernel, [(4, FACE + 4, 8, 128)], smem, [got])
    leaving, ac = lax.optimization_barrier((leaving, ac))
    cross = to_slabs(leaving, False)
    ac_boxes = around_chips(ac)
    sent, coef = run(
        mid_kernel, [(8, GOT, 8, 128), (2, 8, 2, 8, 128)], smem, [got, cross], [(12, FACE, 8, 128)],
    )
    coef_other = swap_cores(coef)
    sent, *ac_boxes = lax.optimization_barrier((sent, *ac_boxes))
    halo = among(sent)
    faces = (4, 5, 16, 128)
    coarse = (28, 32, 128)
    held = [(8, 8, 16, 128), faces, faces]
    ac_boxes = both_cores(ac_boxes)
    ac_cross = to_slabs(run(faces_kernel, [faces], smem, ac_boxes, held[:1]), True)
    ac_other = swap_cores(ac_cross)
    halo, ac_cross, ac_other, coef_other = lax.optimization_barrier((halo, ac_cross, ac_other, coef_other))
    rc, u_b, f_r, f_b, i_r, i_b = run(
        fine_down_kernel, [(8, 16, 128)] + [fine] * 5, smem, [u_init, source, coeffs, halo],
        [fine, (16, 32, 128), (256, 128)],
    )
    boxes = both_cores(around_chips(rc))
    leaving = run(faces_kernel, [faces], smem, boxes, held[:1])
    leaving, ac_cross, ac_other, coef = lax.optimization_barrier((leaving, ac_cross, ac_other, coef))
    cross = to_slabs(leaving, True)
    weights = run(
        weights_kernel, [(16, 16, 128)], [meta], [coef, coef_other],
        [(26, 16, 128)] * 6 + [(8, 2, 8, 128)] * 2,
    )
    ca_r, ci_r, ci_b, ab = run(
        coarse_coef_kernel, [coarse] * 3 + [(22, 16, 128)], smem, ac_boxes + [ac_cross, ac_other],
        held + [coarse, (22, 32, 128), (352, 128)],
    )
    cross, weights, ca_r, ci_r, ci_b, ab = lax.optimization_barrier((cross, weights, ca_r, ci_r, ci_b, ab))
    rb, rb_send, part, ec_b, r_r, r_b = run(
        coarse_down_kernel, [(22, 16, 128), (18, 16, 128), (8, 128)] + [coarse] * 3, smem,
        boxes + [cross, swap_cores(cross), weights, ca_r, ci_r, ci_b, ab],
        held + [coarse, (22, 32, 128), (352, 128)],
    )
    cross = to_slabs(rb_send, True)
    near, far = ring_sums(part, 1)
    cross, near, far = lax.optimization_barrier((cross, near, far))
    other = swap_cores(cross)
    part = (part + swap_cores(near)) + (near + far)
    near, far = ring_sums(part, 4)
    sums = [part, near, far, swap_cores(near)]
    bottom = (28, 16, 128)
    es = run(
        bottom_kernel, [(22, 16, 128)], [meta], [rb, cross, other],
        [bottom] * 6 + [(18, 16, 128)] * 2,
    )
    return run(
        up_kernel, [(1, 32, 32, 128)], smem,
        sums + [es, ec_b, r_r, r_b, ci_r, ci_b, u_b, f_r, f_b, i_r, i_b],
        [(16, 32, 128)] * 2 + [(224, 128), (14, 32, 128), (640, 128), (20, 2, 64, 128), (22, 40, 256), (22, 40, 256)],
    )


def solution(mesh):
    placed = P(ALL, None, None, None)
    return jax.shard_map(
        body, mesh=mesh, in_specs=(placed, placed, placed, P()), out_specs=placed, check_vma=False
    )
```

```python
import jax
import jax.numpy as jnp
from jax import lax
from jax.experimental import pallas as pl
from jax.experimental.pallas import tpu as pltpu
from jax.sharding import PartitionSpec as P

LB = ("level", "bottom")
ALL = ("slab", "level", "bottom")
SLABS = 16
OWN = 5
F32 = jnp.float32
VMEM_SPEC = pl.BlockSpec(memory_space=pltpu.VMEM)
SMEM_SPEC = pl.BlockSpec(memory_space=pltpu.SMEM)
EXACT = lax.Precision.HIGHEST


def run(kernel, outs, smem, vmem, scratch=()):
    shapes = [jax.ShapeDtypeStruct(s, F32) for s in outs]
    single = len(shapes) == 1
    return pl.pallas_call(
        kernel,
        out_shape=shapes[0] if single else shapes,
        in_specs=[SMEM_SPEC] * len(smem) + [VMEM_SPEC] * len(vmem),
        out_specs=VMEM_SPEC if single else [VMEM_SPEC] * len(shapes),
        scratch_shapes=[pltpu.VMEM(s, F32) for s in scratch],
        compiler_params=pltpu.CompilerParams(vmem_limit_bytes=20 << 20),
    )(*smem, *vmem)


def iota(shape, dim):
    return lax.broadcasted_iota(jnp.int32, shape, dim)


def odd(rows, cols):
    return ((iota((rows, cols), 0) + iota((rows, cols), 1)) & 1) == 1


def place_of(meta, bricks):
    slab, me = meta[0], meta[1]
    place = jnp.int32(0)
    for i in range(8):
        place = place + jnp.where(bricks[slab, i] == me, i, 0)
    return slab, me, place & 1, (place >> 1) & 1, place >> 2


def is_zero(scalar, shape=(8, 128)):
    return jnp.full(shape, scalar, jnp.int32) == 0


ARRAYS = 5
FACE = 17
SENT_Y, SENT_X, SENT_COEF, SENT = 17, 27, 30, 32
GOT_ROWS, GOT_STRIPS, GOT_Y, GOT_X, GOT = 17, 20, 22, 32, 35


def face_planes(j):
    return [(1 + j, 0), (1 + j, 1), (1 + j, 2), (0, j)]


def merge_strips(placed, base=None):
    group = iota((8, 128), 1) // 8
    total = jnp.zeros((8, 128), F32) if base is None else base
    for pos, strip in placed:
        moved = pltpu.roll(strip, 8 * pos, 1) if pos else strip
        total = jnp.where(group == pos, moved, total)
    return total


def swap_lanes(cells):
    lane = iota(cells.shape, 1)
    return jnp.where((lane & 1) == 0, pltpu.roll(cells, cells.shape[1] - 1, 1), pltpu.roll(cells, 1, 1))


def pack_shell(get, out, bit_x, bit_y):
    x0, y0 = is_zero(bit_x), is_zero(bit_y)
    mask = odd(32, 128)
    for k in range(8):
        high, j = k >= 4, k % 4
        for i, (c, far) in enumerate(face_planes(j)):
            out[k, 4 * i : 4 * i + 4] = get(c, 15 - far if high else far).reshape(4, 8, 128)
        t = 12 if high else 3
        one, two = get(1, t), swap_lanes(get(3, t))
        both = jnp.where(mask, one, two) if high else jnp.where(mask, two, one)
        out[k, 16] = both[8 * j : 8 * j + 8]
        strips = []
        for tl in range(2):
            for c in range(ARRAYS):
                v = get(c, 2 * k + tl)
                out[k, SENT_Y + tl * ARRAYS + c] = jnp.where(y0, v[24:32], v[0:8])
                for g in range(4):
                    tile = v[8 * g : 8 * g + 8]
                    strips.append(jnp.where(x0, pltpu.roll(tile, 8, 1), tile))
        for i in range(3):
            out[k, SENT_X + i] = merge_strips(list(enumerate(strips[16 * i : 16 * i + 16])))


def cross_kernel(meta, bricks, recv, out):
    slab, me = meta[0], meta[1]
    for i in range(4):
        src = jnp.where(me >= 4, bricks[slab, 4 + i], bricks[slab, i])
        out[i, 0:FACE] = recv[src, 0:FACE]
        for j in range(2):
            coef = recv[bricks[slab, 2 * i + j], SENT_COEF:SENT]
            out[i, FACE + 2 * j : FACE + 2 * j + 2] = coef


def mid_kernel(meta, bricks, recv, cross, out, coef, faces):
    slab, me = meta[0], meta[1]
    faces[0:8] = recv[:, 0:FACE]
    faces[8:12] = cross[:, 0:FACE]
    for p in range(8):
        coef[0, p] = recv[bricks[slab, p], SENT_COEF:SENT]
        j = FACE + 2 * (p & 1)
        coef[1, p] = cross[p >> 1, j : j + 2]
    row = iota((8, 128), 0)
    for p in range(8):
        bx, by, bz = p & 1, (p >> 1) & 1, p >> 2
        dest = bricks[slab, p]
        same = me >= 4 if bz else me < 4

        def src(q):
            return jnp.where(same, bricks[slab, (q & 3) + 4 * (1 - bz)], 8 + (q & 3))

        def strip_of(tile):
            return pltpu.roll(tile, 8, 1) if bx else tile

        def rows_of(at):
            one, two, three, last = (faces[at, 4 * i + (3 if by else 0)] for i in range(4))
            if by:
                shared = jnp.where(row >= 3, two, pltpu.roll(three, 3, 0))
            else:
                shared = jnp.where(row < 5, two, pltpu.roll(three, 5, 0))
            return [one, shared, last]

        at_own, at_y, at_x, at_xy = src(p), src(p ^ 2), src(p ^ 1), src(p ^ 3)
        out[dest, 0:FACE] = faces[at_own]
        for i, tile in enumerate(rows_of(at_y)):
            out[dest, GOT_ROWS + i] = tile
        strips = [strip_of(faces[at_x, i]) for i in range(16)] + [strip_of(tile) for tile in rows_of(at_xy)]
        from_y, from_x, from_xy = bricks[slab, p ^ 2], bricks[slab, p ^ 1], bricks[slab, p ^ 3]
        strips += [strip_of(recv[from_xy, SENT_Y + i]) for i in range(2 * ARRAYS)]
        for i in range(2):
            out[dest, GOT_STRIPS + i] = merge_strips(list(enumerate(strips[16 * i : 16 * i + 16])))
        out[dest, GOT_Y:GOT_X] = recv[from_y, SENT_Y:SENT_X]
        out[dest, GOT_X:GOT] = recv[from_x, SENT_X:SENT_COEF]


def unpack_shell(recv, grids, bit_x, bit_y):
    row, lane = iota((8, 128), 0), iota((8, 128), 1)
    x0, y0 = is_zero(bit_x), is_zero(bit_y)
    in_x = (x0 & (lane < 8)) | (jnp.logical_not(x0) & (lane >= 120))
    five = (y0 & (row < 5)) | (jnp.logical_not(y0) & (row >= 3))
    three = (y0 & (row < 3)) | (jnp.logical_not(y0) & (row >= 5))
    seven = (y0 & (row != 7)) | (jnp.logical_not(y0) & (row != 0))
    mask = odd(8, 128)

    def cut(c, tile):
        return jnp.where(seven, tile, 0.0) if c >= 3 else tile

    def strip(tile, pos):
        shift = (jnp.where(bit_x == 0, 0, 120) + 128 - 8 * pos) % 128
        return jnp.where(in_x, pltpu.roll(tile, shift, 1), 0.0)

    def rows_of(tiles):
        one, shared, last = tiles
        moved = jnp.where(y0, pltpu.roll(shared, 3, 0), pltpu.roll(shared, 5, 0))
        return [one, jnp.where(five, shared, 0.0), jnp.where(three, moved, 0.0), last]

    for k in range(8):
        high, j = k >= 4, k % 4
        rows = rows_of([recv[k, GOT_ROWS + i] for i in range(3)])
        sides = rows_of([strip(recv[k, GOT_STRIPS + 1], i) for i in range(3)])
        for i, (c, far) in enumerate(face_planes(j)):
            at = OWN - 1 - far if high else OWN + 16 + far
            for g in range(4):
                grids[c][at, 8 * g : 8 * g + 8, 0:128] = recv[k, 4 * i + g]
                grids[c][at, 8 * g : 8 * g + 8, 128:256] = strip(recv[k, GOT_STRIPS], 4 * i + g)
            grids[c][at, 32:40, 0:128] = cut(c, rows[i])
            grids[c][at, 32:40, 128:256] = cut(c, sides[i])
        at = 1 if high else 24
        both = recv[k, 16]
        other = swap_lanes(both)
        other = jnp.where(mask, other, 0.0) if high else jnp.where(mask, 0.0, other)
        for c, cells in ((1, both), (3, other)):
            grids[c][at, 8 * j : 8 * j + 8, 0:128] = cells
            grids[c][at, 8 * j : 8 * j + 8, 128:256] = jnp.zeros((8, 128), F32)
            grids[c][at, 32:40] = jnp.zeros((8, 256), F32)
        for tl in range(2):
            for c in range(ARRAYS):
                i = tl * ARRAYS + c
                at = OWN + 2 * k + tl
                grids[c][at, 32:40, 0:128] = cut(c, recv[k, GOT_Y + i])
                grids[c][at, 32:40, 128:256] = cut(c, strip(recv[k, GOT_STRIPS + 1], 3 + i))
                for g in range(4):
                    n = 4 * i + g
                    side = strip(recv[k, GOT_X + n // 16], n % 16)
                    grids[c][at, 8 * g : 8 * g + 8, 128:256] = side


def pair_of(cells, t, red, mask):
    low, high = cells[0, 2 * t], cells[0, 2 * t + 1]
    return jnp.where(mask, high, low) if red else jnp.where(mask, low, high)


def pack_bottom_coef(a, out, small):
    for i in range(8):
        planes = (a[0, 4 * i] + a[0, 4 * i + 1]) + (a[0, 4 * i + 2] + a[0, 4 * i + 3])
        small[i] = planes
    rows = []
    for i in range(8):
        first = small[i, pl.ds(0, 8, stride=4), :] + small[i, pl.ds(1, 8, stride=4), :]
        rows.append(first + (small[i, pl.ds(2, 8, stride=4), :] + small[i, pl.ds(3, 8, stride=4), :]))
    fold = pick(128, 128, lambda r, c: (r >> 2) == (c & 31)) * (1.0 / 64)
    cells = jnp.dot(jnp.concatenate(rows, 0), fold, precision=EXACT, preferred_element_type=F32)
    group = iota((8, 128), 1) >> 5
    for h in range(2):
        tile = cells[32 * h : 32 * h + 8]
        for j in range(1, 4):
            tile = jnp.where(group == j, cells[32 * h + 8 * j : 32 * h + 8 * j + 8], tile)
        for k in range(8):
            out[k, SENT_COEF + h] = tile


def pack_coarse(planes, small, out):
    twice = pick(128, 128, lambda r, c: (r >> 1) == (c & 63)) * 0.125
    row, lane = iota((16, 128), 0), iota((16, 128), 1)
    even = ((row + lane + (lane >> 6)) & 1) == 0
    for t in range(16):
        small[16 * t : 16 * t + 16] = planes[t, pl.ds(0, 16, stride=2), :] + planes[t, pl.ds(1, 16, stride=2), :]
    summed = jnp.dot(small[...], twice, precision=EXACT, preferred_element_type=F32)
    summed = summed.reshape(16, 16, 128)
    for j in range(8):
        out[j] = jnp.where(even, summed[2 * j], summed[2 * j + 1])


def first_kernel(meta, bricks, u, f, a, out, ac, small, planes, rows, inverse):
    _, _, bit_x, bit_y, _ = place_of(meta, bricks)
    mask = odd(32, 128)
    inverse[...] = 1.0 / (a[...] + 6.0)
    sources = ((u, False), (f, True), (f, False), (inverse, True), (inverse, False))

    def get(c, t):
        return pair_of(sources[c][0], t, sources[c][1], mask)

    pack_shell(get, out, bit_x, bit_y)
    pack_bottom_coef(a, out, small)
    for t in range(16):
        planes[t] = a[0, 2 * t] + a[0, 2 * t + 1]
    pack_coarse(planes, rows, ac)


def around(src, k, red, mask, edges, cut=None):
    here = src[k]
    rows, cols = here.shape
    above, below = src[k + 1], src[k - 1]
    other = jnp.where(mask, above, below) if red else jnp.where(mask, below, above)
    up, down = pltpu.roll(here, 1, 0), pltpu.roll(here, rows - 1, 0)
    left, right = pltpu.roll(here, 1, 1), pltpu.roll(here, cols - 1, 1)
    if edges:
        row, lane = iota((rows, cols), 0), iota((rows, cols), 1)
        up, down = jnp.where(row == 0, 0.0, up), jnp.where(row == rows - 1, 0.0, down)
        if edges == 2:
            left, right = jnp.where(lane == 0, 0.0, left), jnp.where(lane == cols - 1, 0.0, right)
    if cut is not None:
        up, down = jnp.where(cut[0], 0.0, up), jnp.where(cut[1], 0.0, down)
    return ((here + other) + (up + down)) + (left + right)


def half_sweep(dst, src, force, inverse, lo, hi, red, mask, scale, edges, cut=None):
    def step(k, carry):
        total = around(src, k, red, mask, edges, cut)
        if scale != 1.0:
            total = scale * total
        dst[k] = (force[k] + total) * inverse[k]
        return carry

    lax.fori_loop(lo, hi, step, 0, unroll=True)


def select_dot(cells, chosen):
    half, total = chosen.astype(jnp.bfloat16), None
    for _ in range(3):
        part = cells.astype(jnp.bfloat16)
        cells = cells - part.astype(F32)
        moved = jnp.dot(part, half, preferred_element_type=F32)
        total = moved if total is None else total + moved
    return total


def pick(rows, cols, keep):
    return jnp.where(keep(iota((rows, cols), 0), iota((rows, cols), 1)), 1.0, 0.0).astype(F32)


def fine_down_kernel(meta, bricks, u, f, a, recv, rc, u_b, f_r, f_b, i_r, i_b, u_r, resid, small):
    _, _, bit_x, bit_y, _ = place_of(meta, bricks)
    own = odd(32, 128)
    for t in range(16):
        here = (OWN + t, slice(0, 32), slice(0, 128))
        u_b[here] = pair_of(u, t, False, own)
        f_r[here], f_b[here] = pair_of(f, t, True, own), pair_of(f, t, False, own)
        i_r[here], i_b[here] = 1.0 / (pair_of(a, t, True, own) + 6.0), 1.0 / (pair_of(a, t, False, own) + 6.0)
    unpack_shell(recv, (u_b, f_r, f_b, i_r, i_b), bit_x, bit_y)
    zero = jnp.zeros((40, 256), F32)
    for k in (0, 25):
        u_r[k] = zero
        u_b[k] = zero
    for k in (1, 24):
        f_b[k] = zero
        i_b[k] = zero
    row = iota((40, 256), 0)
    y0 = is_zero(bit_y, (40, 256))
    y1 = jnp.logical_not(y0)
    mask = odd(40, 256)
    cut = (y0 & (row == 0), y1 & (row == 31))
    half_sweep(u_r, u_b, f_r, i_r, 1, 25, True, mask, 1.0, 0, cut)
    half_sweep(u_b, u_r, f_b, i_b, 1, 25, False, mask, 1.0, 0)
    half_sweep(u_r, u_b, f_r, i_r, 2, 24, True, mask, 1.0, 0)
    half_sweep(u_b, u_r, f_b, i_b, 3, 23, False, mask, 1.0, 0)
    for t in range(16):
        total = around(u_b, OWN + t, True, mask, 0)[0:32, 0:128]
        diag = pair_of(a, t, True, own) + 6.0
        here = (OWN + t, slice(0, 32), slice(0, 128))
        resid[t] = f_r[here] + total - diag * u_r[here]
    pack_coarse(resid, small, rc)


def slot_of(member, me):
    return jnp.where((member >> 2) == (me >> 2), 0, 4) + ((me - member) & 3)


def faces_kernel(meta, bricks, *refs):
    boxes, (out, held) = refs[:8], refs[8:]
    slab, me = meta[0], meta[1]
    for i, box in enumerate(boxes):
        held[i] = box[...]
    start = jnp.where(me < 4, 3, 0)
    for i in range(4):
        member = jnp.where(me < 4, bricks[slab, 4 + i], bricks[slab, i])
        out[i] = held[slot_of(member, me), pl.ds(start, 5)]


def sort_sides(me, one, two, low, high):
    @pl.when(me < 4)
    def _():
        low[...] = one[...]
        high[...] = two[...]

    @pl.when(me >= 4)
    def _():
        low[...] = two[...]
        high[...] = one[...]


def assemble(meta, bricks, boxes, one, two, red, black, held, low, high):
    slab, me = meta[0], meta[1]
    for i, box in enumerate(boxes):
        held[i] = box[...]
    sort_sides(me, one, two, low, high)
    left = iota((16, 128), 1) < 64

    def put(k, by, west, east):
        rows = slice(16 * by, 16 * by + 16)
        red[k, rows] = jnp.where(left, west, pltpu.roll(east, 64, 1))
        black[k, rows] = jnp.where(left, pltpu.roll(west, 64, 1), east)

    for by in range(2):
        for bz in range(2):
            west = slot_of(bricks[slab, 2 * by + 4 * bz], me)
            east = slot_of(bricks[slab, 2 * by + 4 * bz + 1], me)
            for j in range(8):
                put(6 + 8 * bz + j, by, held[west, j], held[east, j])
        for j in range(5):
            put(1 + j, by, low[2 * by, j], low[2 * by + 1, j])
            put(22 + j, by, high[2 * by, j], high[2 * by + 1, j])


def to_bottom(planes, small, half):
    for n in range(22):
        small[16 * n : 16 * n + 16] = planes[n, pl.ds(0, 16, stride=2), :] + planes[n, pl.ds(1, 16, stride=2), :]
    fold = pick(128, 128, lambda r, c: (r >> 1) == c - 64 * half) * 0.125
    return jnp.dot(small[...], fold, precision=EXACT, preferred_element_type=F32).reshape(22, 16, 128)


def coarse_coef_kernel(meta, bricks, *refs):
    boxes, (one, two) = refs[:8], refs[8:10]
    a_r, i_r, i_b, ab = refs[10:14]
    held, low, high, a_b, planes, small = refs[14:]
    slab = meta[0]
    assemble(meta, bricks, boxes, one, two, a_r, a_b, held, low, high)
    for k in range(1, 27):
        keep = jnp.full((32, 128), 0, jnp.int32) == 0
        if k < 6:
            keep = jnp.logical_not(is_zero(slab, (32, 128)))
        if k >= 22:
            keep = jnp.logical_not(is_zero(slab - (SLABS - 1), (32, 128)))
        i_r[k] = jnp.where(keep, 1.0 / (a_r[k] + 1.5), 0.0)
        i_b[k] = jnp.where(keep, 1.0 / (a_b[k] + 1.5), 0.0)
    for n in range(22):
        planes[n] = a_r[3 + n] + a_b[3 + n]
    ab[...] = to_bottom(planes, small, 1)


def coarse_down_kernel(meta, bricks, *refs):
    boxes, (one, two, weights, a_r, i_r, i_b, ab) = refs[:8], refs[8:15]
    rb, rb_send, part, e_b, r_r, r_b = refs[15:21]
    held, low, high, e_r, resid, small = refs[21:]
    me = meta[1]
    assemble(meta, bricks, boxes, one, two, r_r, r_b, held, low, high)
    for k in (0, 27):
        e_r[k] = jnp.zeros((32, 128), F32)
        e_b[k] = jnp.zeros((32, 128), F32)
    for k in range(1, 27):
        e_r[k] = r_r[k] * i_r[k]
    mask = odd(32, 128)
    half_sweep(e_b, e_r, r_b, i_b, 1, 27, False, mask, 0.25, 2)
    half_sweep(e_r, e_b, r_r, i_r, 1, 27, True, mask, 0.25, 2)
    half_sweep(e_b, e_r, r_b, i_b, 1, 27, False, mask, 0.25, 2)
    for n in range(22):
        k = n + 3
        total = 0.25 * around(e_b, k, True, mask, 2)
        resid[n] = r_r[k] + total - (a_r[k] + 1.5) * e_r[k]
    rb[...] = to_bottom(resid, small, 0) + ab[...]
    rb_send[0:18] = rb[pl.ds(jnp.where(me < 4, 1, 3), 18)]
    total = jnp.zeros((16, 128), F32)
    for i in range(16):
        total = total + rb[3 + i] * weights[i]
    total = total[0:8] + total[8:16]
    part[...] = total
    rb_send[18, 0:8] = total
    rb_send[18, 8:16] = total


def bottom_kernel(meta, rb, one, two, es, e_r, e_b, g_r, g_b, i_r, i_b, low, high):
    slab, me = meta[0], meta[1]
    sort_sides(me, one, two, low, high)
    mask = odd(16, 128)
    left = iota((16, 128), 1) < 64
    zero = jnp.zeros((16, 128), F32)
    for k in (0, 27):
        e_r[k] = zero
        e_b[k] = zero
    for j in range(26):
        planes = []
        for n in (2 * j, 2 * j + 1):
            planes.append(low[n] if n < 18 else rb[n - 15] if n < 34 else high[n - 34])
        keep = left
        if j < 9:
            keep = left & jnp.logical_not(is_zero(slab, (16, 128)))
        if j >= 17:
            keep = left & jnp.logical_not(is_zero(slab - (SLABS - 1), (16, 128)))
        for red in (True, False):
            cells = jnp.where(mask, planes[1], planes[0]) if red else jnp.where(mask, planes[0], planes[1])
            force = jnp.where(left, cells, 0.0)
            inverse = jnp.where(keep, 1.0 / (pltpu.roll(cells, 64, 1) + 0.375), 0.0)
            if red:
                g_r[1 + j], i_r[1 + j], e_r[1 + j] = force, inverse, force * inverse
            else:
                g_b[1 + j], i_b[1 + j] = force, inverse
    half_sweep(e_b, e_r, g_b, i_b, 1, 27, False, mask, 0.0625, 1)

    def sweep(n, carry):
        half_sweep(e_r, e_b, g_r, i_r, 1, 27, True, mask, 0.0625, 1)
        half_sweep(e_b, e_r, g_b, i_b, 1, 27, False, mask, 0.0625, 1)
        return carry

    lax.fori_loop(0, 7, sweep, 0)
    for i in range(22):
        k, upper = (15 + i) // 2 + 1, (15 + i) % 2
        es[i] = jnp.where(mask, e_r[k], e_b[k]) if upper else jnp.where(mask, e_b[k], e_r[k])


def weights_kernel(meta, here, there, out, t_r, t_b, w_r, w_b, i_r, i_b, low, high):
    slab, me = meta[0], meta[1]

    @pl.when(me < 4)
    def _():
        low[...] = there[1]
        high[...] = here[1]

    @pl.when(me >= 4)
    def _():
        low[...] = here[1]
        high[...] = there[1]

    lane = iota((8, 128), 1)

    def plane(boxes, z):
        rows = []
        for by in range(2):
            place, shift = 4 * (z >> 3) + 2 * by, 32 * (z & 3)
            west = pltpu.roll(boxes(place, (z & 7) >> 2), (128 - shift) % 128, 1)
            east = pltpu.roll(boxes(place + 1, (z & 7) >> 2), (160 - shift) % 128, 1)
            rows.append(jnp.where(lane < 32, west, east))
        return jnp.concatenate(rows, 0)

    parts = (lambda p, h: low[p, h], lambda p, h: here[0, p, h], lambda p, h: high[p, h])
    mask = odd(16, 128)
    left = iota((16, 128), 1) < 64
    zero = jnp.zeros((16, 128), F32)
    for k in (0, 25):
        t_r[k] = zero
        t_b[k] = zero
    for j in range(24):
        lower, upper = (plane(parts[(2 * j + i) // 16], (2 * j + i) % 16) for i in range(2))
        keep = left
        if j < 8:
            keep = left & jnp.logical_not(is_zero(slab, (16, 128)))
        if j >= 16:
            keep = left & jnp.logical_not(is_zero(slab - (SLABS - 1), (16, 128)))
        i_r[1 + j] = jnp.where(keep, 1.0 / (jnp.where(mask, upper, lower) + 0.375), 0.0)
        i_b[1 + j] = jnp.where(keep, 1.0 / (jnp.where(mask, lower, upper) + 0.375), 0.0)
    for k in range(1, 25):
        t_b[k] = i_b[k]
        w_b[k] = i_b[k]
    for k in range(1, 25):
        t = i_r[k] * (1.0 + 0.0625 * around(t_b, k, True, mask, 1))
        t_r[k] = t
        w_r[k] = t

    def sweep(n, carry):
        for k in range(1, 25):
            t = i_b[k] * (0.0625 * around(t_r, k, False, mask, 1))
            t_b[k] = t
            w_b[k] = w_b[k] + t
        for k in range(1, 25):
            t = i_r[k] * (0.0625 * around(t_b, k, True, mask, 1))
            t_r[k] = t
            w_r[k] = w_r[k] + t
        return carry

    lax.fori_loop(0, 7, sweep, 0)
    for j in range(8):
        red, black = w_r[9 + j], w_b[9 + j]
        out[2 * j] = jnp.where(mask, black, red)
        out[2 * j + 1] = jnp.where(mask, red, black)


def up_kernel(
    meta, bricks, sum_0, sum_1, sum_2, sum_3, es, ec_b, r_r, r_b, ci_r, ci_b, u1_b, f_r, f_b, i_r, i_b, out,
    e_r, e_b, small, wide, planes, tall, u_r, u_b,
):
    slab, _, bit_x, bit_y, bit_z = place_of(meta, bricks)
    total = (sum_0[...] + sum_1[...]) + (sum_2[...] + sum_3[...])
    mean = jnp.sum(total) * (1.0 / (SLABS * 16 * 16 * 64))
    base = 8 * bit_z
    no_low = jnp.where((slab == 0) & (bit_z == 0), 0, 1)
    no_high = jnp.where((slab == SLABS - 1) & (bit_z == 1), 0, 1)
    for j in range(14):
        shifted = es[base + j] - mean
        if j < 3:
            shifted = jnp.where(is_zero(no_low, (16, 128)), 0.0, shifted)
        if j >= 11:
            shifted = jnp.where(is_zero(no_high, (16, 128)), 0.0, shifted)
        small[16 * j : 16 * j + 16] = shifted
    spread = pick(128, 128, lambda r, c: r == (c >> 1))
    small[...] = select_dot(small[...], spread)
    for j in range(14):
        rows = small[16 * j : 16 * j + 16]
        wide[j, pl.ds(0, 16, stride=2), :] = rows
        wide[j, pl.ds(1, 16, stride=2), :] = rows
    for k in (0, 15):
        e_r[k] = jnp.zeros((32, 128), F32)
        e_b[k] = jnp.zeros((32, 128), F32)
    for j in range(14):
        e_b[1 + j] = ec_b[base + 3 + j] + wide[j]
    coarse = odd(32, 128)
    r_r, r_b, ci_r, ci_b = (grid.at[pl.ds(base + 2, 16)] for grid in (r_r, r_b, ci_r, ci_b))
    half_sweep(e_r, e_b, r_r, ci_r, 1, 15, True, coarse, 0.25, 2)
    half_sweep(e_b, e_r, r_b, ci_b, 2, 14, False, coarse, 0.25, 2)
    half_sweep(e_r, e_b, r_r, ci_r, 2, 14, True, coarse, 0.25, 2)
    half_sweep(e_b, e_r, r_b, ci_b, 3, 13, False, coarse, 0.25, 2)
    for n in range(20):
        k, upper = n // 2 + 3, n % 2
        red, black = e_r[k], e_b[k]
        planes[32 * n : 32 * n + 32] = jnp.where(coarse, red, black) if upper else jnp.where(coarse, black, red)

    lane = iota((128, 256), 1)
    x0 = is_zero(bit_x, (128, 256))
    start = jnp.where(lane < 128, 64 * bit_x + (lane >> 1), (lane >> 1) + jnp.where(x0, 0, -64))
    usable = (lane < 128) | (x0 & (lane < 136)) | (jnp.logical_not(x0) & (lane >= 248))
    spread = jnp.where(usable & (iota((128, 256), 0) == start), 1.0, 0.0).astype(F32)
    tall_rows = select_dot(planes[...], spread)
    for n in range(20):
        rows = tall_rows[32 * n : 32 * n + 32]
        for h in range(2):
            tall[n, h, pl.ds(0, 32, stride=2), :] = rows[:, 128 * h : 128 * h + 128]
            tall[n, h, pl.ds(1, 32, stride=2), :] = rows[:, 128 * h : 128 * h + 128]
    for k in (0, 21):
        u_r[k] = jnp.zeros((40, 256), F32)
        u_b[k] = jnp.zeros((40, 256), F32)
    row = iota((8, 128), 0)
    y0 = is_zero(bit_y)
    in_y = (y0 & (row != 7)) | (jnp.logical_not(y0) & (row != 0))
    own_start = pl.multiple_of(32 * bit_y, 32)
    side_start = pl.multiple_of(32 - 8 * bit_y, 8)
    for n in range(20):
        for h in range(2):
            lanes = slice(128 * h, 128 * h + 128)
            side = jnp.where(in_y, tall[n, h, pl.ds(side_start, 8), :], 0.0)
            u_b[1 + n, 0:32, lanes] = u1_b[3 + n, 0:32, lanes] + tall[n, h, pl.ds(own_start, 32), :]
            u_b[1 + n, 32:40, lanes] = u1_b[3 + n, 32:40, lanes] + side
    mask = odd(40, 256)
    f_r, f_b, i_r, i_b = (grid.at[2:24] for grid in (f_r, f_b, i_r, i_b))
    half_sweep(u_r, u_b, f_r, i_r, 1, 21, True, mask, 1.0, 0)
    half_sweep(u_b, u_r, f_b, i_b, 2, 20, False, mask, 1.0, 0)
    half_sweep(u_r, u_b, f_r, i_r, 2, 20, True, mask, 1.0, 0)
    half_sweep(u_b, u_r, f_b, i_b, 3, 19, False, mask, 1.0, 0)
    own = odd(32, 128)
    for t in range(16):
        red, black = u_r[3 + t, 0:32, 0:128], u_b[3 + t, 0:32, 0:128]
        out[0, 2 * t] = jnp.where(own, black, red)
        out[0, 2 * t + 1] = jnp.where(own, red, black)


def swap_cores(x):
    return lax.ppermute(x, "level", [(0, 1), (1, 0)])


def to_slabs(x, up_first, wrap=False):
    pairs = []
    for s in range(SLABS if wrap else SLABS - 1):
        for m in range(8):
            low, high = s * 8 + m, (s + 1) % SLABS * 8 + m
            pairs.append((low, high) if (m < 4) == up_first else (high, low))
    return lax.ppermute(x, ALL, pairs)


def around_chips(x):
    return [x] + [lax.ppermute(x, "bottom", [(i, (i + d) % 4) for i in range(4)]) for d in range(1, 4)]


def both_cores(boxes):
    return boxes + [swap_cores(box) for box in boxes]


def fours_apart(x):
    beside = [(8 * s + m, 8 * ((s + (4 if m < 4 else 12)) % SLABS) + m) for s in range(SLABS) for m in range(8)]
    across = [(s, (s + 8) % SLABS) for s in range(SLABS)]
    return lax.ppermute(x, ALL, beside), lax.ppermute(x, "slab", across)


def among(x):
    return lax.all_to_all(x, LB, split_axis=0, concat_axis=0, tiled=True)


def body(u_init, source, coeffs, brick_map):
    meta = jnp.stack([lax.axis_index("slab"), lax.axis_index(LB)]).astype(jnp.int32)
    smem = [meta, brick_map]
    fine = (26, 40, 256)
    packed, ac = run(
        first_kernel, [(8, SENT, 8, 128), (8, 16, 128)], smem, [u_init, source, coeffs],
        [(8, 32, 128), (16, 32, 128), (256, 128), (1, 32, 32, 128)],
    )
    got = among(packed)
    leaving = run(cross_kernel, [(4, FACE + 4, 8, 128)], smem, [got])
    leaving, ac = lax.optimization_barrier((leaving, ac))
    cross = to_slabs(leaving, False)
    ac_boxes = around_chips(ac)
    sent, coef = run(
        mid_kernel, [(8, GOT, 8, 128), (2, 8, 2, 8, 128)], smem, [got, cross], [(12, FACE, 8, 128)],
    )
    coef_other = swap_cores(coef)
    sent, *ac_boxes = lax.optimization_barrier((sent, *ac_boxes))
    halo = among(sent)
    faces = (4, 5, 16, 128)
    coarse = (28, 32, 128)
    held = [(8, 8, 16, 128), faces, faces]
    ac_boxes = both_cores(ac_boxes)
    ac_cross = to_slabs(run(faces_kernel, [faces], smem, ac_boxes, held[:1]), True)
    ac_other = swap_cores(ac_cross)
    halo, ac_cross, ac_other, coef_other = lax.optimization_barrier((halo, ac_cross, ac_other, coef_other))
    rc, u_b, f_r, f_b, i_r, i_b = run(
        fine_down_kernel, [(8, 16, 128)] + [fine] * 5, smem, [u_init, source, coeffs, halo],
        [fine, (16, 32, 128), (256, 128)],
    )
    boxes = both_cores(around_chips(rc))
    leaving = run(faces_kernel, [faces], smem, boxes, held[:1])
    leaving, ac_cross, ac_other, coef = lax.optimization_barrier((leaving, ac_cross, ac_other, coef))
    cross = to_slabs(leaving, True)
    weights = run(
        weights_kernel, [(16, 16, 128)], [meta], [coef, coef_other],
        [(26, 16, 128)] * 6 + [(8, 2, 8, 128)] * 2,
    )
    ca_r, ci_r, ci_b, ab = run(
        coarse_coef_kernel, [coarse] * 3 + [(22, 16, 128)], smem, ac_boxes + [ac_cross, ac_other],
        held + [coarse, (22, 32, 128), (352, 128)],
    )
    cross, weights, ca_r, ci_r, ci_b, ab = lax.optimization_barrier((cross, weights, ca_r, ci_r, ci_b, ab))
    rb, rb_send, part, ec_b, r_r, r_b = run(
        coarse_down_kernel, [(22, 16, 128), (19, 16, 128), (8, 128)] + [coarse] * 3, smem,
        boxes + [cross, swap_cores(cross), weights, ca_r, ci_r, ci_b, ab],
        held + [coarse, (22, 32, 128), (352, 128)],
    )
    cross = to_slabs(rb_send, True, wrap=True)
    far = lax.ppermute(part, "slab", [(s, (s - 2) % SLABS) for s in range(SLABS)])
    cross, far = lax.optimization_barrier((cross, far))
    other = swap_cores(cross)
    part = (part + far) + (cross[18, 0:8] + other[18, 0:8])
    near, far = fours_apart(part)
    sums = [part, near, far, swap_cores(near)]
    bottom = (28, 16, 128)
    es = run(
        bottom_kernel, [(22, 16, 128)], [meta], [rb, cross, other],
        [bottom] * 6 + [(19, 16, 128)] * 2,
    )
    return run(
        up_kernel, [(1, 32, 32, 128)], smem,
        sums + [es, ec_b, r_r, r_b, ci_r, ci_b, u_b, f_r, f_b, i_r, i_b],
        [(16, 32, 128)] * 2 + [(224, 128), (14, 32, 128), (640, 128), (20, 2, 64, 128), (22, 40, 256), (22, 40, 256)],
    )


def solution(mesh):
    placed = P(ALL, None, None, None)
    return jax.shard_map(
        body, mesh=mesh, in_specs=(placed, placed, placed, P()), out_specs=placed, check_vma=False
    )
```

```python
import jax
import jax.numpy as jnp
from jax import lax
from jax.experimental import pallas as pl
from jax.experimental.pallas import tpu as pltpu
from jax.sharding import PartitionSpec as P

LB = ("level", "bottom")
ALL = ("slab", "level", "bottom")
SLABS = 16
OWN = 5
F32 = jnp.float32
VMEM_SPEC = pl.BlockSpec(memory_space=pltpu.VMEM)
SMEM_SPEC = pl.BlockSpec(memory_space=pltpu.SMEM)
EXACT = lax.Precision.HIGHEST


def run(kernel, outs, smem, vmem, scratch=()):
    shapes = [jax.ShapeDtypeStruct(s, F32) for s in outs]
    single = len(shapes) == 1
    return pl.pallas_call(
        kernel,
        out_shape=shapes[0] if single else shapes,
        in_specs=[SMEM_SPEC] * len(smem) + [VMEM_SPEC] * len(vmem),
        out_specs=VMEM_SPEC if single else [VMEM_SPEC] * len(shapes),
        scratch_shapes=[pltpu.VMEM(s, F32) for s in scratch],
        compiler_params=pltpu.CompilerParams(vmem_limit_bytes=20 << 20),
    )(*smem, *vmem)


def iota(shape, dim):
    return lax.broadcasted_iota(jnp.int32, shape, dim)


def odd(rows, cols):
    return ((iota((rows, cols), 0) + iota((rows, cols), 1)) & 1) == 1


def place_of(meta, bricks):
    slab, me = meta[0], meta[1]
    place = jnp.int32(0)
    for i in range(8):
        place = place + jnp.where(bricks[slab, i] == me, i, 0)
    return slab, me, place & 1, (place >> 1) & 1, place >> 2


def is_zero(scalar, shape=(8, 128)):
    return jnp.full(shape, scalar, jnp.int32) == 0


ARRAYS = 5
FACE = 17
SENT_Y, SENT_X, SENT = 17, 27, 30
GOT_ROWS, GOT_STRIPS, GOT_Y, GOT_X, GOT = 17, 20, 22, 32, 35


def face_planes(j):
    return [(1 + j, 0), (1 + j, 1), (1 + j, 2), (0, j)]


def merge_strips(placed, base=None):
    group = iota((8, 128), 1) // 8
    total = jnp.zeros((8, 128), F32) if base is None else base
    for pos, strip in placed:
        moved = pltpu.roll(strip, 8 * pos, 1) if pos else strip
        total = jnp.where(group == pos, moved, total)
    return total


def swap_lanes(cells):
    lane = iota(cells.shape, 1)
    return jnp.where((lane & 1) == 0, pltpu.roll(cells, cells.shape[1] - 1, 1), pltpu.roll(cells, 1, 1))


def pack_shell(get, out, bit_x, bit_y):
    x0, y0 = is_zero(bit_x), is_zero(bit_y)
    mask = odd(32, 128)
    for k in range(8):
        high, j = k >= 4, k % 4
        for i, (c, far) in enumerate(face_planes(j)):
            out[k, 4 * i : 4 * i + 4] = get(c, 15 - far if high else far).reshape(4, 8, 128)
        t = 12 if high else 3
        one, two = get(1, t), swap_lanes(get(3, t))
        both = jnp.where(mask, one, two) if high else jnp.where(mask, two, one)
        out[k, 16] = both[8 * j : 8 * j + 8]
        strips = []
        for tl in range(2):
            for c in range(ARRAYS):
                v = get(c, 2 * k + tl)
                out[k, SENT_Y + tl * ARRAYS + c] = jnp.where(y0, v[24:32], v[0:8])
                for g in range(4):
                    tile = v[8 * g : 8 * g + 8]
                    strips.append(jnp.where(x0, pltpu.roll(tile, 8, 1), tile))
        for i in range(3):
            out[k, SENT_X + i] = merge_strips(list(enumerate(strips[16 * i : 16 * i + 16])))


def cross_kernel(meta, bricks, recv, out):
    slab, me = meta[0], meta[1]
    for i in range(4):
        src = jnp.where(me >= 4, bricks[slab, 4 + i], bricks[slab, i])
        out[i] = recv[src, 0:FACE]


def mid_kernel(meta, bricks, recv, cross, out, faces):
    slab, me = meta[0], meta[1]
    faces[0:8] = recv[:, 0:FACE]
    faces[8:12] = cross[...]
    row = iota((8, 128), 0)
    for p in range(8):
        bx, by, bz = p & 1, (p >> 1) & 1, p >> 2
        dest = bricks[slab, p]
        same = me >= 4 if bz else me < 4

        def src(q):
            return jnp.where(same, bricks[slab, (q & 3) + 4 * (1 - bz)], 8 + (q & 3))

        def strip_of(tile):
            return pltpu.roll(tile, 8, 1) if bx else tile

        def rows_of(at):
            one, two, three, last = (faces[at, 4 * i + (3 if by else 0)] for i in range(4))
            if by:
                shared = jnp.where(row >= 3, two, pltpu.roll(three, 3, 0))
            else:
                shared = jnp.where(row < 5, two, pltpu.roll(three, 5, 0))
            return [one, shared, last]

        at_own, at_y, at_x, at_xy = src(p), src(p ^ 2), src(p ^ 1), src(p ^ 3)
        out[dest, 0:FACE] = faces[at_own]
        for i, tile in enumerate(rows_of(at_y)):
            out[dest, GOT_ROWS + i] = tile
        strips = [strip_of(faces[at_x, i]) for i in range(16)] + [strip_of(tile) for tile in rows_of(at_xy)]
        from_y, from_x, from_xy = bricks[slab, p ^ 2], bricks[slab, p ^ 1], bricks[slab, p ^ 3]
        strips += [strip_of(recv[from_xy, SENT_Y + i]) for i in range(2 * ARRAYS)]
        for i in range(2):
            out[dest, GOT_STRIPS + i] = merge_strips(list(enumerate(strips[16 * i : 16 * i + 16])))
        out[dest, GOT_Y:GOT_X] = recv[from_y, SENT_Y:SENT_X]
        out[dest, GOT_X:GOT] = recv[from_x, SENT_X:SENT]


def unpack_shell(recv, grids, bit_x, bit_y):
    row, lane = iota((8, 128), 0), iota((8, 128), 1)
    x0, y0 = is_zero(bit_x), is_zero(bit_y)
    in_x = (x0 & (lane < 8)) | (jnp.logical_not(x0) & (lane >= 120))
    five = (y0 & (row < 5)) | (jnp.logical_not(y0) & (row >= 3))
    three = (y0 & (row < 3)) | (jnp.logical_not(y0) & (row >= 5))
    seven = (y0 & (row != 7)) | (jnp.logical_not(y0) & (row != 0))
    mask = odd(8, 128)

    def cut(c, tile):
        return jnp.where(seven, tile, 0.0) if c >= 3 else tile

    def strip(tile, pos):
        shift = (jnp.where(bit_x == 0, 0, 120) + 128 - 8 * pos) % 128
        return jnp.where(in_x, pltpu.roll(tile, shift, 1), 0.0)

    def rows_of(tiles):
        one, shared, last = tiles
        moved = jnp.where(y0, pltpu.roll(shared, 3, 0), pltpu.roll(shared, 5, 0))
        return [one, jnp.where(five, shared, 0.0), jnp.where(three, moved, 0.0), last]

    for k in range(8):
        high, j = k >= 4, k % 4
        rows = rows_of([recv[k, GOT_ROWS + i] for i in range(3)])
        sides = rows_of([strip(recv[k, GOT_STRIPS + 1], i) for i in range(3)])
        for i, (c, far) in enumerate(face_planes(j)):
            at = OWN - 1 - far if high else OWN + 16 + far
            for g in range(4):
                grids[c][at, 8 * g : 8 * g + 8, 0:128] = recv[k, 4 * i + g]
                grids[c][at, 8 * g : 8 * g + 8, 128:256] = strip(recv[k, GOT_STRIPS], 4 * i + g)
            grids[c][at, 32:40, 0:128] = cut(c, rows[i])
            grids[c][at, 32:40, 128:256] = cut(c, sides[i])
        at = 1 if high else 24
        both = recv[k, 16]
        other = swap_lanes(both)
        other = jnp.where(mask, other, 0.0) if high else jnp.where(mask, 0.0, other)
        for c, cells in ((1, both), (3, other)):
            grids[c][at, 8 * j : 8 * j + 8, 0:128] = cells
            grids[c][at, 8 * j : 8 * j + 8, 128:256] = jnp.zeros((8, 128), F32)
            grids[c][at, 32:40] = jnp.zeros((8, 256), F32)
        for tl in range(2):
            for c in range(ARRAYS):
                i = tl * ARRAYS + c
                at = OWN + 2 * k + tl
                grids[c][at, 32:40, 0:128] = cut(c, recv[k, GOT_Y + i])
                grids[c][at, 32:40, 128:256] = cut(c, strip(recv[k, GOT_STRIPS + 1], 3 + i))
                for g in range(4):
                    n = 4 * i + g
                    side = strip(recv[k, GOT_X + n // 16], n % 16)
                    grids[c][at, 8 * g : 8 * g + 8, 128:256] = side


def pair_of(cells, t, red, mask):
    low, high = cells[0, 2 * t], cells[0, 2 * t + 1]
    return jnp.where(mask, high, low) if red else jnp.where(mask, low, high)


def pack_bottom_coef(a, ac, small):
    for i in range(8):
        planes = (a[0, 4 * i] + a[0, 4 * i + 1]) + (a[0, 4 * i + 2] + a[0, 4 * i + 3])
        small[i] = planes
    rows = []
    for i in range(8):
        first = small[i, pl.ds(0, 8, stride=4), :] + small[i, pl.ds(1, 8, stride=4), :]
        rows.append(first + (small[i, pl.ds(2, 8, stride=4), :] + small[i, pl.ds(3, 8, stride=4), :]))
    fold = pick(128, 128, lambda r, c: (r >> 2) == (c & 31)) * (1.0 / 64)
    cells = jnp.dot(jnp.concatenate(rows, 0), fold, precision=EXACT, preferred_element_type=F32)
    group = iota((8, 128), 1) >> 5
    for h in range(2):
        tile = cells[32 * h : 32 * h + 8]
        for j in range(1, 4):
            tile = jnp.where(group == j, cells[32 * h + 8 * j : 32 * h + 8 * j + 8], tile)
        ac[8, 8 * h : 8 * h + 8] = tile


def pack_coarse(planes, small, out):
    twice = pick(128, 128, lambda r, c: (r >> 1) == (c & 63)) * 0.125
    row, lane = iota((16, 128), 0), iota((16, 128), 1)
    even = ((row + lane + (lane >> 6)) & 1) == 0
    for t in range(16):
        small[16 * t : 16 * t + 16] = planes[t, pl.ds(0, 16, stride=2), :] + planes[t, pl.ds(1, 16, stride=2), :]
    summed = jnp.dot(small[...], twice, precision=EXACT, preferred_element_type=F32)
    summed = summed.reshape(16, 16, 128)
    for j in range(8):
        out[j] = jnp.where(even, summed[2 * j], summed[2 * j + 1])


def first_kernel(meta, bricks, u, f, a, out, ac, small, planes, rows, inverse):
    _, _, bit_x, bit_y, _ = place_of(meta, bricks)
    mask = odd(32, 128)
    inverse[...] = 1.0 / (a[...] + 6.0)
    sources = ((u, False), (f, True), (f, False), (inverse, True), (inverse, False))

    def get(c, t):
        return pair_of(sources[c][0], t, sources[c][1], mask)

    pack_shell(get, out, bit_x, bit_y)
    pack_bottom_coef(a, ac, small)
    for t in range(16):
        planes[t] = a[0, 2 * t] + a[0, 2 * t + 1]
    pack_coarse(planes, rows, ac)


def around(src, k, red, mask, edges, cut=None):
    here = src[k]
    rows, cols = here.shape
    above, below = src[k + 1], src[k - 1]
    other = jnp.where(mask, above, below) if red else jnp.where(mask, below, above)
    up, down = pltpu.roll(here, 1, 0), pltpu.roll(here, rows - 1, 0)
    left, right = pltpu.roll(here, 1, 1), pltpu.roll(here, cols - 1, 1)
    if edges:
        row, lane = iota((rows, cols), 0), iota((rows, cols), 1)
        up, down = jnp.where(row == 0, 0.0, up), jnp.where(row == rows - 1, 0.0, down)
        if edges == 2:
            left, right = jnp.where(lane == 0, 0.0, left), jnp.where(lane == cols - 1, 0.0, right)
    if cut is not None:
        up, down = jnp.where(cut[0], 0.0, up), jnp.where(cut[1], 0.0, down)
    return ((here + other) + (up + down)) + (left + right)


def half_sweep(dst, src, force, inverse, lo, hi, red, mask, scale, edges, cut=None):
    def step(k, carry):
        total = around(src, k, red, mask, edges, cut)
        if scale != 1.0:
            total = scale * total
        dst[k] = (force[k] + total) * inverse[k]
        return carry

    lax.fori_loop(lo, hi, step, 0, unroll=True)


def select_dot(cells, chosen):
    half, total = chosen.astype(jnp.bfloat16), None
    for _ in range(3):
        part = cells.astype(jnp.bfloat16)
        cells = cells - part.astype(F32)
        moved = jnp.dot(part, half, preferred_element_type=F32)
        total = moved if total is None else total + moved
    return total


def pick(rows, cols, keep):
    return jnp.where(keep(iota((rows, cols), 0), iota((rows, cols), 1)), 1.0, 0.0).astype(F32)


def fine_down_kernel(meta, bricks, u, f, a, recv, rc, u_b, f_r, f_b, i_r, i_b, u_r, resid, small):
    _, _, bit_x, bit_y, _ = place_of(meta, bricks)
    own = odd(32, 128)
    for t in range(16):
        here = (OWN + t, slice(0, 32), slice(0, 128))
        u_b[here] = pair_of(u, t, False, own)
        f_r[here], f_b[here] = pair_of(f, t, True, own), pair_of(f, t, False, own)
        i_r[here], i_b[here] = 1.0 / (pair_of(a, t, True, own) + 6.0), 1.0 / (pair_of(a, t, False, own) + 6.0)
    unpack_shell(recv, (u_b, f_r, f_b, i_r, i_b), bit_x, bit_y)
    zero = jnp.zeros((40, 256), F32)
    for k in (0, 25):
        u_r[k] = zero
        u_b[k] = zero
    for k in (1, 24):
        f_b[k] = zero
        i_b[k] = zero
    row = iota((40, 256), 0)
    y0 = is_zero(bit_y, (40, 256))
    y1 = jnp.logical_not(y0)
    mask = odd(40, 256)
    cut = (y0 & (row == 0), y1 & (row == 31))
    half_sweep(u_r, u_b, f_r, i_r, 1, 25, True, mask, 1.0, 0, cut)
    half_sweep(u_b, u_r, f_b, i_b, 1, 25, False, mask, 1.0, 0)
    half_sweep(u_r, u_b, f_r, i_r, 2, 24, True, mask, 1.0, 0)
    half_sweep(u_b, u_r, f_b, i_b, 3, 23, False, mask, 1.0, 0)
    for t in range(16):
        total = around(u_b, OWN + t, True, mask, 0)[0:32, 0:128]
        diag = pair_of(a, t, True, own) + 6.0
        here = (OWN + t, slice(0, 32), slice(0, 128))
        resid[t] = f_r[here] + total - diag * u_r[here]
    pack_coarse(resid, small, rc)


def slot_of(member, me):
    return jnp.where((member >> 2) == (me >> 2), 0, 4) + ((me - member) & 3)


def faces_kernel(meta, bricks, *refs):
    boxes, (out, held) = refs[:8], refs[8:]
    slab, me = meta[0], meta[1]
    for i, box in enumerate(boxes):
        held[i] = box[...]
    start = jnp.where(me < 4, 3, 0)
    for i in range(4):
        member = jnp.where(me < 4, bricks[slab, 4 + i], bricks[slab, i])
        out[i, 0:5] = held[slot_of(member, me), pl.ds(start, 5)]
        for j in range(5, out.shape[1]):
            out[i, j] = held[slot_of(bricks[slab, 2 * i + j - 5], me), 8]


def sort_sides(me, one, two, low, high):
    @pl.when(me < 4)
    def _():
        low[...] = one[...]
        high[...] = two[...]

    @pl.when(me >= 4)
    def _():
        low[...] = two[...]
        high[...] = one[...]


def assemble(meta, bricks, boxes, one, two, red, black, held, low, high):
    slab, me = meta[0], meta[1]
    for i, box in enumerate(boxes):
        held[i] = box[...]
    sort_sides(me, one, two, low, high)
    left = iota((16, 128), 1) < 64

    def put(k, by, west, east):
        rows = slice(16 * by, 16 * by + 16)
        red[k, rows] = jnp.where(left, west, pltpu.roll(east, 64, 1))
        black[k, rows] = jnp.where(left, pltpu.roll(west, 64, 1), east)

    for by in range(2):
        for bz in range(2):
            west = slot_of(bricks[slab, 2 * by + 4 * bz], me)
            east = slot_of(bricks[slab, 2 * by + 4 * bz + 1], me)
            for j in range(8):
                put(6 + 8 * bz + j, by, held[west, j], held[east, j])
        for j in range(5):
            put(1 + j, by, low[2 * by, j], low[2 * by + 1, j])
            put(22 + j, by, high[2 * by, j], high[2 * by + 1, j])


def to_bottom(planes, small, half):
    for n in range(22):
        small[16 * n : 16 * n + 16] = planes[n, pl.ds(0, 16, stride=2), :] + planes[n, pl.ds(1, 16, stride=2), :]
    fold = pick(128, 128, lambda r, c: (r >> 1) == c - 64 * half) * 0.125
    return jnp.dot(small[...], fold, precision=EXACT, preferred_element_type=F32).reshape(22, 16, 128)


def coarse_coef_kernel(meta, bricks, *refs):
    boxes, (one, two) = refs[:8], refs[8:10]
    a_r, i_r, i_b, ab, coef = refs[10:15]
    held, low, high, a_b, planes, small = refs[15:]
    slab, me = meta[0], meta[1]
    assemble(meta, bricks, boxes, one, two, a_r, a_b, held, low, high)
    for p in range(8):
        coef[0, p] = low[p >> 1, 5 + (p & 1)]
        coef[1, p] = held[slot_of(bricks[slab, p], me), 8]
        coef[2, p] = high[p >> 1, 5 + (p & 1)]
    for k in range(1, 27):
        keep = jnp.full((32, 128), 0, jnp.int32) == 0
        if k < 6:
            keep = jnp.logical_not(is_zero(slab, (32, 128)))
        if k >= 22:
            keep = jnp.logical_not(is_zero(slab - (SLABS - 1), (32, 128)))
        i_r[k] = jnp.where(keep, 1.0 / (a_r[k] + 1.5), 0.0)
        i_b[k] = jnp.where(keep, 1.0 / (a_b[k] + 1.5), 0.0)
    for n in range(22):
        planes[n] = a_r[3 + n] + a_b[3 + n]
    ab[...] = to_bottom(planes, small, 1)


def coarse_down_kernel(meta, bricks, *refs):
    boxes, (one, two, weights, a_r, i_r, i_b, ab) = refs[:8], refs[8:15]
    rb, rb_send, part, e_b, r_r, r_b = refs[15:21]
    held, low, high, e_r, resid, small = refs[21:]
    me = meta[1]
    assemble(meta, bricks, boxes, one, two, r_r, r_b, held, low, high)
    for k in (0, 27):
        e_r[k] = jnp.zeros((32, 128), F32)
        e_b[k] = jnp.zeros((32, 128), F32)
    for k in range(1, 27):
        e_r[k] = r_r[k] * i_r[k]
    mask = odd(32, 128)
    half_sweep(e_b, e_r, r_b, i_b, 1, 27, False, mask, 0.25, 2)
    half_sweep(e_r, e_b, r_r, i_r, 1, 27, True, mask, 0.25, 2)
    half_sweep(e_b, e_r, r_b, i_b, 1, 27, False, mask, 0.25, 2)
    for n in range(22):
        k = n + 3
        total = 0.25 * around(e_b, k, True, mask, 2)
        resid[n] = r_r[k] + total - (a_r[k] + 1.5) * e_r[k]
    rb[...] = to_bottom(resid, small, 0) + ab[...]
    rb_send[0:18] = rb[pl.ds(jnp.where(me < 4, 1, 3), 18)]
    total = jnp.zeros((16, 128), F32)
    for i in range(16):
        total = total + rb[3 + i] * weights[i]
    total = total[0:8] + total[8:16]
    part[...] = total
    rb_send[18, 0:8] = total
    rb_send[18, 8:16] = total


def bottom_kernel(meta, rb, one, two, es, e_r, e_b, g_r, g_b, i_r, i_b, low, high):
    slab, me = meta[0], meta[1]
    sort_sides(me, one, two, low, high)
    mask = odd(16, 128)
    left = iota((16, 128), 1) < 64
    zero = jnp.zeros((16, 128), F32)
    for k in (0, 27):
        e_r[k] = zero
        e_b[k] = zero
    for j in range(26):
        planes = []
        for n in (2 * j, 2 * j + 1):
            planes.append(low[n] if n < 18 else rb[n - 15] if n < 34 else high[n - 34])
        keep = left
        if j < 9:
            keep = left & jnp.logical_not(is_zero(slab, (16, 128)))
        if j >= 17:
            keep = left & jnp.logical_not(is_zero(slab - (SLABS - 1), (16, 128)))
        for red in (True, False):
            cells = jnp.where(mask, planes[1], planes[0]) if red else jnp.where(mask, planes[0], planes[1])
            force = jnp.where(left, cells, 0.0)
            inverse = jnp.where(keep, 1.0 / (pltpu.roll(cells, 64, 1) + 0.375), 0.0)
            if red:
                g_r[1 + j], i_r[1 + j], e_r[1 + j] = force, inverse, force * inverse
            else:
                g_b[1 + j], i_b[1 + j] = force, inverse
    half_sweep(e_b, e_r, g_b, i_b, 1, 27, False, mask, 0.0625, 1)

    def sweep(n, carry):
        half_sweep(e_r, e_b, g_r, i_r, 1, 27, True, mask, 0.0625, 1)
        half_sweep(e_b, e_r, g_b, i_b, 1, 27, False, mask, 0.0625, 1)
        return carry

    lax.fori_loop(0, 7, sweep, 0)
    for i in range(22):
        k, upper = (15 + i) // 2 + 1, (15 + i) % 2
        es[i] = jnp.where(mask, e_r[k], e_b[k]) if upper else jnp.where(mask, e_b[k], e_r[k])


def weights_kernel(meta, coef, out, t_r, t_b, w_r, w_b, i_r, i_b):
    slab = meta[0]
    lane = iota((8, 128), 1)

    def plane(part, z):
        rows = []
        for by in range(2):
            place, shift = 4 * (z >> 3) + 2 * by, 32 * (z & 3)
            here = slice(8 * ((z & 7) >> 2), 8 * ((z & 7) >> 2) + 8)
            west = pltpu.roll(coef[part, place, here], (128 - shift) % 128, 1)
            east = pltpu.roll(coef[part, place + 1, here], (160 - shift) % 128, 1)
            rows.append(jnp.where(lane < 32, west, east))
        return jnp.concatenate(rows, 0)

    mask = odd(16, 128)
    left = iota((16, 128), 1) < 64
    zero = jnp.zeros((16, 128), F32)
    for k in (0, 25):
        t_r[k] = zero
        t_b[k] = zero
    for j in range(24):
        lower, upper = (plane((2 * j + i) // 16, (2 * j + i) % 16) for i in range(2))
        keep = left
        if j < 8:
            keep = left & jnp.logical_not(is_zero(slab, (16, 128)))
        if j >= 16:
            keep = left & jnp.logical_not(is_zero(slab - (SLABS - 1), (16, 128)))
        i_r[1 + j] = jnp.where(keep, 1.0 / (jnp.where(mask, upper, lower) + 0.375), 0.0)
        i_b[1 + j] = jnp.where(keep, 1.0 / (jnp.where(mask, lower, upper) + 0.375), 0.0)
    for k in range(1, 25):
        t_b[k] = i_b[k]
        w_b[k] = i_b[k]
    for k in range(1, 25):
        t = i_r[k] * (1.0 + 0.0625 * around(t_b, k, True, mask, 1))
        t_r[k] = t
        w_r[k] = t

    def sweep(n, carry):
        for k in range(1, 25):
            t = i_b[k] * (0.0625 * around(t_r, k, False, mask, 1))
            t_b[k] = t
            w_b[k] = w_b[k] + t
        for k in range(1, 25):
            t = i_r[k] * (0.0625 * around(t_b, k, True, mask, 1))
            t_r[k] = t
            w_r[k] = w_r[k] + t
        return carry

    lax.fori_loop(0, 7, sweep, 0)
    for j in range(8):
        red, black = w_r[9 + j], w_b[9 + j]
        out[2 * j] = jnp.where(mask, black, red)
        out[2 * j + 1] = jnp.where(mask, red, black)


def up_kernel(
    meta, bricks, sum_0, sum_1, sum_2, sum_3, es, ec_b, r_r, r_b, ci_r, ci_b, u1_b, f_r, f_b, i_r, i_b, out,
    e_r, e_b, small, wide, planes, tall, u_r, u_b,
):
    slab, _, bit_x, bit_y, bit_z = place_of(meta, bricks)
    total = (sum_0[...] + sum_1[...]) + (sum_2[...] + sum_3[...])
    mean = jnp.sum(total) * (1.0 / (SLABS * 16 * 16 * 64))
    base = 8 * bit_z
    no_low = jnp.where((slab == 0) & (bit_z == 0), 0, 1)
    no_high = jnp.where((slab == SLABS - 1) & (bit_z == 1), 0, 1)
    for j in range(14):
        shifted = es[base + j] - mean
        if j < 3:
            shifted = jnp.where(is_zero(no_low, (16, 128)), 0.0, shifted)
        if j >= 11:
            shifted = jnp.where(is_zero(no_high, (16, 128)), 0.0, shifted)
        small[16 * j : 16 * j + 16] = shifted
    spread = pick(128, 128, lambda r, c: r == (c >> 1))
    small[...] = select_dot(small[...], spread)
    for j in range(14):
        rows = small[16 * j : 16 * j + 16]
        wide[j, pl.ds(0, 16, stride=2), :] = rows
        wide[j, pl.ds(1, 16, stride=2), :] = rows
    for k in (0, 15):
        e_r[k] = jnp.zeros((32, 128), F32)
        e_b[k] = jnp.zeros((32, 128), F32)
    for j in range(14):
        e_b[1 + j] = ec_b[base + 3 + j] + wide[j]
    coarse = odd(32, 128)
    r_r, r_b, ci_r, ci_b = (grid.at[pl.ds(base + 2, 16)] for grid in (r_r, r_b, ci_r, ci_b))
    half_sweep(e_r, e_b, r_r, ci_r, 1, 15, True, coarse, 0.25, 2)
    half_sweep(e_b, e_r, r_b, ci_b, 2, 14, False, coarse, 0.25, 2)
    half_sweep(e_r, e_b, r_r, ci_r, 2, 14, True, coarse, 0.25, 2)
    half_sweep(e_b, e_r, r_b, ci_b, 3, 13, False, coarse, 0.25, 2)
    for n in range(20):
        k, upper = n // 2 + 3, n % 2
        red, black = e_r[k], e_b[k]
        planes[32 * n : 32 * n + 32] = jnp.where(coarse, red, black) if upper else jnp.where(coarse, black, red)

    lane = iota((128, 256), 1)
    x0 = is_zero(bit_x, (128, 256))
    start = jnp.where(lane < 128, 64 * bit_x + (lane >> 1), (lane >> 1) + jnp.where(x0, 0, -64))
    usable = (lane < 128) | (x0 & (lane < 136)) | (jnp.logical_not(x0) & (lane >= 248))
    spread = jnp.where(usable & (iota((128, 256), 0) == start), 1.0, 0.0).astype(F32)
    tall_rows = select_dot(planes[...], spread)
    for n in range(20):
        rows = tall_rows[32 * n : 32 * n + 32]
        for h in range(2):
            tall[n, h, pl.ds(0, 32, stride=2), :] = rows[:, 128 * h : 128 * h + 128]
            tall[n, h, pl.ds(1, 32, stride=2), :] = rows[:, 128 * h : 128 * h + 128]
    for k in (0, 21):
        u_r[k] = jnp.zeros((40, 256), F32)
        u_b[k] = jnp.zeros((40, 256), F32)
    row = iota((8, 128), 0)
    y0 = is_zero(bit_y)
    in_y = (y0 & (row != 7)) | (jnp.logical_not(y0) & (row != 0))
    own_start = pl.multiple_of(32 * bit_y, 32)
    side_start = pl.multiple_of(32 - 8 * bit_y, 8)
    for n in range(20):
        for h in range(2):
            lanes = slice(128 * h, 128 * h + 128)
            side = jnp.where(in_y, tall[n, h, pl.ds(side_start, 8), :], 0.0)
            u_b[1 + n, 0:32, lanes] = u1_b[3 + n, 0:32, lanes] + tall[n, h, pl.ds(own_start, 32), :]
            u_b[1 + n, 32:40, lanes] = u1_b[3 + n, 32:40, lanes] + side
    mask = odd(40, 256)
    f_r, f_b, i_r, i_b = (grid.at[2:24] for grid in (f_r, f_b, i_r, i_b))
    half_sweep(u_r, u_b, f_r, i_r, 1, 21, True, mask, 1.0, 0)
    half_sweep(u_b, u_r, f_b, i_b, 2, 20, False, mask, 1.0, 0)
    half_sweep(u_r, u_b, f_r, i_r, 2, 20, True, mask, 1.0, 0)
    half_sweep(u_b, u_r, f_b, i_b, 3, 19, False, mask, 1.0, 0)
    own = odd(32, 128)
    for t in range(16):
        red, black = u_r[3 + t, 0:32, 0:128], u_b[3 + t, 0:32, 0:128]
        out[0, 2 * t] = jnp.where(own, black, red)
        out[0, 2 * t + 1] = jnp.where(own, red, black)


def swap_cores(x):
    return lax.ppermute(x, "level", [(0, 1), (1, 0)])


def to_slabs(x, up_first, wrap=False):
    pairs = []
    for s in range(SLABS if wrap else SLABS - 1):
        for m in range(8):
            low, high = s * 8 + m, (s + 1) % SLABS * 8 + m
            pairs.append((low, high) if (m < 4) == up_first else (high, low))
    return lax.ppermute(x, ALL, pairs)


def around_chips(x):
    return [x] + [lax.ppermute(x, "bottom", [(i, (i + d) % 4) for i in range(4)]) for d in range(1, 4)]


def both_cores(boxes):
    return boxes + [swap_cores(box) for box in boxes]


def fours_apart(x):
    beside = [(8 * s + m, 8 * ((s + (4 if m < 4 else 12)) % SLABS) + m) for s in range(SLABS) for m in range(8)]
    across = [(s, (s + 8) % SLABS) for s in range(SLABS)]
    return lax.ppermute(x, ALL, beside), lax.ppermute(x, "slab", across)


def among(x):
    return lax.all_to_all(x, LB, split_axis=0, concat_axis=0, tiled=True)


def body(u_init, source, coeffs, brick_map):
    meta = jnp.stack([lax.axis_index("slab"), lax.axis_index(LB)]).astype(jnp.int32)
    smem = [meta, brick_map]
    fine = (26, 40, 256)
    packed, ac = run(
        first_kernel, [(8, SENT, 8, 128), (9, 16, 128)], smem, [u_init, source, coeffs],
        [(8, 32, 128), (16, 32, 128), (256, 128), (1, 32, 32, 128)],
    )
    got = among(packed)
    leaving = run(cross_kernel, [(4, FACE, 8, 128)], smem, [got])
    leaving, ac = lax.optimization_barrier((leaving, ac))
    cross = to_slabs(leaving, False)
    ac_boxes = around_chips(ac)
    sent = run(mid_kernel, [(8, GOT, 8, 128)], smem, [got, cross], [(12, FACE, 8, 128)])
    sent, *ac_boxes = lax.optimization_barrier((sent, *ac_boxes))
    halo = among(sent)
    faces = (4, 5, 16, 128)
    coarse = (28, 32, 128)
    held = [(8, 8, 16, 128), faces, faces]
    ac_boxes = both_cores(ac_boxes)
    ac_held = [(8, 9, 16, 128), (4, 7, 16, 128), (4, 7, 16, 128)]
    ac_cross = to_slabs(run(faces_kernel, ac_held[1:2], smem, ac_boxes, ac_held[:1]), True)
    ac_other = swap_cores(ac_cross)
    halo, ac_cross, ac_other = lax.optimization_barrier((halo, ac_cross, ac_other))
    rc, u_b, f_r, f_b, i_r, i_b = run(
        fine_down_kernel, [(8, 16, 128)] + [fine] * 5, smem, [u_init, source, coeffs, halo],
        [fine, (16, 32, 128), (256, 128)],
    )
    boxes = both_cores(around_chips(rc))
    leaving = run(faces_kernel, [faces], smem, boxes, held[:1])
    leaving, ac_cross, ac_other = lax.optimization_barrier((leaving, ac_cross, ac_other))
    cross = to_slabs(leaving, True)
    ca_r, ci_r, ci_b, ab, coef = run(
        coarse_coef_kernel, [coarse] * 3 + [(22, 16, 128), (3, 8, 16, 128)], smem, ac_boxes + [ac_cross, ac_other],
        ac_held + [coarse, (22, 32, 128), (352, 128)],
    )
    weights = run(weights_kernel, [(16, 16, 128)], [meta], [coef], [(26, 16, 128)] * 6)
    cross, weights, ca_r, ci_r, ci_b, ab = lax.optimization_barrier((cross, weights, ca_r, ci_r, ci_b, ab))
    rb, rb_send, part, ec_b, r_r, r_b = run(
        coarse_down_kernel, [(22, 16, 128), (19, 16, 128), (8, 128)] + [coarse] * 3, smem,
        boxes + [cross, swap_cores(cross), weights, ca_r, ci_r, ci_b, ab],
        held + [coarse, (22, 32, 128), (352, 128)],
    )
    cross = to_slabs(rb_send, True, wrap=True)
    far = lax.ppermute(part, "slab", [(s, (s - 2) % SLABS) for s in range(SLABS)])
    cross, far = lax.optimization_barrier((cross, far))
    other = swap_cores(cross)
    part = (part + far) + (cross[18, 0:8] + other[18, 0:8])
    near, far = fours_apart(part)
    sums = [part, near, far, swap_cores(near)]
    bottom = (28, 16, 128)
    es = run(
        bottom_kernel, [(22, 16, 128)], [meta], [rb, cross, other],
        [bottom] * 6 + [(19, 16, 128)] * 2,
    )
    return run(
        up_kernel, [(1, 32, 32, 128)], smem,
        sums + [es, ec_b, r_r, r_b, ci_r, ci_b, u_b, f_r, f_b, i_r, i_b],
        [(16, 32, 128)] * 2 + [(224, 128), (14, 32, 128), (640, 128), (20, 2, 64, 128), (22, 40, 256), (22, 40, 256)],
    )


def solution(mesh):
    placed = P(ALL, None, None, None)
    return jax.shard_map(
        body, mesh=mesh, in_specs=(placed, placed, placed, P()), out_specs=placed, check_vma=False
    )
```

```python
import jax
import jax.numpy as jnp
from jax import lax
from jax.experimental import pallas as pl
from jax.experimental.pallas import tpu as pltpu
from jax.sharding import PartitionSpec as P

LB = ("level", "bottom")
ALL = ("slab", "level", "bottom")
SLABS = 16
OWN = 5
F32 = jnp.float32
VMEM_SPEC = pl.BlockSpec(memory_space=pltpu.VMEM)
SMEM_SPEC = pl.BlockSpec(memory_space=pltpu.SMEM)
EXACT = lax.Precision.HIGHEST


def run(kernel, outs, smem, vmem, scratch=()):
    shapes = [jax.ShapeDtypeStruct(s, F32) for s in outs]
    single = len(shapes) == 1
    return pl.pallas_call(
        kernel,
        out_shape=shapes[0] if single else shapes,
        in_specs=[SMEM_SPEC] * len(smem) + [VMEM_SPEC] * len(vmem),
        out_specs=VMEM_SPEC if single else [VMEM_SPEC] * len(shapes),
        scratch_shapes=[pltpu.VMEM(s, F32) for s in scratch],
        compiler_params=pltpu.CompilerParams(vmem_limit_bytes=20 << 20),
    )(*smem, *vmem)


def iota(shape, dim):
    return lax.broadcasted_iota(jnp.int32, shape, dim)


def odd(rows, cols):
    return ((iota((rows, cols), 0) + iota((rows, cols), 1)) & 1) == 1


def place_of(meta, bricks):
    slab, me = meta[0], meta[1]
    place = jnp.int32(0)
    for i in range(8):
        place = place + jnp.where(bricks[slab, i] == me, i, 0)
    return slab, me, place & 1, (place >> 1) & 1, place >> 2


def is_zero(scalar, shape=(8, 128)):
    return jnp.full(shape, scalar, jnp.int32) == 0


ARRAYS = 5
FACE = 17
SENT_Y, SENT_X, SENT = 17, 26, 29
GOT_ROWS, GOT_STRIPS, GOT_Y, GOT_X, GOT = 17, 20, 22, 31, 34
ROOM = (2, 4, 7)


def face_planes(j):
    return [(1 + j, 0), (1 + j, 1), (1 + j, 2), (0, j)]


def merge_strips(placed, base=None):
    group = iota((8, 128), 1) // 8
    total = jnp.zeros((8, 128), F32) if base is None else base
    for pos, strip in placed:
        moved = pltpu.roll(strip, 8 * pos, 1) if pos else strip
        total = jnp.where(group == pos, moved, total)
    return total


def swap_lanes(cells):
    lane = iota(cells.shape, 1)
    return jnp.where((lane & 1) == 0, pltpu.roll(cells, cells.shape[1] - 1, 1), pltpu.roll(cells, 1, 1))


def pack_shell(get, out, bit_x, bit_y):
    x0, y0 = is_zero(bit_x), is_zero(bit_y)
    mask = odd(32, 128)
    row = iota((8, 128), 0)
    free = (y0 & (row < 2)) | (jnp.logical_not(y0) & (row >= 6))
    for k in range(8):
        high, j = k >= 4, k % 4
        for i, (c, far) in enumerate(face_planes(j)):
            out[k, 4 * i : 4 * i + 4] = get(c, 15 - far if high else far).reshape(4, 8, 128)
        t = 12 if high else 3
        one, two = get(1, t), swap_lanes(get(3, t))
        both = jnp.where(mask, one, two) if high else jnp.where(mask, two, one)
        out[k, 16] = both[8 * j : 8 * j + 8]
        strips, rows = [], []
        for tl in range(2):
            for c in range(ARRAYS):
                v = get(c, 2 * k + tl)
                rows.append(jnp.where(y0, v[24:32], v[0:8]))
                for g in range(4):
                    tile = v[8 * g : 8 * g + 8]
                    strips.append(jnp.where(x0, pltpu.roll(tile, 8, 1), tile))
        last = rows.pop()
        for i, at in enumerate(ROOM):
            rows[at] = jnp.where(free, pltpu.roll(last, 6 - 2 * i, 0), rows[at])
        for i, tile in enumerate(rows):
            out[k, SENT_Y + i] = tile
        for i in range(3):
            out[k, SENT_X + i] = merge_strips(list(enumerate(strips[16 * i : 16 * i + 16])))


def cross_kernel(meta, bricks, recv, out):
    slab, me = meta[0], meta[1]
    for i in range(4):
        src = jnp.where(me >= 4, bricks[slab, 4 + i], bricks[slab, i])
        out[i] = recv[src, 0:FACE]


def mid_kernel(meta, bricks, recv, cross, out, faces):
    slab, me = meta[0], meta[1]
    faces[0:8] = recv[:, 0:FACE]
    faces[8:12] = cross[...]
    row = iota((8, 128), 0)
    for p in range(8):
        bx, by, bz = p & 1, (p >> 1) & 1, p >> 2
        dest = bricks[slab, p]
        same = me >= 4 if bz else me < 4

        def src(q):
            return jnp.where(same, bricks[slab, (q & 3) + 4 * (1 - bz)], 8 + (q & 3))

        def strip_of(tile):
            return pltpu.roll(tile, 8, 1) if bx else tile

        def rows_of(at):
            one, two, three, last = (faces[at, 4 * i + (3 if by else 0)] for i in range(4))
            if by:
                shared = jnp.where(row >= 3, two, pltpu.roll(three, 3, 0))
            else:
                shared = jnp.where(row < 5, two, pltpu.roll(three, 5, 0))
            return [one, shared, last]

        at_own, at_y, at_x, at_xy = src(p), src(p ^ 2), src(p ^ 1), src(p ^ 3)
        out[dest, 0:FACE] = faces[at_own]
        for i, tile in enumerate(rows_of(at_y)):
            out[dest, GOT_ROWS + i] = tile
        strips = [strip_of(faces[at_x, i]) for i in range(16)] + [strip_of(tile) for tile in rows_of(at_xy)]
        from_y, from_x, from_xy = bricks[slab, p ^ 2], bricks[slab, p ^ 1], bricks[slab, p ^ 3]
        strips += [strip_of(recv[from_xy, SENT_Y + i]) for i in range(SENT_X - SENT_Y)]
        for i in range(2):
            out[dest, GOT_STRIPS + i] = merge_strips(list(enumerate(strips[16 * i : 16 * i + 16])))
        out[dest, GOT_Y:GOT_X] = recv[from_y, SENT_Y:SENT_X]
        out[dest, GOT_X:GOT] = recv[from_x, SENT_X:SENT]


def unpack_shell(recv, grids, bit_x, bit_y):
    row, lane = iota((8, 128), 0), iota((8, 128), 1)
    x0, y0 = is_zero(bit_x), is_zero(bit_y)
    in_x = (x0 & (lane < 8)) | (jnp.logical_not(x0) & (lane >= 120))
    five = (y0 & (row < 5)) | (jnp.logical_not(y0) & (row >= 3))
    three = (y0 & (row < 3)) | (jnp.logical_not(y0) & (row >= 5))
    seven = (y0 & (row != 7)) | (jnp.logical_not(y0) & (row != 0))
    mask = odd(8, 128)

    def cut(c, tile):
        return jnp.where(seven, tile, 0.0) if c >= 3 else tile

    def strip(tile, pos):
        shift = (jnp.where(bit_x == 0, 0, 120) + 128 - 8 * pos) % 128
        return jnp.where(in_x, pltpu.roll(tile, shift, 1), 0.0)

    def rows_of(tiles):
        one, shared, last = tiles
        moved = jnp.where(y0, pltpu.roll(shared, 3, 0), pltpu.roll(shared, 5, 0))
        return [one, jnp.where(five, shared, 0.0), jnp.where(three, moved, 0.0), last]

    def with_last(tiles):
        pair = jnp.where(y0, row >> 1, (row >> 1) - 1)
        last = jnp.zeros((8, 128), F32)
        for i, at in enumerate(ROOM):
            last = jnp.where(pair == i, pltpu.roll(tiles[at], 2 + 2 * i, 0), last)
        return tiles + [last]

    for k in range(8):
        high, j = k >= 4, k % 4
        rows = rows_of([recv[k, GOT_ROWS + i] for i in range(3)])
        sides = rows_of([strip(recv[k, GOT_STRIPS + 1], i) for i in range(3)])
        for i, (c, far) in enumerate(face_planes(j)):
            at = OWN - 1 - far if high else OWN + 16 + far
            for g in range(4):
                grids[c][at, 8 * g : 8 * g + 8, 0:128] = recv[k, 4 * i + g]
                grids[c][at, 8 * g : 8 * g + 8, 128:256] = strip(recv[k, GOT_STRIPS], 4 * i + g)
            grids[c][at, 32:40, 0:128] = cut(c, rows[i])
            grids[c][at, 32:40, 128:256] = cut(c, sides[i])
        at = 1 if high else 24
        both = recv[k, 16]
        other = swap_lanes(both)
        other = jnp.where(mask, other, 0.0) if high else jnp.where(mask, 0.0, other)
        for c, cells in ((1, both), (3, other)):
            grids[c][at, 8 * j : 8 * j + 8, 0:128] = cells
            grids[c][at, 8 * j : 8 * j + 8, 128:256] = jnp.zeros((8, 128), F32)
            grids[c][at, 32:40] = jnp.zeros((8, 256), F32)
        rows = with_last([recv[k, GOT_Y + i] for i in range(GOT_X - GOT_Y)])
        sides = with_last([strip(recv[k, GOT_STRIPS + 1], 3 + i) for i in range(GOT_X - GOT_Y)])
        for tl in range(2):
            for c in range(ARRAYS):
                i = tl * ARRAYS + c
                at = OWN + 2 * k + tl
                grids[c][at, 32:40, 0:128] = cut(c, rows[i])
                grids[c][at, 32:40, 128:256] = cut(c, sides[i])
                for g in range(4):
                    n = 4 * i + g
                    side = strip(recv[k, GOT_X + n // 16], n % 16)
                    grids[c][at, 8 * g : 8 * g + 8, 128:256] = side


def pair_of(cells, t, red, mask):
    low, high = cells[0, 2 * t], cells[0, 2 * t + 1]
    return jnp.where(mask, high, low) if red else jnp.where(mask, low, high)


def pack_bottom_coef(a, ac, small):
    for i in range(8):
        planes = (a[0, 4 * i] + a[0, 4 * i + 1]) + (a[0, 4 * i + 2] + a[0, 4 * i + 3])
        small[i] = planes
    rows = []
    for i in range(8):
        first = small[i, pl.ds(0, 8, stride=4), :] + small[i, pl.ds(1, 8, stride=4), :]
        rows.append(first + (small[i, pl.ds(2, 8, stride=4), :] + small[i, pl.ds(3, 8, stride=4), :]))
    fold = pick(128, 128, lambda r, c: (r >> 2) == (c & 31)) * (1.0 / 64)
    cells = jnp.dot(jnp.concatenate(rows, 0), fold, precision=EXACT, preferred_element_type=F32)
    group = iota((8, 128), 1) >> 5
    for h in range(2):
        tile = cells[32 * h : 32 * h + 8]
        for j in range(1, 4):
            tile = jnp.where(group == j, cells[32 * h + 8 * j : 32 * h + 8 * j + 8], tile)
        ac[8, 8 * h : 8 * h + 8] = tile


def pack_coarse(planes, small, out):
    twice = pick(128, 128, lambda r, c: (r >> 1) == (c & 63)) * 0.125
    row, lane = iota((16, 128), 0), iota((16, 128), 1)
    even = ((row + lane + (lane >> 6)) & 1) == 0
    for t in range(16):
        small[16 * t : 16 * t + 16] = planes[t, pl.ds(0, 16, stride=2), :] + planes[t, pl.ds(1, 16, stride=2), :]
    summed = jnp.dot(small[...], twice, precision=EXACT, preferred_element_type=F32)
    summed = summed.reshape(16, 16, 128)
    for j in range(8):
        out[j] = jnp.where(even, summed[2 * j], summed[2 * j + 1])


def first_kernel(meta, bricks, u, f, a, out, ac, small, planes, rows, inverse):
    _, _, bit_x, bit_y, _ = place_of(meta, bricks)
    mask = odd(32, 128)
    inverse[...] = 1.0 / (a[...] + 6.0)
    sources = ((u, False), (f, True), (f, False), (inverse, True), (inverse, False))

    def get(c, t):
        return pair_of(sources[c][0], t, sources[c][1], mask)

    pack_shell(get, out, bit_x, bit_y)
    pack_bottom_coef(a, ac, small)
    for t in range(16):
        planes[t] = a[0, 2 * t] + a[0, 2 * t + 1]
    pack_coarse(planes, rows, ac)


def around(src, k, red, mask, edges, cut=None):
    here = src[k]
    rows, cols = here.shape
    above, below = src[k + 1], src[k - 1]
    other = jnp.where(mask, above, below) if red else jnp.where(mask, below, above)
    up, down = pltpu.roll(here, 1, 0), pltpu.roll(here, rows - 1, 0)
    left, right = pltpu.roll(here, 1, 1), pltpu.roll(here, cols - 1, 1)
    if edges:
        row, lane = iota((rows, cols), 0), iota((rows, cols), 1)
        up, down = jnp.where(row == 0, 0.0, up), jnp.where(row == rows - 1, 0.0, down)
        if edges == 2:
            left, right = jnp.where(lane == 0, 0.0, left), jnp.where(lane == cols - 1, 0.0, right)
    if cut is not None:
        up, down = jnp.where(cut[0], 0.0, up), jnp.where(cut[1], 0.0, down)
    return ((here + other) + (up + down)) + (left + right)


def half_sweep(dst, src, force, inverse, lo, hi, red, mask, scale, edges, cut=None):
    def step(k, carry):
        total = around(src, k, red, mask, edges, cut)
        if scale != 1.0:
            total = scale * total
        dst[k] = (force[k] + total) * inverse[k]
        return carry

    lax.fori_loop(lo, hi, step, 0, unroll=True)


def select_dot(cells, chosen):
    half, total = chosen.astype(jnp.bfloat16), None
    for _ in range(3):
        part = cells.astype(jnp.bfloat16)
        cells = cells - part.astype(F32)
        moved = jnp.dot(part, half, preferred_element_type=F32)
        total = moved if total is None else total + moved
    return total


def pick(rows, cols, keep):
    return jnp.where(keep(iota((rows, cols), 0), iota((rows, cols), 1)), 1.0, 0.0).astype(F32)


def fine_down_kernel(meta, bricks, u, f, a, recv, rc, u_b, f_r, f_b, i_r, i_b, u_r, resid, small):
    _, _, bit_x, bit_y, _ = place_of(meta, bricks)
    own = odd(32, 128)
    for t in range(16):
        here = (OWN + t, slice(0, 32), slice(0, 128))
        u_b[here] = pair_of(u, t, False, own)
        f_r[here], f_b[here] = pair_of(f, t, True, own), pair_of(f, t, False, own)
        i_r[here], i_b[here] = 1.0 / (pair_of(a, t, True, own) + 6.0), 1.0 / (pair_of(a, t, False, own) + 6.0)
    unpack_shell(recv, (u_b, f_r, f_b, i_r, i_b), bit_x, bit_y)
    zero = jnp.zeros((40, 256), F32)
    for k in (0, 25):
        u_r[k] = zero
        u_b[k] = zero
    for k in (1, 24):
        f_b[k] = zero
        i_b[k] = zero
    row = iota((40, 256), 0)
    y0 = is_zero(bit_y, (40, 256))
    y1 = jnp.logical_not(y0)
    mask = odd(40, 256)
    cut = (y0 & (row == 0), y1 & (row == 31))
    half_sweep(u_r, u_b, f_r, i_r, 1, 25, True, mask, 1.0, 0, cut)
    half_sweep(u_b, u_r, f_b, i_b, 1, 25, False, mask, 1.0, 0)
    half_sweep(u_r, u_b, f_r, i_r, 2, 24, True, mask, 1.0, 0)
    half_sweep(u_b, u_r, f_b, i_b, 3, 23, False, mask, 1.0, 0)
    for t in range(16):
        total = around(u_b, OWN + t, True, mask, 0)[0:32, 0:128]
        diag = pair_of(a, t, True, own) + 6.0
        here = (OWN + t, slice(0, 32), slice(0, 128))
        resid[t] = f_r[here] + total - diag * u_r[here]
    pack_coarse(resid, small, rc)


def slot_of(member, me):
    return jnp.where((member >> 2) == (me >> 2), 0, 4) + ((me - member) & 3)


def faces_kernel(meta, bricks, *refs):
    boxes, (out, held) = refs[:8], refs[8:]
    slab, me = meta[0], meta[1]
    for i, box in enumerate(boxes):
        held[i] = box[...]
    start = jnp.where(me < 4, 3, 0)
    for i in range(4):
        member = jnp.where(me < 4, bricks[slab, 4 + i], bricks[slab, i])
        out[i, 0:5] = held[slot_of(member, me), pl.ds(start, 5)]
        for j in range(5, out.shape[1]):
            out[i, j] = held[slot_of(bricks[slab, 2 * i + j - 5], me), 8]


def sort_sides(me, one, two, low, high):
    @pl.when(me < 4)
    def _():
        low[...] = one[...]
        high[...] = two[...]

    @pl.when(me >= 4)
    def _():
        low[...] = two[...]
        high[...] = one[...]


def assemble(meta, bricks, boxes, one, two, red, black, held, low, high):
    slab, me = meta[0], meta[1]
    for i, box in enumerate(boxes):
        held[i] = box[...]
    sort_sides(me, one, two, low, high)
    left = iota((16, 128), 1) < 64

    def put(k, by, west, east):
        rows = slice(16 * by, 16 * by + 16)
        red[k, rows] = jnp.where(left, west, pltpu.roll(east, 64, 1))
        black[k, rows] = jnp.where(left, pltpu.roll(west, 64, 1), east)

    for by in range(2):
        for bz in range(2):
            west = slot_of(bricks[slab, 2 * by + 4 * bz], me)
            east = slot_of(bricks[slab, 2 * by + 4 * bz + 1], me)
            for j in range(8):
                put(6 + 8 * bz + j, by, held[west, j], held[east, j])
        for j in range(5):
            put(1 + j, by, low[2 * by, j], low[2 * by + 1, j])
            put(22 + j, by, high[2 * by, j], high[2 * by + 1, j])


def to_bottom(planes, small, half):
    for n in range(22):
        small[16 * n : 16 * n + 16] = planes[n, pl.ds(0, 16, stride=2), :] + planes[n, pl.ds(1, 16, stride=2), :]
    fold = pick(128, 128, lambda r, c: (r >> 1) == c - 64 * half) * 0.125
    return jnp.dot(small[...], fold, precision=EXACT, preferred_element_type=F32).reshape(22, 16, 128)


def coarse_coef_kernel(meta, bricks, *refs):
    boxes, (one, two) = refs[:8], refs[8:10]
    a_r, i_r, i_b, ab, coef = refs[10:15]
    held, low, high, a_b, planes, small = refs[15:]
    slab, me = meta[0], meta[1]
    assemble(meta, bricks, boxes, one, two, a_r, a_b, held, low, high)
    for p in range(8):
        coef[0, p] = low[p >> 1, 5 + (p & 1)]
        coef[1, p] = held[slot_of(bricks[slab, p], me), 8]
        coef[2, p] = high[p >> 1, 5 + (p & 1)]
    for k in range(1, 27):
        keep = jnp.full((32, 128), 0, jnp.int32) == 0
        if k < 6:
            keep = jnp.logical_not(is_zero(slab, (32, 128)))
        if k >= 22:
            keep = jnp.logical_not(is_zero(slab - (SLABS - 1), (32, 128)))
        i_r[k] = jnp.where(keep, 1.0 / (a_r[k] + 1.5), 0.0)
        i_b[k] = jnp.where(keep, 1.0 / (a_b[k] + 1.5), 0.0)
    for n in range(22):
        planes[n] = a_r[3 + n] + a_b[3 + n]
    ab[...] = to_bottom(planes, small, 1)


def coarse_down_kernel(meta, bricks, *refs):
    boxes, (one, two, weights, a_r, i_r, i_b, ab) = refs[:8], refs[8:15]
    rb, rb_send, part, e_b, r_r, r_b = refs[15:21]
    held, low, high, e_r, resid, small = refs[21:]
    me = meta[1]
    assemble(meta, bricks, boxes, one, two, r_r, r_b, held, low, high)
    for k in (0, 27):
        e_r[k] = jnp.zeros((32, 128), F32)
        e_b[k] = jnp.zeros((32, 128), F32)
    for k in range(1, 27):
        e_r[k] = r_r[k] * i_r[k]
    mask = odd(32, 128)
    half_sweep(e_b, e_r, r_b, i_b, 1, 27, False, mask, 0.25, 2)
    half_sweep(e_r, e_b, r_r, i_r, 1, 27, True, mask, 0.25, 2)
    half_sweep(e_b, e_r, r_b, i_b, 1, 27, False, mask, 0.25, 2)
    for n in range(22):
        k = n + 3
        total = 0.25 * around(e_b, k, True, mask, 2)
        resid[n] = r_r[k] + total - (a_r[k] + 1.5) * e_r[k]
    rb[...] = to_bottom(resid, small, 0) + ab[...]
    rb_send[0:18] = rb[pl.ds(jnp.where(me < 4, 1, 3), 18)]
    total = jnp.zeros((16, 128), F32)
    for i in range(16):
        total = total + rb[3 + i] * weights[i]
    total = total[0:8] + total[8:16]
    part[...] = total
    rb_send[18, 0:8] = total
    rb_send[18, 8:16] = total


def bottom_kernel(meta, rb, one, two, es, e_r, e_b, g_r, g_b, i_r, i_b, low, high):
    slab, me = meta[0], meta[1]
    sort_sides(me, one, two, low, high)
    mask = odd(16, 128)
    left = iota((16, 128), 1) < 64
    zero = jnp.zeros((16, 128), F32)
    for k in (0, 27):
        e_r[k] = zero
        e_b[k] = zero
    for j in range(26):
        planes = []
        for n in (2 * j, 2 * j + 1):
            planes.append(low[n] if n < 18 else rb[n - 15] if n < 34 else high[n - 34])
        keep = left
        if j < 9:
            keep = left & jnp.logical_not(is_zero(slab, (16, 128)))
        if j >= 17:
            keep = left & jnp.logical_not(is_zero(slab - (SLABS - 1), (16, 128)))
        for red in (True, False):
            cells = jnp.where(mask, planes[1], planes[0]) if red else jnp.where(mask, planes[0], planes[1])
            force = jnp.where(left, cells, 0.0)
            inverse = jnp.where(keep, 1.0 / (pltpu.roll(cells, 64, 1) + 0.375), 0.0)
            if red:
                g_r[1 + j], i_r[1 + j], e_r[1 + j] = force, inverse, force * inverse
            else:
                g_b[1 + j], i_b[1 + j] = force, inverse
    half_sweep(e_b, e_r, g_b, i_b, 1, 27, False, mask, 0.0625, 1)

    def sweep(n, carry):
        half_sweep(e_r, e_b, g_r, i_r, 1, 27, True, mask, 0.0625, 1)
        half_sweep(e_b, e_r, g_b, i_b, 1, 27, False, mask, 0.0625, 1)
        return carry

    lax.fori_loop(0, 7, sweep, 0)
    for i in range(22):
        k, upper = (15 + i) // 2 + 1, (15 + i) % 2
        es[i] = jnp.where(mask, e_r[k], e_b[k]) if upper else jnp.where(mask, e_b[k], e_r[k])


def weights_kernel(meta, coef, out, t_r, t_b, w_r, w_b, i_r, i_b):
    slab = meta[0]
    lane = iota((8, 128), 1)

    def plane(part, z):
        rows = []
        for by in range(2):
            place, shift = 4 * (z >> 3) + 2 * by, 32 * (z & 3)
            here = slice(8 * ((z & 7) >> 2), 8 * ((z & 7) >> 2) + 8)
            west = pltpu.roll(coef[part, place, here], (128 - shift) % 128, 1)
            east = pltpu.roll(coef[part, place + 1, here], (160 - shift) % 128, 1)
            rows.append(jnp.where(lane < 32, west, east))
        return jnp.concatenate(rows, 0)

    mask = odd(16, 128)
    left = iota((16, 128), 1) < 64
    zero = jnp.zeros((16, 128), F32)
    for k in (0, 25):
        t_r[k] = zero
        t_b[k] = zero
    for j in range(24):
        lower, upper = (plane((2 * j + i) // 16, (2 * j + i) % 16) for i in range(2))
        keep = left
        if j < 8:
            keep = left & jnp.logical_not(is_zero(slab, (16, 128)))
        if j >= 16:
            keep = left & jnp.logical_not(is_zero(slab - (SLABS - 1), (16, 128)))
        i_r[1 + j] = jnp.where(keep, 1.0 / (jnp.where(mask, upper, lower) + 0.375), 0.0)
        i_b[1 + j] = jnp.where(keep, 1.0 / (jnp.where(mask, lower, upper) + 0.375), 0.0)
    for k in range(1, 25):
        t_b[k] = i_b[k]
        w_b[k] = i_b[k]
    for k in range(1, 25):
        t = i_r[k] * (1.0 + 0.0625 * around(t_b, k, True, mask, 1))
        t_r[k] = t
        w_r[k] = t

    def sweep(n, carry):
        for k in range(1, 25):
            t = i_b[k] * (0.0625 * around(t_r, k, False, mask, 1))
            t_b[k] = t
            w_b[k] = w_b[k] + t
        for k in range(1, 25):
            t = i_r[k] * (0.0625 * around(t_b, k, True, mask, 1))
            t_r[k] = t
            w_r[k] = w_r[k] + t
        return carry

    lax.fori_loop(0, 7, sweep, 0)
    for j in range(8):
        red, black = w_r[9 + j], w_b[9 + j]
        out[2 * j] = jnp.where(mask, black, red)
        out[2 * j + 1] = jnp.where(mask, red, black)


def up_kernel(
    meta, bricks, sum_0, sum_1, sum_2, sum_3, es, ec_b, r_r, r_b, ci_r, ci_b, u1_b, f_r, f_b, i_r, i_b, out,
    e_r, e_b, small, wide, planes, tall, u_r, u_b,
):
    slab, _, bit_x, bit_y, bit_z = place_of(meta, bricks)
    total = (sum_0[...] + sum_1[...]) + (sum_2[...] + sum_3[...])
    mean = jnp.sum(total) * (1.0 / (SLABS * 16 * 16 * 64))
    base = 8 * bit_z
    no_low = jnp.where((slab == 0) & (bit_z == 0), 0, 1)
    no_high = jnp.where((slab == SLABS - 1) & (bit_z == 1), 0, 1)
    for j in range(14):
        shifted = es[base + j] - mean
        if j < 3:
            shifted = jnp.where(is_zero(no_low, (16, 128)), 0.0, shifted)
        if j >= 11:
            shifted = jnp.where(is_zero(no_high, (16, 128)), 0.0, shifted)
        small[16 * j : 16 * j + 16] = shifted
    spread = pick(128, 128, lambda r, c: r == (c >> 1))
    small[...] = select_dot(small[...], spread)
    for j in range(14):
        rows = small[16 * j : 16 * j + 16]
        wide[j, pl.ds(0, 16, stride=2), :] = rows
        wide[j, pl.ds(1, 16, stride=2), :] = rows
    for k in (0, 15):
        e_r[k] = jnp.zeros((32, 128), F32)
        e_b[k] = jnp.zeros((32, 128), F32)
    for j in range(14):
        e_b[1 + j] = ec_b[base + 3 + j] + wide[j]
    coarse = odd(32, 128)
    r_r, r_b, ci_r, ci_b = (grid.at[pl.ds(base + 2, 16)] for grid in (r_r, r_b, ci_r, ci_b))
    half_sweep(e_r, e_b, r_r, ci_r, 1, 15, True, coarse, 0.25, 2)
    half_sweep(e_b, e_r, r_b, ci_b, 2, 14, False, coarse, 0.25, 2)
    half_sweep(e_r, e_b, r_r, ci_r, 2, 14, True, coarse, 0.25, 2)
    half_sweep(e_b, e_r, r_b, ci_b, 3, 13, False, coarse, 0.25, 2)
    for n in range(20):
        k, upper = n // 2 + 3, n % 2
        red, black = e_r[k], e_b[k]
        planes[32 * n : 32 * n + 32] = jnp.where(coarse, red, black) if upper else jnp.where(coarse, black, red)

    lane = iota((128, 256), 1)
    x0 = is_zero(bit_x, (128, 256))
    start = jnp.where(lane < 128, 64 * bit_x + (lane >> 1), (lane >> 1) + jnp.where(x0, 0, -64))
    usable = (lane < 128) | (x0 & (lane < 136)) | (jnp.logical_not(x0) & (lane >= 248))
    spread = jnp.where(usable & (iota((128, 256), 0) == start), 1.0, 0.0).astype(F32)
    tall_rows = select_dot(planes[...], spread)
    for n in range(20):
        rows = tall_rows[32 * n : 32 * n + 32]
        for h in range(2):
            tall[n, h, pl.ds(0, 32, stride=2), :] = rows[:, 128 * h : 128 * h + 128]
            tall[n, h, pl.ds(1, 32, stride=2), :] = rows[:, 128 * h : 128 * h + 128]
    for k in (0, 21):
        u_r[k] = jnp.zeros((40, 256), F32)
        u_b[k] = jnp.zeros((40, 256), F32)
    row = iota((8, 128), 0)
    y0 = is_zero(bit_y)
    in_y = (y0 & (row != 7)) | (jnp.logical_not(y0) & (row != 0))
    own_start = pl.multiple_of(32 * bit_y, 32)
    side_start = pl.multiple_of(32 - 8 * bit_y, 8)
    for n in range(20):
        for h in range(2):
            lanes = slice(128 * h, 128 * h + 128)
            side = jnp.where(in_y, tall[n, h, pl.ds(side_start, 8), :], 0.0)
            u_b[1 + n, 0:32, lanes] = u1_b[3 + n, 0:32, lanes] + tall[n, h, pl.ds(own_start, 32), :]
            u_b[1 + n, 32:40, lanes] = u1_b[3 + n, 32:40, lanes] + side
    mask = odd(40, 256)
    f_r, f_b, i_r, i_b = (grid.at[2:24] for grid in (f_r, f_b, i_r, i_b))
    half_sweep(u_r, u_b, f_r, i_r, 1, 21, True, mask, 1.0, 0)
    half_sweep(u_b, u_r, f_b, i_b, 2, 20, False, mask, 1.0, 0)
    half_sweep(u_r, u_b, f_r, i_r, 2, 20, True, mask, 1.0, 0)
    half_sweep(u_b, u_r, f_b, i_b, 3, 19, False, mask, 1.0, 0)
    own = odd(32, 128)
    for t in range(16):
        red, black = u_r[3 + t, 0:32, 0:128], u_b[3 + t, 0:32, 0:128]
        out[0, 2 * t] = jnp.where(own, black, red)
        out[0, 2 * t + 1] = jnp.where(own, red, black)


def swap_cores(x):
    return lax.ppermute(x, "level", [(0, 1), (1, 0)])


def to_slabs(x, up_first, wrap=False):
    pairs = []
    for s in range(SLABS if wrap else SLABS - 1):
        for m in range(8):
            low, high = s * 8 + m, (s + 1) % SLABS * 8 + m
            pairs.append((low, high) if (m < 4) == up_first else (high, low))
    return lax.ppermute(x, ALL, pairs)


def around_chips(x):
    return [x] + [lax.ppermute(x, "bottom", [(i, (i + d) % 4) for i in range(4)]) for d in range(1, 4)]


def both_cores(boxes):
    return boxes + [swap_cores(box) for box in boxes]


def fours_apart(x):
    beside = [(8 * s + m, 8 * ((s + (4 if m < 4 else 12)) % SLABS) + m) for s in range(SLABS) for m in range(8)]
    across = [(s, (s + 8) % SLABS) for s in range(SLABS)]
    return lax.ppermute(x, ALL, beside), lax.ppermute(x, "slab", across)


def among(x):
    return lax.all_to_all(x, LB, split_axis=0, concat_axis=0, tiled=True)


def body(u_init, source, coeffs, brick_map):
    meta = jnp.stack([lax.axis_index("slab"), lax.axis_index(LB)]).astype(jnp.int32)
    smem = [meta, brick_map]
    fine = (26, 40, 256)
    packed, ac = run(
        first_kernel, [(8, SENT, 8, 128), (9, 16, 128)], smem, [u_init, source, coeffs],
        [(8, 32, 128), (16, 32, 128), (256, 128), (1, 32, 32, 128)],
    )
    got = among(packed)
    leaving = run(cross_kernel, [(4, FACE, 8, 128)], smem, [got])
    leaving, ac = lax.optimization_barrier((leaving, ac))
    cross = to_slabs(leaving, False)
    ac_boxes = around_chips(ac)
    sent = run(mid_kernel, [(8, GOT, 8, 128)], smem, [got, cross], [(12, FACE, 8, 128)])
    sent, *ac_boxes = lax.optimization_barrier((sent, *ac_boxes))
    halo = among(sent)
    faces = (4, 5, 16, 128)
    coarse = (28, 32, 128)
    held = [(8, 8, 16, 128), faces, faces]
    ac_boxes = both_cores(ac_boxes)
    ac_held = [(8, 9, 16, 128), (4, 7, 16, 128), (4, 7, 16, 128)]
    ac_cross = to_slabs(run(faces_kernel, ac_held[1:2], smem, ac_boxes, ac_held[:1]), True)
    ac_other = swap_cores(ac_cross)
    halo, ac_cross, ac_other = lax.optimization_barrier((halo, ac_cross, ac_other))
    rc, u_b, f_r, f_b, i_r, i_b = run(
        fine_down_kernel, [(8, 16, 128)] + [fine] * 5, smem, [u_init, source, coeffs, halo],
        [fine, (16, 32, 128), (256, 128)],
    )
    boxes = both_cores(around_chips(rc))
    leaving = run(faces_kernel, [faces], smem, boxes, held[:1])
    leaving, ac_cross, ac_other = lax.optimization_barrier((leaving, ac_cross, ac_other))
    cross = to_slabs(leaving, True)
    ca_r, ci_r, ci_b, ab, coef = run(
        coarse_coef_kernel, [coarse] * 3 + [(22, 16, 128), (3, 8, 16, 128)], smem, ac_boxes + [ac_cross, ac_other],
        ac_held + [coarse, (22, 32, 128), (352, 128)],
    )
    weights = run(weights_kernel, [(16, 16, 128)], [meta], [coef], [(26, 16, 128)] * 6)
    cross, weights, ca_r, ci_r, ci_b, ab = lax.optimization_barrier((cross, weights, ca_r, ci_r, ci_b, ab))
    rb, rb_send, part, ec_b, r_r, r_b = run(
        coarse_down_kernel, [(22, 16, 128), (19, 16, 128), (8, 128)] + [coarse] * 3, smem,
        boxes + [cross, swap_cores(cross), weights, ca_r, ci_r, ci_b, ab],
        held + [coarse, (22, 32, 128), (352, 128)],
    )
    cross = to_slabs(rb_send, True, wrap=True)
    far = lax.ppermute(part, "slab", [(s, (s - 2) % SLABS) for s in range(SLABS)])
    cross, far = lax.optimization_barrier((cross, far))
    other = swap_cores(cross)
    part = (part + far) + (cross[18, 0:8] + other[18, 0:8])
    near, far = fours_apart(part)
    sums = [part, near, far, swap_cores(near)]
    bottom = (28, 16, 128)
    es = run(
        bottom_kernel, [(22, 16, 128)], [meta], [rb, cross, other],
        [bottom] * 6 + [(19, 16, 128)] * 2,
    )
    return run(
        up_kernel, [(1, 32, 32, 128)], smem,
        sums + [es, ec_b, r_r, r_b, ci_r, ci_b, u_b, f_r, f_b, i_r, i_b],
        [(16, 32, 128)] * 2 + [(224, 128), (14, 32, 128), (640, 128), (20, 2, 64, 128), (22, 40, 256), (22, 40, 256)],
    )


def solution(mesh):
    placed = P(ALL, None, None, None)
    return jax.shard_map(
        body, mesh=mesh, in_specs=(placed, placed, placed, P()), out_specs=placed, check_vma=False
    )
```

```python
import jax
import jax.numpy as jnp
from jax import lax
from jax.experimental import pallas as pl
from jax.experimental.pallas import tpu as pltpu
from jax.sharding import PartitionSpec as P

LB = ("level", "bottom")
ALL = ("slab", "level", "bottom")
SLABS = 16
OWN = 5
F32 = jnp.float32
VMEM_SPEC = pl.BlockSpec(memory_space=pltpu.VMEM)
SMEM_SPEC = pl.BlockSpec(memory_space=pltpu.SMEM)
EXACT = lax.Precision.HIGHEST


def run(kernel, outs, smem, vmem, scratch=()):
    shapes = [jax.ShapeDtypeStruct(s, F32) for s in outs]
    single = len(shapes) == 1
    return pl.pallas_call(
        kernel,
        out_shape=shapes[0] if single else shapes,
        in_specs=[SMEM_SPEC] * len(smem) + [VMEM_SPEC] * len(vmem),
        out_specs=VMEM_SPEC if single else [VMEM_SPEC] * len(shapes),
        scratch_shapes=[pltpu.VMEM(s, F32) for s in scratch],
        compiler_params=pltpu.CompilerParams(vmem_limit_bytes=20 << 20),
    )(*smem, *vmem)


def iota(shape, dim):
    return lax.broadcasted_iota(jnp.int32, shape, dim)


def odd(rows, cols):
    return ((iota((rows, cols), 0) + iota((rows, cols), 1)) & 1) == 1


def place_of(meta, bricks):
    slab, me = meta[0], meta[1]
    place = jnp.int32(0)
    for i in range(8):
        place = place + jnp.where(bricks[slab, i] == me, i, 0)
    return slab, me, place & 1, (place >> 1) & 1, place >> 2


def is_zero(scalar, shape=(8, 128)):
    return jnp.full(shape, scalar, jnp.int32) == 0


ARRAYS = 5
FACE = 17
SENT_Y, SENT_X, SENT = 17, 26, 29
GOT_ROWS, GOT_STRIPS, GOT_Y, GOT_X, GOT = 17, 20, 22, 31, 34
ROOM = (2, 4, 7)


def face_planes(j):
    return [(1 + j, 0), (1 + j, 1), (1 + j, 2), (0, j)]


def merge_strips(placed, base=None):
    group = iota((8, 128), 1) // 8
    total = jnp.zeros((8, 128), F32) if base is None else base
    for pos, strip in placed:
        moved = pltpu.roll(strip, 8 * pos, 1) if pos else strip
        total = jnp.where(group == pos, moved, total)
    return total


def swap_lanes(cells):
    lane = iota(cells.shape, 1)
    return jnp.where((lane & 1) == 0, pltpu.roll(cells, cells.shape[1] - 1, 1), pltpu.roll(cells, 1, 1))


def pack_shell(get, out, bit_x, bit_y):
    x0, y0 = is_zero(bit_x), is_zero(bit_y)
    mask = odd(32, 128)
    row = iota((8, 128), 0)
    free = (y0 & (row < 2)) | (jnp.logical_not(y0) & (row >= 6))
    for k in range(8):
        high, j = k >= 4, k % 4
        for i, (c, far) in enumerate(face_planes(j)):
            out[k, 4 * i : 4 * i + 4] = get(c, 15 - far if high else far).reshape(4, 8, 128)
        t = 12 if high else 3
        one, two = get(1, t), swap_lanes(get(3, t))
        both = jnp.where(mask, one, two) if high else jnp.where(mask, two, one)
        out[k, 16] = both[8 * j : 8 * j + 8]
        strips, rows = [], []
        for tl in range(2):
            for c in range(ARRAYS):
                v = get(c, 2 * k + tl)
                rows.append(jnp.where(y0, v[24:32], v[0:8]))
                for g in range(4):
                    tile = v[8 * g : 8 * g + 8]
                    strips.append(jnp.where(x0, pltpu.roll(tile, 8, 1), tile))
        last = rows.pop()
        for i, at in enumerate(ROOM):
            rows[at] = jnp.where(free, pltpu.roll(last, 6 - 2 * i, 0), rows[at])
        for i, tile in enumerate(rows):
            out[k, SENT_Y + i] = tile
        for i in range(3):
            out[k, SENT_X + i] = merge_strips(list(enumerate(strips[16 * i : 16 * i + 16])))


def cross_kernel(meta, bricks, recv, out):
    slab, me = meta[0], meta[1]
    for i in range(4):
        src = jnp.where(me >= 4, bricks[slab, 4 + i], bricks[slab, i])
        out[i] = recv[src, 0:FACE]


def mid_kernel(meta, bricks, recv, cross, out, faces):
    slab, me = meta[0], meta[1]
    faces[0:8] = recv[:, 0:FACE]
    faces[8:12] = cross[...]
    row = iota((8, 128), 0)
    for p in range(8):
        bx, by, bz = p & 1, (p >> 1) & 1, p >> 2
        dest = bricks[slab, p]
        same = me >= 4 if bz else me < 4

        def src(q):
            return jnp.where(same, bricks[slab, (q & 3) + 4 * (1 - bz)], 8 + (q & 3))

        def strip_of(tile):
            return pltpu.roll(tile, 8, 1) if bx else tile

        def rows_of(at):
            one, two, three, last = (faces[at, 4 * i + (3 if by else 0)] for i in range(4))
            if by:
                shared = jnp.where(row >= 3, two, pltpu.roll(three, 3, 0))
            else:
                shared = jnp.where(row < 5, two, pltpu.roll(three, 5, 0))
            return [one, shared, last]

        at_own, at_y, at_x, at_xy = src(p), src(p ^ 2), src(p ^ 1), src(p ^ 3)
        out[dest, 0:FACE] = faces[at_own]
        for i, tile in enumerate(rows_of(at_y)):
            out[dest, GOT_ROWS + i] = tile
        strips = [strip_of(faces[at_x, i]) for i in range(16)] + [strip_of(tile) for tile in rows_of(at_xy)]
        from_y, from_x, from_xy = bricks[slab, p ^ 2], bricks[slab, p ^ 1], bricks[slab, p ^ 3]
        strips += [strip_of(recv[from_xy, SENT_Y + i]) for i in range(SENT_X - SENT_Y)]
        for i in range(2):
            out[dest, GOT_STRIPS + i] = merge_strips(list(enumerate(strips[16 * i : 16 * i + 16])))
        out[dest, GOT_Y:GOT_X] = recv[from_y, SENT_Y:SENT_X]
        out[dest, GOT_X:GOT] = recv[from_x, SENT_X:SENT]


def unpack_shell(recv, grids, bit_x, bit_y):
    row, lane = iota((8, 128), 0), iota((8, 128), 1)
    x0, y0 = is_zero(bit_x), is_zero(bit_y)
    in_x = (x0 & (lane < 8)) | (jnp.logical_not(x0) & (lane >= 120))
    five = (y0 & (row < 5)) | (jnp.logical_not(y0) & (row >= 3))
    three = (y0 & (row < 3)) | (jnp.logical_not(y0) & (row >= 5))
    seven = (y0 & (row != 7)) | (jnp.logical_not(y0) & (row != 0))
    mask = odd(8, 128)

    def cut(c, tile):
        return jnp.where(seven, tile, 0.0) if c >= 3 else tile

    def strip(tile, pos):
        shift = (jnp.where(bit_x == 0, 0, 120) + 128 - 8 * pos) % 128
        return jnp.where(in_x, pltpu.roll(tile, shift, 1), 0.0)

    def rows_of(tiles):
        one, shared, last = tiles
        moved = jnp.where(y0, pltpu.roll(shared, 3, 0), pltpu.roll(shared, 5, 0))
        return [one, jnp.where(five, shared, 0.0), jnp.where(three, moved, 0.0), last]

    def with_last(tiles):
        pair = jnp.where(y0, row >> 1, (row >> 1) - 1)
        last = jnp.zeros((8, 128), F32)
        for i, at in enumerate(ROOM):
            last = jnp.where(pair == i, pltpu.roll(tiles[at], 2 + 2 * i, 0), last)
        return tiles + [last]

    for k in range(8):
        high, j = k >= 4, k % 4
        rows = rows_of([recv[k, GOT_ROWS + i] for i in range(3)])
        sides = rows_of([strip(recv[k, GOT_STRIPS + 1], i) for i in range(3)])
        for i, (c, far) in enumerate(face_planes(j)):
            at = OWN - 1 - far if high else OWN + 16 + far
            for g in range(4):
                grids[c][at, 8 * g : 8 * g + 8, 0:128] = recv[k, 4 * i + g]
                grids[c][at, 8 * g : 8 * g + 8, 128:256] = strip(recv[k, GOT_STRIPS], 4 * i + g)
            grids[c][at, 32:40, 0:128] = cut(c, rows[i])
            grids[c][at, 32:40, 128:256] = cut(c, sides[i])
        at = 1 if high else 24
        both = recv[k, 16]
        other = swap_lanes(both)
        other = jnp.where(mask, other, 0.0) if high else jnp.where(mask, 0.0, other)
        for c, cells in ((1, both), (3, other)):
            grids[c][at, 8 * j : 8 * j + 8, 0:128] = cells
            grids[c][at, 8 * j : 8 * j + 8, 128:256] = jnp.zeros((8, 128), F32)
            grids[c][at, 32:40] = jnp.zeros((8, 256), F32)
        rows = with_last([recv[k, GOT_Y + i] for i in range(GOT_X - GOT_Y)])
        sides = with_last([strip(recv[k, GOT_STRIPS + 1], 3 + i) for i in range(GOT_X - GOT_Y)])
        for tl in range(2):
            for c in range(ARRAYS):
                i = tl * ARRAYS + c
                at = OWN + 2 * k + tl
                grids[c][at, 32:40, 0:128] = cut(c, rows[i])
                grids[c][at, 32:40, 128:256] = cut(c, sides[i])
                for g in range(4):
                    n = 4 * i + g
                    side = strip(recv[k, GOT_X + n // 16], n % 16)
                    grids[c][at, 8 * g : 8 * g + 8, 128:256] = side


def pair_of(cells, t, red, mask):
    low, high = cells[0, 2 * t], cells[0, 2 * t + 1]
    return jnp.where(mask, high, low) if red else jnp.where(mask, low, high)


def pack_bottom_coef(a, ac, small):
    for i in range(8):
        planes = (a[0, 4 * i] + a[0, 4 * i + 1]) + (a[0, 4 * i + 2] + a[0, 4 * i + 3])
        small[i] = planes
    rows = []
    for i in range(8):
        first = small[i, pl.ds(0, 8, stride=4), :] + small[i, pl.ds(1, 8, stride=4), :]
        rows.append(first + (small[i, pl.ds(2, 8, stride=4), :] + small[i, pl.ds(3, 8, stride=4), :]))
    fold = pick(128, 128, lambda r, c: (r >> 2) == (c & 31)) * (1.0 / 64)
    cells = jnp.dot(jnp.concatenate(rows, 0), fold, precision=EXACT, preferred_element_type=F32)
    group = iota((8, 128), 1) >> 5
    for h in range(2):
        tile = cells[32 * h : 32 * h + 8]
        for j in range(1, 4):
            tile = jnp.where(group == j, cells[32 * h + 8 * j : 32 * h + 8 * j + 8], tile)
        ac[8, 8 * h : 8 * h + 8] = tile


def pack_coarse(planes, small, out):
    twice = pick(128, 128, lambda r, c: (r >> 1) == (c & 63)) * 0.125
    row, lane = iota((16, 128), 0), iota((16, 128), 1)
    even = ((row + lane + (lane >> 6)) & 1) == 0
    for t in range(16):
        small[16 * t : 16 * t + 16] = planes[t, pl.ds(0, 16, stride=2), :] + planes[t, pl.ds(1, 16, stride=2), :]
    summed = jnp.dot(small[...], twice, precision=EXACT, preferred_element_type=F32)
    summed = summed.reshape(16, 16, 128)
    for j in range(8):
        out[j] = jnp.where(even, summed[2 * j], summed[2 * j + 1])


def first_kernel(meta, bricks, u, f, a, out, ac, small, planes, rows, inverse):
    _, _, bit_x, bit_y, _ = place_of(meta, bricks)
    mask = odd(32, 128)
    inverse[...] = 1.0 / (a[...] + 6.0)
    sources = ((u, False), (f, True), (f, False), (inverse, True), (inverse, False))

    def get(c, t):
        return pair_of(sources[c][0], t, sources[c][1], mask)

    pack_shell(get, out, bit_x, bit_y)
    pack_bottom_coef(a, ac, small)
    for t in range(16):
        planes[t] = a[0, 2 * t] + a[0, 2 * t + 1]
    pack_coarse(planes, rows, ac)


def around(src, k, red, mask, edges, cut=None):
    here = src[k]
    rows, cols = here.shape
    above, below = src[k + 1], src[k - 1]
    other = jnp.where(mask, above, below) if red else jnp.where(mask, below, above)
    up, down = pltpu.roll(here, 1, 0), pltpu.roll(here, rows - 1, 0)
    left, right = pltpu.roll(here, 1, 1), pltpu.roll(here, cols - 1, 1)
    if edges:
        row, lane = iota((rows, cols), 0), iota((rows, cols), 1)
        up, down = jnp.where(row == 0, 0.0, up), jnp.where(row == rows - 1, 0.0, down)
        if edges == 2:
            left, right = jnp.where(lane == 0, 0.0, left), jnp.where(lane == cols - 1, 0.0, right)
    if cut is not None:
        up, down = jnp.where(cut[0], 0.0, up), jnp.where(cut[1], 0.0, down)
    return ((here + other) + (up + down)) + (left + right)


def half_sweep(dst, src, force, inverse, lo, hi, red, mask, scale, edges, cut=None):
    def step(k, carry):
        total = around(src, k, red, mask, edges, cut)
        if scale != 1.0:
            total = scale * total
        dst[k] = (force[k] + total) * inverse[k]
        return carry

    lax.fori_loop(lo, hi, step, 0, unroll=True)


def select_dot(cells, chosen):
    half, total = chosen.astype(jnp.bfloat16), None
    for _ in range(3):
        part = cells.astype(jnp.bfloat16)
        cells = cells - part.astype(F32)
        moved = jnp.dot(part, half, preferred_element_type=F32)
        total = moved if total is None else total + moved
    return total


def pick(rows, cols, keep):
    return jnp.where(keep(iota((rows, cols), 0), iota((rows, cols), 1)), 1.0, 0.0).astype(F32)


def fine_down_kernel(meta, bricks, u, f, a, recv, rc, u_b, f_r, f_b, i_r, i_b, u_r, resid, small):
    _, _, bit_x, bit_y, _ = place_of(meta, bricks)
    own = odd(32, 128)
    for t in range(16):
        here = (OWN + t, slice(0, 32), slice(0, 128))
        u_b[here] = pair_of(u, t, False, own)
        f_r[here], f_b[here] = pair_of(f, t, True, own), pair_of(f, t, False, own)
        i_r[here], i_b[here] = 1.0 / (pair_of(a, t, True, own) + 6.0), 1.0 / (pair_of(a, t, False, own) + 6.0)
    unpack_shell(recv, (u_b, f_r, f_b, i_r, i_b), bit_x, bit_y)
    zero = jnp.zeros((40, 256), F32)
    for k in (0, 25):
        u_r[k] = zero
        u_b[k] = zero
    for k in (1, 24):
        f_b[k] = zero
        i_b[k] = zero
    row = iota((40, 256), 0)
    y0 = is_zero(bit_y, (40, 256))
    y1 = jnp.logical_not(y0)
    mask = odd(40, 256)
    cut = (y0 & (row == 0), y1 & (row == 31))
    half_sweep(u_r, u_b, f_r, i_r, 1, 25, True, mask, 1.0, 0, cut)
    half_sweep(u_b, u_r, f_b, i_b, 1, 25, False, mask, 1.0, 0)
    half_sweep(u_r, u_b, f_r, i_r, 2, 24, True, mask, 1.0, 0)
    half_sweep(u_b, u_r, f_b, i_b, 3, 23, False, mask, 1.0, 0)
    for t in range(16):
        total = around(u_b, OWN + t, True, mask, 0)[0:32, 0:128]
        diag = pair_of(a, t, True, own) + 6.0
        here = (OWN + t, slice(0, 32), slice(0, 128))
        resid[t] = f_r[here] + total - diag * u_r[here]
    pack_coarse(resid, small, rc)


def slot_of(member, me):
    return jnp.where((member >> 2) == (me >> 2), 0, 4) + ((me - member) & 3)


def faces_kernel(meta, bricks, *refs):
    boxes, (out, held) = refs[:8], refs[8:]
    slab, me = meta[0], meta[1]
    for i, box in enumerate(boxes):
        held[i] = box[...]
    start = jnp.where(me < 4, 3, 0)
    for i in range(4):
        member = jnp.where(me < 4, bricks[slab, 4 + i], bricks[slab, i])
        out[i, 0:5] = held[slot_of(member, me), pl.ds(start, 5)]
        for j in range(5, out.shape[1]):
            out[i, j] = held[slot_of(bricks[slab, 2 * i + j - 5], me), 8]


def sort_sides(me, one, two, low, high):
    @pl.when(me < 4)
    def _():
        low[...] = one[...]
        high[...] = two[...]

    @pl.when(me >= 4)
    def _():
        low[...] = two[...]
        high[...] = one[...]


def assemble(meta, bricks, boxes, one, two, red, black, held, low, high):
    slab, me = meta[0], meta[1]
    for i, box in enumerate(boxes):
        held[i] = box[...]
    sort_sides(me, one, two, low, high)
    left = iota((16, 128), 1) < 64

    def put(k, by, west, east):
        rows = slice(16 * by, 16 * by + 16)
        red[k, rows] = jnp.where(left, west, pltpu.roll(east, 64, 1))
        black[k, rows] = jnp.where(left, pltpu.roll(west, 64, 1), east)

    for by in range(2):
        for bz in range(2):
            west = slot_of(bricks[slab, 2 * by + 4 * bz], me)
            east = slot_of(bricks[slab, 2 * by + 4 * bz + 1], me)
            for j in range(8):
                put(6 + 8 * bz + j, by, held[west, j], held[east, j])
        for j in range(5):
            put(1 + j, by, low[2 * by, j], low[2 * by + 1, j])
            put(22 + j, by, high[2 * by, j], high[2 * by + 1, j])


def to_bottom(planes, small, half):
    for n in range(22):
        small[16 * n : 16 * n + 16] = planes[n, pl.ds(0, 16, stride=2), :] + planes[n, pl.ds(1, 16, stride=2), :]
    fold = pick(128, 128, lambda r, c: (r >> 1) == c - 64 * half) * 0.125
    return jnp.dot(small[...], fold, precision=EXACT, preferred_element_type=F32).reshape(22, 16, 128)


def coarse_coef_kernel(meta, bricks, *refs):
    boxes, (one, two) = refs[:8], refs[8:10]
    a_r, i_r, i_b, ab, coef = refs[10:15]
    held, low, high, a_b, planes, small = refs[15:]
    slab, me = meta[0], meta[1]
    assemble(meta, bricks, boxes, one, two, a_r, a_b, held, low, high)
    for p in range(8):
        coef[0, p] = low[p >> 1, 5 + (p & 1)]
        coef[1, p] = held[slot_of(bricks[slab, p], me), 8]
        coef[2, p] = high[p >> 1, 5 + (p & 1)]
    for k in range(1, 27):
        keep = jnp.full((32, 128), 0, jnp.int32) == 0
        if k < 6:
            keep = jnp.logical_not(is_zero(slab, (32, 128)))
        if k >= 22:
            keep = jnp.logical_not(is_zero(slab - (SLABS - 1), (32, 128)))
        i_r[k] = jnp.where(keep, 1.0 / (a_r[k] + 1.5), 0.0)
        i_b[k] = jnp.where(keep, 1.0 / (a_b[k] + 1.5), 0.0)
    for n in range(22):
        planes[n] = a_r[3 + n] + a_b[3 + n]
    ab[...] = to_bottom(planes, small, 1)


def coarse_down_kernel(meta, bricks, *refs):
    boxes, (one, two, weights, a_r, i_r, i_b, ab) = refs[:8], refs[8:15]
    rb, rb_send, part, e_b, r_r, r_b = refs[15:21]
    held, low, high, e_r, resid, small = refs[21:]
    me = meta[1]
    assemble(meta, bricks, boxes, one, two, r_r, r_b, held, low, high)
    for k in (0, 27):
        e_r[k] = jnp.zeros((32, 128), F32)
        e_b[k] = jnp.zeros((32, 128), F32)
    for k in range(1, 27):
        e_r[k] = r_r[k] * i_r[k]
    mask = odd(32, 128)
    half_sweep(e_b, e_r, r_b, i_b, 1, 27, False, mask, 0.25, 2)
    half_sweep(e_r, e_b, r_r, i_r, 1, 27, True, mask, 0.25, 2)
    half_sweep(e_b, e_r, r_b, i_b, 1, 27, False, mask, 0.25, 2)
    for n in range(22):
        k = n + 3
        total = 0.25 * around(e_b, k, True, mask, 2)
        resid[n] = r_r[k] + total - (a_r[k] + 1.5) * e_r[k]
    rb[...] = to_bottom(resid, small, 0) + ab[...]
    rb_send[0:18] = rb[pl.ds(jnp.where(me < 4, 1, 3), 18)]
    total = jnp.zeros((16, 128), F32)
    for i in range(16):
        total = total + rb[3 + i] * weights[i]
    total = total[0:8] + total[8:16]
    part[...] = total
    rb_send[18, 0:8] = total
    rb_send[18, 8:16] = total


def bottom_kernel(meta, rb, one, two, es, e_r, e_b, g_r, g_b, i_r, i_b, low, high):
    slab, me = meta[0], meta[1]
    sort_sides(me, one, two, low, high)
    mask = odd(16, 128)
    left = iota((16, 128), 1) < 64
    zero = jnp.zeros((16, 128), F32)
    for k in (0, 27):
        e_r[k] = zero
        e_b[k] = zero
    for j in range(26):
        planes = []
        for n in (2 * j, 2 * j + 1):
            planes.append(low[n] if n < 18 else rb[n - 15] if n < 34 else high[n - 34])
        keep = left
        if j < 9:
            keep = left & jnp.logical_not(is_zero(slab, (16, 128)))
        if j >= 17:
            keep = left & jnp.logical_not(is_zero(slab - (SLABS - 1), (16, 128)))
        for red in (True, False):
            cells = jnp.where(mask, planes[1], planes[0]) if red else jnp.where(mask, planes[0], planes[1])
            force = jnp.where(left, cells, 0.0)
            inverse = jnp.where(keep, 1.0 / (pltpu.roll(cells, 64, 1) + 0.375), 0.0)
            if red:
                g_r[1 + j], i_r[1 + j], e_r[1 + j] = force, inverse, force * inverse
            else:
                g_b[1 + j], i_b[1 + j] = force, inverse
    for n in range(2, 17):
        far = (20 - n) // 2
        if n % 2:
            half_sweep(e_r, e_b, g_r, i_r, 10 - far, 18 + far, True, mask, 0.0625, 1)
        else:
            half_sweep(e_b, e_r, g_b, i_b, 10 - far, 18 + far, False, mask, 0.0625, 1)
    for i in range(22):
        k, upper = (15 + i) // 2 + 1, (15 + i) % 2
        es[i] = jnp.where(mask, e_r[k], e_b[k]) if upper else jnp.where(mask, e_b[k], e_r[k])


def weights_kernel(meta, coef, out, t_r, t_b, w_r, w_b, i_r, i_b):
    slab = meta[0]
    lane = iota((8, 128), 1)

    def plane(part, z):
        rows = []
        for by in range(2):
            place, shift = 4 * (z >> 3) + 2 * by, 32 * (z & 3)
            here = slice(8 * ((z & 7) >> 2), 8 * ((z & 7) >> 2) + 8)
            west = pltpu.roll(coef[part, place, here], (128 - shift) % 128, 1)
            east = pltpu.roll(coef[part, place + 1, here], (160 - shift) % 128, 1)
            rows.append(jnp.where(lane < 32, west, east))
        return jnp.concatenate(rows, 0)

    mask = odd(16, 128)
    left = iota((16, 128), 1) < 64
    zero = jnp.zeros((16, 128), F32)
    for k in (0, 25):
        t_r[k] = zero
        t_b[k] = zero
    for j in range(24):
        lower, upper = (plane((2 * j + i) // 16, (2 * j + i) % 16) for i in range(2))
        keep = left
        if j < 8:
            keep = left & jnp.logical_not(is_zero(slab, (16, 128)))
        if j >= 16:
            keep = left & jnp.logical_not(is_zero(slab - (SLABS - 1), (16, 128)))
        i_r[1 + j] = jnp.where(keep, 1.0 / (jnp.where(mask, upper, lower) + 0.375), 0.0)
        i_b[1 + j] = jnp.where(keep, 1.0 / (jnp.where(mask, lower, upper) + 0.375), 0.0)
    for k in range(1, 25):
        t_b[k] = i_b[k]
        w_b[k] = i_b[k]
    for k in range(1, 25):
        t = i_r[k] * (1.0 + 0.0625 * around(t_b, k, True, mask, 1))
        t_r[k] = t
        w_r[k] = t

    def sweep(n, carry):
        for k in range(1, 25):
            t = i_b[k] * (0.0625 * around(t_r, k, False, mask, 1))
            t_b[k] = t
            w_b[k] = w_b[k] + t
        for k in range(1, 25):
            t = i_r[k] * (0.0625 * around(t_b, k, True, mask, 1))
            t_r[k] = t
            w_r[k] = w_r[k] + t
        return carry

    lax.fori_loop(0, 7, sweep, 0)
    for j in range(8):
        red, black = w_r[9 + j], w_b[9 + j]
        out[2 * j] = jnp.where(mask, black, red)
        out[2 * j + 1] = jnp.where(mask, red, black)


def up_kernel(
    meta, bricks, sum_0, sum_1, sum_2, sum_3, es, ec_b, r_r, r_b, ci_r, ci_b, u1_b, f_r, f_b, i_r, i_b, out,
    e_r, e_b, small, wide, planes, tall, u_r, u_b,
):
    slab, _, bit_x, bit_y, bit_z = place_of(meta, bricks)
    total = (sum_0[...] + sum_1[...]) + (sum_2[...] + sum_3[...])
    mean = jnp.sum(total) * (1.0 / (SLABS * 16 * 16 * 64))
    base = 8 * bit_z
    no_low = jnp.where((slab == 0) & (bit_z == 0), 0, 1)
    no_high = jnp.where((slab == SLABS - 1) & (bit_z == 1), 0, 1)
    for j in range(14):
        shifted = es[base + j] - mean
        if j < 3:
            shifted = jnp.where(is_zero(no_low, (16, 128)), 0.0, shifted)
        if j >= 11:
            shifted = jnp.where(is_zero(no_high, (16, 128)), 0.0, shifted)
        small[16 * j : 16 * j + 16] = shifted
    spread = pick(128, 128, lambda r, c: r == (c >> 1))
    small[...] = select_dot(small[...], spread)
    for j in range(14):
        rows = small[16 * j : 16 * j + 16]
        wide[j, pl.ds(0, 16, stride=2), :] = rows
        wide[j, pl.ds(1, 16, stride=2), :] = rows
    for k in (0, 15):
        e_r[k] = jnp.zeros((32, 128), F32)
        e_b[k] = jnp.zeros((32, 128), F32)
    for j in range(14):
        e_b[1 + j] = ec_b[base + 3 + j] + wide[j]
    coarse = odd(32, 128)
    r_r, r_b, ci_r, ci_b = (grid.at[pl.ds(base + 2, 16)] for grid in (r_r, r_b, ci_r, ci_b))
    half_sweep(e_r, e_b, r_r, ci_r, 1, 15, True, coarse, 0.25, 2)
    half_sweep(e_b, e_r, r_b, ci_b, 2, 14, False, coarse, 0.25, 2)
    half_sweep(e_r, e_b, r_r, ci_r, 2, 14, True, coarse, 0.25, 2)
    half_sweep(e_b, e_r, r_b, ci_b, 3, 13, False, coarse, 0.25, 2)
    for n in range(20):
        k, upper = n // 2 + 3, n % 2
        red, black = e_r[k], e_b[k]
        planes[32 * n : 32 * n + 32] = jnp.where(coarse, red, black) if upper else jnp.where(coarse, black, red)

    lane = iota((128, 256), 1)
    x0 = is_zero(bit_x, (128, 256))
    start = jnp.where(lane < 128, 64 * bit_x + (lane >> 1), (lane >> 1) + jnp.where(x0, 0, -64))
    usable = (lane < 128) | (x0 & (lane < 136)) | (jnp.logical_not(x0) & (lane >= 248))
    spread = jnp.where(usable & (iota((128, 256), 0) == start), 1.0, 0.0).astype(F32)
    tall_rows = select_dot(planes[...], spread)
    for n in range(20):
        rows = tall_rows[32 * n : 32 * n + 32]
        for h in range(2):
            tall[n, h, pl.ds(0, 32, stride=2), :] = rows[:, 128 * h : 128 * h + 128]
            tall[n, h, pl.ds(1, 32, stride=2), :] = rows[:, 128 * h : 128 * h + 128]
    for k in (0, 21):
        u_r[k] = jnp.zeros((40, 256), F32)
        u_b[k] = jnp.zeros((40, 256), F32)
    row = iota((8, 128), 0)
    y0 = is_zero(bit_y)
    in_y = (y0 & (row != 7)) | (jnp.logical_not(y0) & (row != 0))
    own_start = pl.multiple_of(32 * bit_y, 32)
    side_start = pl.multiple_of(32 - 8 * bit_y, 8)
    for n in range(20):
        for h in range(2):
            lanes = slice(128 * h, 128 * h + 128)
            side = jnp.where(in_y, tall[n, h, pl.ds(side_start, 8), :], 0.0)
            u_b[1 + n, 0:32, lanes] = u1_b[3 + n, 0:32, lanes] + tall[n, h, pl.ds(own_start, 32), :]
            u_b[1 + n, 32:40, lanes] = u1_b[3 + n, 32:40, lanes] + side
    mask = odd(40, 256)
    f_r, f_b, i_r, i_b = (grid.at[2:24] for grid in (f_r, f_b, i_r, i_b))
    half_sweep(u_r, u_b, f_r, i_r, 1, 21, True, mask, 1.0, 0)
    half_sweep(u_b, u_r, f_b, i_b, 2, 20, False, mask, 1.0, 0)
    half_sweep(u_r, u_b, f_r, i_r, 2, 20, True, mask, 1.0, 0)
    half_sweep(u_b, u_r, f_b, i_b, 3, 19, False, mask, 1.0, 0)
    own = odd(32, 128)
    for t in range(16):
        red, black = u_r[3 + t, 0:32, 0:128], u_b[3 + t, 0:32, 0:128]
        out[0, 2 * t] = jnp.where(own, black, red)
        out[0, 2 * t + 1] = jnp.where(own, red, black)


def swap_cores(x):
    return lax.ppermute(x, "level", [(0, 1), (1, 0)])


def to_slabs(x, up_first, wrap=False):
    pairs = []
    for s in range(SLABS if wrap else SLABS - 1):
        for m in range(8):
            low, high = s * 8 + m, (s + 1) % SLABS * 8 + m
            pairs.append((low, high) if (m < 4) == up_first else (high, low))
    return lax.ppermute(x, ALL, pairs)


def around_chips(x):
    return [x] + [lax.ppermute(x, "bottom", [(i, (i + d) % 4) for i in range(4)]) for d in range(1, 4)]


def both_cores(boxes):
    return boxes + [swap_cores(box) for box in boxes]


def fours_apart(x):
    beside = [(8 * s + m, 8 * ((s + (4 if m < 4 else 12)) % SLABS) + m) for s in range(SLABS) for m in range(8)]
    across = [(s, (s + 8) % SLABS) for s in range(SLABS)]
    return lax.ppermute(x, ALL, beside), lax.ppermute(x, "slab", across)


def among(x):
    return lax.all_to_all(x, LB, split_axis=0, concat_axis=0, tiled=True)


def body(u_init, source, coeffs, brick_map):
    meta = jnp.stack([lax.axis_index("slab"), lax.axis_index(LB)]).astype(jnp.int32)
    smem = [meta, brick_map]
    fine = (26, 40, 256)
    packed, ac = run(
        first_kernel, [(8, SENT, 8, 128), (9, 16, 128)], smem, [u_init, source, coeffs],
        [(8, 32, 128), (16, 32, 128), (256, 128), (1, 32, 32, 128)],
    )
    got = among(packed)
    leaving = run(cross_kernel, [(4, FACE, 8, 128)], smem, [got])
    leaving, ac = lax.optimization_barrier((leaving, ac))
    cross = to_slabs(leaving, False)
    ac_boxes = around_chips(ac)
    sent = run(mid_kernel, [(8, GOT, 8, 128)], smem, [got, cross], [(12, FACE, 8, 128)])
    sent, *ac_boxes = lax.optimization_barrier((sent, *ac_boxes))
    halo = among(sent)
    faces = (4, 5, 16, 128)
    coarse = (28, 32, 128)
    held = [(8, 8, 16, 128), faces, faces]
    ac_boxes = both_cores(ac_boxes)
    ac_held = [(8, 9, 16, 128), (4, 7, 16, 128), (4, 7, 16, 128)]
    ac_cross = to_slabs(run(faces_kernel, ac_held[1:2], smem, ac_boxes, ac_held[:1]), True)
    ac_other = swap_cores(ac_cross)
    halo, ac_cross, ac_other = lax.optimization_barrier((halo, ac_cross, ac_other))
    rc, u_b, f_r, f_b, i_r, i_b = run(
        fine_down_kernel, [(8, 16, 128)] + [fine] * 5, smem, [u_init, source, coeffs, halo],
        [fine, (16, 32, 128), (256, 128)],
    )
    boxes = both_cores(around_chips(rc))
    leaving = run(faces_kernel, [faces], smem, boxes, held[:1])
    leaving, ac_cross, ac_other = lax.optimization_barrier((leaving, ac_cross, ac_other))
    cross = to_slabs(leaving, True)
    ca_r, ci_r, ci_b, ab, coef = run(
        coarse_coef_kernel, [coarse] * 3 + [(22, 16, 128), (3, 8, 16, 128)], smem, ac_boxes + [ac_cross, ac_other],
        ac_held + [coarse, (22, 32, 128), (352, 128)],
    )
    weights = run(weights_kernel, [(16, 16, 128)], [meta], [coef], [(26, 16, 128)] * 6)
    cross, weights, ca_r, ci_r, ci_b, ab = lax.optimization_barrier((cross, weights, ca_r, ci_r, ci_b, ab))
    rb, rb_send, part, ec_b, r_r, r_b = run(
        coarse_down_kernel, [(22, 16, 128), (19, 16, 128), (8, 128)] + [coarse] * 3, smem,
        boxes + [cross, swap_cores(cross), weights, ca_r, ci_r, ci_b, ab],
        held + [coarse, (22, 32, 128), (352, 128)],
    )
    cross = to_slabs(rb_send, True, wrap=True)
    far = lax.ppermute(part, "slab", [(s, (s - 2) % SLABS) for s in range(SLABS)])
    cross, far = lax.optimization_barrier((cross, far))
    other = swap_cores(cross)
    part = (part + far) + (cross[18, 0:8] + other[18, 0:8])
    near, far = fours_apart(part)
    sums = [part, near, far, swap_cores(near)]
    bottom = (28, 16, 128)
    es = run(
        bottom_kernel, [(22, 16, 128)], [meta], [rb, cross, other],
        [bottom] * 6 + [(19, 16, 128)] * 2,
    )
    return run(
        up_kernel, [(1, 32, 32, 128)], smem,
        sums + [es, ec_b, r_r, r_b, ci_r, ci_b, u_b, f_r, f_b, i_r, i_b],
        [(16, 32, 128)] * 2 + [(224, 128), (14, 32, 128), (640, 128), (20, 2, 64, 128), (22, 40, 256), (22, 40, 256)],
    )


def solution(mesh):
    placed = P(ALL, None, None, None)
    return jax.shard_map(
        body, mesh=mesh, in_specs=(placed, placed, placed, P()), out_specs=placed, check_vma=False
    )
```

```python
import jax
import jax.numpy as jnp
from jax import lax
from jax.experimental import pallas as pl
from jax.experimental.pallas import tpu as pltpu
from jax.sharding import PartitionSpec as P

LB = ("level", "bottom")
ALL = ("slab", "level", "bottom")
SLABS = 16
OWN = 5
F32 = jnp.float32
VMEM_SPEC = pl.BlockSpec(memory_space=pltpu.VMEM)
SMEM_SPEC = pl.BlockSpec(memory_space=pltpu.SMEM)
EXACT = lax.Precision.HIGHEST


def run(kernel, outs, smem, vmem, scratch=()):
    shapes = [jax.ShapeDtypeStruct(s, F32) for s in outs]
    single = len(shapes) == 1
    return pl.pallas_call(
        kernel,
        out_shape=shapes[0] if single else shapes,
        in_specs=[SMEM_SPEC] * len(smem) + [VMEM_SPEC] * len(vmem),
        out_specs=VMEM_SPEC if single else [VMEM_SPEC] * len(shapes),
        scratch_shapes=[pltpu.VMEM(s, F32) for s in scratch],
        compiler_params=pltpu.CompilerParams(vmem_limit_bytes=20 << 20),
    )(*smem, *vmem)


def iota(shape, dim):
    return lax.broadcasted_iota(jnp.int32, shape, dim)


def odd(rows, cols):
    return ((iota((rows, cols), 0) + iota((rows, cols), 1)) & 1) == 1


def place_of(meta, bricks):
    slab, me = meta[0], meta[1]
    place = jnp.int32(0)
    for i in range(8):
        place = place + jnp.where(bricks[slab, i] == me, i, 0)
    return slab, me, place & 1, (place >> 1) & 1, place >> 2


def is_zero(scalar, shape=(8, 128)):
    return jnp.full(shape, scalar, jnp.int32) == 0


ARRAYS = 5
FACE = 17
SENT_Y, SENT_X, SENT = 17, 26, 29
GOT_ROWS, GOT_STRIPS, GOT_Y, GOT_X, GOT = 17, 20, 22, 31, 34
ROOM = (2, 4, 7)


def face_planes(j):
    return [(1 + j, 0), (1 + j, 1), (1 + j, 2), (0, j)]


def merge_strips(placed, base=None):
    group = iota((8, 128), 1) // 8
    total = jnp.zeros((8, 128), F32) if base is None else base
    for pos, strip in placed:
        moved = pltpu.roll(strip, 8 * pos, 1) if pos else strip
        total = jnp.where(group == pos, moved, total)
    return total


def swap_lanes(cells):
    lane = iota(cells.shape, 1)
    return jnp.where((lane & 1) == 0, pltpu.roll(cells, cells.shape[1] - 1, 1), pltpu.roll(cells, 1, 1))


def pack_shell(get, out, bit_x, bit_y):
    x0, y0 = is_zero(bit_x), is_zero(bit_y)
    mask = odd(32, 128)
    row = iota((8, 128), 0)
    free = (y0 & (row < 2)) | (jnp.logical_not(y0) & (row >= 6))
    for k in range(8):
        high, j = k >= 4, k % 4
        for i, (c, far) in enumerate(face_planes(j)):
            out[k, 4 * i : 4 * i + 4] = get(c, 15 - far if high else far).reshape(4, 8, 128)
        t = 12 if high else 3
        one, two = get(1, t), swap_lanes(get(3, t))
        both = jnp.where(mask, one, two) if high else jnp.where(mask, two, one)
        out[k, 16] = both[8 * j : 8 * j + 8]
        strips, rows = [], []
        for tl in range(2):
            for c in range(ARRAYS):
                v = get(c, 2 * k + tl)
                rows.append(jnp.where(y0, v[24:32], v[0:8]))
                for g in range(4):
                    tile = v[8 * g : 8 * g + 8]
                    strips.append(jnp.where(x0, pltpu.roll(tile, 8, 1), tile))
        last = rows.pop()
        for i, at in enumerate(ROOM):
            rows[at] = jnp.where(free, pltpu.roll(last, 6 - 2 * i, 0), rows[at])
        for i, tile in enumerate(rows):
            out[k, SENT_Y + i] = tile
        for i in range(3):
            out[k, SENT_X + i] = merge_strips(list(enumerate(strips[16 * i : 16 * i + 16])))


def cross_kernel(meta, bricks, recv, out):
    slab, me = meta[0], meta[1]
    for i in range(4):
        src = jnp.where(me >= 4, bricks[slab, 4 + i], bricks[slab, i])
        out[i] = recv[src, 0:FACE]


def mid_kernel(meta, bricks, recv, cross, out, faces):
    slab, me = meta[0], meta[1]
    faces[0:8] = recv[:, 0:FACE]
    faces[8:12] = cross[...]
    row = iota((8, 128), 0)
    for p in range(8):
        bx, by, bz = p & 1, (p >> 1) & 1, p >> 2
        dest = bricks[slab, p]
        same = me >= 4 if bz else me < 4

        def src(q):
            return jnp.where(same, bricks[slab, (q & 3) + 4 * (1 - bz)], 8 + (q & 3))

        def strip_of(tile):
            return pltpu.roll(tile, 8, 1) if bx else tile

        def rows_of(at):
            one, two, three, last = (faces[at, 4 * i + (3 if by else 0)] for i in range(4))
            if by:
                shared = jnp.where(row >= 3, two, pltpu.roll(three, 3, 0))
            else:
                shared = jnp.where(row < 5, two, pltpu.roll(three, 5, 0))
            return [one, shared, last]

        at_own, at_y, at_x, at_xy = src(p), src(p ^ 2), src(p ^ 1), src(p ^ 3)
        out[dest, 0:FACE] = faces[at_own]
        for i, tile in enumerate(rows_of(at_y)):
            out[dest, GOT_ROWS + i] = tile
        strips = [strip_of(faces[at_x, i]) for i in range(16)] + [strip_of(tile) for tile in rows_of(at_xy)]
        from_y, from_x, from_xy = bricks[slab, p ^ 2], bricks[slab, p ^ 1], bricks[slab, p ^ 3]
        strips += [strip_of(recv[from_xy, SENT_Y + i]) for i in range(SENT_X - SENT_Y)]
        for i in range(2):
            out[dest, GOT_STRIPS + i] = merge_strips(list(enumerate(strips[16 * i : 16 * i + 16])))
        out[dest, GOT_Y:GOT_X] = recv[from_y, SENT_Y:SENT_X]
        out[dest, GOT_X:GOT] = recv[from_x, SENT_X:SENT]


def unpack_shell(recv, grids, bit_x, bit_y):
    row, lane = iota((8, 128), 0), iota((8, 128), 1)
    x0, y0 = is_zero(bit_x), is_zero(bit_y)
    in_x = (x0 & (lane < 8)) | (jnp.logical_not(x0) & (lane >= 120))
    five = (y0 & (row < 5)) | (jnp.logical_not(y0) & (row >= 3))
    three = (y0 & (row < 3)) | (jnp.logical_not(y0) & (row >= 5))
    seven = (y0 & (row != 7)) | (jnp.logical_not(y0) & (row != 0))
    mask = odd(8, 128)

    def cut(c, tile):
        return jnp.where(seven, tile, 0.0) if c >= 3 else tile

    def strip(tile, pos):
        shift = (jnp.where(bit_x == 0, 0, 120) + 128 - 8 * pos) % 128
        return jnp.where(in_x, pltpu.roll(tile, shift, 1), 0.0)

    def rows_of(tiles):
        one, shared, last = tiles
        moved = jnp.where(y0, pltpu.roll(shared, 3, 0), pltpu.roll(shared, 5, 0))
        return [one, jnp.where(five, shared, 0.0), jnp.where(three, moved, 0.0), last]

    def with_last(tiles):
        pair = jnp.where(y0, row >> 1, (row >> 1) - 1)
        last = jnp.zeros((8, 128), F32)
        for i, at in enumerate(ROOM):
            last = jnp.where(pair == i, pltpu.roll(tiles[at], 2 + 2 * i, 0), last)
        return tiles + [last]

    for k in range(8):
        high, j = k >= 4, k % 4
        rows = rows_of([recv[k, GOT_ROWS + i] for i in range(3)])
        sides = rows_of([strip(recv[k, GOT_STRIPS + 1], i) for i in range(3)])
        for i, (c, far) in enumerate(face_planes(j)):
            at = OWN - 1 - far if high else OWN + 16 + far
            for g in range(4):
                grids[c][at, 8 * g : 8 * g + 8, 0:128] = recv[k, 4 * i + g]
                grids[c][at, 8 * g : 8 * g + 8, 128:256] = strip(recv[k, GOT_STRIPS], 4 * i + g)
            grids[c][at, 32:40, 0:128] = cut(c, rows[i])
            grids[c][at, 32:40, 128:256] = cut(c, sides[i])
        at = 1 if high else 24
        both = recv[k, 16]
        other = swap_lanes(both)
        other = jnp.where(mask, other, 0.0) if high else jnp.where(mask, 0.0, other)
        for c, cells in ((1, both), (3, other)):
            grids[c][at, 8 * j : 8 * j + 8, 0:128] = cells
            grids[c][at, 8 * j : 8 * j + 8, 128:256] = jnp.zeros((8, 128), F32)
            grids[c][at, 32:40] = jnp.zeros((8, 256), F32)
        rows = with_last([recv[k, GOT_Y + i] for i in range(GOT_X - GOT_Y)])
        sides = with_last([strip(recv[k, GOT_STRIPS + 1], 3 + i) for i in range(GOT_X - GOT_Y)])
        for tl in range(2):
            for c in range(ARRAYS):
                i = tl * ARRAYS + c
                at = OWN + 2 * k + tl
                grids[c][at, 32:40, 0:128] = cut(c, rows[i])
                grids[c][at, 32:40, 128:256] = cut(c, sides[i])
                for g in range(4):
                    n = 4 * i + g
                    side = strip(recv[k, GOT_X + n // 16], n % 16)
                    grids[c][at, 8 * g : 8 * g + 8, 128:256] = side


def pair_of(cells, t, red, mask):
    low, high = cells[0, 2 * t], cells[0, 2 * t + 1]
    return jnp.where(mask, high, low) if red else jnp.where(mask, low, high)


def pack_bottom_coef(a, ac, small):
    for i in range(8):
        planes = (a[0, 4 * i] + a[0, 4 * i + 1]) + (a[0, 4 * i + 2] + a[0, 4 * i + 3])
        small[i] = planes
    rows = []
    for i in range(8):
        first = small[i, pl.ds(0, 8, stride=4), :] + small[i, pl.ds(1, 8, stride=4), :]
        rows.append(first + (small[i, pl.ds(2, 8, stride=4), :] + small[i, pl.ds(3, 8, stride=4), :]))
    fold = pick(128, 128, lambda r, c: (r >> 2) == (c & 31)) * (1.0 / 64)
    cells = jnp.dot(jnp.concatenate(rows, 0), fold, precision=EXACT, preferred_element_type=F32)
    group = iota((8, 128), 1) >> 5
    for h in range(2):
        tile = cells[32 * h : 32 * h + 8]
        for j in range(1, 4):
            tile = jnp.where(group == j, cells[32 * h + 8 * j : 32 * h + 8 * j + 8], tile)
        ac[8, 8 * h : 8 * h + 8] = tile


def pack_coarse(planes, small, out):
    twice = pick(128, 128, lambda r, c: (r >> 1) == (c & 63)) * 0.125
    row, lane = iota((16, 128), 0), iota((16, 128), 1)
    even = ((row + lane + (lane >> 6)) & 1) == 0
    for t in range(16):
        small[16 * t : 16 * t + 16] = planes[t, pl.ds(0, 16, stride=2), :] + planes[t, pl.ds(1, 16, stride=2), :]
    summed = jnp.dot(small[...], twice, precision=EXACT, preferred_element_type=F32)
    summed = summed.reshape(16, 16, 128)
    for j in range(8):
        out[j] = jnp.where(even, summed[2 * j], summed[2 * j + 1])


def first_kernel(meta, bricks, u, f, a, out, ac, small, planes, rows, inverse):
    _, _, bit_x, bit_y, _ = place_of(meta, bricks)
    mask = odd(32, 128)
    inverse[...] = 1.0 / (a[...] + 6.0)
    sources = ((u, False), (f, True), (f, False), (inverse, True), (inverse, False))

    def get(c, t):
        return pair_of(sources[c][0], t, sources[c][1], mask)

    pack_shell(get, out, bit_x, bit_y)
    pack_bottom_coef(a, ac, small)
    for t in range(16):
        planes[t] = a[0, 2 * t] + a[0, 2 * t + 1]
    pack_coarse(planes, rows, ac)


def around(src, k, red, mask, edges, cut=None):
    here = src[k]
    rows, cols = here.shape
    above, below = src[k + 1], src[k - 1]
    other = jnp.where(mask, above, below) if red else jnp.where(mask, below, above)
    up, down = pltpu.roll(here, 1, 0), pltpu.roll(here, rows - 1, 0)
    left, right = pltpu.roll(here, 1, 1), pltpu.roll(here, cols - 1, 1)
    if edges:
        row, lane = iota((rows, cols), 0), iota((rows, cols), 1)
        up, down = jnp.where(row == 0, 0.0, up), jnp.where(row == rows - 1, 0.0, down)
        if edges == 2:
            left, right = jnp.where(lane == 0, 0.0, left), jnp.where(lane == cols - 1, 0.0, right)
    if cut is not None:
        up, down = jnp.where(cut[0], 0.0, up), jnp.where(cut[1], 0.0, down)
    return ((here + other) + (up + down)) + (left + right)


def half_sweep(dst, src, force, inverse, lo, hi, red, mask, scale, edges, cut=None):
    def step(k, carry):
        total = around(src, k, red, mask, edges, cut)
        if scale != 1.0:
            total = scale * total
        dst[k] = (force[k] + total) * inverse[k]
        return carry

    lax.fori_loop(lo, hi, step, 0, unroll=True)


def select_dot(cells, chosen):
    half, total = chosen.astype(jnp.bfloat16), None
    for _ in range(3):
        part = cells.astype(jnp.bfloat16)
        cells = cells - part.astype(F32)
        moved = jnp.dot(part, half, preferred_element_type=F32)
        total = moved if total is None else total + moved
    return total


def pick(rows, cols, keep):
    return jnp.where(keep(iota((rows, cols), 0), iota((rows, cols), 1)), 1.0, 0.0).astype(F32)


def fine_down_kernel(meta, bricks, u, f, a, recv, rc, u_b, f_r, f_b, i_r, i_b, u_r, resid, small):
    _, _, bit_x, bit_y, _ = place_of(meta, bricks)
    own = odd(32, 128)
    for t in range(16):
        here = (OWN + t, slice(0, 32), slice(0, 128))
        u_b[here] = pair_of(u, t, False, own)
        f_r[here], f_b[here] = pair_of(f, t, True, own), pair_of(f, t, False, own)
        i_r[here], i_b[here] = 1.0 / (pair_of(a, t, True, own) + 6.0), 1.0 / (pair_of(a, t, False, own) + 6.0)
    unpack_shell(recv, (u_b, f_r, f_b, i_r, i_b), bit_x, bit_y)
    zero = jnp.zeros((40, 256), F32)
    for k in (0, 25):
        u_r[k] = zero
        u_b[k] = zero
    for k in (1, 24):
        f_b[k] = zero
        i_b[k] = zero
    row = iota((40, 256), 0)
    y0 = is_zero(bit_y, (40, 256))
    y1 = jnp.logical_not(y0)
    mask = odd(40, 256)
    cut = (y0 & (row == 0), y1 & (row == 31))
    half_sweep(u_r, u_b, f_r, i_r, 1, 25, True, mask, 1.0, 0, cut)
    half_sweep(u_b, u_r, f_b, i_b, 1, 25, False, mask, 1.0, 0)
    half_sweep(u_r, u_b, f_r, i_r, 2, 24, True, mask, 1.0, 0)
    half_sweep(u_b, u_r, f_b, i_b, 3, 23, False, mask, 1.0, 0)
    for t in range(16):
        total = around(u_b, OWN + t, True, mask, 0)[0:32, 0:128]
        diag = pair_of(a, t, True, own) + 6.0
        here = (OWN + t, slice(0, 32), slice(0, 128))
        resid[t] = f_r[here] + total - diag * u_r[here]
    pack_coarse(resid, small, rc)


def slot_of(member, me):
    return jnp.where((member >> 2) == (me >> 2), 0, 4) + ((me - member) & 3)


def faces_kernel(meta, bricks, *refs):
    boxes, (out, held) = refs[:8], refs[8:]
    slab, me = meta[0], meta[1]
    for i, box in enumerate(boxes):
        held[i] = box[...]
    start = jnp.where(me < 4, 3, 0)
    for i in range(4):
        member = jnp.where(me < 4, bricks[slab, 4 + i], bricks[slab, i])
        out[i, 0:5] = held[slot_of(member, me), pl.ds(start, 5)]
        for j in range(5, out.shape[1]):
            out[i, j] = held[slot_of(bricks[slab, 2 * i + j - 5], me), 8]


def sort_sides(me, one, two, low, high):
    @pl.when(me < 4)
    def _():
        low[...] = one[...]
        high[...] = two[...]

    @pl.when(me >= 4)
    def _():
        low[...] = two[...]
        high[...] = one[...]


def assemble(meta, bricks, boxes, one, two, red, black, held, low, high):
    slab, me = meta[0], meta[1]
    for i, box in enumerate(boxes):
        held[i] = box[...]
    sort_sides(me, one, two, low, high)
    left = iota((16, 128), 1) < 64

    def put(k, by, west, east):
        rows = slice(16 * by, 16 * by + 16)
        red[k, rows] = jnp.where(left, west, pltpu.roll(east, 64, 1))
        black[k, rows] = jnp.where(left, pltpu.roll(west, 64, 1), east)

    for by in range(2):
        for bz in range(2):
            west = slot_of(bricks[slab, 2 * by + 4 * bz], me)
            east = slot_of(bricks[slab, 2 * by + 4 * bz + 1], me)
            for j in range(8):
                put(6 + 8 * bz + j, by, held[west, j], held[east, j])
        for j in range(5):
            put(1 + j, by, low[2 * by, j], low[2 * by + 1, j])
            put(22 + j, by, high[2 * by, j], high[2 * by + 1, j])


def to_bottom(planes, small, half):
    for n in range(22):
        small[16 * n : 16 * n + 16] = planes[n, pl.ds(0, 16, stride=2), :] + planes[n, pl.ds(1, 16, stride=2), :]
    fold = pick(128, 128, lambda r, c: (r >> 1) == c - 64 * half) * 0.125
    return jnp.dot(small[...], fold, precision=EXACT, preferred_element_type=F32).reshape(22, 16, 128)


def coarse_coef_kernel(meta, bricks, *refs):
    boxes, (one, two) = refs[:8], refs[8:10]
    a_r, i_r, i_b, ab, coef = refs[10:15]
    held, low, high, a_b, planes, small = refs[15:]
    slab, me = meta[0], meta[1]
    assemble(meta, bricks, boxes, one, two, a_r, a_b, held, low, high)
    for p in range(8):
        coef[0, p] = low[p >> 1, 5 + (p & 1)]
        coef[1, p] = held[slot_of(bricks[slab, p], me), 8]
        coef[2, p] = high[p >> 1, 5 + (p & 1)]
    for k in range(1, 27):
        keep = jnp.full((32, 128), 0, jnp.int32) == 0
        if k < 6:
            keep = jnp.logical_not(is_zero(slab, (32, 128)))
        if k >= 22:
            keep = jnp.logical_not(is_zero(slab - (SLABS - 1), (32, 128)))
        i_r[k] = jnp.where(keep, 1.0 / (a_r[k] + 1.5), 0.0)
        i_b[k] = jnp.where(keep, 1.0 / (a_b[k] + 1.5), 0.0)
    for n in range(22):
        planes[n] = a_r[3 + n] + a_b[3 + n]
    ab[...] = to_bottom(planes, small, 1)


def coarse_down_kernel(meta, bricks, *refs):
    boxes, (one, two, weights, a_r, i_r, i_b, ab) = refs[:8], refs[8:15]
    rb, rb_send, part, e_b, r_r, r_b = refs[15:21]
    held, low, high, e_r, resid, small = refs[21:]
    me = meta[1]
    assemble(meta, bricks, boxes, one, two, r_r, r_b, held, low, high)
    for k in (0, 27):
        e_r[k] = jnp.zeros((32, 128), F32)
        e_b[k] = jnp.zeros((32, 128), F32)
    for k in range(1, 27):
        e_r[k] = r_r[k] * i_r[k]
    mask = odd(32, 128)
    half_sweep(e_b, e_r, r_b, i_b, 1, 27, False, mask, 0.25, 2)
    half_sweep(e_r, e_b, r_r, i_r, 1, 27, True, mask, 0.25, 2)
    half_sweep(e_b, e_r, r_b, i_b, 1, 27, False, mask, 0.25, 2)
    for n in range(22):
        k = n + 3
        total = 0.25 * around(e_b, k, True, mask, 2)
        resid[n] = r_r[k] + total - (a_r[k] + 1.5) * e_r[k]
    rb[...] = to_bottom(resid, small, 0) + ab[...]
    rb_send[0:18] = rb[pl.ds(jnp.where(me < 4, 1, 3), 18)]
    total = jnp.zeros((16, 128), F32)
    for i in range(16):
        total = total + rb[3 + i] * weights[i]
    total = total[0:8] + total[8:16]
    part[...] = total
    rb_send[18, 0:8] = total
    rb_send[18, 8:16] = total


def bottom_kernel(meta, rb, one, two, es, e_r, e_b, g_r, g_b, i_r, i_b, low, high):
    slab, me = meta[0], meta[1]
    sort_sides(me, one, two, low, high)
    mask = odd(16, 128)
    left = iota((16, 128), 1) < 64
    zero = jnp.zeros((16, 128), F32)
    for k in (0, 27):
        e_r[k] = zero
        e_b[k] = zero
    for j in range(26):
        planes = []
        for n in (2 * j, 2 * j + 1):
            planes.append(low[n] if n < 18 else rb[n - 15] if n < 34 else high[n - 34])
        keep = left
        if j < 9:
            keep = left & jnp.logical_not(is_zero(slab, (16, 128)))
        if j >= 17:
            keep = left & jnp.logical_not(is_zero(slab - (SLABS - 1), (16, 128)))
        for red in (True, False):
            cells = jnp.where(mask, planes[1], planes[0]) if red else jnp.where(mask, planes[0], planes[1])
            force = jnp.where(left, cells, 0.0)
            inverse = jnp.where(keep, 1.0 / (pltpu.roll(cells, 64, 1) + 0.375), 0.0)
            if red:
                g_r[1 + j], i_r[1 + j], e_r[1 + j] = force, inverse, force * inverse
            else:
                g_b[1 + j], i_b[1 + j] = force, inverse
    for n in range(2, 17):
        far = (20 - n) // 2
        if n % 2:
            half_sweep(e_r, e_b, g_r, i_r, 10 - far, 18 + far, True, mask, 0.0625, 1)
        else:
            half_sweep(e_b, e_r, g_b, i_b, 10 - far, 18 + far, False, mask, 0.0625, 1)
    for i in range(22):
        k, upper = (15 + i) // 2 + 1, (15 + i) % 2
        es[i] = jnp.where(mask, e_r[k], e_b[k]) if upper else jnp.where(mask, e_b[k], e_r[k])


def weights_kernel(meta, coef, out, t_r, t_b, w_r, w_b, i_r, i_b):
    slab = meta[0]
    lane = iota((8, 128), 1)

    def plane(part, z):
        rows = []
        for by in range(2):
            place, shift = 4 * (z >> 3) + 2 * by, 32 * (z & 3)
            here = slice(8 * ((z & 7) >> 2), 8 * ((z & 7) >> 2) + 8)
            west = pltpu.roll(coef[part, place, here], (128 - shift) % 128, 1)
            east = pltpu.roll(coef[part, place + 1, here], (160 - shift) % 128, 1)
            rows.append(jnp.where(lane < 32, west, east))
        return jnp.concatenate(rows, 0)

    mask = odd(16, 128)
    left = iota((16, 128), 1) < 64
    zero = jnp.zeros((16, 128), F32)
    for k in (0, 25):
        t_r[k] = zero
        t_b[k] = zero
    for j in range(24):
        lower, upper = (plane((2 * j + i) // 16, (2 * j + i) % 16) for i in range(2))
        keep = left
        if j < 8:
            keep = left & jnp.logical_not(is_zero(slab, (16, 128)))
        if j >= 16:
            keep = left & jnp.logical_not(is_zero(slab - (SLABS - 1), (16, 128)))
        i_r[1 + j] = jnp.where(keep, 1.0 / (jnp.where(mask, upper, lower) + 0.375), 0.0)
        i_b[1 + j] = jnp.where(keep, 1.0 / (jnp.where(mask, lower, upper) + 0.375), 0.0)
    for k in range(1, 25):
        t_b[k] = i_b[k]
        w_b[k] = i_b[k]
    for k in range(1, 25):
        t = i_r[k] * (1.0 + 0.0625 * around(t_b, k, True, mask, 1))
        t_r[k] = t
        w_r[k] = t
    for n in range(3, 17):
        far = (17 - n) // 2
        for k in range(9 - far, 17 + far):
            if n % 2:
                t = i_b[k] * (0.0625 * around(t_r, k, False, mask, 1))
                t_b[k] = t
                w_b[k] = w_b[k] + t
            else:
                t = i_r[k] * (0.0625 * around(t_b, k, True, mask, 1))
                t_r[k] = t
                w_r[k] = w_r[k] + t
    for j in range(8):
        red, black = w_r[9 + j], w_b[9 + j]
        out[2 * j] = jnp.where(mask, black, red)
        out[2 * j + 1] = jnp.where(mask, red, black)


def up_kernel(
    meta, bricks, sum_0, sum_1, sum_2, sum_3, es, ec_b, r_r, r_b, ci_r, ci_b, u1_b, f_r, f_b, i_r, i_b, out,
    e_r, e_b, small, wide, planes, tall, u_r, u_b,
):
    slab, _, bit_x, bit_y, bit_z = place_of(meta, bricks)
    total = (sum_0[...] + sum_1[...]) + (sum_2[...] + sum_3[...])
    mean = jnp.sum(total) * (1.0 / (SLABS * 16 * 16 * 64))
    base = 8 * bit_z
    no_low = jnp.where((slab == 0) & (bit_z == 0), 0, 1)
    no_high = jnp.where((slab == SLABS - 1) & (bit_z == 1), 0, 1)
    for j in range(14):
        shifted = es[base + j] - mean
        if j < 3:
            shifted = jnp.where(is_zero(no_low, (16, 128)), 0.0, shifted)
        if j >= 11:
            shifted = jnp.where(is_zero(no_high, (16, 128)), 0.0, shifted)
        small[16 * j : 16 * j + 16] = shifted
    spread = pick(128, 128, lambda r, c: r == (c >> 1))
    small[...] = select_dot(small[...], spread)
    for j in range(14):
        rows = small[16 * j : 16 * j + 16]
        wide[j, pl.ds(0, 16, stride=2), :] = rows
        wide[j, pl.ds(1, 16, stride=2), :] = rows
    for k in (0, 15):
        e_r[k] = jnp.zeros((32, 128), F32)
        e_b[k] = jnp.zeros((32, 128), F32)
    for j in range(14):
        e_b[1 + j] = ec_b[base + 3 + j] + wide[j]
    coarse = odd(32, 128)
    r_r, r_b, ci_r, ci_b = (grid.at[pl.ds(base + 2, 16)] for grid in (r_r, r_b, ci_r, ci_b))
    half_sweep(e_r, e_b, r_r, ci_r, 1, 15, True, coarse, 0.25, 2)
    half_sweep(e_b, e_r, r_b, ci_b, 2, 14, False, coarse, 0.25, 2)
    half_sweep(e_r, e_b, r_r, ci_r, 2, 14, True, coarse, 0.25, 2)
    half_sweep(e_b, e_r, r_b, ci_b, 3, 13, False, coarse, 0.25, 2)
    for n in range(20):
        k, upper = n // 2 + 3, n % 2
        red, black = e_r[k], e_b[k]
        planes[32 * n : 32 * n + 32] = jnp.where(coarse, red, black) if upper else jnp.where(coarse, black, red)

    lane = iota((128, 256), 1)
    x0 = is_zero(bit_x, (128, 256))
    start = jnp.where(lane < 128, 64 * bit_x + (lane >> 1), (lane >> 1) + jnp.where(x0, 0, -64))
    usable = (lane < 128) | (x0 & (lane < 136)) | (jnp.logical_not(x0) & (lane >= 248))
    spread = jnp.where(usable & (iota((128, 256), 0) == start), 1.0, 0.0).astype(F32)
    tall_rows = select_dot(planes[...], spread)
    for n in range(20):
        rows = tall_rows[32 * n : 32 * n + 32]
        for h in range(2):
            tall[n, h, pl.ds(0, 32, stride=2), :] = rows[:, 128 * h : 128 * h + 128]
            tall[n, h, pl.ds(1, 32, stride=2), :] = rows[:, 128 * h : 128 * h + 128]
    for k in (0, 21):
        u_r[k] = jnp.zeros((40, 256), F32)
        u_b[k] = jnp.zeros((40, 256), F32)
    row = iota((8, 128), 0)
    y0 = is_zero(bit_y)
    in_y = (y0 & (row != 7)) | (jnp.logical_not(y0) & (row != 0))
    own_start = pl.multiple_of(32 * bit_y, 32)
    side_start = pl.multiple_of(32 - 8 * bit_y, 8)
    for n in range(20):
        for h in range(2):
            lanes = slice(128 * h, 128 * h + 128)
            side = jnp.where(in_y, tall[n, h, pl.ds(side_start, 8), :], 0.0)
            u_b[1 + n, 0:32, lanes] = u1_b[3 + n, 0:32, lanes] + tall[n, h, pl.ds(own_start, 32), :]
            u_b[1 + n, 32:40, lanes] = u1_b[3 + n, 32:40, lanes] + side
    mask = odd(40, 256)
    f_r, f_b, i_r, i_b = (grid.at[2:24] for grid in (f_r, f_b, i_r, i_b))
    half_sweep(u_r, u_b, f_r, i_r, 1, 21, True, mask, 1.0, 0)
    half_sweep(u_b, u_r, f_b, i_b, 2, 20, False, mask, 1.0, 0)
    half_sweep(u_r, u_b, f_r, i_r, 2, 20, True, mask, 1.0, 0)
    half_sweep(u_b, u_r, f_b, i_b, 3, 19, False, mask, 1.0, 0)
    own = odd(32, 128)
    for t in range(16):
        red, black = u_r[3 + t, 0:32, 0:128], u_b[3 + t, 0:32, 0:128]
        out[0, 2 * t] = jnp.where(own, black, red)
        out[0, 2 * t + 1] = jnp.where(own, red, black)


def swap_cores(x):
    return lax.ppermute(x, "level", [(0, 1), (1, 0)])


def to_slabs(x, up_first, wrap=False):
    pairs = []
    for s in range(SLABS if wrap else SLABS - 1):
        for m in range(8):
            low, high = s * 8 + m, (s + 1) % SLABS * 8 + m
            pairs.append((low, high) if (m < 4) == up_first else (high, low))
    return lax.ppermute(x, ALL, pairs)


def around_chips(x):
    return [x] + [lax.ppermute(x, "bottom", [(i, (i + d) % 4) for i in range(4)]) for d in range(1, 4)]


def both_cores(boxes):
    return boxes + [swap_cores(box) for box in boxes]


def fours_apart(x):
    beside = [(8 * s + m, 8 * ((s + (4 if m < 4 else 12)) % SLABS) + m) for s in range(SLABS) for m in range(8)]
    across = [(s, (s + 8) % SLABS) for s in range(SLABS)]
    return lax.ppermute(x, ALL, beside), lax.ppermute(x, "slab", across)


def among(x):
    return lax.all_to_all(x, LB, split_axis=0, concat_axis=0, tiled=True)


def body(u_init, source, coeffs, brick_map):
    meta = jnp.stack([lax.axis_index("slab"), lax.axis_index(LB)]).astype(jnp.int32)
    smem = [meta, brick_map]
    fine = (26, 40, 256)
    packed, ac = run(
        first_kernel, [(8, SENT, 8, 128), (9, 16, 128)], smem, [u_init, source, coeffs],
        [(8, 32, 128), (16, 32, 128), (256, 128), (1, 32, 32, 128)],
    )
    got = among(packed)
    leaving = run(cross_kernel, [(4, FACE, 8, 128)], smem, [got])
    leaving, ac = lax.optimization_barrier((leaving, ac))
    cross = to_slabs(leaving, False)
    ac_boxes = around_chips(ac)
    sent = run(mid_kernel, [(8, GOT, 8, 128)], smem, [got, cross], [(12, FACE, 8, 128)])
    sent, *ac_boxes = lax.optimization_barrier((sent, *ac_boxes))
    halo = among(sent)
    faces = (4, 5, 16, 128)
    coarse = (28, 32, 128)
    held = [(8, 8, 16, 128), faces, faces]
    ac_boxes = both_cores(ac_boxes)
    ac_held = [(8, 9, 16, 128), (4, 7, 16, 128), (4, 7, 16, 128)]
    ac_cross = to_slabs(run(faces_kernel, ac_held[1:2], smem, ac_boxes, ac_held[:1]), True)
    ac_other = swap_cores(ac_cross)
    halo, ac_cross, ac_other = lax.optimization_barrier((halo, ac_cross, ac_other))
    rc, u_b, f_r, f_b, i_r, i_b = run(
        fine_down_kernel, [(8, 16, 128)] + [fine] * 5, smem, [u_init, source, coeffs, halo],
        [fine, (16, 32, 128), (256, 128)],
    )
    boxes = both_cores(around_chips(rc))
    leaving = run(faces_kernel, [faces], smem, boxes, held[:1])
    leaving, ac_cross, ac_other = lax.optimization_barrier((leaving, ac_cross, ac_other))
    cross = to_slabs(leaving, True)
    ca_r, ci_r, ci_b, ab, coef = run(
        coarse_coef_kernel, [coarse] * 3 + [(22, 16, 128), (3, 8, 16, 128)], smem, ac_boxes + [ac_cross, ac_other],
        ac_held + [coarse, (22, 32, 128), (352, 128)],
    )
    weights = run(weights_kernel, [(16, 16, 128)], [meta], [coef], [(26, 16, 128)] * 6)
    cross, weights, ca_r, ci_r, ci_b, ab = lax.optimization_barrier((cross, weights, ca_r, ci_r, ci_b, ab))
    rb, rb_send, part, ec_b, r_r, r_b = run(
        coarse_down_kernel, [(22, 16, 128), (19, 16, 128), (8, 128)] + [coarse] * 3, smem,
        boxes + [cross, swap_cores(cross), weights, ca_r, ci_r, ci_b, ab],
        held + [coarse, (22, 32, 128), (352, 128)],
    )
    cross = to_slabs(rb_send, True, wrap=True)
    far = lax.ppermute(part, "slab", [(s, (s - 2) % SLABS) for s in range(SLABS)])
    cross, far = lax.optimization_barrier((cross, far))
    other = swap_cores(cross)
    part = (part + far) + (cross[18, 0:8] + other[18, 0:8])
    near, far = fours_apart(part)
    sums = [part, near, far, swap_cores(near)]
    bottom = (28, 16, 128)
    es = run(
        bottom_kernel, [(22, 16, 128)], [meta], [rb, cross, other],
        [bottom] * 6 + [(19, 16, 128)] * 2,
    )
    return run(
        up_kernel, [(1, 32, 32, 128)], smem,
        sums + [es, ec_b, r_r, r_b, ci_r, ci_b, u_b, f_r, f_b, i_r, i_b],
        [(16, 32, 128)] * 2 + [(224, 128), (14, 32, 128), (640, 128), (20, 2, 64, 128), (22, 40, 256), (22, 40, 256)],
    )


def solution(mesh):
    placed = P(ALL, None, None, None)
    return jax.shard_map(
        body, mesh=mesh, in_specs=(placed, placed, placed, P()), out_specs=placed, check_vma=False
    )
```
